32 devices in a mesh: gx: 4 (over y, core), gy: 8 (over z, x).
Axes of the slice: x: 2, y: 2, z: 4, core: 2. Of those that a mesh axis runs over, the one named last changes fastest.
Arguments:
- adjoint_in: float32 [19, 64, 4, 1024], P(None, 'gx', None, 'gy'), may hold values from -6 to 6
- velocity: bfloat16 [2, 3, 64, 4, 1024], P(None, None, 'gx', None, 'gy')
- solid_tiles: int32 [16, 4, 256], P('gx', None, 'gy'), may hold values from 0 to 1, as said below
- link_blocked: int32 [18, 64, 4, 1024], P(None, 'gx', None, 'gy'), may hold values from 0 to 1, as said below
Outputs:
- adjoint_out: float32 [19, 64, 4, 1024], P(None, 'gx', None, 'gy')
- drag_sens: float32 [1], replicated
The draws below stay inside these ranges and needn't reach their ends.
Inputs may be any that keep to these rules, and one draw needn't show every extreme that they name: `solid_tiles`: 1 on the levels below a tile's building height, heights 0 to 3 per tile. `link_blocked`: entry i - 1 is 1 exactly where the cell x + c_i (periodic in the plane) is solid or lies outside the 4 levels.
All inputs are finite; a program needn't handle non-finite values.
Results may differ from the reference program's by a relative error of at most 0.0003.
Values sent between devices are 32-bit elements; how exact they have to be, the bound alone decides.
No kernel may reach another device: no remote copies, remote signals or barrier semaphores. Data moves between devices by JAX's collectives and lax.ppermute only.
A program may use at most 64 MiB of HBM per device.

```python
import math
import jax
import jax.numpy as jnp
from jax import lax

Q = 19
Z = 4
TILE = 4
STEPS = 2
NX = 64
NY = 1024


lattice_speeds = ((0, 0, 0), (1, 0, 0), (-1, 0, 0), (0, 1, 0), (0, -1, 0), (0, 0, 1), (0, 0, -1), (1, 1, 0), (-1, -1, 0), (1, -1, 0), (-1, 1, 0), (1, 0, 1), (-1, 0, -1), (1, 0, -1), (-1, 0, 1), (0, 1, 1), (0, -1, -1), (0, 1, -1), (0, -1, 1))


def solid_tile_grid(key):
    heights = jnp.maximum(jax.random.randint(jax.random.fold_in(key, 11), (NX // TILE, NY // TILE), -4, Z), 0)
    level = lax.broadcasted_iota(jnp.int32, (NX // TILE, Z, NY // TILE), 1)
    return (level < heights[:, None, :]).astype(jnp.int32)


def draw_solid_tiles(key, part):
    return solid_tile_grid(key)


def draw_link_blocked(key, part):
    tiles = solid_tile_grid(key)
    cells = jnp.repeat(jnp.repeat(tiles, TILE, axis=0), TILE, axis=2)
    flags = []
    for number in range(1, 19):
        speed = lattice_speeds[number]
        target = jnp.roll(cells, (-speed[0], -speed[1]), axis=(0, 2))
        if speed[2] == 1:
            target = jnp.concatenate([target[:, 1:], jnp.ones_like(target[:, :1])], axis=1)
        elif speed[2] == -1:
            target = jnp.concatenate([jnp.ones_like(target[:, :1]), target[:, :-1]], axis=1)
        flags.append(target)
    return jnp.stack(flags).astype(jnp.int32)


def draw_velocity(key, part):
    shape = (STEPS, 3, NX, Z, NY)
    position = lax.broadcasted_iota(jnp.float32, shape, 2) / (NX - 1)
    raw = jnp.clip(jax.random.normal(key, shape, jnp.float32), -3.0, 3.0)
    scale = 0.03 * (1.0 + 2.0 * position)
    return (raw * scale).astype(jnp.bfloat16)


def block_scale(own_key, shape, split, least, largest):
    gain = 1.0
    for dim, parts in split:
        steps = jax.random.uniform(jax.random.fold_in(jax.random.fold_in(own_key, 6), dim), (parts,), jnp.float32, least / len(split), largest / len(split))
        gain = gain * jnp.repeat(jnp.exp(steps), shape[dim] // parts).reshape((-1,) + (1,) * (len(shape) - 1 - dim))
    return gain


def noise(rng, shape, spread, limit, shards=(), dtype=jnp.bfloat16):
    array = spread * jax.random.normal(rng, shape, jnp.float32)
    if shards:
        array = array * block_scale(rng, shape, shards, -0.22, 0.18)
    return jnp.clip(array, -limit, limit).astype(dtype)


def setup_inputs(seed: int = 0) -> dict:
    seeds = jax.random.split(jax.random.key(seed), 5)
    adjoint_in = noise(seeds[0], (Q, NX, Z, NY), 1.0, 6.0, ((1, 4), (3, 8)), jnp.float32)
    velocity = draw_velocity(jax.random.fold_in(seeds[4], 71), 0)
    solid_tiles = draw_solid_tiles(jax.random.fold_in(seeds[4], 71), 0)
    link_blocked = draw_link_blocked(jax.random.fold_in(seeds[4], 71), 0)
    return dict(adjoint_in=adjoint_in, velocity=velocity, solid_tiles=solid_tiles, link_blocked=link_blocked)


lattice_speeds = ((0, 0, 0), (1, 0, 0), (-1, 0, 0), (0, 1, 0), (0, -1, 0), (0, 0, 1), (0, 0, -1), (1, 1, 0), (-1, -1, 0), (1, -1, 0), (-1, 1, 0), (1, 0, 1), (-1, 0, -1), (1, 0, -1), (-1, 0, 1), (0, 1, 1), (0, -1, -1), (0, 1, -1), (0, -1, 1))
lattice_weights = (1.0 / 3.0,) + (1.0 / 18.0,) * 6 + (1.0 / 36.0,) * 12
relax_rate = 1.6
drag_factor = 20.0

def opposite_of(number):
    return number + 1 if number % 2 == 1 else number - 1

def shift_level(field, lift):
    if lift == 1:
        return jnp.concatenate([field[:, 1:], jnp.zeros_like(field[:, :1])], axis=1)
    if lift == -1:
        return jnp.concatenate([jnp.zeros_like(field[:, :1]), field[:, :-1]], axis=1)
    return field

def adjoint_collide(moved, flow, fluid):
    speed_sq = flow[0] * flow[0] + flow[1] * flow[1] + flow[2] * flow[2]
    scalar_part = jnp.zeros_like(speed_sq)
    vector_part = [jnp.zeros_like(speed_sq) for axis_number in range(3)]
    drag_local = jnp.zeros_like(speed_sq)
    for number in range(19):
        speed = lattice_speeds[number]
        along = speed[0] * flow[0] + speed[1] * flow[1] + speed[2] * flow[2]
        weighted = lattice_weights[number] * moved[number]
        scalar_part = scalar_part + weighted * (1.0 + 3.0 * along + 4.5 * along * along - 1.5 * speed_sq)
        for axis_number in range(3):
            vector_part[axis_number] = vector_part[axis_number] + weighted * (3.0 * speed[axis_number] + 9.0 * along * speed[axis_number] - 3.0 * flow[axis_number])
        drag_local = drag_local + 3.0 * weighted * along
    results = []
    for number in range(19):
        speed = lattice_speeds[number]
        projected = scalar_part
        for axis_number in range(3):
            projected = projected + vector_part[axis_number] * (speed[axis_number] - flow[axis_number])
        results.append(fluid * ((1.0 - relax_rate) * moved[number] + relax_rate * projected))
    return (jnp.stack(results), jnp.sum(fluid * drag_local))

def reference(adjoint_in, velocity, solid_tiles, link_blocked):
    solid = jnp.repeat(jnp.repeat(solid_tiles, TILE, axis=0), TILE, axis=2)
    fluid = 1.0 - solid.astype(jnp.float32)
    state = adjoint_in
    total = jnp.zeros((), jnp.float32)
    for adjoint_step in range(STEPS):
        flow = velocity[adjoint_step].astype(jnp.float32)
        moved = [state[0]]
        for number in range(1, 19):
            speed = lattice_speeds[number]
            source = jnp.roll(state[number], (-speed[0], -speed[1]), axis=(0, 2))
            source = shift_level(source, speed[2])
            bounced = state[opposite_of(number)] + 2.0 * speed[0]
            moved.append(jnp.where(link_blocked[number - 1] == 1, bounced, source))
        state, drag_local = adjoint_collide(moved, flow, fluid)
        total = total + drag_local
    scale = drag_factor / math.sqrt(NX * NY * Z)
    return (state, (-scale * total).reshape(1))
```

```python
import math

import jax
import jax.numpy as jnp
from jax import lax
from jax.sharding import PartitionSpec as P

TILE = 4
STEPS = 2


lattice_speeds = (
    (0, 0, 0),
    (1, 0, 0),
    (-1, 0, 0),
    (0, 1, 0),
    (0, -1, 0),
    (0, 0, 1),
    (0, 0, -1),
    (1, 1, 0),
    (-1, -1, 0),
    (1, -1, 0),
    (-1, 1, 0),
    (1, 0, 1),
    (-1, 0, -1),
    (1, 0, -1),
    (-1, 0, 1),
    (0, 1, 1),
    (0, -1, -1),
    (0, 1, -1),
    (0, -1, 1),
)
lattice_weights = (1.0 / 3.0,) + (1.0 / 18.0,) * 6 + (1.0 / 36.0,) * 12
relax_rate = 1.6
drag_factor = 20.0


def with_halo(block, sides, width):
    for axis, dim in sides:
        count = lax.axis_size(axis)
        forward = [(i, i + 1) for i in range(count - 1)]
        forward.append((count - 1, 0))
        backward = [(target, source) for source, target in forward]
        low = lax.ppermute(
            lax.slice_in_dim(block, block.shape[dim] - width, None, axis=dim), axis, forward
        )
        high = lax.ppermute(lax.slice_in_dim(block, 0, width, axis=dim), axis, backward)
        block = jnp.concatenate([low, block, high], axis=dim)
    return block


def opposite_of(number):
    return number + 1 if number % 2 == 1 else number - 1


def shift_level(field, lift):
    if lift == 1:
        return jnp.concatenate([field[:, 1:], jnp.zeros_like(field[:, :1])], axis=1)
    if lift == -1:
        return jnp.concatenate([jnp.zeros_like(field[:, :1]), field[:, :-1]], axis=1)
    return field


def adjoint_collide(moved, flow, fluid):
    speed_sq = flow[0] * flow[0] + flow[1] * flow[1] + flow[2] * flow[2]
    scalar_part = jnp.zeros_like(speed_sq)
    vector_part = [jnp.zeros_like(speed_sq) for axis_number in range(3)]
    drag_local = jnp.zeros_like(speed_sq)
    for number in range(19):
        speed = lattice_speeds[number]
        along = speed[0] * flow[0] + speed[1] * flow[1] + speed[2] * flow[2]
        weighted = lattice_weights[number] * moved[number]
        scalar_part = scalar_part + weighted * (
            1.0 + 3.0 * along + 4.5 * along * along - 1.5 * speed_sq
        )
        for axis_number in range(3):
            vector_part[axis_number] = vector_part[axis_number] + weighted * (
                3.0 * speed[axis_number]
                + 9.0 * along * speed[axis_number]
                - 3.0 * flow[axis_number]
            )
        drag_local = drag_local + 3.0 * weighted * along
    results = []
    for number in range(19):
        speed = lattice_speeds[number]
        projected = scalar_part
        for axis_number in range(3):
            projected = projected + vector_part[axis_number] * (
                speed[axis_number] - flow[axis_number]
            )
        results.append(fluid * ((1.0 - relax_rate) * moved[number] + relax_rate * projected))
    return (jnp.stack(results), fluid * drag_local)


def stream_back(padded, centre, blocked, span_x, span_y):
    moved = [centre[0]]
    for number in range(1, 19):
        speed = lattice_speeds[number]
        source = padded[
            number, 1 + speed[0] : 1 + speed[0] + span_x, :, 1 + speed[1] : 1 + speed[1] + span_y
        ]
        source = shift_level(source, speed[2])
        bounced = centre[opposite_of(number)] + 2.0 * speed[0]
        moved.append(jnp.where(blocked[number - 1] == 1, bounced, source))
    return moved


def per_device(adjoint_in, velocity, solid_tiles, link_blocked):
    rows_x = adjoint_in.shape[1]
    rows_y = adjoint_in.shape[3]
    levels = adjoint_in.shape[2]
    solid = jnp.repeat(jnp.repeat(solid_tiles, TILE, axis=0), TILE, axis=2)
    fluid = 1.0 - solid.astype(jnp.float32)
    state = adjoint_in
    step_terms = []
    for adjoint_step in range(STEPS):
        flow = velocity[adjoint_step].astype(jnp.float32)
        padded = with_halo(state, (("gx", 1), ("gy", 3)), 1)
        moved = stream_back(padded, state, link_blocked, rows_x, rows_y)
        state, drag_field = adjoint_collide(moved, flow, fluid)
        step_terms.append(jnp.sum(drag_field))
    count = lax.axis_size("gx") * lax.axis_size("gy")
    own = step_terms[0] + step_terms[1]
    shared = lax.all_to_all(
        jnp.broadcast_to(own.reshape(1, 1, 1), (count, 1, 128)),
        ("gx", "gy"),
        split_axis=0,
        concat_axis=0,
        tiled=True,
    )
    total = jnp.sum(shared[:, 0, 0])
    cell_count = rows_x * lax.axis_size("gx") * rows_y * lax.axis_size("gy") * levels
    scale = drag_factor / math.sqrt(cell_count)
    return (state, (-scale * total).reshape(1))


def solution(mesh):
    placed = (
        P(None, "gx", None, "gy"),
        P(None, None, "gx", None, "gy"),
        P("gx", None, "gy"),
        P(None, "gx", None, "gy"),
    )
    return jax.shard_map(
        per_device,
        mesh=mesh,
        in_specs=placed,
        out_specs=(P(None, "gx", None, "gy"), P()),
        check_vma=False,
    )
```

```python
import math

import jax
import jax.numpy as jnp
from jax import lax
from jax.experimental import pallas as pl
from jax.experimental.pallas import tpu as pltpu
from jax.sharding import PartitionSpec as P

TILE = 4
STEPS = 2

lattice_speeds = (
    (0, 0, 0),
    (1, 0, 0),
    (-1, 0, 0),
    (0, 1, 0),
    (0, -1, 0),
    (0, 0, 1),
    (0, 0, -1),
    (1, 1, 0),
    (-1, -1, 0),
    (1, -1, 0),
    (-1, 1, 0),
    (1, 0, 1),
    (-1, 0, -1),
    (1, 0, -1),
    (-1, 0, 1),
    (0, 1, 1),
    (0, -1, -1),
    (0, 1, -1),
    (0, -1, 1),
)
relax_rate = 1.6
drag_factor = 20.0
LEVELS = 4
LANES = 128
GUARD = 8

x_up = [n for n in range(19) if lattice_speeds[n][0] == 1]
x_down = [n for n in range(19) if lattice_speeds[n][0] == -1]
y_up = [n for n in range(19) if lattice_speeds[n][1] == 1]
y_down = [n for n in range(19) if lattice_speeds[n][1] == -1]
vmem = pl.BlockSpec(memory_space=pltpu.VMEM)


def opposite_of(number):
    return number + 1 if number % 2 == 1 else number - 1


def lane_index():
    return lax.broadcasted_iota(jnp.int32, (8, LANES), 1)


def pack_edges(read, rows, x_low, x_high, y_low, y_high):
    lane = lane_index()
    groups = rows // 8
    for slot, number in enumerate(x_up):
        x_low[slot] = read(number, 0, LEVELS)
    for slot, number in enumerate(x_down):
        x_high[slot] = read(number, rows - LEVELS, LEVELS)
    for numbers, out, edge in ((y_up, y_low, 0), (y_down, y_high, LANES - 1)):
        packed = jnp.zeros((8, LANES), jnp.float32)
        for slot, number in enumerate(numbers):
            for group in range(groups):
                place = slot * groups + group
                value = pltpu.roll(read(number, 8 * group, 8), (place - edge) % LANES, 1)
                packed = jnp.where(lane == place, value, packed)
        out[...] = packed


def fill_gathered(read, rows, gathered, halos):
    x_after, x_before, y_after, y_before, corners = halos
    lane = lane_index()
    groups = rows // 8
    y_after_all = y_after[...]
    y_before_all = y_before[...]
    for number in range(1, 19):
        cx, cy, cz = lattice_speeds[number]
        for group in range(groups):
            value = read(number, 8 * group, 8)
            if cy == 1:
                place = y_up.index(number) * groups + group
                halo = pltpu.roll(y_after_all, (LANES - 1 - place) % LANES, 1)
                value = jnp.where(lane == LANES - 1, halo, pltpu.roll(value, LANES - 1, 1))
            elif cy == -1:
                place = y_down.index(number) * groups + group
                halo = pltpu.roll(y_before_all, (-place) % LANES, 1)
                value = jnp.where(lane == 0, halo, pltpu.roll(value, 1, 1))
            gathered[number, pl.ds(GUARD + 8 * group, 8), :] = value
        if cx == 0:
            continue
        if cx == 1:
            row = x_after[x_up.index(number)]
            first = GUARD + rows
        else:
            row = x_before[x_down.index(number)]
            first = GUARD - LEVELS
        if cy != 0:
            corner = corners[(cx, cy)][...]
            edge = 0 if cy == 1 else LANES - 1
            row = jnp.where(lane[:LEVELS] == edge, corner, row)
            row = pltpu.roll(row, (-cy) % LANES, 1)
        gathered[number, pl.ds(first, LEVELS), :] = row


def collide(moved, flow, fluid):
    ux, uy, uz = flow
    total = {n: moved[n] + moved[n + 1] for n in range(1, 19, 2)}
    gap = {n: moved[n] - moved[n + 1] for n in range(1, 19, 2)}
    xy, xz, yz = total[7] + total[9], total[11] + total[13], total[15] + total[17]
    axis_x, axis_y, axis_z = 2.0 * total[1], 2.0 * total[3], 2.0 * total[5]
    density = 12.0 * moved[0] + (axis_x + axis_y + axis_z) + (xy + xz + yz)
    pxx = axis_x + xy + xz
    pyy = axis_y + xy + yz
    pzz = axis_z + xz + yz
    pxy = total[7] - total[9]
    pxz = total[11] - total[13]
    pyz = total[15] - total[17]
    dx = 2.0 * gap[1] + (gap[7] + gap[9]) + (gap[11] + gap[13])
    dy = 2.0 * gap[3] + (gap[7] - gap[9]) + (gap[15] + gap[17])
    dz = 2.0 * gap[5] + (gap[11] - gap[13]) + (gap[15] - gap[17])
    vx = pxx * ux + pxy * uy + pxz * uz
    vy = pxy * ux + pyy * uy + pyz * uz
    vz = pxz * ux + pyz * uy + pzz * uz
    speed_sq = ux * ux + uy * uy + uz * uz
    drag = fluid * (ux * dx + uy * dy + uz * dz)
    scaled = (relax_rate / 36.0) * fluid
    base = scaled * (density + 1.5 * (speed_sq * density) - 4.5 * (ux * vx + uy * vy + uz * vz))
    scaled3 = 3.0 * scaled
    bx = scaled3 * (dx + 3.0 * vx - ux * density)
    by = scaled3 * (dy + 3.0 * vy - uy * density)
    bz = scaled3 * (dz + 3.0 * vz - uz * density)
    keep = (1.0 - relax_rate) * fluid
    results = [keep * moved[0] + base]
    for number in range(1, 19, 2):
        along = None
        for speed, part in zip(lattice_speeds[number], (bx, by, bz)):
            if speed == 0:
                continue
            if along is None:
                along = part if speed == 1 else -part
            else:
                along = along + part if speed == 1 else along - part
        results.append(keep * moved[number] + (base + along))
        results.append(keep * moved[number + 1] + (base - along))
    return results, drag


def spread_fluid(solid):
    tiles = solid.shape[1]
    row = lax.broadcasted_iota(jnp.int32, (tiles, LANES), 0)
    column = lax.broadcasted_iota(jnp.int32, (tiles, LANES), 1)
    spread = (column // TILE == row).astype(jnp.float32)
    fluid = 1.0 - jnp.dot(solid[...].astype(jnp.float32), spread, preferred_element_type=jnp.float32)
    blocks = []
    for tile_row in range(solid.shape[0] // LEVELS):
        part = fluid[tile_row * LEVELS : (tile_row + 1) * LEVELS]
        blocks.append(jnp.concatenate([part, part], axis=0))
    return blocks


def run_step(step, read, write, gathered, velocity, blocked, solid, rows):
    fluid_blocks = spread_fluid(solid)
    drag_sum = jnp.zeros((8, LANES), jnp.float32)
    for pair in range(rows // 16):
        flow_pair = [velocity[step, axis, pl.ds(16 * pair, 16), :].astype(jnp.float32) for axis in range(3)]
        for half in range(2):
            first = 16 * pair + 8 * half
            flow = [part[8 * half : 8 * half + 8] for part in flow_pair]
            here = [read(n, first, 8) for n in range(19)]
            moved = [here[0]]
            for number in range(1, 19):
                cx, cy, cz = lattice_speeds[number]
                source = gathered[number, pl.ds(GUARD + first + LEVELS * cx + cz, 8), :]
                bounced = here[opposite_of(number)]
                if cx != 0:
                    bounced = bounced + 2.0 * cx
                moved.append(jnp.where(blocked[number - 1, pl.ds(first, 8), :] == 1, bounced, source))
            results, drag = collide(moved, flow, fluid_blocks[first // (LEVELS * TILE)])
            for number in range(19):
                write(number, first, results[number])
            drag_sum = drag_sum + drag
    return drag_sum


def pack_kernel(state, x_low, x_high, y_low, y_high):
    def read(number, first, count):
        return state[number, pl.ds(first, count), :]

    pack_edges(read, state.shape[1], x_low, x_high, y_low, y_high)


def step_kernel(step, last, *refs):
    if last:
        (state, xa, xb, ya, yb, c0, c1, c2, c3, velocity, blocked, solid, before, out, shared, gathered) = refs
    else:
        (state, xa, xb, ya, yb, c0, c1, c2, c3, velocity, blocked, solid, out, drag_out) = refs[:14]
        x_low, x_high, y_low, y_high, gathered = refs[14:]
    rows = state.shape[1]

    def read(number, first, count):
        return state[number, pl.ds(first, count), :]

    def write(number, first, value):
        out[number, pl.ds(first, 8), :] = value

    corners = {(1, 1): c0, (-1, -1): c1, (1, -1): c2, (-1, 1): c3}
    fill_gathered(read, rows, gathered, (xa, xb, ya, yb, corners))
    drag_sum = run_step(step, read, write, gathered, velocity, blocked, solid, rows)
    if last:
        drag_sum = drag_sum + before[...]
        shared[...] = jnp.broadcast_to(jnp.sum(drag_sum), shared.shape)
    else:
        drag_out[...] = drag_sum

        def read_out(number, first, count):
            return out[number, pl.ds(first, count), :]

        pack_edges(read_out, rows, x_low, x_high, y_low, y_high)


def exchange(x_low, x_high, y_low, y_high):
    nx, ny = lax.axis_size("gx"), lax.axis_size("gy")
    from_after_x = [((i + 1) % nx, i) for i in range(nx)]
    from_before_x = [(i, (i + 1) % nx) for i in range(nx)]
    from_after_y = [((i + 1) % ny, i) for i in range(ny)]
    from_before_y = [(i, (i + 1) % ny) for i in range(ny)]

    def diagonal(cx, cy):
        return [
            (((i + cx) % nx) * ny + (j + cy) % ny, i * ny + j) for i in range(nx) for j in range(ny)
        ]

    both = ("gx", "gy")
    x_after = lax.ppermute(x_low, "gx", from_after_x)
    x_before = lax.ppermute(x_high, "gx", from_before_x)
    y_after = lax.ppermute(y_low, "gy", from_after_y)
    y_before = lax.ppermute(y_high, "gy", from_before_y)
    c0 = lax.ppermute(x_low[x_up.index(7)], both, diagonal(1, 1))
    c1 = lax.ppermute(x_high[x_down.index(8)], both, diagonal(-1, -1))
    c2 = lax.ppermute(x_low[x_up.index(9)], both, diagonal(1, -1))
    c3 = lax.ppermute(x_high[x_down.index(10)], both, diagonal(-1, 1))
    return x_after, x_before, y_after, y_before, c0, c1, c2, c3


def per_device(adjoint_in, velocity, solid_tiles, link_blocked):
    rows_x, levels, rows_y = adjoint_in.shape[1:]
    rows = rows_x * levels
    state = adjoint_in.reshape(19, rows, rows_y)
    flow = velocity.reshape(STEPS, 3, rows, rows_y)
    solid = solid_tiles.reshape(-1, solid_tiles.shape[2])
    blocked = link_blocked.reshape(18, rows, rows_y)
    edges = (
        jax.ShapeDtypeStruct((5, levels, rows_y), jnp.float32),
        jax.ShapeDtypeStruct((5, levels, rows_y), jnp.float32),
        jax.ShapeDtypeStruct((8, rows_y), jnp.float32),
        jax.ShapeDtypeStruct((8, rows_y), jnp.float32),
    )
    field = jax.ShapeDtypeStruct(state.shape, jnp.float32)
    scratch = [pltpu.VMEM((19, rows + 2 * GUARD, rows_y), jnp.float32)]
    params = pltpu.CompilerParams(vmem_limit_bytes=16 * 1024 * 1024)
    packed = pl.pallas_call(
        pack_kernel, out_shape=edges, in_specs=[vmem], out_specs=(vmem,) * 4, compiler_params=params
    )(state)
    halos = exchange(*packed)
    results = pl.pallas_call(
        lambda *refs: step_kernel(0, False, *refs),
        out_shape=(field, jax.ShapeDtypeStruct((8, rows_y), jnp.float32)) + edges,
        in_specs=[vmem] * 12,
        out_specs=(vmem,) * 6,
        scratch_shapes=scratch,
        compiler_params=params,
    )(state, *halos, flow, blocked, solid)
    state, drag = results[:2]
    halos = exchange(*results[2:])
    count = lax.axis_size("gx") * lax.axis_size("gy")
    state, own = pl.pallas_call(
        lambda *refs: step_kernel(1, True, *refs),
        out_shape=(field, jax.ShapeDtypeStruct((count, 1, rows_y), jnp.float32)),
        in_specs=[vmem] * 13,
        out_specs=(vmem,) * 2,
        scratch_shapes=scratch,
        compiler_params=params,
    )(state, *halos, flow, blocked, solid, drag)
    shared = lax.all_to_all(own, ("gx", "gy"), split_axis=0, concat_axis=0, tiled=True)
    cell_count = rows * rows_y * count
    scale = drag_factor / math.sqrt(cell_count) * 3.0 / 36.0
    total = jnp.sum(shared[:, 0, 0])
    return (state.reshape(adjoint_in.shape), (-scale * total).reshape(1))


def solution(mesh):
    placed = (
        P(None, "gx", None, "gy"),
        P(None, None, "gx", None, "gy"),
        P("gx", None, "gy"),
        P(None, "gx", None, "gy"),
    )
    return jax.shard_map(
        per_device,
        mesh=mesh,
        in_specs=placed,
        out_specs=(P(None, "gx", None, "gy"), P()),
        check_vma=False,
    )
```

```python
import math

import jax
import jax.numpy as jnp
from jax import lax
from jax.experimental import pallas as pl
from jax.experimental.pallas import tpu as pltpu
from jax.sharding import PartitionSpec as P

TILE = 4
STEPS = 2

lattice_speeds = (
    (0, 0, 0),
    (1, 0, 0),
    (-1, 0, 0),
    (0, 1, 0),
    (0, -1, 0),
    (0, 0, 1),
    (0, 0, -1),
    (1, 1, 0),
    (-1, -1, 0),
    (1, -1, 0),
    (-1, 1, 0),
    (1, 0, 1),
    (-1, 0, -1),
    (1, 0, -1),
    (-1, 0, 1),
    (0, 1, 1),
    (0, -1, -1),
    (0, 1, -1),
    (0, -1, 1),
)
relax_rate = 1.6
drag_factor = 20.0
LEVELS = 4
LANES = 128
GUARD = 8

x_up = [n for n in range(19) if lattice_speeds[n][0] == 1]
x_down = [n for n in range(19) if lattice_speeds[n][0] == -1]
y_up = [n for n in range(19) if lattice_speeds[n][1] == 1]
y_down = [n for n in range(19) if lattice_speeds[n][1] == -1]
vmem = pl.BlockSpec(memory_space=pltpu.VMEM)

FLOW = 19
SOLID = 22
SECOND = 23
QUANTITIES = 28
BEFORE_LANE = 16
AFTER_LANE = 32


def opposite_of(number):
    return number + 1 if number % 2 == 1 else number - 1


def lane_index(rows=8):
    return lax.broadcasted_iota(jnp.int32, (rows, LANES), 1)


def spread_solid(solid):
    tiles = solid.shape[1]
    row = lax.broadcasted_iota(jnp.int32, (tiles, LANES), 0)
    column = lax.broadcasted_iota(jnp.int32, (tiles, LANES), 1)
    spread = (column // TILE == row).astype(jnp.float32)
    cells = jnp.dot(solid[...].astype(jnp.float32), spread, preferred_element_type=jnp.float32)
    blocks = []
    for tile_row in range(solid.shape[0] // LEVELS):
        part = cells[tile_row * LEVELS : (tile_row + 1) * LEVELS]
        blocks.append(jnp.concatenate([part, part], axis=0))
    return blocks


def flow_blocks(velocity, step, rows):
    blocks = []
    for pair in range(rows // 16):
        both = [velocity[step, axis, pl.ds(16 * pair, 16), :].astype(jnp.float32) for axis in range(3)]
        blocks.append([part[:8] for part in both])
        blocks.append([part[8:] for part in both])
    return blocks


def row_message_kernel(state, velocity, solid, low, high):
    rows = state.shape[1]
    solid_parts = spread_solid(solid)
    flow = flow_blocks(velocity, 0, rows)
    for out, first, second, group, moving in (
        (low, 0, LEVELS, 0, x_up),
        (high, rows - LEVELS, rows - 2 * LEVELS, -1, x_down),
    ):
        for number in range(19):
            out[number] = state[number, pl.ds(first, LEVELS), :]
        start = first % 8
        for axis in range(3):
            out[FLOW + axis] = flow[group][axis][start : start + LEVELS]
        out[SOLID] = solid_parts[group][:LEVELS]
        for slot, number in enumerate(moving):
            out[SECOND + slot] = state[number, pl.ds(second, LEVELS), :]


def slot_place(slot, group, groups):
    per_block = LANES // groups
    return slot // per_block, (slot % per_block) * groups + group


def column_message_kernel(state, velocity, solid, after, before, low, high, ends):
    rows = state.shape[1]
    groups = rows // 8 + 2
    solid_parts = spread_solid(solid)
    flow = flow_blocks(velocity, 0, rows)
    lane = lane_index()
    for slot in range(SECOND):
        ends[0, slot, pl.ds(LEVELS, LEVELS), :] = before[slot]
        ends[1, slot, pl.ds(0, LEVELS), :] = after[slot]
        in_second = SOLID if slot == SOLID else None
        low_second = SECOND + x_down.index(slot) if slot in x_down else in_second
        high_second = SECOND + x_up.index(slot) if slot in x_up else in_second
        if low_second is not None:
            ends[0, slot, pl.ds(0, LEVELS), :] = before[low_second]
        else:
            ends[0, slot, pl.ds(0, LEVELS), :] = jnp.zeros((LEVELS, LANES), jnp.float32)
        if high_second is not None:
            ends[1, slot, pl.ds(LEVELS, LEVELS), :] = after[high_second]
        else:
            ends[1, slot, pl.ds(LEVELS, LEVELS), :] = jnp.zeros((LEVELS, LANES), jnp.float32)

    def block(slot, group):
        if group == 0:
            return ends[0, slot]
        if group == groups - 1:
            return ends[1, slot]
        if slot < FLOW:
            return state[slot, pl.ds(8 * (group - 1), 8), :]
        if slot < SOLID:
            return flow[group - 1][slot - FLOW]
        return solid_parts[(group - 1) * 8 // (LEVELS * TILE)]

    count = low.shape[0]
    low_parts = [jnp.zeros((8, LANES), jnp.float32) for _ in range(count)]
    high_parts = [jnp.zeros((8, LANES), jnp.float32) for _ in range(count)]
    for slot in range(SECOND):
        for group in range(groups):
            value = block(slot, group)
            part, place = slot_place(slot, group, groups)
            turned = pltpu.roll(value, (place + 1) % LANES, 1)
            low_parts[part] = jnp.where(lane == place + 1, turned, low_parts[part])
            high_parts[part] = jnp.where(lane == place, turned, high_parts[part])
            for moving, parts, edge, ahead in ((y_up, low_parts, 1, 1), (y_down, high_parts, LANES - 2, 0)):
                if slot in moving:
                    part, place = slot_place(SECOND + moving.index(slot), group, groups)
                    turned = pltpu.roll(value, (place + ahead - edge) % LANES, 1)
                    parts[part] = jnp.where(lane == place + ahead, turned, parts[part])
    for part in range(count):
        low[part] = low_parts[part]
        high[part] = high_parts[part]


def collide(moved, flow, fluid):
    ux, uy, uz = flow
    total = {n: moved[n] + moved[n + 1] for n in range(1, 19, 2)}
    gap = {n: moved[n] - moved[n + 1] for n in range(1, 19, 2)}
    xy, xz, yz = total[7] + total[9], total[11] + total[13], total[15] + total[17]
    axis_x, axis_y, axis_z = 2.0 * total[1], 2.0 * total[3], 2.0 * total[5]
    density = 12.0 * moved[0] + (axis_x + axis_y + axis_z) + (xy + xz + yz)
    pxx = axis_x + xy + xz
    pyy = axis_y + xy + yz
    pzz = axis_z + xz + yz
    pxy = total[7] - total[9]
    pxz = total[11] - total[13]
    pyz = total[15] - total[17]
    dx = 2.0 * gap[1] + (gap[7] + gap[9]) + (gap[11] + gap[13])
    dy = 2.0 * gap[3] + (gap[7] - gap[9]) + (gap[15] + gap[17])
    dz = 2.0 * gap[5] + (gap[11] - gap[13]) + (gap[15] - gap[17])
    vx = pxx * ux + pxy * uy + pxz * uz
    vy = pxy * ux + pyy * uy + pyz * uz
    vz = pxz * ux + pyz * uy + pzz * uz
    speed_sq = ux * ux + uy * uy + uz * uz
    drag = fluid * (ux * dx + uy * dy + uz * dz)
    scaled = (relax_rate / 36.0) * fluid
    base = scaled * (density + 1.5 * (speed_sq * density) - 4.5 * (ux * vx + uy * vy + uz * vz))
    scaled3 = 3.0 * scaled
    bx = scaled3 * (dx + 3.0 * vx - ux * density)
    by = scaled3 * (dy + 3.0 * vy - uy * density)
    bz = scaled3 * (dz + 3.0 * vz - uz * density)
    keep = (1.0 - relax_rate) * fluid
    results = [keep * moved[0] + base]
    for number in range(1, 19, 2):
        along = None
        for speed, part in zip(lattice_speeds[number], (bx, by, bz)):
            if speed == 0:
                continue
            if along is None:
                along = part if speed == 1 else -part
            else:
                along = along + part if speed == 1 else along - part
        results.append(keep * moved[number] + (base + along))
        results.append(keep * moved[number + 1] + (base - along))
    return results, drag


def outside(cz):
    level = lax.broadcasted_iota(jnp.int32, (8, LANES), 0) % LEVELS
    return level == (LEVELS - 1 if cz == 1 else 0)


def link_closed(solid_there, cz):
    closed = solid_there > 0.5
    return closed | outside(cz) if cz != 0 else closed


def shift_lanes(value, cy, edge_value):
    lane = lane_index(value.shape[0])
    if cy == 1:
        return jnp.where(lane == LANES - 1, edge_value, pltpu.roll(value, LANES - 1, 1))
    return jnp.where(lane == 0, edge_value, pltpu.roll(value, 1, 1))


def step_cells(held, shifted, first, flow, fluid, closed):
    here = [held[n, pl.ds(first, 8), :] for n in range(19)]
    moved = [here[0]]
    for number in range(1, 19):
        cx, cy, cz = lattice_speeds[number]
        field = held if cy == 0 else shifted
        if cx == cy == cz == 0:
            source = here[number]
        else:
            source = field[number, pl.ds(first + LEVELS * cx + cz, 8), :]
        bounced = here[opposite_of(number)]
        if cx != 0:
            bounced = bounced + 2.0 * cx
        moved.append(jnp.where(closed(number), bounced, source))
    return collide(moved, flow, fluid)


def main_kernel(
    state, velocity, blocked, solid, after, before, y_after, y_before, low, high, out, shared,
    held, shifted, later, row_flow, solid_rows,
):
    rows = state.shape[1]
    groups = rows // 8 + 2
    own = GUARD + 8
    near, far = own - LEVELS, own + rows
    lane = lane_index()
    solid_parts = spread_solid(solid)

    def column(message, slot, lane_first, group=0):
        part, place = slot_place(slot, group, groups)
        ahead = 1 if message is y_after or message is low else 0
        return pltpu.roll(message[part], (lane_first - place - ahead) % LANES, 1)

    for number in range(19):
        for group in range(rows // 8):
            held[number, pl.ds(own + 8 * group, 8), :] = state[number, pl.ds(8 * group, 8), :]
        held[number, pl.ds(near, LEVELS), :] = before[number]
        held[number, pl.ds(far, LEVELS), :] = after[number]
        if number in x_down:
            held[number, pl.ds(near - LEVELS, LEVELS), :] = before[SECOND + x_down.index(number)]
        if number in x_up:
            held[number, pl.ds(far + LEVELS, LEVELS), :] = after[SECOND + x_up.index(number)]
    for number in y_up + y_down:
        cy = lattice_speeds[number][1]
        for group in range(groups):
            value = held[number, pl.ds(GUARD + 8 * group, 8), :]
            if cy == 1:
                edge = column(y_after, number, LANES - 1, group)
            else:
                edge = column(y_before, number, 0, group)
            shifted[number, pl.ds(GUARD + 8 * group, 8), :] = shift_lanes(value, cy, edge)

    for group in (0, 1, groups - 2, groups - 1):
        first = GUARD + 8 * group
        if group == 0:
            solid_rows[0, pl.ds(first, LEVELS), :] = before[SOLID]
            solid_rows[0, pl.ds(first + LEVELS, LEVELS), :] = before[SOLID]
        elif group == groups - 1:
            solid_rows[0, pl.ds(first, LEVELS), :] = after[SOLID]
            solid_rows[0, pl.ds(first + LEVELS, LEVELS), :] = after[SOLID]
        else:
            solid_rows[0, pl.ds(first, 8), :] = solid_parts[(group - 1) * 8 // (LEVELS * TILE)]
        value = solid_rows[0, pl.ds(first, 8), :]
        solid_rows[1, pl.ds(first, 8), :] = shift_lanes(value, 1, column(y_after, SOLID, LANES - 1, group))
        solid_rows[2, pl.ds(first, 8), :] = shift_lanes(value, -1, column(y_before, SOLID, 0, group))
    for axis in range(3):
        row_flow[axis, pl.ds(0, LEVELS), :] = before[FLOW + axis]
        row_flow[axis, pl.ds(LEVELS, LEVELS), :] = after[FLOW + axis]
    row_flow[3, pl.ds(0, LEVELS), :] = before[SOLID]
    row_flow[3, pl.ds(LEVELS, LEVELS), :] = after[SOLID]

    def both_rows(field, index, shift):
        ends = [field[index, pl.ds(place + shift, LEVELS), :] for place in (near, far)]
        return jnp.concatenate(ends, axis=0)

    here = [both_rows(held, n, 0) for n in range(19)]
    moved = [here[0]]
    for number in range(1, 19):
        cx, cy, cz = lattice_speeds[number]
        shift = LEVELS * cx + cz
        source = both_rows(held if cy == 0 else shifted, number, shift)
        closed = link_closed(both_rows(solid_rows, cy % 3, shift), cz)
        moved.append(jnp.where(closed, here[opposite_of(number)] + 2.0 * cx, source))
    row_results, _ = collide(moved, [row_flow[axis] for axis in range(3)], 1.0 - row_flow[3])

    def columns(number_before, number_after, message_before, message_after):
        return jnp.where(
            lane < AFTER_LANE,
            column(message_before, number_before, BEFORE_LANE),
            column(message_after, number_after, AFTER_LANE),
        )

    def neighbours(slot, cy):
        if cy == 0:
            return columns(slot, slot, y_before, y_after)
        if cy == 1:
            beyond = SOLID if slot == SOLID else SECOND + y_up.index(slot)
            return columns(slot, beyond, low, y_after)
        beyond = SOLID if slot == SOLID else SECOND + y_down.index(slot)
        return columns(beyond, slot, y_before, high)

    upper = lax.broadcasted_iota(jnp.int32, (8, LANES), 0) < LEVELS

    def shift_rows(value, cx, cz):
        if cx != 0:
            swapped = pltpu.roll(value, LEVELS, 0)
            if cx == 1:
                value = jnp.where(upper, swapped, pltpu.roll(swapped, LANES - 1, 1))
            else:
                value = jnp.where(upper, pltpu.roll(swapped, 1, 1), swapped)
        if cz != 0:
            value = pltpu.roll(value, (-cz) % 8, 0)
        return value

    here = [neighbours(n, 0) for n in range(19)]
    solid_columns = [neighbours(SOLID, cy) for cy in (0, 1, -1)]
    moved = [here[0]]
    for number in range(1, 19):
        cx, cy, cz = lattice_speeds[number]
        source = shift_rows(here[number] if cy == 0 else neighbours(number, cy), cx, cz)
        closed = link_closed(shift_rows(solid_columns[cy % 3], cx, cz), cz)
        moved.append(jnp.where(closed, here[opposite_of(number)] + 2.0 * cx, source))
    column_flow = [neighbours(FLOW + axis, 0) for axis in range(3)]
    column_results, _ = collide(moved, column_flow, 1.0 - solid_columns[0])

    def closed_at(first):
        return lambda number: blocked[number - 1, pl.ds(first, 8), :] == 1

    def fluid_at(first):
        return 1.0 - solid_parts[first // (LEVELS * TILE)]

    drag_sum = jnp.zeros((8, LANES), jnp.float32)
    flow = flow_blocks(velocity, 0, rows)
    for group in range(rows // 8):
        first = 8 * group
        results, drag = step_cells(
            held, shifted, own + first, flow[group], fluid_at(first), closed_at(first)
        )
        for number in range(19):
            later[number, pl.ds(own + first, 8), :] = results[number]
        drag_sum = drag_sum + drag
    for number in x_down:
        later[number, pl.ds(near, LEVELS), :] = row_results[number][:LEVELS]
    for number in x_up:
        later[number, pl.ds(far, LEVELS), :] = row_results[number][LEVELS:]
    for number in y_up + y_down:
        cy = lattice_speeds[number][1]
        for group in range(groups):
            value = later[number, pl.ds(GUARD + 8 * group, 8), :]
            if cy == 1:
                edge = pltpu.roll(column_results[number], (LANES - 1 - AFTER_LANE - group) % LANES, 1)
            else:
                edge = pltpu.roll(column_results[number], (-BEFORE_LANE - group) % LANES, 1)
            shifted[number, pl.ds(GUARD + 8 * group, 8), :] = shift_lanes(value, cy, edge)

    flow = flow_blocks(velocity, 1, rows)
    for group in range(rows // 8):
        first = 8 * group
        results, drag = step_cells(
            later, shifted, own + first, flow[group], fluid_at(first), closed_at(first)
        )
        for number in range(19):
            out[number, pl.ds(first, 8), :] = results[number]
        drag_sum = drag_sum + drag
    shared[...] = jnp.broadcast_to(jnp.sum(drag_sum), shared.shape)


def swap_edges(low, high, axis):
    count = lax.axis_size(axis)
    from_after = [((i + 1) % count, i) for i in range(count)]
    from_before = [(i, (i + 1) % count) for i in range(count)]
    return lax.ppermute(low, axis, from_after), lax.ppermute(high, axis, from_before)


def per_device(adjoint_in, velocity, solid_tiles, link_blocked):
    rows_x, levels, rows_y = adjoint_in.shape[1:]
    rows = rows_x * levels
    padded = rows + 16 + 2 * GUARD
    groups = rows // 8 + 2
    parts = -(-QUANTITIES // (LANES // groups))
    state = adjoint_in.reshape(19, rows, rows_y)
    flow = velocity.reshape(STEPS, 3, rows, rows_y)
    solid = solid_tiles.reshape(-1, solid_tiles.shape[2])
    blocked = link_blocked.reshape(18, rows, rows_y)

    def shape_of(*sizes):
        return jax.ShapeDtypeStruct(sizes, jnp.float32)

    params = pltpu.CompilerParams(vmem_limit_bytes=16 * 1024 * 1024)
    row_low, row_high = pl.pallas_call(
        row_message_kernel,
        out_shape=(shape_of(QUANTITIES, levels, rows_y),) * 2,
        in_specs=[vmem] * 3,
        out_specs=(vmem,) * 2,
        compiler_params=params,
    )(state, flow, solid)
    after, before = swap_edges(row_low, row_high, "gx")
    low, high = pl.pallas_call(
        column_message_kernel,
        out_shape=(shape_of(parts, 8, rows_y),) * 2,
        in_specs=[vmem] * 5,
        out_specs=(vmem,) * 2,
        scratch_shapes=[pltpu.VMEM((2, SECOND, 8, rows_y), jnp.float32)],
        compiler_params=params,
    )(state, flow, solid, after, before)
    y_after, y_before = swap_edges(low, high, "gy")
    count = lax.axis_size("gx") * lax.axis_size("gy")
    field = pltpu.VMEM((19, padded, rows_y), jnp.float32)
    result, own = pl.pallas_call(
        main_kernel,
        out_shape=(shape_of(19, rows, rows_y), shape_of(count, 1, rows_y)),
        in_specs=[vmem] * 10,
        out_specs=(vmem,) * 2,
        scratch_shapes=[
            field,
            field,
            field,
            pltpu.VMEM((4, 8, rows_y), jnp.float32),
            pltpu.VMEM((3, padded, rows_y), jnp.float32),
        ],
        compiler_params=params,
    )(state, flow, blocked, solid, after, before, y_after, y_before, low, high)
    shared = lax.all_to_all(own, ("gx", "gy"), split_axis=0, concat_axis=0, tiled=True)
    cell_count = rows * rows_y * count
    scale = drag_factor / math.sqrt(cell_count) * 3.0 / 36.0
    total = jnp.sum(shared[:, 0, 0])
    return (result.reshape(adjoint_in.shape), (-scale * total).reshape(1))


def solution(mesh):
    placed = (
        P(None, "gx", None, "gy"),
        P(None, None, "gx", None, "gy"),
        P("gx", None, "gy"),
        P(None, "gx", None, "gy"),
    )
    return jax.shard_map(
        per_device,
        mesh=mesh,
        in_specs=placed,
        out_specs=(P(None, "gx", None, "gy"), P()),
        check_vma=False,
    )
```

```python
import math

import jax
import jax.numpy as jnp
from jax import lax
from jax.experimental import pallas as pl
from jax.experimental.pallas import tpu as pltpu
from jax.sharding import PartitionSpec as P

TILE = 4
STEPS = 2

lattice_speeds = (
    (0, 0, 0),
    (1, 0, 0),
    (-1, 0, 0),
    (0, 1, 0),
    (0, -1, 0),
    (0, 0, 1),
    (0, 0, -1),
    (1, 1, 0),
    (-1, -1, 0),
    (1, -1, 0),
    (-1, 1, 0),
    (1, 0, 1),
    (-1, 0, -1),
    (1, 0, -1),
    (-1, 0, 1),
    (0, 1, 1),
    (0, -1, -1),
    (0, 1, -1),
    (0, -1, 1),
)
relax_rate = 1.6
drag_factor = 20.0
LEVELS = 4
LANES = 128
GUARD = 8

x_up = [n for n in range(19) if lattice_speeds[n][0] == 1]
x_down = [n for n in range(19) if lattice_speeds[n][0] == -1]
y_up = [n for n in range(19) if lattice_speeds[n][1] == 1]
y_down = [n for n in range(19) if lattice_speeds[n][1] == -1]
vmem = pl.BlockSpec(memory_space=pltpu.VMEM)

FLOW = 19
SOLID = 22
SECOND = 23
QUANTITIES = 28
BEFORE_LANE = 16
AFTER_LANE = 32


def opposite_of(number):
    return number + 1 if number % 2 == 1 else number - 1


def lane_index(rows=8):
    return lax.broadcasted_iota(jnp.int32, (rows, LANES), 1)


def spread_solid(solid):
    tiles = solid.shape[1]
    row = lax.broadcasted_iota(jnp.int32, (tiles, LANES), 0)
    column = lax.broadcasted_iota(jnp.int32, (tiles, LANES), 1)
    spread = (column // TILE == row).astype(jnp.float32)
    cells = jnp.dot(solid[...].astype(jnp.float32), spread, preferred_element_type=jnp.float32)
    blocks = []
    for tile_row in range(solid.shape[0] // LEVELS):
        part = cells[tile_row * LEVELS : (tile_row + 1) * LEVELS]
        blocks.append(jnp.concatenate([part, part], axis=0))
    return blocks


def flow_blocks(velocity, step, rows):
    blocks = []
    for pair in range(rows // 16):
        both = [velocity[step, axis, pl.ds(16 * pair, 16), :].astype(jnp.float32) for axis in range(3)]
        blocks.append([part[:8] for part in both])
        blocks.append([part[8:] for part in both])
    return blocks


def ring(slots, axis):
    count = slots.shape[0]
    place = lax.axis_index(axis)
    return slots.at[lax.rem(place + count - 1, count)], slots.at[lax.rem(place + 1, count)]


def row_message_kernel(state, velocity, solid, sent):
    rows = state.shape[1]
    low, high = ring(sent, "gx")
    solid_parts = spread_solid(solid)
    flow = flow_blocks(velocity, 0, rows)
    for out, first, second, group, moving in (
        (low, 0, LEVELS, 0, x_up),
        (high, rows - LEVELS, rows - 2 * LEVELS, -1, x_down),
    ):
        for number in range(19):
            out[number] = state[number, pl.ds(first, LEVELS), :]
        start = first % 8
        for axis in range(3):
            out[FLOW + axis] = flow[group][axis][start : start + LEVELS]
        out[SOLID] = solid_parts[group][:LEVELS]
        for slot, number in enumerate(moving):
            out[SECOND + slot] = state[number, pl.ds(second, LEVELS), :]


def slot_place(slot, group, groups):
    per_block = LANES // groups
    return slot // per_block, (slot % per_block) * groups + group


def column_message_kernel(state, velocity, solid, row_slots, sent, ends):
    rows = state.shape[1]
    before, after = ring(row_slots, "gx")
    low, high = ring(sent, "gy")
    groups = rows // 8 + 2
    solid_parts = spread_solid(solid)
    flow = flow_blocks(velocity, 0, rows)
    lane = lane_index()
    for slot in range(SECOND):
        ends[0, slot, pl.ds(LEVELS, LEVELS), :] = before[slot]
        ends[1, slot, pl.ds(0, LEVELS), :] = after[slot]
        in_second = SOLID if slot == SOLID else None
        low_second = SECOND + x_down.index(slot) if slot in x_down else in_second
        high_second = SECOND + x_up.index(slot) if slot in x_up else in_second
        if low_second is not None:
            ends[0, slot, pl.ds(0, LEVELS), :] = before[low_second]
        else:
            ends[0, slot, pl.ds(0, LEVELS), :] = jnp.zeros((LEVELS, LANES), jnp.float32)
        if high_second is not None:
            ends[1, slot, pl.ds(LEVELS, LEVELS), :] = after[high_second]
        else:
            ends[1, slot, pl.ds(LEVELS, LEVELS), :] = jnp.zeros((LEVELS, LANES), jnp.float32)

    def block(slot, group):
        if group == 0:
            return ends[0, slot]
        if group == groups - 1:
            return ends[1, slot]
        if slot < FLOW:
            return state[slot, pl.ds(8 * (group - 1), 8), :]
        if slot < SOLID:
            return flow[group - 1][slot - FLOW]
        return solid_parts[(group - 1) * 8 // (LEVELS * TILE)]

    count = low.shape[0]
    low_parts = [jnp.zeros((8, LANES), jnp.float32) for _ in range(count)]
    high_parts = [jnp.zeros((8, LANES), jnp.float32) for _ in range(count)]
    for slot in range(SECOND):
        for group in range(groups):
            value = block(slot, group)
            part, place = slot_place(slot, group, groups)
            turned = pltpu.roll(value, (place + 1) % LANES, 1)
            low_parts[part] = jnp.where(lane == place + 1, turned, low_parts[part])
            high_parts[part] = jnp.where(lane == place, turned, high_parts[part])
            for moving, parts, edge, ahead in ((y_up, low_parts, 1, 1), (y_down, high_parts, LANES - 2, 0)):
                if slot in moving:
                    part, place = slot_place(SECOND + moving.index(slot), group, groups)
                    turned = pltpu.roll(value, (place + ahead - edge) % LANES, 1)
                    parts[part] = jnp.where(lane == place + ahead, turned, parts[part])
    for part in range(count):
        low[part] = low_parts[part]
        high[part] = high_parts[part]


def collide(moved, flow, fluid):
    ux, uy, uz = flow
    total = {n: moved[n] + moved[n + 1] for n in range(1, 19, 2)}
    gap = {n: moved[n] - moved[n + 1] for n in range(1, 19, 2)}
    xy, xz, yz = total[7] + total[9], total[11] + total[13], total[15] + total[17]
    axis_x, axis_y, axis_z = 2.0 * total[1], 2.0 * total[3], 2.0 * total[5]
    density = 12.0 * moved[0] + (axis_x + axis_y + axis_z) + (xy + xz + yz)
    pxx = axis_x + xy + xz
    pyy = axis_y + xy + yz
    pzz = axis_z + xz + yz
    pxy = total[7] - total[9]
    pxz = total[11] - total[13]
    pyz = total[15] - total[17]
    dx = 2.0 * gap[1] + (gap[7] + gap[9]) + (gap[11] + gap[13])
    dy = 2.0 * gap[3] + (gap[7] - gap[9]) + (gap[15] + gap[17])
    dz = 2.0 * gap[5] + (gap[11] - gap[13]) + (gap[15] - gap[17])
    vx = pxx * ux + pxy * uy + pxz * uz
    vy = pxy * ux + pyy * uy + pyz * uz
    vz = pxz * ux + pyz * uy + pzz * uz
    speed_sq = ux * ux + uy * uy + uz * uz
    drag = fluid * (ux * dx + uy * dy + uz * dz)
    scaled = (relax_rate / 36.0) * fluid
    base = scaled * (density + 1.5 * (speed_sq * density) - 4.5 * (ux * vx + uy * vy + uz * vz))
    scaled3 = 3.0 * scaled
    bx = scaled3 * (dx + 3.0 * vx - ux * density)
    by = scaled3 * (dy + 3.0 * vy - uy * density)
    bz = scaled3 * (dz + 3.0 * vz - uz * density)
    keep = (1.0 - relax_rate) * fluid
    results = [keep * moved[0] + base]
    for number in range(1, 19, 2):
        along = None
        for speed, part in zip(lattice_speeds[number], (bx, by, bz)):
            if speed == 0:
                continue
            if along is None:
                along = part if speed == 1 else -part
            else:
                along = along + part if speed == 1 else along - part
        results.append(keep * moved[number] + (base + along))
        results.append(keep * moved[number + 1] + (base - along))
    return results, drag


def outside(cz):
    level = lax.broadcasted_iota(jnp.int32, (8, LANES), 0) % LEVELS
    return level == (LEVELS - 1 if cz == 1 else 0)


def link_closed(solid_there, cz):
    closed = solid_there > 0.5
    return closed | outside(cz) if cz != 0 else closed


def shift_lanes(value, cy, edge_value):
    lane = lane_index(value.shape[0])
    if cy == 1:
        return jnp.where(lane == LANES - 1, edge_value, pltpu.roll(value, LANES - 1, 1))
    return jnp.where(lane == 0, edge_value, pltpu.roll(value, 1, 1))


def step_cells(held, shifted, first, flow, fluid, closed):
    here = [held[n, pl.ds(first, 8), :] for n in range(19)]
    moved = [here[0]]
    for number in range(1, 19):
        cx, cy, cz = lattice_speeds[number]
        field = held if cy == 0 else shifted
        if cx == cy == cz == 0:
            source = here[number]
        else:
            source = field[number, pl.ds(first + LEVELS * cx + cz, 8), :]
        bounced = here[opposite_of(number)]
        if cx != 0:
            bounced = bounced + 2.0 * cx
        moved.append(jnp.where(closed(number), bounced, source))
    return collide(moved, flow, fluid)


def main_kernel(
    state, velocity, blocked, solid, row_slots, column_slots, sent, out, shared,
    held, shifted, later, row_flow, solid_rows,
):
    rows = state.shape[1]
    before, after = ring(row_slots, "gx")
    y_before, y_after = ring(column_slots, "gy")
    low, high = ring(sent, "gy")
    groups = rows // 8 + 2
    own = GUARD + 8
    near, far = own - LEVELS, own + rows
    lane = lane_index()
    solid_parts = spread_solid(solid)

    def column(message, slot, lane_first, group=0):
        part, place = slot_place(slot, group, groups)
        ahead = 1 if message is y_after or message is low else 0
        return pltpu.roll(message[part], (lane_first - place - ahead) % LANES, 1)

    for number in range(19):
        for group in range(rows // 8):
            held[number, pl.ds(own + 8 * group, 8), :] = state[number, pl.ds(8 * group, 8), :]
        held[number, pl.ds(near, LEVELS), :] = before[number]
        held[number, pl.ds(far, LEVELS), :] = after[number]
        if number in x_down:
            held[number, pl.ds(near - LEVELS, LEVELS), :] = before[SECOND + x_down.index(number)]
        if number in x_up:
            held[number, pl.ds(far + LEVELS, LEVELS), :] = after[SECOND + x_up.index(number)]
    for number in y_up + y_down:
        cy = lattice_speeds[number][1]
        for group in range(groups):
            value = held[number, pl.ds(GUARD + 8 * group, 8), :]
            if cy == 1:
                edge = column(y_after, number, LANES - 1, group)
            else:
                edge = column(y_before, number, 0, group)
            shifted[number, pl.ds(GUARD + 8 * group, 8), :] = shift_lanes(value, cy, edge)

    for group in (0, 1, groups - 2, groups - 1):
        first = GUARD + 8 * group
        if group == 0:
            solid_rows[0, pl.ds(first, LEVELS), :] = before[SOLID]
            solid_rows[0, pl.ds(first + LEVELS, LEVELS), :] = before[SOLID]
        elif group == groups - 1:
            solid_rows[0, pl.ds(first, LEVELS), :] = after[SOLID]
            solid_rows[0, pl.ds(first + LEVELS, LEVELS), :] = after[SOLID]
        else:
            solid_rows[0, pl.ds(first, 8), :] = solid_parts[(group - 1) * 8 // (LEVELS * TILE)]
        value = solid_rows[0, pl.ds(first, 8), :]
        solid_rows[1, pl.ds(first, 8), :] = shift_lanes(value, 1, column(y_after, SOLID, LANES - 1, group))
        solid_rows[2, pl.ds(first, 8), :] = shift_lanes(value, -1, column(y_before, SOLID, 0, group))
    for axis in range(3):
        row_flow[axis, pl.ds(0, LEVELS), :] = before[FLOW + axis]
        row_flow[axis, pl.ds(LEVELS, LEVELS), :] = after[FLOW + axis]
    row_flow[3, pl.ds(0, LEVELS), :] = before[SOLID]
    row_flow[3, pl.ds(LEVELS, LEVELS), :] = after[SOLID]

    def both_rows(field, index, shift):
        ends = [field[index, pl.ds(place + shift, LEVELS), :] for place in (near, far)]
        return jnp.concatenate(ends, axis=0)

    here = [both_rows(held, n, 0) for n in range(19)]
    moved = [here[0]]
    for number in range(1, 19):
        cx, cy, cz = lattice_speeds[number]
        shift = LEVELS * cx + cz
        source = both_rows(held if cy == 0 else shifted, number, shift)
        closed = link_closed(both_rows(solid_rows, cy % 3, shift), cz)
        moved.append(jnp.where(closed, here[opposite_of(number)] + 2.0 * cx, source))
    row_results, _ = collide(moved, [row_flow[axis] for axis in range(3)], 1.0 - row_flow[3])

    def columns(number_before, number_after, message_before, message_after):
        return jnp.where(
            lane < AFTER_LANE,
            column(message_before, number_before, BEFORE_LANE),
            column(message_after, number_after, AFTER_LANE),
        )

    def neighbours(slot, cy):
        if cy == 0:
            return columns(slot, slot, y_before, y_after)
        if cy == 1:
            beyond = SOLID if slot == SOLID else SECOND + y_up.index(slot)
            return columns(slot, beyond, low, y_after)
        beyond = SOLID if slot == SOLID else SECOND + y_down.index(slot)
        return columns(beyond, slot, y_before, high)

    upper = lax.broadcasted_iota(jnp.int32, (8, LANES), 0) < LEVELS

    def shift_rows(value, cx, cz):
        if cx != 0:
            swapped = pltpu.roll(value, LEVELS, 0)
            if cx == 1:
                value = jnp.where(upper, swapped, pltpu.roll(swapped, LANES - 1, 1))
            else:
                value = jnp.where(upper, pltpu.roll(swapped, 1, 1), swapped)
        if cz != 0:
            value = pltpu.roll(value, (-cz) % 8, 0)
        return value

    here = [neighbours(n, 0) for n in range(19)]
    solid_columns = [neighbours(SOLID, cy) for cy in (0, 1, -1)]
    moved = [here[0]]
    for number in range(1, 19):
        cx, cy, cz = lattice_speeds[number]
        source = shift_rows(here[number] if cy == 0 else neighbours(number, cy), cx, cz)
        closed = link_closed(shift_rows(solid_columns[cy % 3], cx, cz), cz)
        moved.append(jnp.where(closed, here[opposite_of(number)] + 2.0 * cx, source))
    column_flow = [neighbours(FLOW + axis, 0) for axis in range(3)]
    column_results, _ = collide(moved, column_flow, 1.0 - solid_columns[0])

    def closed_at(first):
        return lambda number: blocked[number - 1, pl.ds(first, 8), :] == 1

    def fluid_at(first):
        return 1.0 - solid_parts[first // (LEVELS * TILE)]

    drag_sum = jnp.zeros((8, LANES), jnp.float32)
    flow = flow_blocks(velocity, 0, rows)
    for group in range(rows // 8):
        first = 8 * group
        results, drag = step_cells(
            held, shifted, own + first, flow[group], fluid_at(first), closed_at(first)
        )
        for number in range(19):
            later[number, pl.ds(own + first, 8), :] = results[number]
        drag_sum = drag_sum + drag
    for number in x_down:
        later[number, pl.ds(near, LEVELS), :] = row_results[number][:LEVELS]
    for number in x_up:
        later[number, pl.ds(far, LEVELS), :] = row_results[number][LEVELS:]
    for number in y_up + y_down:
        cy = lattice_speeds[number][1]
        for group in range(groups):
            value = later[number, pl.ds(GUARD + 8 * group, 8), :]
            if cy == 1:
                edge = pltpu.roll(column_results[number], (LANES - 1 - AFTER_LANE - group) % LANES, 1)
            else:
                edge = pltpu.roll(column_results[number], (-BEFORE_LANE - group) % LANES, 1)
            shifted[number, pl.ds(GUARD + 8 * group, 8), :] = shift_lanes(value, cy, edge)

    flow = flow_blocks(velocity, 1, rows)
    for group in range(rows // 8):
        first = 8 * group
        results, drag = step_cells(
            later, shifted, own + first, flow[group], fluid_at(first), closed_at(first)
        )
        for number in range(19):
            out[number, pl.ds(first, 8), :] = results[number]
        drag_sum = drag_sum + drag
    shared[...] = jnp.broadcast_to(jnp.sum(drag_sum), shared.shape)


def swap_slots(slots, axis):
    return lax.all_to_all(slots, axis, split_axis=0, concat_axis=0, tiled=True)


def per_device(adjoint_in, velocity, solid_tiles, link_blocked):
    rows_x, levels, rows_y = adjoint_in.shape[1:]
    rows = rows_x * levels
    padded = rows + 16 + 2 * GUARD
    groups = rows // 8 + 2
    parts = -(-QUANTITIES // (LANES // groups))
    state = adjoint_in.reshape(19, rows, rows_y)
    flow = velocity.reshape(STEPS, 3, rows, rows_y)
    solid = solid_tiles.reshape(-1, solid_tiles.shape[2])
    blocked = link_blocked.reshape(18, rows, rows_y)

    def shape_of(*sizes):
        return jax.ShapeDtypeStruct(sizes, jnp.float32)

    params = pltpu.CompilerParams(vmem_limit_bytes=16 * 1024 * 1024)
    row_slots = pl.pallas_call(
        row_message_kernel,
        out_shape=shape_of(lax.axis_size("gx"), QUANTITIES, levels, rows_y),
        in_specs=[vmem] * 3,
        out_specs=vmem,
        compiler_params=params,
    )(state, flow, solid)
    row_slots = swap_slots(row_slots, "gx")
    sent = pl.pallas_call(
        column_message_kernel,
        out_shape=shape_of(lax.axis_size("gy"), parts, 8, rows_y),
        in_specs=[vmem] * 4,
        out_specs=vmem,
        scratch_shapes=[pltpu.VMEM((2, SECOND, 8, rows_y), jnp.float32)],
        compiler_params=params,
    )(state, flow, solid, row_slots)
    column_slots = swap_slots(sent, "gy")
    count = lax.axis_size("gx") * lax.axis_size("gy")
    field = pltpu.VMEM((19, padded, rows_y), jnp.float32)
    result, own = pl.pallas_call(
        main_kernel,
        out_shape=(shape_of(19, rows, rows_y), shape_of(1, rows_y)),
        in_specs=[vmem] * 7,
        out_specs=(vmem,) * 2,
        scratch_shapes=[
            field,
            field,
            field,
            pltpu.VMEM((4, 8, rows_y), jnp.float32),
            pltpu.VMEM((3, padded, rows_y), jnp.float32),
        ],
        compiler_params=params,
    )(state, flow, blocked, solid, row_slots, column_slots, sent)
    shared = lax.all_gather(own, ("gx", "gy"), axis=0)
    cell_count = rows * rows_y * count
    scale = drag_factor / math.sqrt(cell_count) * 3.0 / 36.0
    total = jnp.sum(shared[:, 0, 0])
    return (result.reshape(adjoint_in.shape), (-scale * total).reshape(1))


def solution(mesh):
    placed = (
        P(None, "gx", None, "gy"),
        P(None, None, "gx", None, "gy"),
        P("gx", None, "gy"),
        P(None, "gx", None, "gy"),
    )
    return jax.shard_map(
        per_device,
        mesh=mesh,
        in_specs=placed,
        out_specs=(P(None, "gx", None, "gy"), P()),
        check_vma=False,
    )
```

```python
import math

import jax
import jax.numpy as jnp
from jax import lax
from jax.experimental import pallas as pl
from jax.experimental.pallas import tpu as pltpu
from jax.sharding import PartitionSpec as P

TILE = 4
STEPS = 2

lattice_speeds = (
    (0, 0, 0),
    (1, 0, 0),
    (-1, 0, 0),
    (0, 1, 0),
    (0, -1, 0),
    (0, 0, 1),
    (0, 0, -1),
    (1, 1, 0),
    (-1, -1, 0),
    (1, -1, 0),
    (-1, 1, 0),
    (1, 0, 1),
    (-1, 0, -1),
    (1, 0, -1),
    (-1, 0, 1),
    (0, 1, 1),
    (0, -1, -1),
    (0, 1, -1),
    (0, -1, 1),
)
relax_rate = 1.6
drag_factor = 20.0
LEVELS = 4
LANES = 128
GUARD = 8

x_up = [n for n in range(19) if lattice_speeds[n][0] == 1]
x_down = [n for n in range(19) if lattice_speeds[n][0] == -1]
y_up = [n for n in range(19) if lattice_speeds[n][1] == 1]
y_down = [n for n in range(19) if lattice_speeds[n][1] == -1]
vmem = pl.BlockSpec(memory_space=pltpu.VMEM)

FLOW = 19
SOLID = 22
SECOND = 23
QUANTITIES = 28
BEFORE_LANE = 16
AFTER_LANE = 32


def opposite_of(number):
    return number + 1 if number % 2 == 1 else number - 1


def lane_index(rows=8):
    return lax.broadcasted_iota(jnp.int32, (rows, LANES), 1)


def spread_solid(solid):
    tiles = solid.shape[1]
    row = lax.broadcasted_iota(jnp.int32, (tiles, LANES), 0)
    column = lax.broadcasted_iota(jnp.int32, (tiles, LANES), 1)
    spread = (column // TILE == row).astype(jnp.float32)
    cells = jnp.dot(solid[...].astype(jnp.float32), spread, preferred_element_type=jnp.float32)
    blocks = []
    for tile_row in range(solid.shape[0] // LEVELS):
        part = cells[tile_row * LEVELS : (tile_row + 1) * LEVELS]
        blocks.append(jnp.concatenate([part, part], axis=0))
    return blocks


def flow_blocks(velocity, step, rows):
    blocks = []
    for pair in range(rows // 16):
        both = [velocity[step, axis, pl.ds(16 * pair, 16), :].astype(jnp.float32) for axis in range(3)]
        blocks.append([part[:8] for part in both])
        blocks.append([part[8:] for part in both])
    return blocks


def on_even(axis):
    return lax.rem(lax.axis_index(axis), 2) == 0


def row_message_kernel(
    state, velocity, solid, first_out, second_out, low_rows, high_rows, low_flow, high_flow, tiles, arrived
):
    rows = state.shape[1]
    copies = [
        pltpu.make_async_copy(source, target, arrived.at[number])
        for number, (source, target) in enumerate(
            (
                (state.at[:, pl.ds(0, 8), :], low_rows),
                (state.at[:, pl.ds(rows - 8, 8), :], high_rows),
                (velocity.at[0, :, pl.ds(0, 16), :], low_flow),
                (velocity.at[0, :, pl.ds(rows - 16, 16), :], high_flow),
                (solid, tiles),
            )
        )
    ]
    for copy in copies:
        copy.start()
    for copy in copies:
        copy.wait()
    even = on_even("gx")
    solid_parts = spread_solid(tiles)

    def put(slot, low, high):
        first_out[slot] = jnp.where(even, high, low)
        second_out[slot] = jnp.where(even, low, high)

    for number in range(19):
        put(number, low_rows[number, pl.ds(0, LEVELS), :], high_rows[number, pl.ds(LEVELS, LEVELS), :])
    for axis in range(3):
        low = low_flow[axis].astype(jnp.float32)
        high = high_flow[axis].astype(jnp.float32)
        put(FLOW + axis, low[:LEVELS], high[16 - LEVELS :])
    put(SOLID, solid_parts[0][:LEVELS], solid_parts[-1][:LEVELS])
    for slot in range(5):
        put(
            SECOND + slot,
            low_rows[x_up[slot], pl.ds(LEVELS, LEVELS), :],
            high_rows[x_down[slot], pl.ds(0, LEVELS), :],
        )


class Chosen:
    def __init__(self, choice, yes, no):
        self.choice, self.yes, self.no = choice, yes, no
        self.shape = yes.shape

    def __getitem__(self, index):
        return jnp.where(self.choice, self.yes[index], self.no[index])


def slot_place(slot, group, groups):
    per_block = LANES // groups
    return slot // per_block, (slot % per_block) * groups + group


def column_message_kernel(
    state, velocity, solid, row_first, row_second, first_out, second_out, ends
):
    rows = state.shape[1]
    even = on_even("gx")
    after, before = Chosen(even, row_first, row_second), Chosen(even, row_second, row_first)
    groups = rows // 8 + 2
    solid_parts = spread_solid(solid)
    flow = flow_blocks(velocity, 0, rows)
    lane = lane_index()
    for slot in range(SECOND):
        ends[0, slot, pl.ds(LEVELS, LEVELS), :] = before[slot]
        ends[1, slot, pl.ds(0, LEVELS), :] = after[slot]
        in_second = SOLID if slot == SOLID else None
        low_second = SECOND + x_down.index(slot) if slot in x_down else in_second
        high_second = SECOND + x_up.index(slot) if slot in x_up else in_second
        if low_second is not None:
            ends[0, slot, pl.ds(0, LEVELS), :] = before[low_second]
        else:
            ends[0, slot, pl.ds(0, LEVELS), :] = jnp.zeros((LEVELS, LANES), jnp.float32)
        if high_second is not None:
            ends[1, slot, pl.ds(LEVELS, LEVELS), :] = after[high_second]
        else:
            ends[1, slot, pl.ds(LEVELS, LEVELS), :] = jnp.zeros((LEVELS, LANES), jnp.float32)

    def block(slot, group):
        if group == 0:
            return ends[0, slot]
        if group == groups - 1:
            return ends[1, slot]
        if slot < FLOW:
            return state[slot, pl.ds(8 * (group - 1), 8), :]
        if slot < SOLID:
            return flow[group - 1][slot - FLOW]
        return solid_parts[(group - 1) * 8 // (LEVELS * TILE)]

    count = first_out.shape[0]
    low_parts = [jnp.zeros((8, LANES), jnp.float32) for _ in range(count)]
    high_parts = [jnp.zeros((8, LANES), jnp.float32) for _ in range(count)]
    for slot in range(SECOND):
        for group in range(groups):
            value = block(slot, group)
            part, place = slot_place(slot, group, groups)
            turned = pltpu.roll(value, (place + 1) % LANES, 1)
            low_parts[part] = jnp.where(lane == place + 1, turned, low_parts[part])
            high_parts[part] = jnp.where(lane == place, turned, high_parts[part])
            for moving, parts, edge, ahead in ((y_up, low_parts, 1, 1), (y_down, high_parts, LANES - 2, 0)):
                if slot in moving:
                    part, place = slot_place(SECOND + moving.index(slot), group, groups)
                    turned = pltpu.roll(value, (place + ahead - edge) % LANES, 1)
                    parts[part] = jnp.where(lane == place + ahead, turned, parts[part])
    even = on_even("gy")
    for part in range(count):
        first_out[part] = jnp.where(even, high_parts[part], low_parts[part])
        second_out[part] = jnp.where(even, low_parts[part], high_parts[part])


def collide(moved, flow, fluid):
    ux, uy, uz = flow
    total = {n: moved[n] + moved[n + 1] for n in range(1, 19, 2)}
    xy, xz, yz = total[7] + total[9], total[11] + total[13], total[15] + total[17]
    axis_x, axis_y, axis_z = 2.0 * total[1], 2.0 * total[3], 2.0 * total[5]
    density = 12.0 * moved[0] + (axis_x + axis_y + axis_z) + (xy + xz + yz)
    pxx = axis_x + xy + xz
    pyy = axis_y + xy + yz
    pzz = axis_z + xz + yz
    pxy = total[7] - total[9]
    pxz = total[11] - total[13]
    pyz = total[15] - total[17]
    dx, dy, dz = momentum(moved)
    vx = pxx * ux + pxy * uy + pxz * uz
    vy = pxy * ux + pyy * uy + pyz * uz
    vz = pxz * ux + pyz * uy + pzz * uz
    speed_sq = ux * ux + uy * uy + uz * uz
    scaled = (relax_rate / 36.0) * fluid
    base = scaled * (density + 1.5 * (speed_sq * density) - 4.5 * (ux * vx + uy * vy + uz * vz))
    scaled3 = 3.0 * scaled
    bx = scaled3 * (dx + 3.0 * vx - ux * density)
    by = scaled3 * (dy + 3.0 * vy - uy * density)
    bz = scaled3 * (dz + 3.0 * vz - uz * density)
    keep = (1.0 - relax_rate) * fluid
    results = [keep * moved[0] + base]
    for number in range(1, 19, 2):
        along = None
        for speed, part in zip(lattice_speeds[number], (bx, by, bz)):
            if speed == 0:
                continue
            if along is None:
                along = part if speed == 1 else -part
            else:
                along = along + part if speed == 1 else along - part
        results.append(keep * moved[number] + (base + along))
        results.append(keep * moved[number + 1] + (base - along))
    return results


def outside(cz):
    level = lax.broadcasted_iota(jnp.int32, (8, LANES), 0) % LEVELS
    return level == (LEVELS - 1 if cz == 1 else 0)


def link_closed(solid_there, cz):
    closed = solid_there > 0.5
    return closed | outside(cz) if cz != 0 else closed


def shift_lanes(value, cy, edge_value):
    lane = lane_index(value.shape[0])
    if cy == 1:
        return jnp.where(lane == LANES - 1, edge_value, pltpu.roll(value, LANES - 1, 1))
    return jnp.where(lane == 0, edge_value, pltpu.roll(value, 1, 1))


def gather_cells(held, shifted, first, closed):
    here = [held[n, pl.ds(first, 8), :] for n in range(19)]
    moved = [here[0]]
    for number in range(1, 19):
        cx, cy, cz = lattice_speeds[number]
        field = held if cy == 0 else shifted
        source = field[number, pl.ds(first + LEVELS * cx + cz, 8), :]
        bounced = here[opposite_of(number)]
        if cx != 0:
            bounced = bounced + 2.0 * cx
        moved.append(jnp.where(closed(number), bounced, source))
    return moved


def momentum(moved):
    gap = {n: moved[n] - moved[n + 1] for n in range(1, 19, 2)}
    dx = 2.0 * gap[1] + (gap[7] + gap[9]) + (gap[11] + gap[13])
    dy = 2.0 * gap[3] + (gap[7] - gap[9]) + (gap[15] + gap[17])
    dz = 2.0 * gap[5] + (gap[11] - gap[13]) + (gap[15] - gap[17])
    return dx, dy, dz


def drag_term(moved, flow, fluid):
    return fluid * sum(speed * part for speed, part in zip(flow, momentum(moved)))


def first_step_kernel(
    state, velocity, blocked, solid, row_first, row_second, column_first, column_second,
    sent_first, sent_second, later, later_shifted, shared, held, shifted, row_flow, solid_rows,
):
    rows = state.shape[1]
    even = on_even("gx")
    after, before = Chosen(even, row_first, row_second), Chosen(even, row_second, row_first)
    even = on_even("gy")
    parts = range(column_first.shape[0])

    def chosen(yes, no):
        return [jnp.where(even, yes[part], no[part]) for part in parts]

    y_after, y_before = chosen(column_first, column_second), chosen(column_second, column_first)
    low, high = chosen(sent_second, sent_first), chosen(sent_first, sent_second)
    groups = rows // 8 + 2
    own = GUARD + 8
    near, far = own - LEVELS, own + rows
    lane = lane_index()
    solid_parts = spread_solid(solid)

    def column(message, slot, lane_first, group=0):
        part, place = slot_place(slot, group, groups)
        ahead = 1 if message is y_after or message is low else 0
        return pltpu.roll(message[part], (lane_first - place - ahead) % LANES, 1)

    for number in range(19):
        for group in range(rows // 8):
            held[number, pl.ds(own + 8 * group, 8), :] = state[number, pl.ds(8 * group, 8), :]
        held[number, pl.ds(near, LEVELS), :] = before[number]
        held[number, pl.ds(far, LEVELS), :] = after[number]
        if number in x_down:
            held[number, pl.ds(near - LEVELS, LEVELS), :] = before[SECOND + x_down.index(number)]
        if number in x_up:
            held[number, pl.ds(far + LEVELS, LEVELS), :] = after[SECOND + x_up.index(number)]
    for number in y_up + y_down:
        cy = lattice_speeds[number][1]
        for group in range(groups):
            value = held[number, pl.ds(GUARD + 8 * group, 8), :]
            if cy == 1:
                edge = column(y_after, number, LANES - 1, group)
            else:
                edge = column(y_before, number, 0, group)
            shifted[number, pl.ds(GUARD + 8 * group, 8), :] = shift_lanes(value, cy, edge)

    for group in (0, 1, groups - 2, groups - 1):
        first = GUARD + 8 * group
        if group == 0:
            solid_rows[0, pl.ds(first, LEVELS), :] = before[SOLID]
            solid_rows[0, pl.ds(first + LEVELS, LEVELS), :] = before[SOLID]
        elif group == groups - 1:
            solid_rows[0, pl.ds(first, LEVELS), :] = after[SOLID]
            solid_rows[0, pl.ds(first + LEVELS, LEVELS), :] = after[SOLID]
        else:
            solid_rows[0, pl.ds(first, 8), :] = solid_parts[(group - 1) * 8 // (LEVELS * TILE)]
        value = solid_rows[0, pl.ds(first, 8), :]
        solid_rows[1, pl.ds(first, 8), :] = shift_lanes(value, 1, column(y_after, SOLID, LANES - 1, group))
        solid_rows[2, pl.ds(first, 8), :] = shift_lanes(value, -1, column(y_before, SOLID, 0, group))
    for axis in range(3):
        row_flow[axis, pl.ds(0, LEVELS), :] = before[FLOW + axis]
        row_flow[axis, pl.ds(LEVELS, LEVELS), :] = after[FLOW + axis]
    row_flow[3, pl.ds(0, LEVELS), :] = before[SOLID]
    row_flow[3, pl.ds(LEVELS, LEVELS), :] = after[SOLID]

    def both_rows(field, index, shift):
        ends = [field[index, pl.ds(place + shift, LEVELS), :] for place in (near, far)]
        return jnp.concatenate(ends, axis=0)

    here = [both_rows(held, n, 0) for n in range(19)]
    moved = [here[0]]
    for number in range(1, 19):
        cx, cy, cz = lattice_speeds[number]
        shift = LEVELS * cx + cz
        source = both_rows(held if cy == 0 else shifted, number, shift)
        closed = link_closed(both_rows(solid_rows, cy % 3, shift), cz)
        moved.append(jnp.where(closed, here[opposite_of(number)] + 2.0 * cx, source))
    row_results = collide(moved, [row_flow[axis] for axis in range(3)], 1.0 - row_flow[3])

    def columns(number_before, number_after, message_before, message_after):
        return jnp.where(
            lane < AFTER_LANE,
            column(message_before, number_before, BEFORE_LANE),
            column(message_after, number_after, AFTER_LANE),
        )

    def neighbours(slot, cy):
        if cy == 0:
            return columns(slot, slot, y_before, y_after)
        if cy == 1:
            beyond = SOLID if slot == SOLID else SECOND + y_up.index(slot)
            return columns(slot, beyond, low, y_after)
        beyond = SOLID if slot == SOLID else SECOND + y_down.index(slot)
        return columns(beyond, slot, y_before, high)

    upper = lax.broadcasted_iota(jnp.int32, (8, LANES), 0) < LEVELS

    def shift_rows(value, cx, cz):
        if cx != 0:
            swapped = pltpu.roll(value, LEVELS, 0)
            if cx == 1:
                value = jnp.where(upper, swapped, pltpu.roll(swapped, LANES - 1, 1))
            else:
                value = jnp.where(upper, pltpu.roll(swapped, 1, 1), swapped)
        if cz != 0:
            value = pltpu.roll(value, (-cz) % 8, 0)
        return value

    here = [neighbours(n, 0) for n in range(19)]
    solid_columns = [neighbours(SOLID, cy) for cy in (0, 1, -1)]
    moved = [here[0]]
    for number in range(1, 19):
        cx, cy, cz = lattice_speeds[number]
        source = shift_rows(here[number] if cy == 0 else neighbours(number, cy), cx, cz)
        closed = link_closed(shift_rows(solid_columns[cy % 3], cx, cz), cz)
        moved.append(jnp.where(closed, here[opposite_of(number)] + 2.0 * cx, source))
    column_flow = [neighbours(FLOW + axis, 0) for axis in range(3)]
    column_results = collide(moved, column_flow, 1.0 - solid_columns[0])

    def closed_at(first):
        return lambda number: blocked[number - 1, pl.ds(first, 8), :] == 1

    def fluid_at(first):
        return 1.0 - solid_parts[first // (LEVELS * TILE)]

    drag_sum = jnp.zeros((8, LANES), jnp.float32)
    flow = flow_blocks(velocity, 0, rows)
    for group in range(rows // 8):
        first = 8 * group
        moved = gather_cells(held, shifted, own + first, closed_at(first))
        results = collide(moved, flow[group], fluid_at(first))
        for number in range(19):
            later[number, pl.ds(own + first, 8), :] = results[number]
        drag_sum = drag_sum + drag_term(moved, flow[group], fluid_at(first))
    for number in x_down:
        later[number, pl.ds(near, LEVELS), :] = row_results[number][:LEVELS]
    for number in x_up:
        later[number, pl.ds(far, LEVELS), :] = row_results[number][LEVELS:]
    for number in y_up + y_down:
        cy = lattice_speeds[number][1]
        for group in range(groups):
            value = later[number, pl.ds(GUARD + 8 * group, 8), :]
            if cy == 1:
                edge = pltpu.roll(column_results[number], (LANES - 1 - AFTER_LANE - group) % LANES, 1)
            else:
                edge = pltpu.roll(column_results[number], (-BEFORE_LANE - group) % LANES, 1)
            later_shifted[number, pl.ds(GUARD + 8 * group, 8), :] = shift_lanes(value, cy, edge)

    flow = flow_blocks(velocity, 1, rows)
    for group in range(rows // 8):
        first = 8 * group
        moved = gather_cells(later, later_shifted, own + first, closed_at(first))
        drag_sum = drag_sum + drag_term(moved, flow[group], fluid_at(first))
    shared[...] = jnp.broadcast_to(jnp.sum(drag_sum), shared.shape)


def second_step_kernel(later, later_shifted, velocity, blocked, solid, out):
    rows = out.shape[1]
    solid_parts = spread_solid(solid)
    flow = flow_blocks(velocity, 1, rows)
    for group in range(rows // 8):
        first = 8 * group

        def closed(number):
            return blocked[number - 1, pl.ds(first, 8), :] == 1

        moved = gather_cells(later, later_shifted, GUARD + 8 + first, closed)
        results = collide(moved, flow[group], 1.0 - solid_parts[first // (LEVELS * TILE)])
        for number in range(19):
            out[number, pl.ds(first, 8), :] = results[number]


def swap_pairs(first, second, axis):
    count = lax.axis_size(axis)
    inside = [(i, i ^ 1) for i in range(count)]
    across = [(i, (i + 1) % count if i % 2 == 1 else (i - 1) % count) for i in range(count)]
    return lax.ppermute(first, axis, inside), lax.ppermute(second, axis, across)


def per_device(adjoint_in, velocity, solid_tiles, link_blocked):
    rows_x, levels, rows_y = adjoint_in.shape[1:]
    rows = rows_x * levels
    padded = rows + 16 + 2 * GUARD
    groups = rows // 8 + 2
    parts = -(-QUANTITIES // (LANES // groups))
    state = adjoint_in.reshape(19, rows, rows_y)
    flow = velocity.reshape(STEPS, 3, rows, rows_y)
    solid = solid_tiles.reshape(-1, solid_tiles.shape[2])
    blocked = link_blocked.reshape(18, rows, rows_y)

    def shape_of(*sizes):
        return jax.ShapeDtypeStruct(sizes, jnp.float32)

    params = pltpu.CompilerParams(vmem_limit_bytes=16 * 1024 * 1024)
    anywhere = pl.BlockSpec(memory_space=pl.ANY)
    row_sent = pl.pallas_call(
        row_message_kernel,
        out_shape=(shape_of(QUANTITIES, levels, rows_y),) * 2,
        in_specs=[anywhere] * 3,
        out_specs=(vmem,) * 2,
        scratch_shapes=[
            pltpu.VMEM((19, 8, rows_y), jnp.float32),
            pltpu.VMEM((19, 8, rows_y), jnp.float32),
            pltpu.VMEM((3, 16, rows_y), velocity.dtype),
            pltpu.VMEM((3, 16, rows_y), velocity.dtype),
            pltpu.VMEM(solid.shape, solid.dtype),
            pltpu.SemaphoreType.DMA((5,)),
        ],
        compiler_params=pltpu.CompilerParams(vmem_limit_bytes=60 * 1024 * 1024),
    )(state, flow, solid)
    row_got = swap_pairs(*row_sent, "gx")
    column_sent = pl.pallas_call(
        column_message_kernel,
        out_shape=(shape_of(parts, 8, rows_y),) * 2,
        in_specs=[vmem] * 5,
        out_specs=(vmem,) * 2,
        scratch_shapes=[pltpu.VMEM((2, SECOND, 8, rows_y), jnp.float32)],
        compiler_params=params,
    )(state, flow, solid, *row_got)
    column_got = swap_pairs(*column_sent, "gy")
    count = lax.axis_size("gx") * lax.axis_size("gy")
    field = pltpu.VMEM((19, padded, rows_y), jnp.float32)
    later, later_shifted, own = pl.pallas_call(
        first_step_kernel,
        out_shape=(shape_of(19, padded, rows_y),) * 2 + (shape_of(count, 1, rows_y),),
        in_specs=[vmem] * 10,
        out_specs=(vmem,) * 3,
        scratch_shapes=[
            field,
            field,
            pltpu.VMEM((4, 8, rows_y), jnp.float32),
            pltpu.VMEM((3, padded, rows_y), jnp.float32),
        ],
        compiler_params=params,
    )(state, flow, blocked, solid, *row_got, *column_got, *column_sent)
    shared = lax.all_to_all(own, ("gx", "gy"), split_axis=0, concat_axis=0, tiled=True)
    result = pl.pallas_call(
        second_step_kernel,
        out_shape=shape_of(19, rows, rows_y),
        in_specs=[vmem] * 5,
        out_specs=vmem,
        compiler_params=params,
        cost_estimate=pl.CostEstimate(flops=4_000_000, bytes_accessed=4_000_000, transcendentals=0),
    )(later, later_shifted, flow, blocked, solid)
    cell_count = rows * rows_y * count
    scale = drag_factor / math.sqrt(cell_count) * 3.0 / 36.0
    total = jnp.sum(shared[:, 0, 0])
    return (result.reshape(adjoint_in.shape), (-scale * total).reshape(1))


def solution(mesh):
    placed = (
        P(None, "gx", None, "gy"),
        P(None, None, "gx", None, "gy"),
        P("gx", None, "gy"),
        P(None, "gx", None, "gy"),
    )
    return jax.shard_map(
        per_device,
        mesh=mesh,
        in_specs=placed,
        out_specs=(P(None, "gx", None, "gy"), P()),
        check_vma=False,
    )
```

```python
import math

import jax
import jax.numpy as jnp
from jax import lax
from jax.experimental import pallas as pl
from jax.experimental.pallas import tpu as pltpu
from jax.sharding import PartitionSpec as P

TILE = 4
STEPS = 2

lattice_speeds = (
    (0, 0, 0),
    (1, 0, 0),
    (-1, 0, 0),
    (0, 1, 0),
    (0, -1, 0),
    (0, 0, 1),
    (0, 0, -1),
    (1, 1, 0),
    (-1, -1, 0),
    (1, -1, 0),
    (-1, 1, 0),
    (1, 0, 1),
    (-1, 0, -1),
    (1, 0, -1),
    (-1, 0, 1),
    (0, 1, 1),
    (0, -1, -1),
    (0, 1, -1),
    (0, -1, 1),
)
relax_rate = 1.6
drag_factor = 20.0
LEVELS = 4
LANES = 128
GUARD = 8

x_up = [n for n in range(19) if lattice_speeds[n][0] == 1]
x_down = [n for n in range(19) if lattice_speeds[n][0] == -1]
y_up = [n for n in range(19) if lattice_speeds[n][1] == 1]
y_down = [n for n in range(19) if lattice_speeds[n][1] == -1]
vmem = pl.BlockSpec(memory_space=pltpu.VMEM)

FLOW = 19
SOLID = 22
SECOND = 23
QUANTITIES = 28
BEFORE_LANE = 16
AFTER_LANE = 32


def opposite_of(number):
    return number + 1 if number % 2 == 1 else number - 1


def lane_index(rows=8):
    return lax.broadcasted_iota(jnp.int32, (rows, LANES), 1)


def spread_solid(solid):
    tiles = solid.shape[1]
    row = lax.broadcasted_iota(jnp.int32, (tiles, LANES), 0)
    column = lax.broadcasted_iota(jnp.int32, (tiles, LANES), 1)
    spread = (column // TILE == row).astype(jnp.float32)
    cells = jnp.dot(solid[...].astype(jnp.float32), spread, preferred_element_type=jnp.float32)
    blocks = []
    for tile_row in range(solid.shape[0] // LEVELS):
        part = cells[tile_row * LEVELS : (tile_row + 1) * LEVELS]
        blocks.append(jnp.concatenate([part, part], axis=0))
    return blocks


def flow_blocks(velocity, step, rows):
    blocks = []
    for pair in range(rows // 16):
        both = [velocity[step, axis, pl.ds(16 * pair, 16), :].astype(jnp.float32) for axis in range(3)]
        blocks.append([part[:8] for part in both])
        blocks.append([part[8:] for part in both])
    return blocks


def on_even(axis):
    return lax.rem(lax.axis_index(axis), 2) == 0


class Chosen:
    def __init__(self, choice, yes, no):
        self.choice, self.yes, self.no = choice, yes, no
        self.shape = yes.shape

    def __getitem__(self, index):
        return jnp.where(self.choice, self.yes[index], self.no[index])


def slot_place(slot, group, groups):
    per_block = LANES // groups
    return slot // per_block, (slot % per_block) * groups + group


def insert_column(parts, slot, group, groups, value, edge, ahead):
    part, place = slot_place(slot, group, groups)
    lane = lane_index()
    turned = pltpu.roll(value, (place + ahead - edge) % LANES, 1)
    parts[part] = jnp.where(lane == place + ahead, turned, parts[part])


def message_kernel(
    state, velocity, solid, row_first, row_second, column_first, column_second, cells, flow, tiles, arrived
):
    rows = state.shape[1]
    groups = rows // 8 + 2
    chunks = ((0, 7), (7, 6), (13, 6))
    copies = [
        pltpu.make_async_copy(velocity.at[0], flow, arrived.at[0]),
        pltpu.make_async_copy(solid, tiles, arrived.at[1]),
    ]
    for number, (first, count) in enumerate(chunks):
        part = pl.ds(first, count)
        copies.append(pltpu.make_async_copy(state.at[part], cells.at[part], arrived.at[2 + number]))
    for copy in copies:
        copy.start()
    x_even, y_even = on_even("gx"), on_even("gy")

    def put(slot, low, high):
        row_first[slot] = jnp.where(x_even, high, low)
        row_second[slot] = jnp.where(x_even, low, high)

    count = column_first.shape[0]
    low_parts = [jnp.zeros((8, LANES), jnp.float32) for _ in range(count)]
    high_parts = [jnp.zeros((8, LANES), jnp.float32) for _ in range(count)]

    def pack(slot, group, value):
        part, place = slot_place(slot, group, groups)
        lane = lane_index()
        turned = pltpu.roll(value, (place + 1) % LANES, 1)
        low_parts[part] = jnp.where(lane == place + 1, turned, low_parts[part])
        high_parts[part] = jnp.where(lane == place, turned, high_parts[part])
        if slot in y_up:
            insert_column(low_parts, SECOND + y_up.index(slot), group, groups, value, 1, 1)
        if slot in y_down:
            insert_column(high_parts, SECOND + y_down.index(slot), group, groups, value, LANES - 2, 0)

    copies[0].wait()
    for axis in range(3):
        blocks = []
        for pair in range(rows // 16):
            both = flow[axis, pl.ds(16 * pair, 16), :].astype(jnp.float32)
            blocks += [both[:8], both[8:]]
        for group, value in enumerate(blocks):
            pack(FLOW + axis, group + 1, value)
        put(FLOW + axis, blocks[0][:LEVELS], blocks[-1][LEVELS:])
    copies[1].wait()
    solid_parts = spread_solid(tiles)
    for group in range(rows // 8):
        pack(SOLID, group + 1, solid_parts[8 * group // (LEVELS * TILE)])
    put(SOLID, solid_parts[0][:LEVELS], solid_parts[-1][:LEVELS])
    for copy, (first, count) in zip(copies[2:], chunks):
        copy.wait()
        for number in range(first, first + count):
            for group in range(rows // 8):
                pack(number, group + 1, cells[number, pl.ds(8 * group, 8), :])
            put(number, cells[number, pl.ds(0, LEVELS), :], cells[number, pl.ds(rows - LEVELS, LEVELS), :])
    for slot in range(5):
        put(
            SECOND + slot,
            cells[x_up[slot], pl.ds(LEVELS, LEVELS), :],
            cells[x_down[slot], pl.ds(rows - 2 * LEVELS, LEVELS), :],
        )
    for part in range(len(low_parts)):
        column_first[part] = jnp.where(y_even, high_parts[part], low_parts[part])
        column_second[part] = jnp.where(y_even, low_parts[part], high_parts[part])


def corner_kernel(column_first, column_second, out):
    even = on_even("gy")
    count = column_first.shape[0]
    for part in range(count):
        out[part] = jnp.where(even, column_first[part], column_second[part])
        out[count + part] = jnp.where(even, column_second[part], column_first[part])


def collide(moved, flow, fluid):
    ux, uy, uz = flow
    total = {n: moved[n] + moved[n + 1] for n in range(1, 19, 2)}
    xy, xz, yz = total[7] + total[9], total[11] + total[13], total[15] + total[17]
    axis_x, axis_y, axis_z = 2.0 * total[1], 2.0 * total[3], 2.0 * total[5]
    density = 12.0 * moved[0] + (axis_x + axis_y + axis_z) + (xy + xz + yz)
    pxx = axis_x + xy + xz
    pyy = axis_y + xy + yz
    pzz = axis_z + xz + yz
    pxy = total[7] - total[9]
    pxz = total[11] - total[13]
    pyz = total[15] - total[17]
    dx, dy, dz = momentum(moved)
    vx = pxx * ux + pxy * uy + pxz * uz
    vy = pxy * ux + pyy * uy + pyz * uz
    vz = pxz * ux + pyz * uy + pzz * uz
    speed_sq = ux * ux + uy * uy + uz * uz
    scaled = (relax_rate / 36.0) * fluid
    base = scaled * (density + 1.5 * (speed_sq * density) - 4.5 * (ux * vx + uy * vy + uz * vz))
    scaled3 = 3.0 * scaled
    bx = scaled3 * (dx + 3.0 * vx - ux * density)
    by = scaled3 * (dy + 3.0 * vy - uy * density)
    bz = scaled3 * (dz + 3.0 * vz - uz * density)
    keep = (1.0 - relax_rate) * fluid
    results = [keep * moved[0] + base]
    for number in range(1, 19, 2):
        along = None
        for speed, part in zip(lattice_speeds[number], (bx, by, bz)):
            if speed == 0:
                continue
            if along is None:
                along = part if speed == 1 else -part
            else:
                along = along + part if speed == 1 else along - part
        results.append(keep * moved[number] + (base + along))
        results.append(keep * moved[number + 1] + (base - along))
    return results


def outside(cz):
    level = lax.broadcasted_iota(jnp.int32, (8, LANES), 0) % LEVELS
    return level == (LEVELS - 1 if cz == 1 else 0)


def link_closed(solid_there, cz):
    closed = solid_there > 0.5
    return closed | outside(cz) if cz != 0 else closed


def shift_lanes(value, cy, edge_value):
    lane = lane_index(value.shape[0])
    if cy == 1:
        return jnp.where(lane == LANES - 1, edge_value, pltpu.roll(value, LANES - 1, 1))
    return jnp.where(lane == 0, edge_value, pltpu.roll(value, 1, 1))


def gather_cells(held, shifted, first, solid_rows):
    here = [held[n, pl.ds(first, 8), :] for n in range(19)]
    moved = [here[0]]
    for number in range(1, 19):
        cx, cy, cz = lattice_speeds[number]
        field = held if cy == 0 else shifted
        there = pl.ds(first + LEVELS * cx + cz, 8)
        source = field[number, there, :]
        closed = link_closed(solid_rows[cy % 3, there, :], cz)
        bounced = here[opposite_of(number)]
        if cx != 0:
            bounced = bounced + 2.0 * cx
        moved.append(jnp.where(closed, bounced, source))
    return moved


def momentum(moved):
    gap = {n: moved[n] - moved[n + 1] for n in range(1, 19, 2)}
    dx = 2.0 * gap[1] + (gap[7] + gap[9]) + (gap[11] + gap[13])
    dy = 2.0 * gap[3] + (gap[7] - gap[9]) + (gap[15] + gap[17])
    dz = 2.0 * gap[5] + (gap[11] - gap[13]) + (gap[15] - gap[17])
    return dx, dy, dz


def drag_term(moved, flow, fluid):
    return fluid * sum(speed * part for speed, part in zip(flow, momentum(moved)))


def first_step_kernel(
    state, velocity, solid, row_first, row_second, column_first, column_second,
    sent_first, sent_second, corner_first, corner_second,
    later, later_shifted, solid_rows, shared, held, shifted, row_flow,
):
    rows = state.shape[1]
    even = on_even("gx")
    after, before = Chosen(even, row_first, row_second), Chosen(even, row_second, row_first)
    corner_after = Chosen(even, corner_first, corner_second)
    corner_before = Chosen(even, corner_second, corner_first)
    even = on_even("gy")
    parts = range(column_first.shape[0])

    def chosen(yes, no):
        return [jnp.where(even, yes[part], no[part]) for part in parts]

    low, high = chosen(sent_second, sent_first), chosen(sent_first, sent_second)
    groups = rows // 8 + 2
    own = GUARD + 8
    near, far = own - LEVELS, own + rows
    lane = lane_index()
    solid_parts = spread_solid(solid)

    def with_corners(yes, no, first_part, ahead):
        whole = []
        group = lax.rem(lane + groups - ahead, groups)
        inside = jnp.logical_and(lane >= ahead, lane < LANES // groups * groups + ahead)
        for part, own_rows in enumerate(chosen(yes, no)):
            above = pltpu.roll(corner_before[first_part + part], LANES - (groups - 2), 1)
            below = pltpu.roll(corner_after[first_part + part], groups - 2, 1)
            own_rows = jnp.where(jnp.logical_and(inside, group == 0), above, own_rows)
            whole.append(jnp.where(jnp.logical_and(inside, group == groups - 1), below, own_rows))
        return whole

    y_after = with_corners(column_first, column_second, 0, 1)
    y_before = with_corners(column_second, column_first, len(parts), 0)

    def column(message, slot, lane_first, group=0):
        part, place = slot_place(slot, group, groups)
        ahead = 1 if message is y_after or message is low else 0
        return pltpu.roll(message[part], (lane_first - place - ahead) % LANES, 1)

    for number in range(19):
        for group in range(rows // 8):
            held[number, pl.ds(own + 8 * group, 8), :] = state[number, pl.ds(8 * group, 8), :]
        held[number, pl.ds(near, LEVELS), :] = before[number]
        held[number, pl.ds(far, LEVELS), :] = after[number]
        if number in x_down:
            held[number, pl.ds(near - LEVELS, LEVELS), :] = before[SECOND + x_down.index(number)]
        if number in x_up:
            held[number, pl.ds(far + LEVELS, LEVELS), :] = after[SECOND + x_up.index(number)]
    for number in y_up + y_down:
        cy = lattice_speeds[number][1]
        for group in range(groups):
            value = held[number, pl.ds(GUARD + 8 * group, 8), :]
            if cy == 1:
                edge = column(y_after, number, LANES - 1, group)
            else:
                edge = column(y_before, number, 0, group)
            shifted[number, pl.ds(GUARD + 8 * group, 8), :] = shift_lanes(value, cy, edge)

    for group in range(groups):
        first = GUARD + 8 * group
        if group in (0, groups - 1):
            halo = before[SOLID] if group == 0 else after[SOLID]
            solid_rows[0, pl.ds(first, LEVELS), :] = halo
            solid_rows[0, pl.ds(first + LEVELS, LEVELS), :] = halo
        else:
            solid_rows[0, pl.ds(first, 8), :] = solid_parts[(group - 1) * 8 // (LEVELS * TILE)]
        value = solid_rows[0, pl.ds(first, 8), :]
        solid_rows[1, pl.ds(first, 8), :] = shift_lanes(value, 1, column(y_after, SOLID, LANES - 1, group))
        solid_rows[2, pl.ds(first, 8), :] = shift_lanes(value, -1, column(y_before, SOLID, 0, group))
    for axis in range(3):
        row_flow[axis, pl.ds(0, LEVELS), :] = before[FLOW + axis]
        row_flow[axis, pl.ds(LEVELS, LEVELS), :] = after[FLOW + axis]
    row_flow[3, pl.ds(0, LEVELS), :] = before[SOLID]
    row_flow[3, pl.ds(LEVELS, LEVELS), :] = after[SOLID]

    for group in (0, groups - 1):
        first = GUARD + 8 * group
        for slot in y_up + [SOLID]:
            value = solid_rows[0, pl.ds(first, 8), :] if slot == SOLID else held[slot, pl.ds(first, 8), :]
            insert_column(low, slot, group, groups, value, 0, 1)
        for slot in y_down + [SOLID]:
            value = solid_rows[0, pl.ds(first, 8), :] if slot == SOLID else held[slot, pl.ds(first, 8), :]
            insert_column(high, slot, group, groups, value, LANES - 1, 0)

    def both_rows(field, index, shift):
        ends = [field[index, pl.ds(place + shift, LEVELS), :] for place in (near, far)]
        return jnp.concatenate(ends, axis=0)

    here = [both_rows(held, n, 0) for n in range(19)]
    moved = [here[0]]
    for number in range(1, 19):
        cx, cy, cz = lattice_speeds[number]
        shift = LEVELS * cx + cz
        source = both_rows(held if cy == 0 else shifted, number, shift)
        closed = link_closed(both_rows(solid_rows, cy % 3, shift), cz)
        moved.append(jnp.where(closed, here[opposite_of(number)] + 2.0 * cx, source))
    row_results = collide(moved, [row_flow[axis] for axis in range(3)], 1.0 - row_flow[3])

    def columns(number_before, number_after, message_before, message_after):
        return jnp.where(
            lane < AFTER_LANE,
            column(message_before, number_before, BEFORE_LANE),
            column(message_after, number_after, AFTER_LANE),
        )

    def neighbours(slot, cy):
        if cy == 0:
            return columns(slot, slot, y_before, y_after)
        if cy == 1:
            beyond = SOLID if slot == SOLID else SECOND + y_up.index(slot)
            return columns(slot, beyond, low, y_after)
        beyond = SOLID if slot == SOLID else SECOND + y_down.index(slot)
        return columns(beyond, slot, y_before, high)

    upper = lax.broadcasted_iota(jnp.int32, (8, LANES), 0) < LEVELS

    def shift_rows(value, cx, cz):
        if cx != 0:
            swapped = pltpu.roll(value, LEVELS, 0)
            if cx == 1:
                value = jnp.where(upper, swapped, pltpu.roll(swapped, LANES - 1, 1))
            else:
                value = jnp.where(upper, pltpu.roll(swapped, 1, 1), swapped)
        if cz != 0:
            value = pltpu.roll(value, (-cz) % 8, 0)
        return value

    here = [neighbours(n, 0) for n in range(19)]
    solid_columns = [neighbours(SOLID, cy) for cy in (0, 1, -1)]
    moved = [here[0]]
    for number in range(1, 19):
        cx, cy, cz = lattice_speeds[number]
        source = shift_rows(here[number] if cy == 0 else neighbours(number, cy), cx, cz)
        closed = link_closed(shift_rows(solid_columns[cy % 3], cx, cz), cz)
        moved.append(jnp.where(closed, here[opposite_of(number)] + 2.0 * cx, source))
    column_flow = [neighbours(FLOW + axis, 0) for axis in range(3)]
    column_results = collide(moved, column_flow, 1.0 - solid_columns[0])

    def fluid_at(first):
        return 1.0 - solid_parts[first // (LEVELS * TILE)]

    drag_sum = jnp.zeros((8, LANES), jnp.float32)
    flow = flow_blocks(velocity, 0, rows)
    for group in range(rows // 8):
        first = 8 * group
        moved = gather_cells(held, shifted, own + first, solid_rows)
        results = collide(moved, flow[group], fluid_at(first))
        for number in range(19):
            later[number, pl.ds(own + first, 8), :] = results[number]
        drag_sum = drag_sum + drag_term(moved, flow[group], fluid_at(first))
    for number in x_down:
        later[number, pl.ds(near, LEVELS), :] = row_results[number][:LEVELS]
    for number in x_up:
        later[number, pl.ds(far, LEVELS), :] = row_results[number][LEVELS:]
    for number in y_up + y_down:
        cy = lattice_speeds[number][1]
        for group in range(groups):
            value = later[number, pl.ds(GUARD + 8 * group, 8), :]
            if cy == 1:
                edge = pltpu.roll(column_results[number], (LANES - 1 - AFTER_LANE - group) % LANES, 1)
            else:
                edge = pltpu.roll(column_results[number], (-BEFORE_LANE - group) % LANES, 1)
            later_shifted[number, pl.ds(GUARD + 8 * group, 8), :] = shift_lanes(value, cy, edge)

    flow = flow_blocks(velocity, 1, rows)
    for group in range(rows // 8):
        first = 8 * group
        moved = gather_cells(later, later_shifted, own + first, solid_rows)
        drag_sum = drag_sum + drag_term(moved, flow[group], fluid_at(first))
    shared[...] = jnp.broadcast_to(jnp.sum(drag_sum), shared.shape)


def second_step_kernel(later, later_shifted, solid_rows, velocity, out):
    rows = out.shape[1]
    flow = flow_blocks(velocity, 1, rows)
    for group in range(rows // 8):
        first = GUARD + 8 + 8 * group
        moved = gather_cells(later, later_shifted, first, solid_rows)
        results = collide(moved, flow[group], 1.0 - solid_rows[0, pl.ds(first, 8), :])
        for number in range(19):
            out[number, pl.ds(8 * group, 8), :] = results[number]


def sum_over(value, axis):
    count = lax.axis_size(axis)
    distance = 1
    while distance < count:
        value = value + lax.ppermute(value, axis, [(i, i ^ distance) for i in range(count)])
        distance *= 2
    return value


def swap_pairs(first, second, axis):
    count = lax.axis_size(axis)
    inside = [(i, i ^ 1) for i in range(count)]
    across = [(i, (i + 1) % count if i % 2 == 1 else (i - 1) % count) for i in range(count)]
    return lax.ppermute(first, axis, inside), lax.ppermute(second, axis, across)


def per_device(adjoint_in, velocity, solid_tiles, link_blocked):
    rows_x, levels, rows_y = adjoint_in.shape[1:]
    rows = rows_x * levels
    padded = rows + 16 + 2 * GUARD
    groups = rows // 8 + 2
    parts = -(-QUANTITIES // (LANES // groups))
    state = adjoint_in.reshape(19, rows, rows_y)
    flow = velocity.reshape(STEPS, 3, rows, rows_y)
    solid = solid_tiles.reshape(-1, solid_tiles.shape[2])

    def shape_of(*sizes):
        return jax.ShapeDtypeStruct(sizes, jnp.float32)

    params = pltpu.CompilerParams(vmem_limit_bytes=16 * 1024 * 1024)
    anywhere = pl.BlockSpec(memory_space=pl.ANY)
    sent = pl.pallas_call(
        message_kernel,
        out_shape=(shape_of(QUANTITIES, levels, rows_y),) * 2 + (shape_of(parts, 8, rows_y),) * 2,
        in_specs=[anywhere] * 3,
        out_specs=(vmem,) * 4,
        scratch_shapes=[
            pltpu.VMEM(state.shape, jnp.float32),
            pltpu.VMEM(flow.shape[1:], velocity.dtype),
            pltpu.VMEM(solid.shape, solid.dtype),
            pltpu.SemaphoreType.DMA((5,)),
        ],
        compiler_params=pltpu.CompilerParams(vmem_limit_bytes=60 * 1024 * 1024),
    )(state, flow, solid)
    column_sent = sent[2:]
    column_got = swap_pairs(*column_sent, "gy")
    row_got = swap_pairs(*sent[:2], "gx")
    corners = pl.pallas_call(
        corner_kernel,
        out_shape=shape_of(2 * parts, 8, rows_y),
        in_specs=[vmem] * 2,
        out_specs=vmem,
        compiler_params=params,
    )(*column_got)
    corner_got = swap_pairs(corners, corners, "gx")
    count = lax.axis_size("gx") * lax.axis_size("gy")
    field = pltpu.VMEM((19, padded, rows_y), jnp.float32)
    later, later_shifted, solid_rows, own = pl.pallas_call(
        first_step_kernel,
        out_shape=(
            shape_of(19, padded, rows_y),
            shape_of(19, padded, rows_y),
            shape_of(3, padded, rows_y),
            shape_of(1, rows_y),
        ),
        in_specs=[vmem] * 11,
        out_specs=(vmem,) * 4,
        scratch_shapes=[field, field, pltpu.VMEM((4, 8, rows_y), jnp.float32)],
        compiler_params=params,
    )(state, flow, solid, *row_got, *column_got, *column_sent, *corner_got)
    total = sum_over(sum_over(own, "gx"), "gy")
    result = pl.pallas_call(
        second_step_kernel,
        out_shape=shape_of(19, rows, rows_y),
        in_specs=[vmem] * 4,
        out_specs=vmem,
        compiler_params=params,
        cost_estimate=pl.CostEstimate(flops=4_000_000, bytes_accessed=4_000_000, transcendentals=0),
    )(later, later_shifted, solid_rows, flow)
    cell_count = rows * rows_y * count
    scale = drag_factor / math.sqrt(cell_count) * 3.0 / 36.0
    return (result.reshape(adjoint_in.shape), -scale * total[0, :1])


def solution(mesh):
    placed = (
        P(None, "gx", None, "gy"),
        P(None, None, "gx", None, "gy"),
        P("gx", None, "gy"),
        P(None, "gx", None, "gy"),
    )
    return jax.shard_map(
        per_device,
        mesh=mesh,
        in_specs=placed,
        out_specs=(P(None, "gx", None, "gy"), P()),
        check_vma=False,
    )
```

```python
import functools
import math

import jax
import jax.numpy as jnp
from jax import lax
from jax.experimental import pallas as pl
from jax.experimental.pallas import tpu as pltpu
from jax.sharding import PartitionSpec as P

TILE = 4
STEPS = 2

lattice_speeds = (
    (0, 0, 0),
    (1, 0, 0),
    (-1, 0, 0),
    (0, 1, 0),
    (0, -1, 0),
    (0, 0, 1),
    (0, 0, -1),
    (1, 1, 0),
    (-1, -1, 0),
    (1, -1, 0),
    (-1, 1, 0),
    (1, 0, 1),
    (-1, 0, -1),
    (1, 0, -1),
    (-1, 0, 1),
    (0, 1, 1),
    (0, -1, -1),
    (0, 1, -1),
    (0, -1, 1),
)
relax_rate = 1.6
drag_factor = 20.0
LEVELS = 4
LANES = 128
GUARD = 8

x_up = [n for n in range(19) if lattice_speeds[n][0] == 1]
x_down = [n for n in range(19) if lattice_speeds[n][0] == -1]
y_up = [n for n in range(19) if lattice_speeds[n][1] == 1]
y_down = [n for n in range(19) if lattice_speeds[n][1] == -1]
vmem = pl.BlockSpec(memory_space=pltpu.VMEM)

FLOW = 19
SOLID = 22
SECOND = 23
QUANTITIES = 28
BEFORE_LANE = 16
AFTER_LANE = 32


def opposite_of(number):
    return number + 1 if number % 2 == 1 else number - 1


def lane_index(rows=8):
    return lax.broadcasted_iota(jnp.int32, (rows, LANES), 1)


def spread_solid(solid):
    tiles = solid.shape[1]
    row = lax.broadcasted_iota(jnp.int32, (tiles, LANES), 0)
    column = lax.broadcasted_iota(jnp.int32, (tiles, LANES), 1)
    spread = (column // TILE == row).astype(jnp.float32)
    cells = jnp.dot(solid[...].astype(jnp.float32), spread, preferred_element_type=jnp.float32)
    blocks = []
    for tile_row in range(solid.shape[0] // LEVELS):
        part = cells[tile_row * LEVELS : (tile_row + 1) * LEVELS]
        blocks.append(jnp.concatenate([part, part], axis=0))
    return blocks


def flow_blocks(velocity, step, rows):
    blocks = []
    for pair in range(rows // 16):
        both = [velocity[step, axis, pl.ds(16 * pair, 16), :].astype(jnp.float32) for axis in range(3)]
        blocks.append([part[:8] for part in both])
        blocks.append([part[8:] for part in both])
    return blocks


def on_even(axis):
    return lax.rem(lax.axis_index(axis), 2) == 0


class Chosen:
    def __init__(self, choice, yes, no):
        self.choice, self.yes, self.no = choice, yes, no
        self.shape = yes.shape

    def __getitem__(self, index):
        return jnp.where(self.choice, self.yes[index], self.no[index])


def slot_place(slot, group, groups):
    per_block = LANES // groups
    return slot // per_block, (slot % per_block) * groups + group


def insert_column(parts, slot, group, groups, value, edge, ahead):
    part, place = slot_place(slot, group, groups)
    lane = lane_index()
    turned = pltpu.roll(value, (place + ahead - edge) % LANES, 1)
    parts[part] = jnp.where(lane == place + ahead, turned, parts[part])


def row_message_kernel(
    state, velocity, solid, row_first, row_second, held, flow, tiles, arrived
):
    rows = state.shape[1]
    own = pl.ds(GUARD + 8, rows)
    copies = [
        pltpu.make_async_copy(state, held.at[:, own, :], arrived.at[0]),
        pltpu.make_async_copy(velocity, flow, arrived.at[1]),
        pltpu.make_async_copy(solid, tiles, arrived.at[2]),
    ]
    for copy in copies:
        copy.start()
    for copy in copies:
        copy.wait()
    even = on_even("gx")
    low_row, high_row = GUARD + 8, GUARD + 8 + rows - LEVELS

    def put(slot, low, high):
        row_first[slot] = jnp.where(even, high, low)
        row_second[slot] = jnp.where(even, low, high)

    for number in range(19):
        put(number, held[number, pl.ds(low_row, LEVELS), :], held[number, pl.ds(high_row, LEVELS), :])
    for axis in range(3):
        low = flow[0, axis, pl.ds(0, 16), :].astype(jnp.float32)
        high = flow[0, axis, pl.ds(rows - 16, 16), :].astype(jnp.float32)
        put(FLOW + axis, low[:LEVELS], high[16 - LEVELS :])
    solid_parts = spread_solid(tiles)
    put(SOLID, solid_parts[0][:LEVELS], solid_parts[-1][:LEVELS])
    for slot in range(5):
        put(
            SECOND + slot,
            held[x_up[slot], pl.ds(low_row + LEVELS, LEVELS), :],
            held[x_down[slot], pl.ds(high_row - LEVELS, LEVELS), :],
        )


def pack_columns(parts, slot, group, groups, value):
    low_parts, high_parts = parts
    part, place = slot_place(slot, group, groups)
    lane = lane_index()
    turned = pltpu.roll(value, (place + 1) % LANES, 1)
    low_parts[part] = jnp.where(lane == place + 1, turned, low_parts[part])
    high_parts[part] = jnp.where(lane == place, turned, high_parts[part])
    if slot in y_up:
        insert_column(low_parts, SECOND + y_up.index(slot), group, groups, value, 1, 1)
    if slot in y_down:
        insert_column(high_parts, SECOND + y_down.index(slot), group, groups, value, LANES - 2, 0)


def own_columns_kernel(held, velocity, solid, low, high):
    rows = velocity.shape[2]
    groups = rows // 8 + 2
    solid_parts = spread_solid(solid)
    flow = flow_blocks(velocity, 0, rows)
    parts = [[jnp.zeros((8, LANES), jnp.float32) for _ in range(low.shape[0])] for _ in range(2)]
    for group in range(1, groups - 1):
        for slot in range(19):
            pack_columns(parts, slot, group, groups, held[slot, pl.ds(GUARD + 8 * group, 8), :])
        for axis in range(3):
            pack_columns(parts, FLOW + axis, group, groups, flow[group - 1][axis])
        pack_columns(parts, SOLID, group, groups, solid_parts[(group - 1) * 8 // (LEVELS * TILE)])
    for part in range(low.shape[0]):
        low[part] = parts[0][part]
        high[part] = parts[1][part]


def halo_columns_kernel(groups, own_low, own_high, row_first, row_second, first_out, second_out, ends):
    count = own_low.shape[0]
    even = on_even("gx")
    after, before = Chosen(even, row_first, row_second), Chosen(even, row_second, row_first)
    parts = [[own_low[part] for part in range(count)], [own_high[part] for part in range(count)]]
    for slot in range(SECOND):
        ends[0, slot, pl.ds(LEVELS, LEVELS), :] = before[slot]
        ends[1, slot, pl.ds(0, LEVELS), :] = after[slot]
        if slot == SOLID:
            low_second, high_second = SOLID, SOLID
        else:
            low_second = SECOND + x_down.index(slot) if slot in x_down else None
            high_second = SECOND + x_up.index(slot) if slot in x_up else None
        blank = jnp.zeros((LEVELS, LANES), jnp.float32)
        ends[0, slot, pl.ds(0, LEVELS), :] = blank if low_second is None else before[low_second]
        ends[1, slot, pl.ds(LEVELS, LEVELS), :] = blank if high_second is None else after[high_second]
        pack_columns(parts, slot, 0, groups, ends[0, slot])
        pack_columns(parts, slot, groups - 1, groups, ends[1, slot])
    even = on_even("gy")
    for part in range(count):
        first_out[part] = jnp.where(even, parts[1][part], parts[0][part])
        second_out[part] = jnp.where(even, parts[0][part], parts[1][part])


def collide(moved, flow, fluid):
    ux, uy, uz = flow
    total = {n: moved[n] + moved[n + 1] for n in range(1, 19, 2)}
    xy, xz, yz = total[7] + total[9], total[11] + total[13], total[15] + total[17]
    axis_x, axis_y, axis_z = 2.0 * total[1], 2.0 * total[3], 2.0 * total[5]
    density = 12.0 * moved[0] + (axis_x + axis_y + axis_z) + (xy + xz + yz)
    pxx = axis_x + xy + xz
    pyy = axis_y + xy + yz
    pzz = axis_z + xz + yz
    pxy = total[7] - total[9]
    pxz = total[11] - total[13]
    pyz = total[15] - total[17]
    dx, dy, dz = momentum(moved)
    vx = pxx * ux + pxy * uy + pxz * uz
    vy = pxy * ux + pyy * uy + pyz * uz
    vz = pxz * ux + pyz * uy + pzz * uz
    speed_sq = ux * ux + uy * uy + uz * uz
    scaled = (relax_rate / 36.0) * fluid
    base = scaled * (density + 1.5 * (speed_sq * density) - 4.5 * (ux * vx + uy * vy + uz * vz))
    scaled3 = 3.0 * scaled
    bx = scaled3 * (dx + 3.0 * vx - ux * density)
    by = scaled3 * (dy + 3.0 * vy - uy * density)
    bz = scaled3 * (dz + 3.0 * vz - uz * density)
    keep = (1.0 - relax_rate) * fluid
    results = [keep * moved[0] + base]
    for number in range(1, 19, 2):
        along = None
        for speed, part in zip(lattice_speeds[number], (bx, by, bz)):
            if speed == 0:
                continue
            if along is None:
                along = part if speed == 1 else -part
            else:
                along = along + part if speed == 1 else along - part
        results.append(keep * moved[number] + (base + along))
        results.append(keep * moved[number + 1] + (base - along))
    return results


def outside(cz):
    level = lax.broadcasted_iota(jnp.int32, (8, LANES), 0) % LEVELS
    return level == (LEVELS - 1 if cz == 1 else 0)


def link_closed(solid_there, cz):
    closed = solid_there > 0.5
    return closed | outside(cz) if cz != 0 else closed


def shift_lanes(value, cy, edge_value):
    lane = lane_index(value.shape[0])
    if cy == 1:
        return jnp.where(lane == LANES - 1, edge_value, pltpu.roll(value, LANES - 1, 1))
    return jnp.where(lane == 0, edge_value, pltpu.roll(value, 1, 1))


def gather_cells(held, shifted, first, solid_rows):
    here = [held[n, pl.ds(first, 8), :] for n in range(19)]
    moved = [here[0]]
    for number in range(1, 19):
        cx, cy, cz = lattice_speeds[number]
        field = held if cy == 0 else shifted
        there = pl.ds(first + LEVELS * cx + cz, 8)
        source = field[number, there, :]
        closed = link_closed(solid_rows[cy % 3, there, :], cz)
        bounced = here[opposite_of(number)]
        if cx != 0:
            bounced = bounced + 2.0 * cx
        moved.append(jnp.where(closed, bounced, source))
    return moved


def momentum(moved):
    gap = {n: moved[n] - moved[n + 1] for n in range(1, 19, 2)}
    dx = 2.0 * gap[1] + (gap[7] + gap[9]) + (gap[11] + gap[13])
    dy = 2.0 * gap[3] + (gap[7] - gap[9]) + (gap[15] + gap[17])
    dz = 2.0 * gap[5] + (gap[11] - gap[13]) + (gap[15] - gap[17])
    return dx, dy, dz


def drag_term(moved, flow, fluid):
    return fluid * sum(speed * part for speed, part in zip(flow, momentum(moved)))


def main_kernel(
    own_held, velocity, solid, row_first, row_second, column_first, column_second,
    sent_first, sent_second, out, shared, held, shifted, later, solid_rows, row_flow,
):
    rows = velocity.shape[2]
    even = on_even("gx")
    after, before = Chosen(even, row_first, row_second), Chosen(even, row_second, row_first)
    even = on_even("gy")
    parts = range(column_first.shape[0])

    def chosen(yes, no):
        return [jnp.where(even, yes[part], no[part]) for part in parts]

    low, high = chosen(sent_second, sent_first), chosen(sent_first, sent_second)
    y_after, y_before = chosen(column_first, column_second), chosen(column_second, column_first)
    groups = rows // 8 + 2
    own = GUARD + 8
    near, far = own - LEVELS, own + rows
    lane = lane_index()
    solid_parts = spread_solid(solid)

    def column(message, slot, lane_first, group=0):
        part, place = slot_place(slot, group, groups)
        ahead = 1 if message is y_after or message is low else 0
        return pltpu.roll(message[part], (lane_first - place - ahead) % LANES, 1)

    for number in range(19):
        for group in range(rows // 8):
            there = pl.ds(own + 8 * group, 8)
            held[number, there, :] = own_held[number, there, :]
        held[number, pl.ds(near, LEVELS), :] = before[number]
        held[number, pl.ds(far, LEVELS), :] = after[number]
        if number in x_down:
            held[number, pl.ds(near - LEVELS, LEVELS), :] = before[SECOND + x_down.index(number)]
        if number in x_up:
            held[number, pl.ds(far + LEVELS, LEVELS), :] = after[SECOND + x_up.index(number)]
    for number in y_up + y_down:
        cy = lattice_speeds[number][1]
        for group in range(groups):
            value = held[number, pl.ds(GUARD + 8 * group, 8), :]
            if cy == 1:
                edge = column(y_after, number, LANES - 1, group)
            else:
                edge = column(y_before, number, 0, group)
            shifted[number, pl.ds(GUARD + 8 * group, 8), :] = shift_lanes(value, cy, edge)

    for group in range(groups):
        first = GUARD + 8 * group
        if group in (0, groups - 1):
            halo = before[SOLID] if group == 0 else after[SOLID]
            solid_rows[0, pl.ds(first, LEVELS), :] = halo
            solid_rows[0, pl.ds(first + LEVELS, LEVELS), :] = halo
        else:
            solid_rows[0, pl.ds(first, 8), :] = solid_parts[(group - 1) * 8 // (LEVELS * TILE)]
        value = solid_rows[0, pl.ds(first, 8), :]
        solid_rows[1, pl.ds(first, 8), :] = shift_lanes(value, 1, column(y_after, SOLID, LANES - 1, group))
        solid_rows[2, pl.ds(first, 8), :] = shift_lanes(value, -1, column(y_before, SOLID, 0, group))
    for axis in range(3):
        row_flow[axis, pl.ds(0, LEVELS), :] = before[FLOW + axis]
        row_flow[axis, pl.ds(LEVELS, LEVELS), :] = after[FLOW + axis]
    row_flow[3, pl.ds(0, LEVELS), :] = before[SOLID]
    row_flow[3, pl.ds(LEVELS, LEVELS), :] = after[SOLID]

    def both_rows(field, index, shift):
        ends = [field[index, pl.ds(place + shift, LEVELS), :] for place in (near, far)]
        return jnp.concatenate(ends, axis=0)

    here = [both_rows(held, n, 0) for n in range(19)]
    moved = [here[0]]
    for number in range(1, 19):
        cx, cy, cz = lattice_speeds[number]
        shift = LEVELS * cx + cz
        source = both_rows(held if cy == 0 else shifted, number, shift)
        closed = link_closed(both_rows(solid_rows, cy % 3, shift), cz)
        moved.append(jnp.where(closed, here[opposite_of(number)] + 2.0 * cx, source))
    row_results = collide(moved, [row_flow[axis] for axis in range(3)], 1.0 - row_flow[3])

    def columns(number_before, number_after, message_before, message_after):
        return jnp.where(
            lane < AFTER_LANE,
            column(message_before, number_before, BEFORE_LANE),
            column(message_after, number_after, AFTER_LANE),
        )

    def neighbours(slot, cy):
        if cy == 0:
            return columns(slot, slot, y_before, y_after)
        if cy == 1:
            beyond = SOLID if slot == SOLID else SECOND + y_up.index(slot)
            return columns(slot, beyond, low, y_after)
        beyond = SOLID if slot == SOLID else SECOND + y_down.index(slot)
        return columns(beyond, slot, y_before, high)

    upper = lax.broadcasted_iota(jnp.int32, (8, LANES), 0) < LEVELS

    def shift_rows(value, cx, cz):
        if cx != 0:
            swapped = pltpu.roll(value, LEVELS, 0)
            if cx == 1:
                value = jnp.where(upper, swapped, pltpu.roll(swapped, LANES - 1, 1))
            else:
                value = jnp.where(upper, pltpu.roll(swapped, 1, 1), swapped)
        if cz != 0:
            value = pltpu.roll(value, (-cz) % 8, 0)
        return value

    here = [neighbours(n, 0) for n in range(19)]
    solid_columns = [neighbours(SOLID, cy) for cy in (0, 1, -1)]
    moved = [here[0]]
    for number in range(1, 19):
        cx, cy, cz = lattice_speeds[number]
        source = shift_rows(here[number] if cy == 0 else neighbours(number, cy), cx, cz)
        closed = link_closed(shift_rows(solid_columns[cy % 3], cx, cz), cz)
        moved.append(jnp.where(closed, here[opposite_of(number)] + 2.0 * cx, source))
    column_flow = [neighbours(FLOW + axis, 0) for axis in range(3)]
    column_results = collide(moved, column_flow, 1.0 - solid_columns[0])

    def fluid_at(first):
        return 1.0 - solid_parts[first // (LEVELS * TILE)]

    drag_sum = jnp.zeros((8, LANES), jnp.float32)
    flow = flow_blocks(velocity, 0, rows)
    for group in range(rows // 8):
        first = 8 * group
        moved = gather_cells(held, shifted, own + first, solid_rows)
        results = collide(moved, flow[group], fluid_at(first))
        for number in range(19):
            later[number, pl.ds(own + first, 8), :] = results[number]
        drag_sum = drag_sum + drag_term(moved, flow[group], fluid_at(first))
    for number in x_down:
        later[number, pl.ds(near, LEVELS), :] = row_results[number][:LEVELS]
    for number in x_up:
        later[number, pl.ds(far, LEVELS), :] = row_results[number][LEVELS:]
    for number in y_up + y_down:
        cy = lattice_speeds[number][1]
        for group in range(groups):
            value = later[number, pl.ds(GUARD + 8 * group, 8), :]
            if cy == 1:
                edge = pltpu.roll(column_results[number], (LANES - 1 - AFTER_LANE - group) % LANES, 1)
            else:
                edge = pltpu.roll(column_results[number], (-BEFORE_LANE - group) % LANES, 1)
            shifted[number, pl.ds(GUARD + 8 * group, 8), :] = shift_lanes(value, cy, edge)

    flow = flow_blocks(velocity, 1, rows)
    for group in range(rows // 8):
        first = 8 * group
        moved = gather_cells(later, shifted, own + first, solid_rows)
        results = collide(moved, flow[group], fluid_at(first))
        for number in range(19):
            out[number, pl.ds(first, 8), :] = results[number]
        drag_sum = drag_sum + drag_term(moved, flow[group], fluid_at(first))
    shared[...] = jnp.broadcast_to(jnp.sum(drag_sum), shared.shape)


def swap_pairs(first, second, axis):
    count = lax.axis_size(axis)
    inside = [(i, i ^ 1) for i in range(count)]
    across = [(i, (i + 1) % count if i % 2 == 1 else (i - 1) % count) for i in range(count)]
    return lax.ppermute(first, axis, inside), lax.ppermute(second, axis, across)


def per_device(adjoint_in, velocity, solid_tiles, link_blocked):
    rows_x, levels, rows_y = adjoint_in.shape[1:]
    rows = rows_x * levels
    padded = rows + 16 + 2 * GUARD
    groups = rows // 8 + 2
    parts = -(-QUANTITIES // (LANES // groups))
    state = adjoint_in.reshape(19, rows, rows_y)
    flow = velocity.reshape(STEPS, 3, rows, rows_y)
    solid = solid_tiles.reshape(-1, solid_tiles.shape[2])

    def shape_of(*sizes):
        return jax.ShapeDtypeStruct(sizes, jnp.float32)

    params = pltpu.CompilerParams(vmem_limit_bytes=16 * 1024 * 1024)
    anywhere = pl.BlockSpec(memory_space=pl.ANY)
    *row_sent, held, flow, tiles = pl.pallas_call(
        row_message_kernel,
        out_shape=(
            pltpu.VMEM((QUANTITIES, levels, rows_y), jnp.float32),
            pltpu.VMEM((QUANTITIES, levels, rows_y), jnp.float32),
            pltpu.VMEM((19, padded, rows_y), jnp.float32),
            pltpu.VMEM(flow.shape, flow.dtype),
            pltpu.VMEM(solid.shape, solid.dtype),
        ),
        in_specs=[anywhere] * 3,
        out_specs=(vmem,) * 5,
        scratch_shapes=[pltpu.SemaphoreType.DMA((3,))],
        compiler_params=params,
    )(*(pltpu.with_memory_space_constraint(value, pltpu.HBM) for value in (state, flow, solid)))
    row_got = swap_pairs(*row_sent, "gx")
    own_columns = pl.pallas_call(
        own_columns_kernel,
        out_shape=(shape_of(parts, 8, rows_y),) * 2,
        in_specs=[vmem] * 3,
        out_specs=(vmem,) * 2,
        compiler_params=params,
        cost_estimate=pl.CostEstimate(flops=2_000_000, bytes_accessed=1_000_000, transcendentals=0),
    )(held, flow, tiles)
    column_sent = pl.pallas_call(
        functools.partial(halo_columns_kernel, groups),
        out_shape=(shape_of(parts, 8, rows_y),) * 2,
        in_specs=[vmem] * 4,
        out_specs=(vmem,) * 2,
        scratch_shapes=[pltpu.VMEM((2, SECOND, 8, rows_y), jnp.float32)],
        compiler_params=params,
    )(*own_columns, *row_got)
    column_got = swap_pairs(*column_sent, "gy")
    count = lax.axis_size("gx") * lax.axis_size("gy")
    field = pltpu.VMEM((19, padded, rows_y), jnp.float32)
    result, own = pl.pallas_call(
        main_kernel,
        out_shape=(shape_of(19, rows, rows_y), shape_of(count, 1, rows_y)),
        in_specs=[vmem] * 9,
        out_specs=(vmem,) * 2,
        scratch_shapes=[
            field,
            field,
            field,
            pltpu.VMEM((3, padded, rows_y), jnp.float32),
            pltpu.VMEM((4, 8, rows_y), jnp.float32),
        ],
        compiler_params=params,
    )(held, flow, tiles, *row_got, *column_got, *column_sent)
    shared = lax.all_to_all(own, ("gx", "gy"), split_axis=0, concat_axis=0, tiled=True)
    cell_count = rows * rows_y * count
    scale = drag_factor / math.sqrt(cell_count) * 3.0 / 36.0
    total = jnp.sum(shared[:, 0, 0])
    return (result.reshape(adjoint_in.shape), (-scale * total).reshape(1))


def solution(mesh):
    placed = (
        P(None, "gx", None, "gy"),
        P(None, None, "gx", None, "gy"),
        P("gx", None, "gy"),
        P(None, "gx", None, "gy"),
    )
    return jax.shard_map(
        per_device,
        mesh=mesh,
        in_specs=placed,
        out_specs=(P(None, "gx", None, "gy"), P()),
        check_vma=False,
    )
```

```python
import functools
import math

import jax
import jax.numpy as jnp
from jax import lax
from jax.experimental import pallas as pl
from jax.experimental.pallas import tpu as pltpu
from jax.sharding import PartitionSpec as P

TILE = 4
STEPS = 2

lattice_speeds = (
    (0, 0, 0),
    (1, 0, 0),
    (-1, 0, 0),
    (0, 1, 0),
    (0, -1, 0),
    (0, 0, 1),
    (0, 0, -1),
    (1, 1, 0),
    (-1, -1, 0),
    (1, -1, 0),
    (-1, 1, 0),
    (1, 0, 1),
    (-1, 0, -1),
    (1, 0, -1),
    (-1, 0, 1),
    (0, 1, 1),
    (0, -1, -1),
    (0, 1, -1),
    (0, -1, 1),
)
relax_rate = 1.6
drag_factor = 20.0
LEVELS = 4
LANES = 128
GUARD = 8

x_up = [n for n in range(19) if lattice_speeds[n][0] == 1]
x_down = [n for n in range(19) if lattice_speeds[n][0] == -1]
y_up = [n for n in range(19) if lattice_speeds[n][1] == 1]
y_down = [n for n in range(19) if lattice_speeds[n][1] == -1]
vmem = pl.BlockSpec(memory_space=pltpu.VMEM)

FLOW = 19
SOLID = 22
NEXT = 23
SECOND = 26
QUANTITIES = 31
NEXT_SECOND = 31
COLUMN_QUANTITIES = 34
BEFORE_LANE = 16
AFTER_LANE = 32


def opposite_of(number):
    return number + 1 if number % 2 == 1 else number - 1


def lane_index(rows=8):
    return lax.broadcasted_iota(jnp.int32, (rows, LANES), 1)


def spread_solid(solid):
    tiles = solid.shape[1]
    row = lax.broadcasted_iota(jnp.int32, (tiles, LANES), 0)
    column = lax.broadcasted_iota(jnp.int32, (tiles, LANES), 1)
    spread = (column // TILE == row).astype(jnp.float32)
    cells = jnp.dot(solid[...].astype(jnp.float32), spread, preferred_element_type=jnp.float32)
    blocks = []
    for tile_row in range(solid.shape[0] // LEVELS):
        part = cells[tile_row * LEVELS : (tile_row + 1) * LEVELS]
        blocks.append(jnp.concatenate([part, part], axis=0))
    return blocks


def flow_blocks(velocity, step, rows):
    blocks = []
    for pair in range(rows // 16):
        both = [velocity[step, axis, pl.ds(16 * pair, 16), :].astype(jnp.float32) for axis in range(3)]
        blocks.append([part[:8] for part in both])
        blocks.append([part[8:] for part in both])
    return blocks


def on_even(axis):
    return lax.rem(lax.axis_index(axis), 2) == 0


class Chosen:
    def __init__(self, choice, yes, no):
        self.choice, self.yes, self.no = choice, yes, no
        self.shape = yes.shape

    def __getitem__(self, index):
        return jnp.where(self.choice, self.yes[index], self.no[index])


def slot_place(slot, group, groups):
    per_block = LANES // groups
    return slot // per_block, (slot % per_block) * groups + group


def insert_column(parts, slot, group, groups, value, edge, ahead):
    part, place = slot_place(slot, group, groups)
    lane = lane_index()
    turned = pltpu.roll(value, (place + ahead - edge) % LANES, 1)
    parts[part] = jnp.where(lane == place + ahead, turned, parts[part])


def row_message_kernel(
    state, velocity, solid, row_first, row_second, held, flow, tiles, arrived
):
    rows = state.shape[1]
    own = pl.ds(GUARD + 8, rows)
    copies = [
        pltpu.make_async_copy(state, held.at[:, own, :], arrived.at[0]),
        pltpu.make_async_copy(velocity, flow, arrived.at[1]),
        pltpu.make_async_copy(solid, tiles, arrived.at[2]),
    ]
    for copy in copies:
        copy.start()
    for copy in copies:
        copy.wait()
    even = on_even("gx")
    low_row, high_row = GUARD + 8, GUARD + 8 + rows - LEVELS

    def put(slot, low, high):
        row_first[slot] = jnp.where(even, high, low)
        row_second[slot] = jnp.where(even, low, high)

    for number in range(19):
        put(number, held[number, pl.ds(low_row, LEVELS), :], held[number, pl.ds(high_row, LEVELS), :])
    for step, slot in ((0, FLOW), (1, NEXT)):
        for axis in range(3):
            low = flow[step, axis, pl.ds(0, 16), :].astype(jnp.float32)
            high = flow[step, axis, pl.ds(rows - 16, 16), :].astype(jnp.float32)
            put(slot + axis, low[:LEVELS], high[16 - LEVELS :])
    solid_parts = spread_solid(tiles)
    put(SOLID, solid_parts[0][:LEVELS], solid_parts[-1][:LEVELS])
    for slot in range(5):
        put(
            SECOND + slot,
            held[x_up[slot], pl.ds(low_row + LEVELS, LEVELS), :],
            held[x_down[slot], pl.ds(high_row - LEVELS, LEVELS), :],
        )


def pack_columns(parts, slot, group, groups, value):
    low_parts, high_parts = parts
    part, place = slot_place(slot, group, groups)
    lane = lane_index()
    turned = pltpu.roll(value, (place + 1) % LANES, 1)
    low_parts[part] = jnp.where(lane == place + 1, turned, low_parts[part])
    high_parts[part] = jnp.where(lane == place, turned, high_parts[part])
    if slot in y_up:
        insert_column(low_parts, SECOND + y_up.index(slot), group, groups, value, 1, 1)
    if slot in y_down:
        insert_column(high_parts, SECOND + y_down.index(slot), group, groups, value, LANES - 2, 0)
    if NEXT <= slot < NEXT + 3:
        insert_column(high_parts, NEXT_SECOND + slot - NEXT, group, groups, value, LANES - 2, 0)


def own_columns_kernel(held, velocity, solid, low, high):
    rows = velocity.shape[2]
    groups = rows // 8 + 2
    solid_parts = spread_solid(solid)
    flow = [flow_blocks(velocity, step, rows) for step in range(2)]
    parts = [[jnp.zeros((8, LANES), jnp.float32) for _ in range(low.shape[0])] for _ in range(2)]
    for group in range(1, groups - 1):
        for slot in range(19):
            pack_columns(parts, slot, group, groups, held[slot, pl.ds(GUARD + 8 * group, 8), :])
        for axis in range(3):
            pack_columns(parts, FLOW + axis, group, groups, flow[0][group - 1][axis])
            pack_columns(parts, NEXT + axis, group, groups, flow[1][group - 1][axis])
        pack_columns(parts, SOLID, group, groups, solid_parts[(group - 1) * 8 // (LEVELS * TILE)])
    for part in range(low.shape[0]):
        low[part] = parts[0][part]
        high[part] = parts[1][part]


def halo_columns_kernel(groups, own_low, own_high, row_first, row_second, low_out, high_out, ends):
    count = own_low.shape[0]
    even = on_even("gx")
    after, before = Chosen(even, row_first, row_second), Chosen(even, row_second, row_first)
    parts = [[own_low[part] for part in range(count)], [own_high[part] for part in range(count)]]
    for slot in range(SECOND):
        ends[0, slot, pl.ds(LEVELS, LEVELS), :] = before[slot]
        ends[1, slot, pl.ds(0, LEVELS), :] = after[slot]
        if slot == SOLID:
            low_second, high_second = SOLID, SOLID
        else:
            low_second = SECOND + x_down.index(slot) if slot in x_down else None
            high_second = SECOND + x_up.index(slot) if slot in x_up else None
        blank = jnp.zeros((LEVELS, LANES), jnp.float32)
        ends[0, slot, pl.ds(0, LEVELS), :] = blank if low_second is None else before[low_second]
        ends[1, slot, pl.ds(LEVELS, LEVELS), :] = blank if high_second is None else after[high_second]
        pack_columns(parts, slot, 0, groups, ends[0, slot])
        pack_columns(parts, slot, groups - 1, groups, ends[1, slot])
    for part in range(count):
        low_out[part] = parts[0][part]
        high_out[part] = parts[1][part]


def collide(moved, flow, fluid):
    ux, uy, uz = flow
    total = {n: moved[n] + moved[n + 1] for n in range(1, 19, 2)}
    xy, xz, yz = total[7] + total[9], total[11] + total[13], total[15] + total[17]
    axis_x, axis_y, axis_z = 2.0 * total[1], 2.0 * total[3], 2.0 * total[5]
    density = 12.0 * moved[0] + (axis_x + axis_y + axis_z) + (xy + xz + yz)
    pxx = axis_x + xy + xz
    pyy = axis_y + xy + yz
    pzz = axis_z + xz + yz
    pxy = total[7] - total[9]
    pxz = total[11] - total[13]
    pyz = total[15] - total[17]
    dx, dy, dz = momentum(moved)
    vx = pxx * ux + pxy * uy + pxz * uz
    vy = pxy * ux + pyy * uy + pyz * uz
    vz = pxz * ux + pyz * uy + pzz * uz
    speed_sq = ux * ux + uy * uy + uz * uz
    scaled = (relax_rate / 36.0) * fluid
    base = scaled * (density + 1.5 * (speed_sq * density) - 4.5 * (ux * vx + uy * vy + uz * vz))
    scaled3 = 3.0 * scaled
    bx = scaled3 * (dx + 3.0 * vx - ux * density)
    by = scaled3 * (dy + 3.0 * vy - uy * density)
    bz = scaled3 * (dz + 3.0 * vz - uz * density)
    keep = (1.0 - relax_rate) * fluid
    results = [keep * moved[0] + base]
    for number in range(1, 19, 2):
        along = None
        for speed, part in zip(lattice_speeds[number], (bx, by, bz)):
            if speed == 0:
                continue
            if along is None:
                along = part if speed == 1 else -part
            else:
                along = along + part if speed == 1 else along - part
        results.append(keep * moved[number] + (base + along))
        results.append(keep * moved[number + 1] + (base - along))
    return results


def outside(cz):
    level = lax.broadcasted_iota(jnp.int32, (8, LANES), 0) % LEVELS
    return level == (LEVELS - 1 if cz == 1 else 0)


def link_closed(solid_there, cz):
    closed = solid_there > 0.5
    return closed | outside(cz) if cz != 0 else closed


def shift_lanes(value, cy, edge_value):
    lane = lane_index(value.shape[0])
    shifted = pltpu.roll(value, -cy % LANES, 1)
    if edge_value is None:
        return shifted
    return jnp.where(lane == (LANES - 1 if cy == 1 else 0), edge_value, shifted)


def gather_cells(held, shifted, first, solid_rows):
    here = [held[n, pl.ds(first, 8), :] for n in range(19)]
    moved, closed = [here[0]], [None]
    for number in range(1, 19):
        cx, cy, cz = lattice_speeds[number]
        field = held if cy == 0 else shifted
        there = pl.ds(first + LEVELS * cx + cz, 8)
        closed.append(link_closed(solid_rows[cy % 3, there, :], cz))
        bounced = here[opposite_of(number)]
        if cx != 0:
            bounced = bounced + 2.0 * cx
        moved.append(jnp.where(closed[number], bounced, field[number, there, :]))
    return moved, closed


def momentum(moved):
    gap = {n: moved[n] - moved[n + 1] for n in range(1, 19, 2)}
    dx = 2.0 * gap[1] + (gap[7] + gap[9]) + (gap[11] + gap[13])
    dy = 2.0 * gap[3] + (gap[7] - gap[9]) + (gap[15] + gap[17])
    dz = 2.0 * gap[5] + (gap[11] - gap[13]) + (gap[15] - gap[17])
    return dx, dy, dz


def drag_term(moved, flow, fluid):
    return fluid * sum(speed * part for speed, part in zip(flow, momentum(moved)))


def along_link(number, vector):
    total = None
    for axis, speed in enumerate(lattice_speeds[number]):
        if speed == 0:
            continue
        part = vector(axis)
        if total is None:
            total = part if speed == 1 else -part
        else:
            total = total + part if speed == 1 else total - part
    return total


def later_drag(results, closed, weight_here, weight_back):
    term = None
    for number in range(1, 19):
        cx = lattice_speeds[number][0]
        here = along_link(number, lambda axis: weight_here[axis])
        back = along_link(number, lambda axis: weight_back(number, axis))
        part = jnp.where(closed[opposite_of(number)], -here, back) * results[number]
        if cx != 0:
            part = part + jnp.where(closed[number], (2.0 * cx) * here, 0.0)
        if number < 7:
            part = 2.0 * part
        term = part if term is None else term + part
    return term


def column_reader(groups):
    def column(message, ahead, slot, lane_first, group=0):
        part, place = slot_place(slot, group, groups)
        return pltpu.roll(message[part], (lane_first - place - ahead) % LANES, 1)

    return column


def fill_held(own_held, before, after, held, rows):
    own = GUARD + 8
    near, far = own - LEVELS, own + rows
    for number in range(19):
        for group in range(rows // 8):
            there = pl.ds(own + 8 * group, 8)
            held[number, there, :] = own_held[number, there, :]
        held[number, pl.ds(near, LEVELS), :] = before[number]
        held[number, pl.ds(far, LEVELS), :] = after[number]
        if number in x_down:
            held[number, pl.ds(near - LEVELS, LEVELS), :] = before[SECOND + x_down.index(number)]
        if number in x_up:
            held[number, pl.ds(far + LEVELS, LEVELS), :] = after[SECOND + x_up.index(number)]


def fill_shifted(field, shifted, groups, edge_of):
    for number in y_up + y_down:
        cy = lattice_speeds[number][1]
        for group in range(groups):
            there = pl.ds(GUARD + 8 * group, 8)
            shifted[number, there, :] = shift_lanes(field[number, there, :], cy, edge_of(number, cy, group))


def fill_solid(solid_parts, before, after, solid_rows, groups, edge_of):
    for group in range(groups):
        first = GUARD + 8 * group
        if group in (0, groups - 1):
            halo = before[SOLID] if group == 0 else after[SOLID]
            solid_rows[0, pl.ds(first, LEVELS), :] = halo
            solid_rows[0, pl.ds(first + LEVELS, LEVELS), :] = halo
        else:
            solid_rows[0, pl.ds(first, 8), :] = solid_parts[(group - 1) * 8 // (LEVELS * TILE)]
        value = solid_rows[0, pl.ds(first, 8), :]
        for cy in (1, -1):
            solid_rows[cy % 3, pl.ds(first, 8), :] = shift_lanes(value, cy, edge_of(SOLID, cy, group))


def shift_rows(value, cx, cz):
    if cx != 0:
        upper = lax.broadcasted_iota(jnp.int32, (8, LANES), 0) < LEVELS
        swapped = pltpu.roll(value, LEVELS, 0)
        if cx == 1:
            value = jnp.where(upper, swapped, pltpu.roll(swapped, LANES - 1, 1))
        else:
            value = jnp.where(upper, pltpu.roll(swapped, 1, 1), swapped)
    if cz != 0:
        value = pltpu.roll(value, (-cz) % 8, 0)
    return value


def gather_columns(neighbours):
    here = [neighbours(n, 0) for n in range(19)]
    solid = {cy: neighbours(SOLID, cy) for cy in (0, 1, -1)}
    moved, closed = [here[0]], [None]
    for number in range(1, 19):
        cx, cy, cz = lattice_speeds[number]
        source = shift_rows(here[number] if cy == 0 else neighbours(number, cy), cx, cz)
        closed.append(link_closed(shift_rows(solid[cy], cx, cz), cz))
        moved.append(jnp.where(closed[number], here[opposite_of(number)] + 2.0 * cx, source))
    return moved, closed, solid


def drag_kernel(
    own_held, velocity, solid, row_first, row_second, y_before, low, shared,
    held, shifted, solid_rows, weights,
):
    rows = velocity.shape[2]
    groups = rows // 8 + 2
    own = GUARD + 8
    near, far = own - LEVELS, own + rows
    even = on_even("gx")
    after, before = Chosen(even, row_first, row_second), Chosen(even, row_second, row_first)
    lane = lane_index()
    solid_parts = spread_solid(solid)
    column = column_reader(groups)

    def edge_of(slot, cy, group):
        return None if cy == 1 else column(y_before, 0, slot, 0, group)

    fill_held(own_held, before, after, held, rows)
    fill_shifted(held, shifted, groups, edge_of)
    fill_solid(solid_parts, before, after, solid_rows, groups, edge_of)

    flow = flow_blocks(velocity, 1, rows)
    for axis in range(3):
        for group in range(rows // 8):
            there = pl.ds(own + 8 * group, 8)
            weights[axis, there, :] = (1.0 - solid_rows[0, there, :]) * flow[group][axis]
        for row, message in ((near, before), (far, after)):
            weights[axis, pl.ds(row, LEVELS), :] = (1.0 - message[SOLID]) * message[NEXT + axis]
        for group in range(groups):
            there = pl.ds(GUARD + 8 * group, 8)
            value = weights[axis, there, :]
            edge = (1.0 - column(y_before, 0, SOLID, 0, group)) * column(y_before, 0, NEXT + axis, 0, group)
            weights[3 + axis, there, :] = shift_lanes(value, 1, None)
            weights[6 + axis, there, :] = shift_lanes(value, -1, edge)

    total = jnp.zeros((8, LANES), jnp.float32)
    flow = flow_blocks(velocity, 0, rows)
    for group in range(rows // 8):
        first = own + 8 * group
        moved, closed = gather_cells(held, shifted, first, solid_rows)
        fluid = 1.0 - solid_parts[8 * group // (LEVELS * TILE)]
        results = collide(moved, flow[group], fluid)

        def back(number, axis):
            cx, cy, cz = lattice_speeds[number]
            return weights[3 * (-cy % 3) + axis, pl.ds(first - LEVELS * cx - cz, 8), :]

        here = [weights[axis, pl.ds(first, 8), :] for axis in range(3)]
        total = total + drag_term(moved, flow[group], fluid) + later_drag(results, closed, here, back)
    total = jnp.where(lane < LANES - 1, total, 0.0)

    def neighbours(slot, cy):
        if cy == 1:
            return column(low, 1, slot, BEFORE_LANE)
        if cy == -1 and slot != SOLID:
            slot = SECOND + y_down.index(slot)
        return column(y_before, 0, slot, BEFORE_LANE)

    moved, closed, solid_columns = gather_columns(neighbours)
    fluid = {cy: 1.0 - solid_columns[cy] for cy in (0, 1, -1)}
    column_flow = [neighbours(FLOW + axis, 0) for axis in range(3)]
    results = collide(moved, column_flow, fluid[0])
    weight = {
        0: [fluid[0] * neighbours(NEXT + axis, 0) for axis in range(3)],
        1: [fluid[1] * neighbours(NEXT + axis, 1) for axis in range(3)],
        -1: [fluid[-1] * neighbours(NEXT_SECOND + axis, 0) for axis in range(3)],
    }

    def back_column(number, axis):
        cx, cy, cz = lattice_speeds[number]
        return shift_rows(weight[-cy][axis], -cx, -cz)

    term = drag_term(moved, column_flow, fluid[0]) + later_drag(results, closed, weight[0], back_column)
    inside = jnp.logical_and(lane > BEFORE_LANE, lane < BEFORE_LANE + groups - 1)
    total = total + jnp.where(inside, term, 0.0)
    shared[...] = jnp.broadcast_to(jnp.sum(total), shared.shape)


def main_kernel(
    own_held, velocity, solid, row_first, row_second, y_after, y_before, low, high, out,
    held, shifted, later, solid_rows, row_flow,
):
    rows = velocity.shape[2]
    groups = rows // 8 + 2
    own = GUARD + 8
    near, far = own - LEVELS, own + rows
    even = on_even("gx")
    after, before = Chosen(even, row_first, row_second), Chosen(even, row_second, row_first)
    lane = lane_index()
    solid_parts = spread_solid(solid)
    column = column_reader(groups)

    def edge_of(slot, cy, group):
        if cy == 1:
            return column(y_after, 1, slot, LANES - 1, group)
        return column(y_before, 0, slot, 0, group)

    fill_held(own_held, before, after, held, rows)
    fill_shifted(held, shifted, groups, edge_of)
    fill_solid(solid_parts, before, after, solid_rows, groups, edge_of)
    for slot, place in ((FLOW, 0), (FLOW + 1, 1), (FLOW + 2, 2), (SOLID, 3)):
        row_flow[place, pl.ds(0, LEVELS), :] = before[slot]
        row_flow[place, pl.ds(LEVELS, LEVELS), :] = after[slot]

    def both_rows(field, index, shift):
        ends = [field[index, pl.ds(place + shift, LEVELS), :] for place in (near, far)]
        return jnp.concatenate(ends, axis=0)

    here = [both_rows(held, n, 0) for n in range(19)]
    moved = [here[0]]
    for number in range(1, 19):
        cx, cy, cz = lattice_speeds[number]
        shift = LEVELS * cx + cz
        source = both_rows(held if cy == 0 else shifted, number, shift)
        closed = link_closed(both_rows(solid_rows, cy % 3, shift), cz)
        moved.append(jnp.where(closed, here[opposite_of(number)] + 2.0 * cx, source))
    row_results = collide(moved, [row_flow[axis] for axis in range(3)], 1.0 - row_flow[3])

    def neighbours(slot, cy):
        beyond = slot if cy == 0 or slot == SOLID else SECOND + (y_up if cy == 1 else y_down).index(slot)
        if cy == 1:
            first, second = column(low, 1, slot, BEFORE_LANE), column(y_after, 1, beyond, AFTER_LANE)
        elif cy == -1:
            first, second = column(y_before, 0, beyond, BEFORE_LANE), column(high, 0, slot, AFTER_LANE)
        else:
            first, second = column(y_before, 0, slot, BEFORE_LANE), column(y_after, 1, slot, AFTER_LANE)
        return jnp.where(lane < AFTER_LANE, first, second)

    moved, _, solid_columns = gather_columns(neighbours)
    column_flow = [neighbours(FLOW + axis, 0) for axis in range(3)]
    column_results = collide(moved, column_flow, 1.0 - solid_columns[0])

    flow = flow_blocks(velocity, 0, rows)
    for group in range(rows // 8):
        first = own + 8 * group
        moved, _ = gather_cells(held, shifted, first, solid_rows)
        results = collide(moved, flow[group], 1.0 - solid_parts[8 * group // (LEVELS * TILE)])
        for number in range(19):
            later[number, pl.ds(first, 8), :] = results[number]
    for number in x_down:
        later[number, pl.ds(near, LEVELS), :] = row_results[number][:LEVELS]
    for number in x_up:
        later[number, pl.ds(far, LEVELS), :] = row_results[number][LEVELS:]

    def later_edge(number, cy, group):
        shift = LANES - 1 - AFTER_LANE - group if cy == 1 else -BEFORE_LANE - group
        return pltpu.roll(column_results[number], shift % LANES, 1)

    fill_shifted(later, shifted, groups, later_edge)

    flow = flow_blocks(velocity, 1, rows)
    for group in range(rows // 8):
        first = 8 * group
        moved, _ = gather_cells(later, shifted, own + first, solid_rows)
        results = collide(moved, flow[group], 1.0 - solid_parts[first // (LEVELS * TILE)])
        for number in range(19):
            out[number, pl.ds(first, 8), :] = results[number]


def swap_pairs(first, second, axis):
    count = lax.axis_size(axis)
    inside = [(i, i ^ 1) for i in range(count)]
    across = [(i, (i + 1) % count if i % 2 == 1 else (i - 1) % count) for i in range(count)]
    second = lax.ppermute(second, axis, across)
    return lax.ppermute(first, axis, inside), second


def per_device(adjoint_in, velocity, solid_tiles, link_blocked):
    rows_x, levels, rows_y = adjoint_in.shape[1:]
    rows = rows_x * levels
    padded = rows + 16 + 2 * GUARD
    groups = rows // 8 + 2
    parts = -(-COLUMN_QUANTITIES // (LANES // groups))
    state = adjoint_in.reshape(19, rows, rows_y)
    flow = velocity.reshape(STEPS, 3, rows, rows_y)
    solid = solid_tiles.reshape(-1, solid_tiles.shape[2])

    def shape_of(*sizes):
        return jax.ShapeDtypeStruct(sizes, jnp.float32)

    params = pltpu.CompilerParams(vmem_limit_bytes=16 * 1024 * 1024)
    anywhere = pl.BlockSpec(memory_space=pl.ANY)
    *row_sent, held, flow, tiles = pl.pallas_call(
        row_message_kernel,
        out_shape=(
            pltpu.VMEM((QUANTITIES, levels, rows_y), jnp.float32),
            pltpu.VMEM((QUANTITIES, levels, rows_y), jnp.float32),
            pltpu.VMEM((19, padded, rows_y), jnp.float32),
            pltpu.VMEM(flow.shape, flow.dtype),
            pltpu.VMEM(solid.shape, solid.dtype),
        ),
        in_specs=[anywhere] * 3,
        out_specs=(vmem,) * 5,
        scratch_shapes=[pltpu.SemaphoreType.DMA((3,))],
        compiler_params=params,
    )(*(pltpu.with_memory_space_constraint(value, pltpu.HBM) for value in (state, flow, solid)))
    row_got = swap_pairs(*row_sent, "gx")
    own_columns = pl.pallas_call(
        own_columns_kernel,
        out_shape=(shape_of(parts, 8, rows_y),) * 2,
        in_specs=[vmem] * 3,
        out_specs=(vmem,) * 2,
        compiler_params=params,
        cost_estimate=pl.CostEstimate(flops=2_000_000, bytes_accessed=1_000_000, transcendentals=0),
    )(held, flow, tiles)
    low, high = pl.pallas_call(
        functools.partial(halo_columns_kernel, groups),
        out_shape=(shape_of(parts, 8, rows_y),) * 2,
        in_specs=[vmem] * 4,
        out_specs=(vmem,) * 2,
        scratch_shapes=[pltpu.VMEM((2, SECOND, 8, rows_y), jnp.float32)],
        compiler_params=params,
    )(*own_columns, *row_got)
    size = lax.axis_size("gy")
    y_before = lax.ppermute(high, "gy", [(i, (i + 1) % size) for i in range(size)])
    y_after = lax.ppermute(low, "gy", [((i + 1) % size, i) for i in range(size)])
    count = lax.axis_size("gx") * size
    field = pltpu.VMEM((19, padded, rows_y), jnp.float32)
    solid_field = pltpu.VMEM((3, padded, rows_y), jnp.float32)
    own = pl.pallas_call(
        drag_kernel,
        out_shape=pltpu.VMEM((count, 1, rows_y), jnp.float32),
        in_specs=[vmem] * 7,
        out_specs=vmem,
        scratch_shapes=[field, field, solid_field, pltpu.VMEM((9, padded, rows_y), jnp.float32)],
        compiler_params=params,
    )(held, flow, tiles, *row_got, y_before, low)
    shared = lax.all_to_all(own, ("gx", "gy"), split_axis=0, concat_axis=0, tiled=True)
    result = pl.pallas_call(
        main_kernel,
        out_shape=shape_of(19, rows, rows_y),
        in_specs=[vmem] * 9,
        out_specs=vmem,
        scratch_shapes=[field, field, field, solid_field, pltpu.VMEM((4, 8, rows_y), jnp.float32)],
        compiler_params=params,
        cost_estimate=pl.CostEstimate(flops=8_000_000, bytes_accessed=4_000_000, transcendentals=0),
    )(held, flow, tiles, *row_got, y_after, y_before, low, high)
    cell_count = rows * rows_y * count
    scale = drag_factor / math.sqrt(cell_count) * 3.0 / 36.0
    total = jnp.sum(shared[:, 0, 0])
    return (result.reshape(adjoint_in.shape), (-scale * total).reshape(1))


def solution(mesh):
    placed = (
        P(None, "gx", None, "gy"),
        P(None, None, "gx", None, "gy"),
        P("gx", None, "gy"),
        P(None, "gx", None, "gy"),
    )
    return jax.shard_map(
        per_device,
        mesh=mesh,
        in_specs=placed,
        out_specs=(P(None, "gx", None, "gy"), P()),
        check_vma=False,
    )
```

```python
import functools
import math

import jax
import jax.numpy as jnp
from jax import lax
from jax.experimental import pallas as pl
from jax.experimental.pallas import tpu as pltpu
from jax.sharding import PartitionSpec as P

TILE = 4
STEPS = 2

lattice_speeds = (
    (0, 0, 0),
    (1, 0, 0),
    (-1, 0, 0),
    (0, 1, 0),
    (0, -1, 0),
    (0, 0, 1),
    (0, 0, -1),
    (1, 1, 0),
    (-1, -1, 0),
    (1, -1, 0),
    (-1, 1, 0),
    (1, 0, 1),
    (-1, 0, -1),
    (1, 0, -1),
    (-1, 0, 1),
    (0, 1, 1),
    (0, -1, -1),
    (0, 1, -1),
    (0, -1, 1),
)
relax_rate = 1.6
drag_factor = 20.0
LEVELS = 4
LANES = 128
GUARD = 8

x_up = [n for n in range(19) if lattice_speeds[n][0] == 1]
x_down = [n for n in range(19) if lattice_speeds[n][0] == -1]
y_up = [n for n in range(19) if lattice_speeds[n][1] == 1]
y_down = [n for n in range(19) if lattice_speeds[n][1] == -1]
vmem = pl.BlockSpec(memory_space=pltpu.VMEM)

FLOW = 19
SOLID = 22
NEXT = 23
SECOND = 26
QUANTITIES = 31
NEXT_SECOND = 31
COLUMN_QUANTITIES = 34
BEFORE_LANE = 16
AFTER_LANE = 32


def opposite_of(number):
    return number + 1 if number % 2 == 1 else number - 1


def lane_index(rows=8):
    return lax.broadcasted_iota(jnp.int32, (rows, LANES), 1)


def spread_solid(solid):
    tiles = solid.shape[1]
    row = lax.broadcasted_iota(jnp.int32, (tiles, LANES), 0)
    column = lax.broadcasted_iota(jnp.int32, (tiles, LANES), 1)
    spread = (column // TILE == row).astype(jnp.float32)
    cells = jnp.dot(solid[...].astype(jnp.float32), spread, preferred_element_type=jnp.float32)
    blocks = []
    for tile_row in range(solid.shape[0] // LEVELS):
        part = cells[tile_row * LEVELS : (tile_row + 1) * LEVELS]
        blocks.append(jnp.concatenate([part, part], axis=0))
    return blocks


def flow_blocks(velocity, step, rows):
    blocks = []
    for pair in range(rows // 16):
        both = [velocity[step, axis, pl.ds(16 * pair, 16), :].astype(jnp.float32) for axis in range(3)]
        blocks.append([part[:8] for part in both])
        blocks.append([part[8:] for part in both])
    return blocks


def on_even(axis):
    return lax.rem(lax.axis_index(axis), 2) == 0


class Chosen:
    def __init__(self, choice, yes, no):
        self.choice, self.yes, self.no = choice, yes, no
        self.shape = yes.shape

    def __getitem__(self, index):
        return jnp.where(self.choice, self.yes[index], self.no[index])


def slot_place(slot, group, groups):
    per_block = LANES // groups
    return slot // per_block, (slot % per_block) * groups + group


def insert_column(parts, slot, group, groups, value, edge, ahead):
    part, place = slot_place(slot, group, groups)
    lane = lane_index()
    turned = pltpu.roll(value, (place + ahead - edge) % LANES, 1)
    parts[part] = jnp.where(lane == place + ahead, turned, parts[part])


def row_message_kernel(
    state, velocity, solid, row_first, row_second, held, flow, tiles, arrived
):
    rows = state.shape[1]
    own = pl.ds(GUARD + 8, rows)
    copies = [
        pltpu.make_async_copy(state, held.at[:, own, :], arrived.at[0]),
        pltpu.make_async_copy(velocity, flow, arrived.at[1]),
        pltpu.make_async_copy(solid, tiles, arrived.at[2]),
    ]
    for copy in copies:
        copy.start()
    for copy in copies:
        copy.wait()
    even = on_even("gx")
    low_row, high_row = GUARD + 8, GUARD + 8 + rows - LEVELS

    def put(slot, low, high):
        row_first[slot] = jnp.where(even, high, low)
        row_second[slot] = jnp.where(even, low, high)

    for number in range(19):
        put(number, held[number, pl.ds(low_row, LEVELS), :], held[number, pl.ds(high_row, LEVELS), :])
    for step, slot in ((0, FLOW), (1, NEXT)):
        for axis in range(3):
            low = flow[step, axis, pl.ds(0, 16), :].astype(jnp.float32)
            high = flow[step, axis, pl.ds(rows - 16, 16), :].astype(jnp.float32)
            put(slot + axis, low[:LEVELS], high[16 - LEVELS :])
    solid_parts = spread_solid(tiles)
    put(SOLID, solid_parts[0][:LEVELS], solid_parts[-1][:LEVELS])
    for slot in range(5):
        put(
            SECOND + slot,
            held[x_up[slot], pl.ds(low_row + LEVELS, LEVELS), :],
            held[x_down[slot], pl.ds(high_row - LEVELS, LEVELS), :],
        )


def pack_columns(parts, slot, group, groups, value):
    low_parts, high_parts = parts
    part, place = slot_place(slot, group, groups)
    lane = lane_index()
    turned = pltpu.roll(value, (place + 1) % LANES, 1)
    low_parts[part] = jnp.where(lane == place + 1, turned, low_parts[part])
    high_parts[part] = jnp.where(lane == place, turned, high_parts[part])
    if slot in y_up:
        insert_column(low_parts, SECOND + y_up.index(slot), group, groups, value, 1, 1)
    if slot in y_down:
        insert_column(high_parts, SECOND + y_down.index(slot), group, groups, value, LANES - 2, 0)
    if NEXT <= slot < NEXT + 3:
        insert_column(high_parts, NEXT_SECOND + slot - NEXT, group, groups, value, LANES - 2, 0)


def own_columns_kernel(held, velocity, solid, low, high):
    rows = velocity.shape[2]
    groups = rows // 8 + 2
    solid_parts = spread_solid(solid)
    flow = [flow_blocks(velocity, step, rows) for step in range(2)]
    parts = [[jnp.zeros((8, LANES), jnp.float32) for _ in range(low.shape[0])] for _ in range(2)]
    for group in range(1, groups - 1):
        for slot in range(19):
            pack_columns(parts, slot, group, groups, held[slot, pl.ds(GUARD + 8 * group, 8), :])
        for axis in range(3):
            pack_columns(parts, FLOW + axis, group, groups, flow[0][group - 1][axis])
            pack_columns(parts, NEXT + axis, group, groups, flow[1][group - 1][axis])
        pack_columns(parts, SOLID, group, groups, solid_parts[(group - 1) * 8 // (LEVELS * TILE)])
    for part in range(low.shape[0]):
        low[part] = parts[0][part]
        high[part] = parts[1][part]


def halo_columns_kernel(groups, own_low, own_high, row_first, row_second, low_out, high_out, ends):
    count = own_low.shape[0]
    even = on_even("gx")
    after, before = Chosen(even, row_first, row_second), Chosen(even, row_second, row_first)
    parts = [[own_low[part] for part in range(count)], [own_high[part] for part in range(count)]]
    for slot in range(SECOND):
        ends[0, slot, pl.ds(LEVELS, LEVELS), :] = before[slot]
        ends[1, slot, pl.ds(0, LEVELS), :] = after[slot]
        if slot == SOLID:
            low_second, high_second = SOLID, SOLID
        else:
            low_second = SECOND + x_down.index(slot) if slot in x_down else None
            high_second = SECOND + x_up.index(slot) if slot in x_up else None
        blank = jnp.zeros((LEVELS, LANES), jnp.float32)
        ends[0, slot, pl.ds(0, LEVELS), :] = blank if low_second is None else before[low_second]
        ends[1, slot, pl.ds(LEVELS, LEVELS), :] = blank if high_second is None else after[high_second]
        pack_columns(parts, slot, 0, groups, ends[0, slot])
        pack_columns(parts, slot, groups - 1, groups, ends[1, slot])
    for part in range(count):
        low_out[part] = parts[0][part]
        high_out[part] = parts[1][part]


def collide(moved, flow, fluid):
    ux, uy, uz = flow
    total = {n: moved[n] + moved[n + 1] for n in range(1, 19, 2)}
    xy, xz, yz = total[7] + total[9], total[11] + total[13], total[15] + total[17]
    axis_x, axis_y, axis_z = 2.0 * total[1], 2.0 * total[3], 2.0 * total[5]
    density = 12.0 * moved[0] + (axis_x + axis_y + axis_z) + (xy + xz + yz)
    pxx = axis_x + xy + xz
    pyy = axis_y + xy + yz
    pzz = axis_z + xz + yz
    pxy = total[7] - total[9]
    pxz = total[11] - total[13]
    pyz = total[15] - total[17]
    dx, dy, dz = momentum(moved)
    vx = pxx * ux + pxy * uy + pxz * uz
    vy = pxy * ux + pyy * uy + pyz * uz
    vz = pxz * ux + pyz * uy + pzz * uz
    speed_sq = ux * ux + uy * uy + uz * uz
    scaled = (relax_rate / 36.0) * fluid
    base = scaled * (density + 1.5 * (speed_sq * density) - 4.5 * (ux * vx + uy * vy + uz * vz))
    scaled3 = 3.0 * scaled
    bx = scaled3 * (dx + 3.0 * vx - ux * density)
    by = scaled3 * (dy + 3.0 * vy - uy * density)
    bz = scaled3 * (dz + 3.0 * vz - uz * density)
    keep = (1.0 - relax_rate) * fluid
    results = [keep * moved[0] + base]
    for number in range(1, 19, 2):
        along = None
        for speed, part in zip(lattice_speeds[number], (bx, by, bz)):
            if speed == 0:
                continue
            if along is None:
                along = part if speed == 1 else -part
            else:
                along = along + part if speed == 1 else along - part
        results.append(keep * moved[number] + (base + along))
        results.append(keep * moved[number + 1] + (base - along))
    return results


def outside(cz):
    level = lax.broadcasted_iota(jnp.int32, (8, LANES), 0) % LEVELS
    return level == (LEVELS - 1 if cz == 1 else 0)


def link_closed(solid_there, cz):
    closed = solid_there > 0.5
    return closed | outside(cz) if cz != 0 else closed


def shift_lanes(value, cy, edge_value):
    lane = lane_index(value.shape[0])
    shifted = pltpu.roll(value, -cy % LANES, 1)
    if edge_value is None:
        return shifted
    return jnp.where(lane == (LANES - 1 if cy == 1 else 0), edge_value, shifted)


def gather_cells(held, shifted, first, solid_rows):
    here = [held[n, pl.ds(first, 8), :] for n in range(19)]
    moved, closed = [here[0]], [None]
    for number in range(1, 19):
        cx, cy, cz = lattice_speeds[number]
        field = held if cy == 0 else shifted
        there = pl.ds(first + LEVELS * cx + cz, 8)
        closed.append(link_closed(solid_rows[cy % 3, there, :], cz))
        bounced = here[opposite_of(number)]
        if cx != 0:
            bounced = bounced + 2.0 * cx
        moved.append(jnp.where(closed[number], bounced, field[number, there, :]))
    return moved, closed


def momentum(moved):
    gap = {n: moved[n] - moved[n + 1] for n in range(1, 19, 2)}
    dx = 2.0 * gap[1] + (gap[7] + gap[9]) + (gap[11] + gap[13])
    dy = 2.0 * gap[3] + (gap[7] - gap[9]) + (gap[15] + gap[17])
    dz = 2.0 * gap[5] + (gap[11] - gap[13]) + (gap[15] - gap[17])
    return dx, dy, dz


def drag_term(moved, flow, fluid):
    return fluid * sum(speed * part for speed, part in zip(flow, momentum(moved)))


def along_link(number, vector):
    total = None
    for axis, speed in enumerate(lattice_speeds[number]):
        if speed == 0:
            continue
        part = vector(axis)
        if total is None:
            total = part if speed == 1 else -part
        else:
            total = total + part if speed == 1 else total - part
    return total


def later_drag(results, closed, weight_here, weight_back):
    term = None
    for number in range(1, 19):
        cx = lattice_speeds[number][0]
        here = along_link(number, lambda axis: weight_here[axis])
        back = along_link(number, lambda axis: weight_back(number, axis))
        part = jnp.where(closed[opposite_of(number)], -here, back) * results[number]
        if cx != 0:
            part = part + jnp.where(closed[number], (2.0 * cx) * here, 0.0)
        if number < 7:
            part = 2.0 * part
        term = part if term is None else term + part
    return term


def column_reader(groups):
    def column(message, ahead, slot, lane_first, group=0):
        part, place = slot_place(slot, group, groups)
        return pltpu.roll(message[part], (lane_first - place - ahead) % LANES, 1)

    return column


def fill_held(own_held, before, after, held, rows):
    own = GUARD + 8
    near, far = own - LEVELS, own + rows
    for number in range(19):
        for group in range(rows // 8):
            there = pl.ds(own + 8 * group, 8)
            held[number, there, :] = own_held[number, there, :]
        held[number, pl.ds(near, LEVELS), :] = before[number]
        held[number, pl.ds(far, LEVELS), :] = after[number]
        if number in x_down:
            held[number, pl.ds(near - LEVELS, LEVELS), :] = before[SECOND + x_down.index(number)]
        if number in x_up:
            held[number, pl.ds(far + LEVELS, LEVELS), :] = after[SECOND + x_up.index(number)]


def fill_shifted(field, shifted, groups, edge_of):
    for number in y_up + y_down:
        cy = lattice_speeds[number][1]
        for group in range(groups):
            there = pl.ds(GUARD + 8 * group, 8)
            shifted[number, there, :] = shift_lanes(field[number, there, :], cy, edge_of(number, cy, group))


def fill_solid(solid_parts, before, after, solid_rows, groups, edge_of):
    for group in range(groups):
        first = GUARD + 8 * group
        if group in (0, groups - 1):
            halo = before[SOLID] if group == 0 else after[SOLID]
            solid_rows[0, pl.ds(first, LEVELS), :] = halo
            solid_rows[0, pl.ds(first + LEVELS, LEVELS), :] = halo
        else:
            solid_rows[0, pl.ds(first, 8), :] = solid_parts[(group - 1) * 8 // (LEVELS * TILE)]
        value = solid_rows[0, pl.ds(first, 8), :]
        for cy in (1, -1):
            solid_rows[cy % 3, pl.ds(first, 8), :] = shift_lanes(value, cy, edge_of(SOLID, cy, group))


def shift_rows(value, cx, cz):
    if cx != 0:
        upper = lax.broadcasted_iota(jnp.int32, (8, LANES), 0) < LEVELS
        swapped = pltpu.roll(value, LEVELS, 0)
        if cx == 1:
            value = jnp.where(upper, swapped, pltpu.roll(swapped, LANES - 1, 1))
        else:
            value = jnp.where(upper, pltpu.roll(swapped, 1, 1), swapped)
    if cz != 0:
        value = pltpu.roll(value, (-cz) % 8, 0)
    return value


def gather_columns(neighbours):
    here = [neighbours(n, 0) for n in range(19)]
    solid = {cy: neighbours(SOLID, cy) for cy in (0, 1, -1)}
    moved, closed = [here[0]], [None]
    for number in range(1, 19):
        cx, cy, cz = lattice_speeds[number]
        source = shift_rows(here[number] if cy == 0 else neighbours(number, cy), cx, cz)
        closed.append(link_closed(shift_rows(solid[cy], cx, cz), cz))
        moved.append(jnp.where(closed[number], here[opposite_of(number)] + 2.0 * cx, source))
    return moved, closed, solid


def drag_kernel(
    own_held, velocity, solid, row_first, row_second, y_before, low, shared,
    held, shifted, solid_rows, weights,
):
    rows = velocity.shape[2]
    groups = rows // 8 + 2
    own = GUARD + 8
    near, far = own - LEVELS, own + rows
    even = on_even("gx")
    after, before = Chosen(even, row_first, row_second), Chosen(even, row_second, row_first)
    lane = lane_index()
    solid_parts = spread_solid(solid)
    column = column_reader(groups)

    def edge_of(slot, cy, group):
        return None if cy == 1 else column(y_before, 0, slot, 0, group)

    fill_held(own_held, before, after, held, rows)
    fill_shifted(held, shifted, groups, edge_of)
    fill_solid(solid_parts, before, after, solid_rows, groups, edge_of)

    flow = flow_blocks(velocity, 1, rows)
    for axis in range(3):
        for group in range(rows // 8):
            there = pl.ds(own + 8 * group, 8)
            weights[axis, there, :] = (1.0 - solid_rows[0, there, :]) * flow[group][axis]
        for row, message in ((near, before), (far, after)):
            weights[axis, pl.ds(row, LEVELS), :] = (1.0 - message[SOLID]) * message[NEXT + axis]
        for group in range(groups):
            there = pl.ds(GUARD + 8 * group, 8)
            value = weights[axis, there, :]
            edge = (1.0 - column(y_before, 0, SOLID, 0, group)) * column(y_before, 0, NEXT + axis, 0, group)
            weights[3 + axis, there, :] = shift_lanes(value, 1, None)
            weights[6 + axis, there, :] = shift_lanes(value, -1, edge)

    total = jnp.zeros((8, LANES), jnp.float32)
    flow = flow_blocks(velocity, 0, rows)
    for group in range(rows // 8):
        first = own + 8 * group
        moved, closed = gather_cells(held, shifted, first, solid_rows)
        fluid = 1.0 - solid_parts[8 * group // (LEVELS * TILE)]
        results = collide(moved, flow[group], fluid)

        def back(number, axis):
            cx, cy, cz = lattice_speeds[number]
            return weights[3 * (-cy % 3) + axis, pl.ds(first - LEVELS * cx - cz, 8), :]

        here = [weights[axis, pl.ds(first, 8), :] for axis in range(3)]
        total = total + drag_term(moved, flow[group], fluid) + later_drag(results, closed, here, back)
    total = jnp.where(lane < LANES - 1, total, 0.0)

    def neighbours(slot, cy):
        if cy == 1:
            return column(low, 1, slot, BEFORE_LANE)
        if cy == -1 and slot != SOLID:
            slot = SECOND + y_down.index(slot)
        return column(y_before, 0, slot, BEFORE_LANE)

    moved, closed, solid_columns = gather_columns(neighbours)
    fluid = {cy: 1.0 - solid_columns[cy] for cy in (0, 1, -1)}
    column_flow = [neighbours(FLOW + axis, 0) for axis in range(3)]
    results = collide(moved, column_flow, fluid[0])
    weight = {
        0: [fluid[0] * neighbours(NEXT + axis, 0) for axis in range(3)],
        1: [fluid[1] * neighbours(NEXT + axis, 1) for axis in range(3)],
        -1: [fluid[-1] * neighbours(NEXT_SECOND + axis, 0) for axis in range(3)],
    }

    def back_column(number, axis):
        cx, cy, cz = lattice_speeds[number]
        return shift_rows(weight[-cy][axis], -cx, -cz)

    term = drag_term(moved, column_flow, fluid[0]) + later_drag(results, closed, weight[0], back_column)
    inside = jnp.logical_and(lane > BEFORE_LANE, lane < BEFORE_LANE + groups - 1)
    total = total + jnp.where(inside, term, 0.0)
    shared[...] = jnp.broadcast_to(jnp.sum(total), shared.shape)


def main_kernel(
    own_held, velocity, solid, row_first, row_second, y_after, y_before, low, high, out,
    held, shifted, later, solid_rows, row_flow,
):
    rows = velocity.shape[2]
    groups = rows // 8 + 2
    own = GUARD + 8
    near, far = own - LEVELS, own + rows
    even = on_even("gx")
    after, before = Chosen(even, row_first, row_second), Chosen(even, row_second, row_first)
    lane = lane_index()
    solid_parts = spread_solid(solid)
    column = column_reader(groups)

    def edge_of(slot, cy, group):
        if cy == 1:
            return column(y_after, 1, slot, LANES - 1, group)
        return column(y_before, 0, slot, 0, group)

    fill_held(own_held, before, after, held, rows)
    fill_shifted(held, shifted, groups, edge_of)
    fill_solid(solid_parts, before, after, solid_rows, groups, edge_of)
    for slot, place in ((FLOW, 0), (FLOW + 1, 1), (FLOW + 2, 2), (SOLID, 3)):
        row_flow[place, pl.ds(0, LEVELS), :] = before[slot]
        row_flow[place, pl.ds(LEVELS, LEVELS), :] = after[slot]

    def both_rows(field, index, shift):
        ends = [field[index, pl.ds(place + shift, LEVELS), :] for place in (near, far)]
        return jnp.concatenate(ends, axis=0)

    here = [both_rows(held, n, 0) for n in range(19)]
    moved = [here[0]]
    for number in range(1, 19):
        cx, cy, cz = lattice_speeds[number]
        shift = LEVELS * cx + cz
        source = both_rows(held if cy == 0 else shifted, number, shift)
        closed = link_closed(both_rows(solid_rows, cy % 3, shift), cz)
        moved.append(jnp.where(closed, here[opposite_of(number)] + 2.0 * cx, source))
    row_results = collide(moved, [row_flow[axis] for axis in range(3)], 1.0 - row_flow[3])

    def neighbours(slot, cy):
        beyond = slot if cy == 0 or slot == SOLID else SECOND + (y_up if cy == 1 else y_down).index(slot)
        if cy == 1:
            first, second = column(low, 1, slot, BEFORE_LANE), column(y_after, 1, beyond, AFTER_LANE)
        elif cy == -1:
            first, second = column(y_before, 0, beyond, BEFORE_LANE), column(high, 0, slot, AFTER_LANE)
        else:
            first, second = column(y_before, 0, slot, BEFORE_LANE), column(y_after, 1, slot, AFTER_LANE)
        return jnp.where(lane < AFTER_LANE, first, second)

    moved, _, solid_columns = gather_columns(neighbours)
    column_flow = [neighbours(FLOW + axis, 0) for axis in range(3)]
    column_results = collide(moved, column_flow, 1.0 - solid_columns[0])

    flow = flow_blocks(velocity, 0, rows)
    for group in range(rows // 8):
        first = own + 8 * group
        moved, _ = gather_cells(held, shifted, first, solid_rows)
        results = collide(moved, flow[group], 1.0 - solid_parts[8 * group // (LEVELS * TILE)])
        for number in range(19):
            later[number, pl.ds(first, 8), :] = results[number]
    for number in x_down:
        later[number, pl.ds(near, LEVELS), :] = row_results[number][:LEVELS]
    for number in x_up:
        later[number, pl.ds(far, LEVELS), :] = row_results[number][LEVELS:]

    def later_edge(number, cy, group):
        shift = LANES - 1 - AFTER_LANE - group if cy == 1 else -BEFORE_LANE - group
        return pltpu.roll(column_results[number], shift % LANES, 1)

    fill_shifted(later, shifted, groups, later_edge)

    flow = flow_blocks(velocity, 1, rows)
    for group in range(rows // 8):
        first = 8 * group
        moved, _ = gather_cells(later, shifted, own + first, solid_rows)
        results = collide(moved, flow[group], 1.0 - solid_parts[first // (LEVELS * TILE)])
        for number in range(19):
            out[number, pl.ds(first, 8), :] = results[number]


def swap_pairs(first, second, axis):
    count = lax.axis_size(axis)
    inside = [(i, i ^ 1) for i in range(count)]
    across = [(i, (i + 1) % count if i % 2 == 1 else (i - 1) % count) for i in range(count)]
    second = lax.ppermute(second, axis, across)
    return lax.ppermute(first, axis, inside), second


def per_device(adjoint_in, velocity, solid_tiles, link_blocked):
    rows_x, levels, rows_y = adjoint_in.shape[1:]
    rows = rows_x * levels
    padded = rows + 16 + 2 * GUARD
    groups = rows // 8 + 2
    parts = -(-COLUMN_QUANTITIES // (LANES // groups))
    state = adjoint_in.reshape(19, rows, rows_y)
    flow = velocity.reshape(STEPS, 3, rows, rows_y)
    solid = solid_tiles.reshape(-1, solid_tiles.shape[2])

    def shape_of(*sizes):
        return jax.ShapeDtypeStruct(sizes, jnp.float32)

    params = pltpu.CompilerParams(vmem_limit_bytes=16 * 1024 * 1024)
    anywhere = pl.BlockSpec(memory_space=pl.ANY)
    *row_sent, held, flow, tiles = pl.pallas_call(
        row_message_kernel,
        out_shape=(
            pltpu.VMEM((QUANTITIES, levels, rows_y), jnp.float32),
            pltpu.VMEM((QUANTITIES, levels, rows_y), jnp.float32),
            pltpu.VMEM((19, padded, rows_y), jnp.float32),
            pltpu.VMEM(flow.shape, flow.dtype),
            pltpu.VMEM(solid.shape, solid.dtype),
        ),
        in_specs=[anywhere] * 3,
        out_specs=(vmem,) * 5,
        scratch_shapes=[pltpu.SemaphoreType.DMA((3,))],
        compiler_params=params,
    )(*(pltpu.with_memory_space_constraint(value, pltpu.HBM) for value in (state, flow, solid)))
    row_got = swap_pairs(*row_sent, "gx")
    own_columns = pl.pallas_call(
        own_columns_kernel,
        out_shape=(shape_of(parts, 8, rows_y),) * 2,
        in_specs=[vmem] * 3,
        out_specs=(vmem,) * 2,
        compiler_params=params,
        cost_estimate=pl.CostEstimate(flops=2_000_000, bytes_accessed=1_000_000, transcendentals=0),
    )(held, flow, tiles)
    low, high = pl.pallas_call(
        functools.partial(halo_columns_kernel, groups),
        out_shape=(shape_of(parts, 8, rows_y),) * 2,
        in_specs=[vmem] * 4,
        out_specs=(vmem,) * 2,
        scratch_shapes=[pltpu.VMEM((2, SECOND, 8, rows_y), jnp.float32)],
        compiler_params=params,
    )(*own_columns, *row_got)
    size = lax.axis_size("gy")
    y_before = lax.ppermute(high, "gy", [(i, (i + 1) % size) for i in range(size)])
    y_after = lax.ppermute(low, "gy", [((i + 1) % size, i) for i in range(size)])
    count = lax.axis_size("gx") * size
    field = pltpu.VMEM((19, padded, rows_y), jnp.float32)
    solid_field = pltpu.VMEM((3, padded, rows_y), jnp.float32)
    own = pl.pallas_call(
        drag_kernel,
        out_shape=pltpu.VMEM((count, 1, rows_y), jnp.float32),
        in_specs=[vmem] * 7,
        out_specs=vmem,
        scratch_shapes=[field, field, solid_field, pltpu.VMEM((9, padded, rows_y), jnp.float32)],
        compiler_params=params,
        cost_estimate=pl.CostEstimate(flops=8_000_000, bytes_accessed=100_000_000, transcendentals=0),
    )(held, flow, tiles, *row_got, y_before, low)
    shared = lax.all_to_all(own, ("gx", "gy"), split_axis=0, concat_axis=0, tiled=True)
    result = pl.pallas_call(
        main_kernel,
        out_shape=shape_of(19, rows, rows_y),
        in_specs=[vmem] * 9,
        out_specs=vmem,
        scratch_shapes=[field, field, field, solid_field, pltpu.VMEM((4, 8, rows_y), jnp.float32)],
        compiler_params=params,
        cost_estimate=pl.CostEstimate(flops=8_000_000, bytes_accessed=200_000_000, transcendentals=0),
    )(held, flow, tiles, *row_got, y_after, y_before, low, high)
    cell_count = rows * rows_y * count
    scale = drag_factor / math.sqrt(cell_count) * 3.0 / 36.0
    total = jnp.sum(shared[:, 0, 0])
    return (result.reshape(adjoint_in.shape), (-scale * total).reshape(1))


def solution(mesh):
    placed = (
        P(None, "gx", None, "gy"),
        P(None, None, "gx", None, "gy"),
        P("gx", None, "gy"),
        P(None, "gx", None, "gy"),
    )
    return jax.shard_map(
        per_device,
        mesh=mesh,
        in_specs=placed,
        out_specs=(P(None, "gx", None, "gy"), P()),
        check_vma=False,
    )
```

```python
import functools
import math

import jax
import jax.numpy as jnp
from jax import lax
from jax.experimental import pallas as pl
from jax.experimental.pallas import tpu as pltpu
from jax.sharding import PartitionSpec as P

TILE = 4
STEPS = 2

lattice_speeds = (
    (0, 0, 0),
    (1, 0, 0),
    (-1, 0, 0),
    (0, 1, 0),
    (0, -1, 0),
    (0, 0, 1),
    (0, 0, -1),
    (1, 1, 0),
    (-1, -1, 0),
    (1, -1, 0),
    (-1, 1, 0),
    (1, 0, 1),
    (-1, 0, -1),
    (1, 0, -1),
    (-1, 0, 1),
    (0, 1, 1),
    (0, -1, -1),
    (0, 1, -1),
    (0, -1, 1),
)
relax_rate = 1.6
drag_factor = 20.0
LEVELS = 4
LANES = 128
GUARD = 8

x_up = [n for n in range(19) if lattice_speeds[n][0] == 1]
x_down = [n for n in range(19) if lattice_speeds[n][0] == -1]
y_up = [n for n in range(19) if lattice_speeds[n][1] == 1]
y_down = [n for n in range(19) if lattice_speeds[n][1] == -1]
vmem = pl.BlockSpec(memory_space=pltpu.VMEM)

FLOW = 19
SOLID = 22
NEXT = 23
SECOND = 26
QUANTITIES = 31
NEXT_SECOND = 31
COLUMN_QUANTITIES = 34
BEFORE_LANE = 16
AFTER_LANE = 32


def opposite_of(number):
    return number + 1 if number % 2 == 1 else number - 1


def lane_index(rows=8):
    return lax.broadcasted_iota(jnp.int32, (rows, LANES), 1)


def spread_solid(solid):
    tiles = solid.shape[1]
    row = lax.broadcasted_iota(jnp.int32, (tiles, LANES), 0)
    column = lax.broadcasted_iota(jnp.int32, (tiles, LANES), 1)
    spread = (column // TILE == row).astype(jnp.float32)
    cells = jnp.dot(solid[...].astype(jnp.float32), spread, preferred_element_type=jnp.float32)
    blocks = []
    for tile_row in range(solid.shape[0] // LEVELS):
        part = cells[tile_row * LEVELS : (tile_row + 1) * LEVELS]
        blocks.append(jnp.concatenate([part, part], axis=0))
    return blocks


def flow_blocks(velocity, step, rows):
    blocks = []
    for pair in range(rows // 16):
        both = [velocity[step, axis, pl.ds(16 * pair, 16), :].astype(jnp.float32) for axis in range(3)]
        blocks.append([part[:8] for part in both])
        blocks.append([part[8:] for part in both])
    return blocks


def on_even(axis):
    return lax.rem(lax.axis_index(axis), 2) == 0


class Chosen:
    def __init__(self, choice, yes, no):
        self.choice, self.yes, self.no = choice, yes, no
        self.shape = yes.shape

    def __getitem__(self, index):
        return jnp.where(self.choice, self.yes[index], self.no[index])


def slot_place(slot, group, groups):
    per_block = LANES // groups
    return slot // per_block, (slot % per_block) * groups + group


def insert_column(parts, slot, group, groups, value, edge, ahead):
    part, place = slot_place(slot, group, groups)
    lane = lane_index()
    turned = pltpu.roll(value, (place + ahead - edge) % LANES, 1)
    parts[part] = jnp.where(lane == place + ahead, turned, parts[part])


def row_message_kernel(
    state, velocity, solid, row_first, row_second, held, flow, tiles, arrived
):
    rows = state.shape[1]
    own = pl.ds(GUARD + 8, rows)
    copies = [
        pltpu.make_async_copy(state, held.at[:, own, :], arrived.at[0]),
        pltpu.make_async_copy(velocity, flow, arrived.at[1]),
        pltpu.make_async_copy(solid, tiles, arrived.at[2]),
    ]
    for copy in copies:
        copy.start()
    for copy in copies:
        copy.wait()
    even = on_even("gx")
    low_row, high_row = GUARD + 8, GUARD + 8 + rows - LEVELS

    def put(slot, low, high):
        row_first[slot] = jnp.where(even, high, low)
        row_second[slot] = jnp.where(even, low, high)

    for number in range(19):
        put(number, held[number, pl.ds(low_row, LEVELS), :], held[number, pl.ds(high_row, LEVELS), :])
    for step, slot in ((0, FLOW), (1, NEXT)):
        for axis in range(3):
            low = flow[step, axis, pl.ds(0, 16), :].astype(jnp.float32)
            high = flow[step, axis, pl.ds(rows - 16, 16), :].astype(jnp.float32)
            put(slot + axis, low[:LEVELS], high[16 - LEVELS :])
    solid_parts = spread_solid(tiles)
    put(SOLID, solid_parts[0][:LEVELS], solid_parts[-1][:LEVELS])
    for slot in range(5):
        put(
            SECOND + slot,
            held[x_up[slot], pl.ds(low_row + LEVELS, LEVELS), :],
            held[x_down[slot], pl.ds(high_row - LEVELS, LEVELS), :],
        )


def pack_columns(parts, slot, group, groups, value):
    low_parts, high_parts = parts
    part, place = slot_place(slot, group, groups)
    lane = lane_index()
    turned = pltpu.roll(value, (place + 1) % LANES, 1)
    low_parts[part] = jnp.where(lane == place + 1, turned, low_parts[part])
    high_parts[part] = jnp.where(lane == place, turned, high_parts[part])
    if slot in y_up:
        insert_column(low_parts, SECOND + y_up.index(slot), group, groups, value, 1, 1)
    if slot in y_down:
        insert_column(high_parts, SECOND + y_down.index(slot), group, groups, value, LANES - 2, 0)
    if NEXT <= slot < NEXT + 3:
        insert_column(low_parts, NEXT_SECOND + slot - NEXT, group, groups, value, 1, 1)
        insert_column(high_parts, NEXT_SECOND + slot - NEXT, group, groups, value, LANES - 2, 0)


def own_columns_kernel(held, velocity, solid, low, high):
    rows = velocity.shape[2]
    groups = rows // 8 + 2
    solid_parts = spread_solid(solid)
    flow = [flow_blocks(velocity, step, rows) for step in range(2)]
    parts = [[jnp.zeros((8, LANES), jnp.float32) for _ in range(low.shape[0])] for _ in range(2)]
    for group in range(1, groups - 1):
        for slot in range(19):
            pack_columns(parts, slot, group, groups, held[slot, pl.ds(GUARD + 8 * group, 8), :])
        for axis in range(3):
            pack_columns(parts, FLOW + axis, group, groups, flow[0][group - 1][axis])
            pack_columns(parts, NEXT + axis, group, groups, flow[1][group - 1][axis])
        pack_columns(parts, SOLID, group, groups, solid_parts[(group - 1) * 8 // (LEVELS * TILE)])
    for part in range(low.shape[0]):
        low[part] = parts[0][part]
        high[part] = parts[1][part]


def halo_columns_kernel(groups, own_low, own_high, row_first, row_second, low_out, high_out, ends):
    count = own_low.shape[0]
    even = on_even("gx")
    after, before = Chosen(even, row_first, row_second), Chosen(even, row_second, row_first)
    parts = [[own_low[part] for part in range(count)], [own_high[part] for part in range(count)]]
    for slot in range(SECOND):
        ends[0, slot, pl.ds(LEVELS, LEVELS), :] = before[slot]
        ends[1, slot, pl.ds(0, LEVELS), :] = after[slot]
        if slot == SOLID:
            low_second, high_second = SOLID, SOLID
        else:
            low_second = SECOND + x_down.index(slot) if slot in x_down else None
            high_second = SECOND + x_up.index(slot) if slot in x_up else None
        blank = jnp.zeros((LEVELS, LANES), jnp.float32)
        ends[0, slot, pl.ds(0, LEVELS), :] = blank if low_second is None else before[low_second]
        ends[1, slot, pl.ds(LEVELS, LEVELS), :] = blank if high_second is None else after[high_second]
        pack_columns(parts, slot, 0, groups, ends[0, slot])
        pack_columns(parts, slot, groups - 1, groups, ends[1, slot])
    for part in range(count):
        low_out[part] = parts[0][part]
        high_out[part] = parts[1][part]


def collide(moved, flow, fluid):
    ux, uy, uz = flow
    total = {n: moved[n] + moved[n + 1] for n in range(1, 19, 2)}
    xy, xz, yz = total[7] + total[9], total[11] + total[13], total[15] + total[17]
    axis_x, axis_y, axis_z = 2.0 * total[1], 2.0 * total[3], 2.0 * total[5]
    density = 12.0 * moved[0] + (axis_x + axis_y + axis_z) + (xy + xz + yz)
    pxx = axis_x + xy + xz
    pyy = axis_y + xy + yz
    pzz = axis_z + xz + yz
    pxy = total[7] - total[9]
    pxz = total[11] - total[13]
    pyz = total[15] - total[17]
    dx, dy, dz = momentum(moved)
    vx = pxx * ux + pxy * uy + pxz * uz
    vy = pxy * ux + pyy * uy + pyz * uz
    vz = pxz * ux + pyz * uy + pzz * uz
    speed_sq = ux * ux + uy * uy + uz * uz
    scaled = (relax_rate / 36.0) * fluid
    base = scaled * (density + 1.5 * (speed_sq * density) - 4.5 * (ux * vx + uy * vy + uz * vz))
    scaled3 = 3.0 * scaled
    bx = scaled3 * (dx + 3.0 * vx - ux * density)
    by = scaled3 * (dy + 3.0 * vy - uy * density)
    bz = scaled3 * (dz + 3.0 * vz - uz * density)
    keep = (1.0 - relax_rate) * fluid
    results = [keep * moved[0] + base]
    for number in range(1, 19, 2):
        along = None
        for speed, part in zip(lattice_speeds[number], (bx, by, bz)):
            if speed == 0:
                continue
            if along is None:
                along = part if speed == 1 else -part
            else:
                along = along + part if speed == 1 else along - part
        results.append(keep * moved[number] + (base + along))
        results.append(keep * moved[number + 1] + (base - along))
    return results


def outside(cz):
    level = lax.broadcasted_iota(jnp.int32, (8, LANES), 0) % LEVELS
    return level == (LEVELS - 1 if cz == 1 else 0)


def link_closed(solid_there, cz):
    closed = solid_there > 0.5
    return closed | outside(cz) if cz != 0 else closed


def shift_lanes(value, cy, edge_value):
    lane = lane_index(value.shape[0])
    shifted = pltpu.roll(value, -cy % LANES, 1)
    if edge_value is None:
        return shifted
    return jnp.where(lane == (LANES - 1 if cy == 1 else 0), edge_value, shifted)


def gather_cells(held, shifted, first, solid_rows):
    here = [held[n, pl.ds(first, 8), :] for n in range(19)]
    moved, closed = [here[0]], [None]
    for number in range(1, 19):
        cx, cy, cz = lattice_speeds[number]
        field = held if cy == 0 else shifted
        there = pl.ds(first + LEVELS * cx + cz, 8)
        closed.append(link_closed(solid_rows[cy % 3, there, :], cz))
        bounced = here[opposite_of(number)]
        if cx != 0:
            bounced = bounced + 2.0 * cx
        moved.append(jnp.where(closed[number], bounced, field[number, there, :]))
    return moved, closed


def momentum(moved):
    gap = {n: moved[n] - moved[n + 1] for n in range(1, 19, 2)}
    dx = 2.0 * gap[1] + (gap[7] + gap[9]) + (gap[11] + gap[13])
    dy = 2.0 * gap[3] + (gap[7] - gap[9]) + (gap[15] + gap[17])
    dz = 2.0 * gap[5] + (gap[11] - gap[13]) + (gap[15] - gap[17])
    return dx, dy, dz


def drag_term(moved, flow, fluid):
    return fluid * sum(speed * part for speed, part in zip(flow, momentum(moved)))


def along_link(number, vector):
    total = None
    for axis, speed in enumerate(lattice_speeds[number]):
        if speed == 0:
            continue
        part = vector(axis)
        if total is None:
            total = part if speed == 1 else -part
        else:
            total = total + part if speed == 1 else total - part
    return total


def later_drag(results, closed, weight_here, weight_back):
    term = None
    for number in range(1, 19):
        cx = lattice_speeds[number][0]
        here = along_link(number, lambda axis: weight_here[axis])
        back = along_link(number, lambda axis: weight_back(number, axis))
        part = jnp.where(closed[opposite_of(number)], -here, back) * results[number]
        if cx != 0:
            part = part + jnp.where(closed[number], (2.0 * cx) * here, 0.0)
        if number < 7:
            part = 2.0 * part
        term = part if term is None else term + part
    return term


def column_reader(groups):
    def column(message, ahead, slot, lane_first, group=0):
        part, place = slot_place(slot, group, groups)
        return pltpu.roll(message[part], (lane_first - place - ahead) % LANES, 1)

    return column


def fill_held(own_held, before, after, held, rows):
    own = GUARD + 8
    near, far = own - LEVELS, own + rows
    for number in range(19):
        for group in range(rows // 8):
            there = pl.ds(own + 8 * group, 8)
            held[number, there, :] = own_held[number, there, :]
        held[number, pl.ds(near, LEVELS), :] = before[number]
        held[number, pl.ds(far, LEVELS), :] = after[number]
        if number in x_down:
            held[number, pl.ds(near - LEVELS, LEVELS), :] = before[SECOND + x_down.index(number)]
        if number in x_up:
            held[number, pl.ds(far + LEVELS, LEVELS), :] = after[SECOND + x_up.index(number)]


def fill_shifted(field, shifted, groups, edge_of):
    for number in y_up + y_down:
        cy = lattice_speeds[number][1]
        for group in range(groups):
            there = pl.ds(GUARD + 8 * group, 8)
            shifted[number, there, :] = shift_lanes(field[number, there, :], cy, edge_of(number, cy, group))


def fill_solid(solid_parts, before, after, solid_rows, groups, edge_of):
    for group in range(groups):
        first = GUARD + 8 * group
        if group in (0, groups - 1):
            halo = before[SOLID] if group == 0 else after[SOLID]
            solid_rows[0, pl.ds(first, LEVELS), :] = halo
            solid_rows[0, pl.ds(first + LEVELS, LEVELS), :] = halo
        else:
            solid_rows[0, pl.ds(first, 8), :] = solid_parts[(group - 1) * 8 // (LEVELS * TILE)]
        value = solid_rows[0, pl.ds(first, 8), :]
        for cy in (1, -1):
            solid_rows[cy % 3, pl.ds(first, 8), :] = shift_lanes(value, cy, edge_of(SOLID, cy, group))


def shift_rows(value, cx, cz):
    if cx != 0:
        upper = lax.broadcasted_iota(jnp.int32, (8, LANES), 0) < LEVELS
        swapped = pltpu.roll(value, LEVELS, 0)
        if cx == 1:
            value = jnp.where(upper, swapped, pltpu.roll(swapped, LANES - 1, 1))
        else:
            value = jnp.where(upper, pltpu.roll(swapped, 1, 1), swapped)
    if cz != 0:
        value = pltpu.roll(value, (-cz) % 8, 0)
    return value


def gather_columns(neighbours):
    here = [neighbours(n, 0) for n in range(19)]
    solid = {cy: neighbours(SOLID, cy) for cy in (0, 1, -1)}
    moved, closed = [here[0]], [None]
    for number in range(1, 19):
        cx, cy, cz = lattice_speeds[number]
        source = shift_rows(here[number] if cy == 0 else neighbours(number, cy), cx, cz)
        closed.append(link_closed(shift_rows(solid[cy], cx, cz), cz))
        moved.append(jnp.where(closed[number], here[opposite_of(number)] + 2.0 * cx, source))
    return moved, closed, solid


def inner_drag_kernel(
    own_held, velocity, solid, row_first, row_second, partial, held, shifted, solid_rows, weights
):
    rows = velocity.shape[2]
    groups = rows // 8 + 2
    own = GUARD + 8
    near, far = own - LEVELS, own + rows
    even = on_even("gx")
    after, before = Chosen(even, row_first, row_second), Chosen(even, row_second, row_first)
    lane = lane_index()
    solid_parts = spread_solid(solid)

    def no_edge(slot, cy, group):
        return None

    fill_held(own_held, before, after, held, rows)
    fill_shifted(held, shifted, groups, no_edge)
    fill_solid(solid_parts, before, after, solid_rows, groups, no_edge)

    flow = flow_blocks(velocity, 1, rows)
    for axis in range(3):
        for group in range(rows // 8):
            there = pl.ds(own + 8 * group, 8)
            weights[axis, there, :] = (1.0 - solid_rows[0, there, :]) * flow[group][axis]
        for row, message in ((near, before), (far, after)):
            weights[axis, pl.ds(row, LEVELS), :] = (1.0 - message[SOLID]) * message[NEXT + axis]
        for group in range(groups):
            there = pl.ds(GUARD + 8 * group, 8)
            value = weights[axis, there, :]
            weights[3 + axis, there, :] = shift_lanes(value, 1, None)
            weights[6 + axis, there, :] = shift_lanes(value, -1, None)

    total = jnp.zeros((8, LANES), jnp.float32)
    flow = flow_blocks(velocity, 0, rows)
    for group in range(rows // 8):
        first = own + 8 * group
        moved, closed = gather_cells(held, shifted, first, solid_rows)
        fluid = 1.0 - solid_parts[8 * group // (LEVELS * TILE)]
        results = collide(moved, flow[group], fluid)

        def back(number, axis):
            cx, cy, cz = lattice_speeds[number]
            return weights[3 * (-cy % 3) + axis, pl.ds(first - LEVELS * cx - cz, 8), :]

        here = [weights[axis, pl.ds(first, 8), :] for axis in range(3)]
        total = total + drag_term(moved, flow[group], fluid) + later_drag(results, closed, here, back)
    inside = jnp.logical_and(lane > 0, lane < LANES - 1)
    partial[...] = jnp.where(inside, total, 0.0)


def edge_drag_kernel(groups, y_before, low, partial, shared):
    lane = lane_index()
    column = column_reader(groups)

    def neighbours(slot, cy):
        ahead = slot
        behind = slot
        if slot < 19 and cy == 1:
            ahead = SECOND + y_up.index(slot)
        if slot < 19 and cy == -1:
            behind = SECOND + y_down.index(slot)
        if NEXT <= slot < NEXT + 3:
            ahead = behind = NEXT_SECOND + slot - NEXT
        if cy == 0:
            first, second = column(y_before, 0, slot, BEFORE_LANE), column(low, 1, slot, AFTER_LANE)
        elif cy == 1:
            first, second = column(low, 1, slot, BEFORE_LANE), column(low, 1, ahead, AFTER_LANE)
        else:
            first, second = column(y_before, 0, behind, BEFORE_LANE), column(y_before, 0, slot, AFTER_LANE)
        return jnp.where(lane < AFTER_LANE, first, second)

    moved, closed, solid_columns = gather_columns(neighbours)
    fluid = {cy: 1.0 - solid_columns[cy] for cy in (0, 1, -1)}
    flow = [neighbours(FLOW + axis, 0) for axis in range(3)]
    results = collide(moved, flow, fluid[0])
    weight = {cy: [fluid[cy] * neighbours(NEXT + axis, cy) for axis in range(3)] for cy in (0, 1, -1)}

    def back(number, axis):
        cx, cy, cz = lattice_speeds[number]
        return shift_rows(weight[-cy][axis], -cx, -cz)

    term = drag_term(moved, flow, fluid[0]) + later_drag(results, closed, weight[0], back)
    place = jnp.where(lane < AFTER_LANE, lane - BEFORE_LANE, lane - AFTER_LANE)
    inside = jnp.logical_and(place > 0, place < groups - 1)
    total = partial[...] + jnp.where(inside, term, 0.0)
    shared[...] = jnp.broadcast_to(jnp.sum(total), shared.shape)


def main_kernel(
    own_held, velocity, solid, row_first, row_second, y_after, y_before, low, high, out,
    held, shifted, later, solid_rows, row_flow,
):
    rows = velocity.shape[2]
    groups = rows // 8 + 2
    own = GUARD + 8
    near, far = own - LEVELS, own + rows
    even = on_even("gx")
    after, before = Chosen(even, row_first, row_second), Chosen(even, row_second, row_first)
    lane = lane_index()
    solid_parts = spread_solid(solid)
    column = column_reader(groups)

    def edge_of(slot, cy, group):
        if cy == 1:
            return column(y_after, 1, slot, LANES - 1, group)
        return column(y_before, 0, slot, 0, group)

    fill_held(own_held, before, after, held, rows)
    fill_shifted(held, shifted, groups, edge_of)
    fill_solid(solid_parts, before, after, solid_rows, groups, edge_of)
    for slot, place in ((FLOW, 0), (FLOW + 1, 1), (FLOW + 2, 2), (SOLID, 3)):
        row_flow[place, pl.ds(0, LEVELS), :] = before[slot]
        row_flow[place, pl.ds(LEVELS, LEVELS), :] = after[slot]

    def both_rows(field, index, shift):
        ends = [field[index, pl.ds(place + shift, LEVELS), :] for place in (near, far)]
        return jnp.concatenate(ends, axis=0)

    here = [both_rows(held, n, 0) for n in range(19)]
    moved = [here[0]]
    for number in range(1, 19):
        cx, cy, cz = lattice_speeds[number]
        shift = LEVELS * cx + cz
        source = both_rows(held if cy == 0 else shifted, number, shift)
        closed = link_closed(both_rows(solid_rows, cy % 3, shift), cz)
        moved.append(jnp.where(closed, here[opposite_of(number)] + 2.0 * cx, source))
    row_results = collide(moved, [row_flow[axis] for axis in range(3)], 1.0 - row_flow[3])

    def neighbours(slot, cy):
        beyond = slot if cy == 0 or slot == SOLID else SECOND + (y_up if cy == 1 else y_down).index(slot)
        if cy == 1:
            first, second = column(low, 1, slot, BEFORE_LANE), column(y_after, 1, beyond, AFTER_LANE)
        elif cy == -1:
            first, second = column(y_before, 0, beyond, BEFORE_LANE), column(high, 0, slot, AFTER_LANE)
        else:
            first, second = column(y_before, 0, slot, BEFORE_LANE), column(y_after, 1, slot, AFTER_LANE)
        return jnp.where(lane < AFTER_LANE, first, second)

    moved, _, solid_columns = gather_columns(neighbours)
    column_flow = [neighbours(FLOW + axis, 0) for axis in range(3)]
    column_results = collide(moved, column_flow, 1.0 - solid_columns[0])

    flow = flow_blocks(velocity, 0, rows)
    for group in range(rows // 8):
        first = own + 8 * group
        moved, _ = gather_cells(held, shifted, first, solid_rows)
        results = collide(moved, flow[group], 1.0 - solid_parts[8 * group // (LEVELS * TILE)])
        for number in range(19):
            later[number, pl.ds(first, 8), :] = results[number]
    for number in x_down:
        later[number, pl.ds(near, LEVELS), :] = row_results[number][:LEVELS]
    for number in x_up:
        later[number, pl.ds(far, LEVELS), :] = row_results[number][LEVELS:]

    def later_edge(number, cy, group):
        shift = LANES - 1 - AFTER_LANE - group if cy == 1 else -BEFORE_LANE - group
        return pltpu.roll(column_results[number], shift % LANES, 1)

    fill_shifted(later, shifted, groups, later_edge)

    flow = flow_blocks(velocity, 1, rows)
    for group in range(rows // 8):
        first = 8 * group
        moved, _ = gather_cells(later, shifted, own + first, solid_rows)
        results = collide(moved, flow[group], 1.0 - solid_parts[first // (LEVELS * TILE)])
        for number in range(19):
            out[number, pl.ds(first, 8), :] = results[number]


def swap_pairs(first, second, axis):
    count = lax.axis_size(axis)
    inside = [(i, i ^ 1) for i in range(count)]
    across = [(i, (i + 1) % count if i % 2 == 1 else (i - 1) % count) for i in range(count)]
    second = lax.ppermute(second, axis, across)
    return lax.ppermute(first, axis, inside), second


def per_device(adjoint_in, velocity, solid_tiles, link_blocked):
    rows_x, levels, rows_y = adjoint_in.shape[1:]
    rows = rows_x * levels
    padded = rows + 16 + 2 * GUARD
    groups = rows // 8 + 2
    parts = -(-COLUMN_QUANTITIES // (LANES // groups))
    state = adjoint_in.reshape(19, rows, rows_y)
    flow = velocity.reshape(STEPS, 3, rows, rows_y)
    solid = solid_tiles.reshape(-1, solid_tiles.shape[2])

    def shape_of(*sizes):
        return jax.ShapeDtypeStruct(sizes, jnp.float32)

    params = pltpu.CompilerParams(vmem_limit_bytes=16 * 1024 * 1024)
    anywhere = pl.BlockSpec(memory_space=pl.ANY)
    *row_sent, held, flow, tiles = pl.pallas_call(
        row_message_kernel,
        out_shape=(
            pltpu.VMEM((QUANTITIES, levels, rows_y), jnp.float32),
            pltpu.VMEM((QUANTITIES, levels, rows_y), jnp.float32),
            pltpu.VMEM((19, padded, rows_y), jnp.float32),
            pltpu.VMEM(flow.shape, flow.dtype),
            pltpu.VMEM(solid.shape, solid.dtype),
        ),
        in_specs=[anywhere] * 3,
        out_specs=(vmem,) * 5,
        scratch_shapes=[pltpu.SemaphoreType.DMA((3,))],
        compiler_params=params,
    )(*(pltpu.with_memory_space_constraint(value, pltpu.HBM) for value in (state, flow, solid)))
    row_got = swap_pairs(*row_sent, "gx")
    own_columns = pl.pallas_call(
        own_columns_kernel,
        out_shape=(shape_of(parts, 8, rows_y),) * 2,
        in_specs=[vmem] * 3,
        out_specs=(vmem,) * 2,
        compiler_params=params,
        cost_estimate=pl.CostEstimate(flops=2_000_000, bytes_accessed=1_000_000, transcendentals=0),
    )(held, flow, tiles)
    low, high = pl.pallas_call(
        functools.partial(halo_columns_kernel, groups),
        out_shape=(shape_of(parts, 8, rows_y),) * 2,
        in_specs=[vmem] * 4,
        out_specs=(vmem,) * 2,
        scratch_shapes=[pltpu.VMEM((2, SECOND, 8, rows_y), jnp.float32)],
        compiler_params=params,
    )(*own_columns, *row_got)
    size = lax.axis_size("gy")
    y_before = lax.ppermute(high, "gy", [(i, (i + 1) % size) for i in range(size)])
    y_after = lax.ppermute(low, "gy", [((i + 1) % size, i) for i in range(size)])
    count = lax.axis_size("gx") * size
    field = pltpu.VMEM((19, padded, rows_y), jnp.float32)
    solid_field = pltpu.VMEM((3, padded, rows_y), jnp.float32)
    partial = pl.pallas_call(
        inner_drag_kernel,
        out_shape=pltpu.VMEM((8, rows_y), jnp.float32),
        in_specs=[vmem] * 5,
        out_specs=vmem,
        scratch_shapes=[field, field, solid_field, pltpu.VMEM((9, padded, rows_y), jnp.float32)],
        compiler_params=params,
        cost_estimate=pl.CostEstimate(flops=2_000_000_000, bytes_accessed=10_000_000, transcendentals=0),
    )(held, flow, tiles, *row_got)
    own = pl.pallas_call(
        functools.partial(edge_drag_kernel, groups),
        out_shape=pltpu.VMEM((count, 1, rows_y), jnp.float32),
        in_specs=[vmem] * 3,
        out_specs=vmem,
        compiler_params=params,
        cost_estimate=pl.CostEstimate(flops=20_000_000_000, bytes_accessed=10_000_000, transcendentals=0),
    )(y_before, low, partial)
    shared = lax.all_to_all(own, ("gx", "gy"), split_axis=0, concat_axis=0, tiled=True)
    result = pl.pallas_call(
        main_kernel,
        out_shape=shape_of(19, rows, rows_y),
        in_specs=[vmem] * 9,
        out_specs=vmem,
        scratch_shapes=[field, field, field, solid_field, pltpu.VMEM((4, 8, rows_y), jnp.float32)],
        compiler_params=params,
        cost_estimate=pl.CostEstimate(flops=200_000_000_000, bytes_accessed=200_000_000, transcendentals=0),
    )(held, flow, tiles, *row_got, y_after, y_before, low, high)
    cell_count = rows * rows_y * count
    scale = drag_factor / math.sqrt(cell_count) * 3.0 / 36.0
    total = jnp.sum(shared[:, 0, 0])
    return (result.reshape(adjoint_in.shape), (-scale * total).reshape(1))


def solution(mesh):
    placed = (
        P(None, "gx", None, "gy"),
        P(None, None, "gx", None, "gy"),
        P("gx", None, "gy"),
        P(None, "gx", None, "gy"),
    )
    return jax.shard_map(
        per_device,
        mesh=mesh,
        in_specs=placed,
        out_specs=(P(None, "gx", None, "gy"), P()),
        check_vma=False,
    )
```

```python
import functools
import math

import jax
import jax.numpy as jnp
from jax import lax
from jax.experimental import pallas as pl
from jax.experimental.pallas import tpu as pltpu
from jax.sharding import PartitionSpec as P

TILE = 4
STEPS = 2

lattice_speeds = (
    (0, 0, 0),
    (1, 0, 0),
    (-1, 0, 0),
    (0, 1, 0),
    (0, -1, 0),
    (0, 0, 1),
    (0, 0, -1),
    (1, 1, 0),
    (-1, -1, 0),
    (1, -1, 0),
    (-1, 1, 0),
    (1, 0, 1),
    (-1, 0, -1),
    (1, 0, -1),
    (-1, 0, 1),
    (0, 1, 1),
    (0, -1, -1),
    (0, 1, -1),
    (0, -1, 1),
)
relax_rate = 1.6
drag_factor = 20.0
LEVELS = 4
LANES = 128
GUARD = 8

x_up = [n for n in range(19) if lattice_speeds[n][0] == 1]
x_down = [n for n in range(19) if lattice_speeds[n][0] == -1]
y_up = [n for n in range(19) if lattice_speeds[n][1] == 1]
y_down = [n for n in range(19) if lattice_speeds[n][1] == -1]
vmem = pl.BlockSpec(memory_space=pltpu.VMEM)

FLOW = 19
SOLID = 22
NEXT = 23
SECOND = 26
QUANTITIES = 31
NEXT_SECOND = 31
COLUMN_QUANTITIES = 34
BEFORE_LANE = 16
AFTER_LANE = 32


def opposite_of(number):
    return number + 1 if number % 2 == 1 else number - 1


def lane_index(rows=8):
    return lax.broadcasted_iota(jnp.int32, (rows, LANES), 1)


def spread_solid(solid):
    tiles = solid.shape[1]
    row = lax.broadcasted_iota(jnp.int32, (tiles, LANES), 0)
    column = lax.broadcasted_iota(jnp.int32, (tiles, LANES), 1)
    spread = (column // TILE == row).astype(jnp.float32)
    cells = jnp.dot(solid[...].astype(jnp.float32), spread, preferred_element_type=jnp.float32)
    blocks = []
    for tile_row in range(solid.shape[0] // LEVELS):
        part = cells[tile_row * LEVELS : (tile_row + 1) * LEVELS]
        blocks.append(jnp.concatenate([part, part], axis=0))
    return blocks


def flow_blocks(velocity, step, rows):
    blocks = []
    for pair in range(rows // 16):
        both = [velocity[step, axis, pl.ds(16 * pair, 16), :].astype(jnp.float32) for axis in range(3)]
        blocks.append([part[:8] for part in both])
        blocks.append([part[8:] for part in both])
    return blocks


def on_even(axis):
    return lax.rem(lax.axis_index(axis), 2) == 0


class Chosen:
    def __init__(self, choice, yes, no):
        self.choice, self.yes, self.no = choice, yes, no
        self.shape = yes.shape

    def __getitem__(self, index):
        return jnp.where(self.choice, self.yes[index], self.no[index])


def slot_place(slot, group, groups):
    per_block = LANES // groups
    return slot // per_block, (slot % per_block) * groups + group


def insert_column(parts, slot, group, groups, value, edge, ahead):
    part, place = slot_place(slot, group, groups)
    lane = lane_index()
    turned = pltpu.roll(value, (place + ahead - edge) % LANES, 1)
    parts[part] = jnp.where(lane == place + ahead, turned, parts[part])


def row_message_kernel(
    state, velocity, solid, row_first, row_second, held, flow, tiles, arrived
):
    rows = state.shape[1]
    own = pl.ds(GUARD + 8, rows)
    copies = [
        pltpu.make_async_copy(state, held.at[:, own, :], arrived.at[0]),
        pltpu.make_async_copy(velocity, flow, arrived.at[1]),
        pltpu.make_async_copy(solid, tiles, arrived.at[2]),
    ]
    for copy in copies:
        copy.start()
    for copy in copies:
        copy.wait()
    even = on_even("gx")
    low_row, high_row = GUARD + 8, GUARD + 8 + rows - LEVELS

    def put(slot, low, high):
        row_first[slot] = jnp.where(even, high, low)
        row_second[slot] = jnp.where(even, low, high)

    for number in range(19):
        put(number, held[number, pl.ds(low_row, LEVELS), :], held[number, pl.ds(high_row, LEVELS), :])
    for step, slot in ((0, FLOW), (1, NEXT)):
        for axis in range(3):
            low = flow[step, axis, pl.ds(0, 16), :].astype(jnp.float32)
            high = flow[step, axis, pl.ds(rows - 16, 16), :].astype(jnp.float32)
            put(slot + axis, low[:LEVELS], high[16 - LEVELS :])
    solid_parts = spread_solid(tiles)
    put(SOLID, solid_parts[0][:LEVELS], solid_parts[-1][:LEVELS])
    for slot in range(5):
        put(
            SECOND + slot,
            held[x_up[slot], pl.ds(low_row + LEVELS, LEVELS), :],
            held[x_down[slot], pl.ds(high_row - LEVELS, LEVELS), :],
        )


def pack_columns(parts, slot, group, groups, value):
    low_parts, high_parts = parts
    part, place = slot_place(slot, group, groups)
    lane = lane_index()
    turned = pltpu.roll(value, (place + 1) % LANES, 1)
    low_parts[part] = jnp.where(lane == place + 1, turned, low_parts[part])
    high_parts[part] = jnp.where(lane == place, turned, high_parts[part])
    if slot in y_up:
        insert_column(low_parts, SECOND + y_up.index(slot), group, groups, value, 1, 1)
    if slot in y_down:
        insert_column(high_parts, SECOND + y_down.index(slot), group, groups, value, LANES - 2, 0)
    if NEXT <= slot < NEXT + 3:
        insert_column(low_parts, NEXT_SECOND + slot - NEXT, group, groups, value, 1, 1)
        insert_column(high_parts, NEXT_SECOND + slot - NEXT, group, groups, value, LANES - 2, 0)


def own_columns_kernel(held, velocity, solid, low, high):
    rows = velocity.shape[2]
    groups = rows // 8 + 2
    solid_parts = spread_solid(solid)
    flow = [flow_blocks(velocity, step, rows) for step in range(2)]
    parts = [[jnp.zeros((8, LANES), jnp.float32) for _ in range(low.shape[0])] for _ in range(2)]
    for group in range(1, groups - 1):
        for slot in range(19):
            pack_columns(parts, slot, group, groups, held[slot, pl.ds(GUARD + 8 * group, 8), :])
        for axis in range(3):
            pack_columns(parts, FLOW + axis, group, groups, flow[0][group - 1][axis])
            pack_columns(parts, NEXT + axis, group, groups, flow[1][group - 1][axis])
        pack_columns(parts, SOLID, group, groups, solid_parts[(group - 1) * 8 // (LEVELS * TILE)])
    for part in range(low.shape[0]):
        low[part] = parts[0][part]
        high[part] = parts[1][part]


def halo_columns_kernel(groups, own_low, own_high, row_first, row_second, low_out, high_out, ends):
    count = own_low.shape[0]
    even = on_even("gx")
    after, before = Chosen(even, row_first, row_second), Chosen(even, row_second, row_first)
    parts = [[own_low[part] for part in range(count)], [own_high[part] for part in range(count)]]
    for slot in range(SECOND):
        ends[0, slot, pl.ds(LEVELS, LEVELS), :] = before[slot]
        ends[1, slot, pl.ds(0, LEVELS), :] = after[slot]
        if slot == SOLID:
            low_second, high_second = SOLID, SOLID
        else:
            low_second = SECOND + x_down.index(slot) if slot in x_down else None
            high_second = SECOND + x_up.index(slot) if slot in x_up else None
        blank = jnp.zeros((LEVELS, LANES), jnp.float32)
        ends[0, slot, pl.ds(0, LEVELS), :] = blank if low_second is None else before[low_second]
        ends[1, slot, pl.ds(LEVELS, LEVELS), :] = blank if high_second is None else after[high_second]
        pack_columns(parts, slot, 0, groups, ends[0, slot])
        pack_columns(parts, slot, groups - 1, groups, ends[1, slot])
    for part in range(count):
        low_out[part] = parts[0][part]
        high_out[part] = parts[1][part]


def collide(moved, flow, fluid):
    ux, uy, uz = flow
    total = {n: moved[n] + moved[n + 1] for n in range(1, 19, 2)}
    xy, xz, yz = total[7] + total[9], total[11] + total[13], total[15] + total[17]
    axis_x, axis_y, axis_z = 2.0 * total[1], 2.0 * total[3], 2.0 * total[5]
    density = 12.0 * moved[0] + (axis_x + axis_y + axis_z) + (xy + xz + yz)
    pxx = axis_x + xy + xz
    pyy = axis_y + xy + yz
    pzz = axis_z + xz + yz
    pxy = total[7] - total[9]
    pxz = total[11] - total[13]
    pyz = total[15] - total[17]
    dx, dy, dz = momentum(moved)
    vx = pxx * ux + pxy * uy + pxz * uz
    vy = pxy * ux + pyy * uy + pyz * uz
    vz = pxz * ux + pyz * uy + pzz * uz
    speed_sq = ux * ux + uy * uy + uz * uz
    scaled = (relax_rate / 36.0) * fluid
    base = scaled * (density + 1.5 * (speed_sq * density) - 4.5 * (ux * vx + uy * vy + uz * vz))
    scaled3 = 3.0 * scaled
    bx = scaled3 * (dx + 3.0 * vx - ux * density)
    by = scaled3 * (dy + 3.0 * vy - uy * density)
    bz = scaled3 * (dz + 3.0 * vz - uz * density)
    keep = (1.0 - relax_rate) * fluid
    results = [keep * moved[0] + base]
    for number in range(1, 19, 2):
        along = None
        for speed, part in zip(lattice_speeds[number], (bx, by, bz)):
            if speed == 0:
                continue
            if along is None:
                along = part if speed == 1 else -part
            else:
                along = along + part if speed == 1 else along - part
        results.append(keep * moved[number] + (base + along))
        results.append(keep * moved[number + 1] + (base - along))
    return results


def outside(cz):
    level = lax.broadcasted_iota(jnp.int32, (8, LANES), 0) % LEVELS
    return level == (LEVELS - 1 if cz == 1 else 0)


def link_closed(solid_there, cz):
    closed = solid_there > 0.5
    return closed | outside(cz) if cz != 0 else closed


def shift_lanes(value, cy, edge_value):
    lane = lane_index(value.shape[0])
    shifted = pltpu.roll(value, -cy % LANES, 1)
    if edge_value is None:
        return shifted
    return jnp.where(lane == (LANES - 1 if cy == 1 else 0), edge_value, shifted)


def gather_cells(held, shifted, first, solid_rows):
    here = [held[n, pl.ds(first, 8), :] for n in range(19)]
    moved, closed = [here[0]], [None]
    for number in range(1, 19):
        cx, cy, cz = lattice_speeds[number]
        field = held if cy == 0 else shifted
        there = pl.ds(first + LEVELS * cx + cz, 8)
        closed.append(link_closed(solid_rows[cy % 3, there, :], cz))
        bounced = here[opposite_of(number)]
        if cx != 0:
            bounced = bounced + 2.0 * cx
        moved.append(jnp.where(closed[number], bounced, field[number, there, :]))
    return moved, closed


def momentum(moved):
    gap = {n: moved[n] - moved[n + 1] for n in range(1, 19, 2)}
    dx = 2.0 * gap[1] + (gap[7] + gap[9]) + (gap[11] + gap[13])
    dy = 2.0 * gap[3] + (gap[7] - gap[9]) + (gap[15] + gap[17])
    dz = 2.0 * gap[5] + (gap[11] - gap[13]) + (gap[15] - gap[17])
    return dx, dy, dz


def drag_term(moved, flow, fluid):
    return fluid * sum(speed * part for speed, part in zip(flow, momentum(moved)))


def along_link(number, vector):
    total = None
    for axis, speed in enumerate(lattice_speeds[number]):
        if speed == 0:
            continue
        part = vector(axis)
        if total is None:
            total = part if speed == 1 else -part
        else:
            total = total + part if speed == 1 else total - part
    return total


def later_drag(results, closed, weight_here, weight_back):
    term = None
    for number in range(1, 19):
        cx = lattice_speeds[number][0]
        here = along_link(number, lambda axis: weight_here[axis])
        back = along_link(number, lambda axis: weight_back(number, axis))
        part = jnp.where(closed[opposite_of(number)], -here, back) * results[number]
        if cx != 0:
            part = part + jnp.where(closed[number], (2.0 * cx) * here, 0.0)
        if number < 7:
            part = 2.0 * part
        term = part if term is None else term + part
    return term


def column_reader(groups):
    def column(message, ahead, slot, lane_first, group=0):
        part, place = slot_place(slot, group, groups)
        return pltpu.roll(message[part], (lane_first - place - ahead) % LANES, 1)

    return column


def fill_held(own_held, before, after, held, rows):
    own = GUARD + 8
    near, far = own - LEVELS, own + rows
    for number in range(19):
        for group in range(rows // 8):
            there = pl.ds(own + 8 * group, 8)
            held[number, there, :] = own_held[number, there, :]
        held[number, pl.ds(near, LEVELS), :] = before[number]
        held[number, pl.ds(far, LEVELS), :] = after[number]
        if number in x_down:
            held[number, pl.ds(near - LEVELS, LEVELS), :] = before[SECOND + x_down.index(number)]
        if number in x_up:
            held[number, pl.ds(far + LEVELS, LEVELS), :] = after[SECOND + x_up.index(number)]


def fill_shifted(field, shifted, groups, edge_of):
    for number in y_up + y_down:
        cy = lattice_speeds[number][1]
        for group in range(groups):
            there = pl.ds(GUARD + 8 * group, 8)
            shifted[number, there, :] = shift_lanes(field[number, there, :], cy, edge_of(number, cy, group))


def fill_solid(solid_parts, before, after, solid_rows, groups, edge_of):
    for group in range(groups):
        first = GUARD + 8 * group
        if group in (0, groups - 1):
            halo = before[SOLID] if group == 0 else after[SOLID]
            solid_rows[0, pl.ds(first, LEVELS), :] = halo
            solid_rows[0, pl.ds(first + LEVELS, LEVELS), :] = halo
        else:
            solid_rows[0, pl.ds(first, 8), :] = solid_parts[(group - 1) * 8 // (LEVELS * TILE)]
        value = solid_rows[0, pl.ds(first, 8), :]
        for cy in (1, -1):
            solid_rows[cy % 3, pl.ds(first, 8), :] = shift_lanes(value, cy, edge_of(SOLID, cy, group))


def shift_rows(value, cx, cz):
    if cx != 0:
        upper = lax.broadcasted_iota(jnp.int32, (8, LANES), 0) < LEVELS
        swapped = pltpu.roll(value, LEVELS, 0)
        if cx == 1:
            value = jnp.where(upper, swapped, pltpu.roll(swapped, LANES - 1, 1))
        else:
            value = jnp.where(upper, pltpu.roll(swapped, 1, 1), swapped)
    if cz != 0:
        value = pltpu.roll(value, (-cz) % 8, 0)
    return value


def gather_columns(neighbours):
    here = [neighbours(n, 0) for n in range(19)]
    solid = {cy: neighbours(SOLID, cy) for cy in (0, 1, -1)}
    moved, closed = [here[0]], [None]
    for number in range(1, 19):
        cx, cy, cz = lattice_speeds[number]
        source = shift_rows(here[number] if cy == 0 else neighbours(number, cy), cx, cz)
        closed.append(link_closed(shift_rows(solid[cy], cx, cz), cz))
        moved.append(jnp.where(closed[number], here[opposite_of(number)] + 2.0 * cx, source))
    return moved, closed, solid


def inner_drag_kernel(
    own_held, velocity, solid, row_first, row_second, partial, held, shifted, solid_rows, weights
):
    rows = velocity.shape[2]
    groups = rows // 8 + 2
    own = GUARD + 8
    near, far = own - LEVELS, own + rows
    even = on_even("gx")
    after, before = Chosen(even, row_first, row_second), Chosen(even, row_second, row_first)
    lane = lane_index()
    solid_parts = spread_solid(solid)

    def no_edge(slot, cy, group):
        return None

    fill_held(own_held, before, after, held, rows)
    fill_shifted(held, shifted, groups, no_edge)
    fill_solid(solid_parts, before, after, solid_rows, groups, no_edge)

    flow = flow_blocks(velocity, 1, rows)
    for axis in range(3):
        for group in range(rows // 8):
            there = pl.ds(own + 8 * group, 8)
            weights[axis, there, :] = (1.0 - solid_rows[0, there, :]) * flow[group][axis]
        for row, message in ((near, before), (far, after)):
            weights[axis, pl.ds(row, LEVELS), :] = (1.0 - message[SOLID]) * message[NEXT + axis]
        for group in range(groups):
            there = pl.ds(GUARD + 8 * group, 8)
            value = weights[axis, there, :]
            weights[3 + axis, there, :] = shift_lanes(value, 1, None)
            weights[6 + axis, there, :] = shift_lanes(value, -1, None)

    total = jnp.zeros((8, LANES), jnp.float32)
    flow = flow_blocks(velocity, 0, rows)
    for group in range(rows // 8):
        first = own + 8 * group
        moved, closed = gather_cells(held, shifted, first, solid_rows)
        fluid = 1.0 - solid_parts[8 * group // (LEVELS * TILE)]
        results = collide(moved, flow[group], fluid)

        def back(number, axis):
            cx, cy, cz = lattice_speeds[number]
            return weights[3 * (-cy % 3) + axis, pl.ds(first - LEVELS * cx - cz, 8), :]

        here = [weights[axis, pl.ds(first, 8), :] for axis in range(3)]
        total = total + drag_term(moved, flow[group], fluid) + later_drag(results, closed, here, back)
    inside = jnp.logical_and(lane > 0, lane < LANES - 1)
    partial[...] = jnp.where(inside, total, 0.0)


def edge_drag_kernel(groups, y_before, low, partial, shared):
    lane = lane_index()
    column = column_reader(groups)

    def neighbours(slot, cy):
        ahead = slot
        behind = slot
        if slot < 19 and cy == 1:
            ahead = SECOND + y_up.index(slot)
        if slot < 19 and cy == -1:
            behind = SECOND + y_down.index(slot)
        if NEXT <= slot < NEXT + 3:
            ahead = behind = NEXT_SECOND + slot - NEXT
        if cy == 0:
            first, second = column(y_before, 0, slot, BEFORE_LANE), column(low, 1, slot, AFTER_LANE)
        elif cy == 1:
            first, second = column(low, 1, slot, BEFORE_LANE), column(low, 1, ahead, AFTER_LANE)
        else:
            first, second = column(y_before, 0, behind, BEFORE_LANE), column(y_before, 0, slot, AFTER_LANE)
        return jnp.where(lane < AFTER_LANE, first, second)

    moved, closed, solid_columns = gather_columns(neighbours)
    fluid = {cy: 1.0 - solid_columns[cy] for cy in (0, 1, -1)}
    flow = [neighbours(FLOW + axis, 0) for axis in range(3)]
    results = collide(moved, flow, fluid[0])
    weight = {cy: [fluid[cy] * neighbours(NEXT + axis, cy) for axis in range(3)] for cy in (0, 1, -1)}

    def back(number, axis):
        cx, cy, cz = lattice_speeds[number]
        return shift_rows(weight[-cy][axis], -cx, -cz)

    term = drag_term(moved, flow, fluid[0]) + later_drag(results, closed, weight[0], back)
    place = jnp.where(lane < AFTER_LANE, lane - BEFORE_LANE, lane - AFTER_LANE)
    inside = jnp.logical_and(place > 0, place < groups - 1)
    total = partial[...] + jnp.where(inside, term, 0.0)
    shared[...] = jnp.broadcast_to(jnp.sum(total), shared.shape)


def main_kernel(
    own_held, velocity, solid, row_first, row_second, y_after, y_before, low, high, out,
    held, shifted, later, solid_rows, row_flow,
):
    rows = velocity.shape[2]
    groups = rows // 8 + 2
    own = GUARD + 8
    near, far = own - LEVELS, own + rows
    even = on_even("gx")
    after, before = Chosen(even, row_first, row_second), Chosen(even, row_second, row_first)
    lane = lane_index()
    solid_parts = spread_solid(solid)
    column = column_reader(groups)

    def edge_of(slot, cy, group):
        if cy == 1:
            return column(y_after, 1, slot, LANES - 1, group)
        return column(y_before, 0, slot, 0, group)

    fill_held(own_held, before, after, held, rows)
    fill_shifted(held, shifted, groups, edge_of)
    fill_solid(solid_parts, before, after, solid_rows, groups, edge_of)
    for slot, place in ((FLOW, 0), (FLOW + 1, 1), (FLOW + 2, 2), (SOLID, 3)):
        row_flow[place, pl.ds(0, LEVELS), :] = before[slot]
        row_flow[place, pl.ds(LEVELS, LEVELS), :] = after[slot]

    def both_rows(field, index, shift):
        ends = [field[index, pl.ds(place + shift, LEVELS), :] for place in (near, far)]
        return jnp.concatenate(ends, axis=0)

    here = [both_rows(held, n, 0) for n in range(19)]
    moved = [here[0]]
    for number in range(1, 19):
        cx, cy, cz = lattice_speeds[number]
        shift = LEVELS * cx + cz
        source = both_rows(held if cy == 0 else shifted, number, shift)
        closed = link_closed(both_rows(solid_rows, cy % 3, shift), cz)
        moved.append(jnp.where(closed, here[opposite_of(number)] + 2.0 * cx, source))
    row_results = collide(moved, [row_flow[axis] for axis in range(3)], 1.0 - row_flow[3])

    def neighbours(slot, cy):
        beyond = slot if cy == 0 or slot == SOLID else SECOND + (y_up if cy == 1 else y_down).index(slot)
        if cy == 1:
            first, second = column(low, 1, slot, BEFORE_LANE), column(y_after, 1, beyond, AFTER_LANE)
        elif cy == -1:
            first, second = column(y_before, 0, beyond, BEFORE_LANE), column(high, 0, slot, AFTER_LANE)
        else:
            first, second = column(y_before, 0, slot, BEFORE_LANE), column(y_after, 1, slot, AFTER_LANE)
        return jnp.where(lane < AFTER_LANE, first, second)

    moved, _, solid_columns = gather_columns(neighbours)
    column_flow = [neighbours(FLOW + axis, 0) for axis in range(3)]
    column_results = collide(moved, column_flow, 1.0 - solid_columns[0])

    flow = flow_blocks(velocity, 0, rows)
    for group in range(rows // 8):
        first = own + 8 * group
        moved, _ = gather_cells(held, shifted, first, solid_rows)
        results = collide(moved, flow[group], 1.0 - solid_parts[8 * group // (LEVELS * TILE)])
        for number in range(19):
            later[number, pl.ds(first, 8), :] = results[number]
    for number in x_down:
        later[number, pl.ds(near, LEVELS), :] = row_results[number][:LEVELS]
    for number in x_up:
        later[number, pl.ds(far, LEVELS), :] = row_results[number][LEVELS:]

    def later_edge(number, cy, group):
        shift = LANES - 1 - AFTER_LANE - group if cy == 1 else -BEFORE_LANE - group
        return pltpu.roll(column_results[number], shift % LANES, 1)

    fill_shifted(later, shifted, groups, later_edge)

    flow = flow_blocks(velocity, 1, rows)
    for group in range(rows // 8):
        first = 8 * group
        moved, _ = gather_cells(later, shifted, own + first, solid_rows)
        results = collide(moved, flow[group], 1.0 - solid_parts[first // (LEVELS * TILE)])
        for number in range(19):
            out[number, pl.ds(first, 8), :] = results[number]


def swap_pairs(first, second, axis):
    count = lax.axis_size(axis)
    inside = [(i, i ^ 1) for i in range(count)]
    across = [(i, (i + 1) % count if i % 2 == 1 else (i - 1) % count) for i in range(count)]
    second = lax.ppermute(second, axis, across)
    return lax.ppermute(first, axis, inside), second


def per_device(adjoint_in, velocity, solid_tiles, link_blocked):
    rows_x, levels, rows_y = adjoint_in.shape[1:]
    rows = rows_x * levels
    padded = rows + 16 + 2 * GUARD
    groups = rows // 8 + 2
    parts = -(-COLUMN_QUANTITIES // (LANES // groups))
    state = adjoint_in.reshape(19, rows, rows_y)
    flow = velocity.reshape(STEPS, 3, rows, rows_y)
    solid = solid_tiles.reshape(-1, solid_tiles.shape[2])

    def shape_of(*sizes):
        return jax.ShapeDtypeStruct(sizes, jnp.float32)

    params = pltpu.CompilerParams(vmem_limit_bytes=16 * 1024 * 1024)
    anywhere = pl.BlockSpec(memory_space=pl.ANY)
    *row_sent, held, flow, tiles = pl.pallas_call(
        row_message_kernel,
        out_shape=(
            pltpu.VMEM((QUANTITIES, levels, rows_y), jnp.float32),
            pltpu.VMEM((QUANTITIES, levels, rows_y), jnp.float32),
            pltpu.VMEM((19, padded, rows_y), jnp.float32),
            pltpu.VMEM(flow.shape, flow.dtype),
            pltpu.VMEM(solid.shape, solid.dtype),
        ),
        in_specs=[anywhere] * 3,
        out_specs=(vmem,) * 5,
        scratch_shapes=[pltpu.SemaphoreType.DMA((3,))],
        compiler_params=params,
    )(*(pltpu.with_memory_space_constraint(value, pltpu.HBM) for value in (state, flow, solid)))
    row_got = swap_pairs(*row_sent, "gx")
    own_columns = pl.pallas_call(
        own_columns_kernel,
        out_shape=(shape_of(parts, 8, rows_y),) * 2,
        in_specs=[vmem] * 3,
        out_specs=(vmem,) * 2,
        compiler_params=params,
        cost_estimate=pl.CostEstimate(flops=2_000_000, bytes_accessed=1_000_000, transcendentals=0),
    )(held, flow, tiles)
    low, high = pl.pallas_call(
        functools.partial(halo_columns_kernel, groups),
        out_shape=(shape_of(parts, 8, rows_y),) * 2,
        in_specs=[vmem] * 4,
        out_specs=(vmem,) * 2,
        scratch_shapes=[pltpu.VMEM((2, SECOND, 8, rows_y), jnp.float32)],
        compiler_params=params,
    )(*own_columns, *row_got)
    size = lax.axis_size("gy")
    y_before = lax.ppermute(high, "gy", [(i, (i + 1) % size) for i in range(size)])
    y_after = lax.ppermute(low, "gy", [((i + 1) % size, i) for i in range(size)])
    count = lax.axis_size("gx") * size
    field = pltpu.VMEM((19, padded, rows_y), jnp.float32)
    solid_field = pltpu.VMEM((3, padded, rows_y), jnp.float32)
    partial = pl.pallas_call(
        inner_drag_kernel,
        out_shape=pltpu.VMEM((8, rows_y), jnp.float32),
        in_specs=[vmem] * 5,
        out_specs=vmem,
        scratch_shapes=[field, field, solid_field, pltpu.VMEM((9, padded, rows_y), jnp.float32)],
        compiler_params=params,
        cost_estimate=pl.CostEstimate(flops=1_000_000, bytes_accessed=1_000_000, transcendentals=0),
    )(held, flow, tiles, *row_got)
    own = pl.pallas_call(
        functools.partial(edge_drag_kernel, groups),
        out_shape=pltpu.VMEM((count, 1, rows_y), jnp.float32),
        in_specs=[vmem] * 3,
        out_specs=vmem,
        compiler_params=params,
        cost_estimate=pl.CostEstimate(flops=20_000_000_000, bytes_accessed=10_000_000, transcendentals=0),
    )(y_before, low, partial)
    shared = lax.all_to_all(own, ("gx", "gy"), split_axis=0, concat_axis=0, tiled=True)
    result = pl.pallas_call(
        main_kernel,
        out_shape=shape_of(19, rows, rows_y),
        in_specs=[vmem] * 9,
        out_specs=vmem,
        scratch_shapes=[field, field, field, solid_field, pltpu.VMEM((4, 8, rows_y), jnp.float32)],
        compiler_params=params,
        cost_estimate=pl.CostEstimate(flops=200_000_000_000, bytes_accessed=200_000_000, transcendentals=0),
    )(held, flow, tiles, *row_got, y_after, y_before, low, high)
    cell_count = rows * rows_y * count
    scale = drag_factor / math.sqrt(cell_count) * 3.0 / 36.0
    total = jnp.sum(shared[:, 0, 0])
    return (result.reshape(adjoint_in.shape), (-scale * total).reshape(1))


def solution(mesh):
    placed = (
        P(None, "gx", None, "gy"),
        P(None, None, "gx", None, "gy"),
        P("gx", None, "gy"),
        P(None, "gx", None, "gy"),
    )
    return jax.shard_map(
        per_device,
        mesh=mesh,
        in_specs=placed,
        out_specs=(P(None, "gx", None, "gy"), P()),
        check_vma=False,
    )
```

```python
import functools
import math

import jax
import jax.numpy as jnp
from jax import lax
from jax.experimental import pallas as pl
from jax.experimental.pallas import tpu as pltpu
from jax.sharding import PartitionSpec as P

TILE = 4
STEPS = 2

lattice_speeds = (
    (0, 0, 0),
    (1, 0, 0),
    (-1, 0, 0),
    (0, 1, 0),
    (0, -1, 0),
    (0, 0, 1),
    (0, 0, -1),
    (1, 1, 0),
    (-1, -1, 0),
    (1, -1, 0),
    (-1, 1, 0),
    (1, 0, 1),
    (-1, 0, -1),
    (1, 0, -1),
    (-1, 0, 1),
    (0, 1, 1),
    (0, -1, -1),
    (0, 1, -1),
    (0, -1, 1),
)
relax_rate = 1.6
drag_factor = 20.0
LEVELS = 4
LANES = 128
GUARD = 8

x_up = [n for n in range(19) if lattice_speeds[n][0] == 1]
x_down = [n for n in range(19) if lattice_speeds[n][0] == -1]
y_up = [n for n in range(19) if lattice_speeds[n][1] == 1]
y_down = [n for n in range(19) if lattice_speeds[n][1] == -1]
vmem = pl.BlockSpec(memory_space=pltpu.VMEM)

FLOW = 19
SOLID = 22
NEXT = 23
SECOND = 26
QUANTITIES = 31
NEXT_SECOND = 31
COLUMN_QUANTITIES = 34
BEFORE_LANE = 16
AFTER_LANE = 32


def opposite_of(number):
    return number + 1 if number % 2 == 1 else number - 1


def lane_index(rows=8):
    return lax.broadcasted_iota(jnp.int32, (rows, LANES), 1)


def spread_solid(solid):
    tiles = solid.shape[1]
    row = lax.broadcasted_iota(jnp.int32, (tiles, LANES), 0)
    column = lax.broadcasted_iota(jnp.int32, (tiles, LANES), 1)
    spread = (column // TILE == row).astype(jnp.float32)
    cells = jnp.dot(solid[...].astype(jnp.float32), spread, preferred_element_type=jnp.float32)
    blocks = []
    for tile_row in range(solid.shape[0] // LEVELS):
        part = cells[tile_row * LEVELS : (tile_row + 1) * LEVELS]
        blocks.append(jnp.concatenate([part, part], axis=0))
    return blocks


def flow_blocks(velocity, step, rows):
    blocks = []
    for pair in range(rows // 16):
        both = [velocity[step, axis, pl.ds(16 * pair, 16), :].astype(jnp.float32) for axis in range(3)]
        blocks.append([part[:8] for part in both])
        blocks.append([part[8:] for part in both])
    return blocks


def on_even(axis):
    return lax.rem(lax.axis_index(axis), 2) == 0


class Chosen:
    def __init__(self, choice, yes, no):
        self.choice, self.yes, self.no = choice, yes, no
        self.shape = yes.shape

    def __getitem__(self, index):
        return jnp.where(self.choice, self.yes[index], self.no[index])


def slot_place(slot, group, groups):
    per_block = LANES // groups
    return slot // per_block, (slot % per_block) * groups + group


def insert_column(parts, slot, group, groups, value, edge, ahead):
    part, place = slot_place(slot, group, groups)
    lane = lane_index()
    turned = pltpu.roll(value, (place + ahead - edge) % LANES, 1)
    parts[part] = jnp.where(lane == place + ahead, turned, parts[part])


def row_message_kernel(
    state, velocity, solid, row_first, row_second, held, flow, tiles, arrived
):
    rows = state.shape[1]
    own = pl.ds(GUARD + 8, rows)
    copies = [
        pltpu.make_async_copy(state, held.at[:, own, :], arrived.at[0]),
        pltpu.make_async_copy(velocity, flow, arrived.at[1]),
        pltpu.make_async_copy(solid, tiles, arrived.at[2]),
    ]
    for copy in copies:
        copy.start()
    for copy in copies:
        copy.wait()
    even = on_even("gx")
    low_row, high_row = GUARD + 8, GUARD + 8 + rows - LEVELS

    def put(slot, low, high):
        row_first[slot] = jnp.where(even, high, low)
        row_second[slot] = jnp.where(even, low, high)

    for number in range(19):
        put(number, held[number, pl.ds(low_row, LEVELS), :], held[number, pl.ds(high_row, LEVELS), :])
    for step, slot in ((0, FLOW), (1, NEXT)):
        for axis in range(3):
            low = flow[step, axis, pl.ds(0, 16), :].astype(jnp.float32)
            high = flow[step, axis, pl.ds(rows - 16, 16), :].astype(jnp.float32)
            put(slot + axis, low[:LEVELS], high[16 - LEVELS :])
    solid_parts = spread_solid(tiles)
    put(SOLID, solid_parts[0][:LEVELS], solid_parts[-1][:LEVELS])
    for slot in range(5):
        put(
            SECOND + slot,
            held[x_up[slot], pl.ds(low_row + LEVELS, LEVELS), :],
            held[x_down[slot], pl.ds(high_row - LEVELS, LEVELS), :],
        )


def pack_columns(parts, slot, group, groups, value):
    low_parts, high_parts = parts
    part, place = slot_place(slot, group, groups)
    lane = lane_index()
    turned = pltpu.roll(value, (place + 1) % LANES, 1)
    low_parts[part] = jnp.where(lane == place + 1, turned, low_parts[part])
    high_parts[part] = jnp.where(lane == place, turned, high_parts[part])
    if slot in y_up:
        insert_column(low_parts, SECOND + y_up.index(slot), group, groups, value, 1, 1)
    if slot in y_down:
        insert_column(high_parts, SECOND + y_down.index(slot), group, groups, value, LANES - 2, 0)
    if NEXT <= slot < NEXT + 3:
        insert_column(low_parts, NEXT_SECOND + slot - NEXT, group, groups, value, 1, 1)
        insert_column(high_parts, NEXT_SECOND + slot - NEXT, group, groups, value, LANES - 2, 0)


def own_columns_kernel(held, velocity, solid, low, high):
    rows = velocity.shape[2]
    groups = rows // 8 + 2
    solid_parts = spread_solid(solid)
    flow = [flow_blocks(velocity, step, rows) for step in range(2)]
    parts = [[jnp.zeros((8, LANES), jnp.float32) for _ in range(low.shape[0])] for _ in range(2)]
    for group in range(1, groups - 1):
        for slot in range(19):
            pack_columns(parts, slot, group, groups, held[slot, pl.ds(GUARD + 8 * group, 8), :])
        for axis in range(3):
            pack_columns(parts, FLOW + axis, group, groups, flow[0][group - 1][axis])
            pack_columns(parts, NEXT + axis, group, groups, flow[1][group - 1][axis])
        pack_columns(parts, SOLID, group, groups, solid_parts[(group - 1) * 8 // (LEVELS * TILE)])
    for part in range(low.shape[0]):
        low[part] = parts[0][part]
        high[part] = parts[1][part]


def halo_columns_kernel(groups, own_low, own_high, row_first, row_second, low_out, high_out, ends):
    count = own_low.shape[0]
    even = on_even("gx")
    after, before = Chosen(even, row_first, row_second), Chosen(even, row_second, row_first)
    parts = [[own_low[part] for part in range(count)], [own_high[part] for part in range(count)]]
    for slot in range(SECOND):
        ends[0, slot, pl.ds(LEVELS, LEVELS), :] = before[slot]
        ends[1, slot, pl.ds(0, LEVELS), :] = after[slot]
        if slot == SOLID:
            low_second, high_second = SOLID, SOLID
        else:
            low_second = SECOND + x_down.index(slot) if slot in x_down else None
            high_second = SECOND + x_up.index(slot) if slot in x_up else None
        blank = jnp.zeros((LEVELS, LANES), jnp.float32)
        ends[0, slot, pl.ds(0, LEVELS), :] = blank if low_second is None else before[low_second]
        ends[1, slot, pl.ds(LEVELS, LEVELS), :] = blank if high_second is None else after[high_second]
        pack_columns(parts, slot, 0, groups, ends[0, slot])
        pack_columns(parts, slot, groups - 1, groups, ends[1, slot])
    for part in range(count):
        low_out[part] = parts[0][part]
        high_out[part] = parts[1][part]


def collide(moved, flow, fluid):
    ux, uy, uz = flow
    total = {n: moved[n] + moved[n + 1] for n in range(1, 19, 2)}
    xy, xz, yz = total[7] + total[9], total[11] + total[13], total[15] + total[17]
    axis_x, axis_y, axis_z = 2.0 * total[1], 2.0 * total[3], 2.0 * total[5]
    density = 12.0 * moved[0] + (axis_x + axis_y + axis_z) + (xy + xz + yz)
    pxx = axis_x + xy + xz
    pyy = axis_y + xy + yz
    pzz = axis_z + xz + yz
    pxy = total[7] - total[9]
    pxz = total[11] - total[13]
    pyz = total[15] - total[17]
    dx, dy, dz = momentum(moved)
    vx = pxx * ux + pxy * uy + pxz * uz
    vy = pxy * ux + pyy * uy + pyz * uz
    vz = pxz * ux + pyz * uy + pzz * uz
    speed_sq = ux * ux + uy * uy + uz * uz
    scaled = (relax_rate / 36.0) * fluid
    base = scaled * (density + 1.5 * (speed_sq * density) - 4.5 * (ux * vx + uy * vy + uz * vz))
    scaled3 = 3.0 * scaled
    bx = scaled3 * (dx + 3.0 * vx - ux * density)
    by = scaled3 * (dy + 3.0 * vy - uy * density)
    bz = scaled3 * (dz + 3.0 * vz - uz * density)
    keep = (1.0 - relax_rate) * fluid
    results = [keep * moved[0] + base]
    for number in range(1, 19, 2):
        along = None
        for speed, part in zip(lattice_speeds[number], (bx, by, bz)):
            if speed == 0:
                continue
            if along is None:
                along = part if speed == 1 else -part
            else:
                along = along + part if speed == 1 else along - part
        results.append(keep * moved[number] + (base + along))
        results.append(keep * moved[number + 1] + (base - along))
    return results


def outside(cz):
    level = lax.broadcasted_iota(jnp.int32, (8, LANES), 0) % LEVELS
    return level == (LEVELS - 1 if cz == 1 else 0)


def link_closed(solid_there, cz):
    closed = solid_there > 0.5
    return closed | outside(cz) if cz != 0 else closed


def shift_lanes(value, cy, edge_value):
    lane = lane_index(value.shape[0])
    shifted = pltpu.roll(value, -cy % LANES, 1)
    if edge_value is None:
        return shifted
    return jnp.where(lane == (LANES - 1 if cy == 1 else 0), edge_value, shifted)


def gather_cells(held, shifted, first, solid_rows):
    here = [held[n, pl.ds(first, 8), :] for n in range(19)]
    moved, closed = [here[0]], [None]
    for number in range(1, 19):
        cx, cy, cz = lattice_speeds[number]
        field = held if cy == 0 else shifted
        there = pl.ds(first + LEVELS * cx + cz, 8)
        closed.append(link_closed(solid_rows[cy % 3, there, :], cz))
        bounced = here[opposite_of(number)]
        if cx != 0:
            bounced = bounced + 2.0 * cx
        moved.append(jnp.where(closed[number], bounced, field[number, there, :]))
    return moved, closed


def momentum(moved):
    gap = {n: moved[n] - moved[n + 1] for n in range(1, 19, 2)}
    dx = 2.0 * gap[1] + (gap[7] + gap[9]) + (gap[11] + gap[13])
    dy = 2.0 * gap[3] + (gap[7] - gap[9]) + (gap[15] + gap[17])
    dz = 2.0 * gap[5] + (gap[11] - gap[13]) + (gap[15] - gap[17])
    return dx, dy, dz


def drag_term(moved, flow, fluid):
    return fluid * sum(speed * part for speed, part in zip(flow, momentum(moved)))


def along_link(number, vector):
    total = None
    for axis, speed in enumerate(lattice_speeds[number]):
        if speed == 0:
            continue
        part = vector(axis)
        if total is None:
            total = part if speed == 1 else -part
        else:
            total = total + part if speed == 1 else total - part
    return total


def later_drag(results, closed, weight_here, weight_back):
    term = None
    for number in range(1, 19):
        cx = lattice_speeds[number][0]
        here = along_link(number, lambda axis: weight_here[axis])
        part = jnp.where(closed[opposite_of(number)], -here, weight_back(number)) * results[number]
        if cx != 0:
            part = part + jnp.where(closed[number], (2.0 * cx) * here, 0.0)
        if number < 7:
            part = 2.0 * part
        term = part if term is None else term + part
    return term


def column_reader(groups):
    def column(message, ahead, slot, lane_first, group=0):
        part, place = slot_place(slot, group, groups)
        return pltpu.roll(message[part], (lane_first - place - ahead) % LANES, 1)

    return column


def fill_held(own_held, before, after, held, rows):
    own = GUARD + 8
    near, far = own - LEVELS, own + rows
    for number in range(19):
        for group in range(rows // 8):
            there = pl.ds(own + 8 * group, 8)
            held[number, there, :] = own_held[number, there, :]
        held[number, pl.ds(near, LEVELS), :] = before[number]
        held[number, pl.ds(far, LEVELS), :] = after[number]
        if number in x_down:
            held[number, pl.ds(near - LEVELS, LEVELS), :] = before[SECOND + x_down.index(number)]
        if number in x_up:
            held[number, pl.ds(far + LEVELS, LEVELS), :] = after[SECOND + x_up.index(number)]


def fill_shifted(field, shifted, groups, edge_of):
    for number in y_up + y_down:
        cy = lattice_speeds[number][1]
        for group in range(groups):
            there = pl.ds(GUARD + 8 * group, 8)
            shifted[number, there, :] = shift_lanes(field[number, there, :], cy, edge_of(number, cy, group))


def fill_solid(solid_parts, before, after, solid_rows, groups, edge_of):
    for group in range(groups):
        first = GUARD + 8 * group
        if group in (0, groups - 1):
            halo = before[SOLID] if group == 0 else after[SOLID]
            solid_rows[0, pl.ds(first, LEVELS), :] = halo
            solid_rows[0, pl.ds(first + LEVELS, LEVELS), :] = halo
        else:
            solid_rows[0, pl.ds(first, 8), :] = solid_parts[(group - 1) * 8 // (LEVELS * TILE)]
        value = solid_rows[0, pl.ds(first, 8), :]
        for cy in (1, -1):
            solid_rows[cy % 3, pl.ds(first, 8), :] = shift_lanes(value, cy, edge_of(SOLID, cy, group))


def shift_rows(value, cx, cz):
    if cx != 0:
        upper = lax.broadcasted_iota(jnp.int32, (8, LANES), 0) < LEVELS
        swapped = pltpu.roll(value, LEVELS, 0)
        if cx == 1:
            value = jnp.where(upper, swapped, pltpu.roll(swapped, LANES - 1, 1))
        else:
            value = jnp.where(upper, pltpu.roll(swapped, 1, 1), swapped)
    if cz != 0:
        value = pltpu.roll(value, (-cz) % 8, 0)
    return value


def gather_columns(neighbours):
    here = [neighbours(n, 0) for n in range(19)]
    solid = {cy: neighbours(SOLID, cy) for cy in (0, 1, -1)}
    moved, closed = [here[0]], [None]
    for number in range(1, 19):
        cx, cy, cz = lattice_speeds[number]
        source = shift_rows(here[number] if cy == 0 else neighbours(number, cy), cx, cz)
        closed.append(link_closed(shift_rows(solid[cy], cx, cz), cz))
        moved.append(jnp.where(closed[number], here[opposite_of(number)] + 2.0 * cx, source))
    return moved, closed, solid


def inner_drag_kernel(
    own_held, velocity, solid, row_first, row_second, low, partial, own_blocks,
    held, shifted, solid_rows, weights,
):
    rows = velocity.shape[2]
    groups = rows // 8 + 2
    own = GUARD + 8
    near, far = own - LEVELS, own + rows
    even = on_even("gx")
    after, before = Chosen(even, row_first, row_second), Chosen(even, row_second, row_first)
    lane = lane_index()
    solid_parts = spread_solid(solid)

    def no_edge(slot, cy, group):
        return None

    fill_held(own_held, before, after, held, rows)
    fill_shifted(held, shifted, groups, no_edge)
    fill_solid(solid_parts, before, after, solid_rows, groups, no_edge)

    flow = flow_blocks(velocity, 1, rows)
    for axis in range(3):
        for group in range(rows // 8):
            there = pl.ds(own + 8 * group, 8)
            weights[axis, there, :] = (1.0 - solid_rows[0, there, :]) * flow[group][axis]
        for row, message in ((near, before), (far, after)):
            weights[axis, pl.ds(row, LEVELS), :] = (1.0 - message[SOLID]) * message[NEXT + axis]
        for group in range(groups):
            there = pl.ds(GUARD + 8 * group, 8)
            value = weights[axis, there, :]
            weights[3 + axis, there, :] = shift_lanes(value, 1, None)
            weights[6 + axis, there, :] = shift_lanes(value, -1, None)

    total = jnp.zeros((8, LANES), jnp.float32)
    flow = flow_blocks(velocity, 0, rows)
    for group in range(rows // 8):
        first = own + 8 * group
        moved, closed = gather_cells(held, shifted, first, solid_rows)
        fluid = 1.0 - solid_parts[8 * group // (LEVELS * TILE)]
        results = collide(moved, flow[group], fluid)

        def back(number):
            cx, cy, cz = lattice_speeds[number]
            there = pl.ds(first - LEVELS * cx - cz, 8)
            return along_link(number, lambda axis: weights[3 * (-cy % 3) + axis, there, :])

        here = [weights[axis, pl.ds(first, 8), :] for axis in range(3)]
        total = total + drag_term(moved, flow[group], fluid) + later_drag(results, closed, here, back)
    inside = jnp.logical_and(lane > 0, lane < LANES - 1)
    partial[...] = jnp.where(inside, total, 0.0)

    column = column_reader(groups)
    for slot in range(SECOND):
        own_blocks[slot] = column(low, 1, slot, AFTER_LANE)
    for place, slot in enumerate(ahead_slots):
        here = column(low, 1, slot, BEFORE_LANE)
        ahead = column(low, 1, second_slot(slot, y_up), AFTER_LANE)
        own_blocks[SECOND + place] = jnp.where(lane < AFTER_LANE, here, ahead)


ahead_slots = y_up + [SOLID, NEXT, NEXT + 1, NEXT + 2]


def second_slot(slot, moving):
    if slot in moving:
        return SECOND + moving.index(slot)
    return NEXT_SECOND + slot - NEXT if NEXT <= slot < NEXT + 3 else slot


def edge_drag_kernel(groups, y_before, own_blocks, partial, shared):
    lane = lane_index()
    column = column_reader(groups)

    def neighbours(slot, cy):
        if cy == 1:
            return own_blocks[SECOND + ahead_slots.index(slot)]
        if cy == 0:
            first, second = column(y_before, 0, slot, BEFORE_LANE), own_blocks[slot]
        else:
            first = column(y_before, 0, second_slot(slot, y_down), BEFORE_LANE)
            second = column(y_before, 0, slot, AFTER_LANE)
        return jnp.where(lane < AFTER_LANE, first, second)

    moved, closed, solid_columns = gather_columns(neighbours)
    fluid = {cy: 1.0 - solid_columns[cy] for cy in (0, 1, -1)}
    flow = [neighbours(FLOW + axis, 0) for axis in range(3)]
    results = collide(moved, flow, fluid[0])
    weight = {cy: [fluid[cy] * neighbours(NEXT + axis, cy) for axis in range(3)] for cy in (0, 1, -1)}

    def back(number):
        cx, cy, cz = lattice_speeds[number]
        return shift_rows(along_link(number, lambda axis: weight[-cy][axis]), -cx, -cz)

    term = drag_term(moved, flow, fluid[0]) + later_drag(results, closed, weight[0], back)
    place = jnp.where(lane < AFTER_LANE, lane - BEFORE_LANE, lane - AFTER_LANE)
    inside = jnp.logical_and(place > 0, place < groups - 1)
    total = partial[...] + jnp.where(inside, term, 0.0)
    shared[...] = jnp.broadcast_to(jnp.sum(total), shared.shape)


def main_kernel(
    own_held, velocity, solid, row_first, row_second, y_after, y_before, low, high, out,
    held, shifted, later, solid_rows, row_flow,
):
    rows = velocity.shape[2]
    groups = rows // 8 + 2
    own = GUARD + 8
    near, far = own - LEVELS, own + rows
    even = on_even("gx")
    after, before = Chosen(even, row_first, row_second), Chosen(even, row_second, row_first)
    lane = lane_index()
    solid_parts = spread_solid(solid)
    column = column_reader(groups)

    def edge_of(slot, cy, group):
        if cy == 1:
            return column(y_after, 1, slot, LANES - 1, group)
        return column(y_before, 0, slot, 0, group)

    fill_held(own_held, before, after, held, rows)
    fill_shifted(held, shifted, groups, edge_of)
    fill_solid(solid_parts, before, after, solid_rows, groups, edge_of)
    for slot, place in ((FLOW, 0), (FLOW + 1, 1), (FLOW + 2, 2), (SOLID, 3)):
        row_flow[place, pl.ds(0, LEVELS), :] = before[slot]
        row_flow[place, pl.ds(LEVELS, LEVELS), :] = after[slot]

    def both_rows(field, index, shift):
        ends = [field[index, pl.ds(place + shift, LEVELS), :] for place in (near, far)]
        return jnp.concatenate(ends, axis=0)

    here = [both_rows(held, n, 0) for n in range(19)]
    moved = [here[0]]
    for number in range(1, 19):
        cx, cy, cz = lattice_speeds[number]
        shift = LEVELS * cx + cz
        source = both_rows(held if cy == 0 else shifted, number, shift)
        closed = link_closed(both_rows(solid_rows, cy % 3, shift), cz)
        moved.append(jnp.where(closed, here[opposite_of(number)] + 2.0 * cx, source))
    row_results = collide(moved, [row_flow[axis] for axis in range(3)], 1.0 - row_flow[3])

    def neighbours(slot, cy):
        beyond = slot if cy == 0 or slot == SOLID else SECOND + (y_up if cy == 1 else y_down).index(slot)
        if cy == 1:
            first, second = column(low, 1, slot, BEFORE_LANE), column(y_after, 1, beyond, AFTER_LANE)
        elif cy == -1:
            first, second = column(y_before, 0, beyond, BEFORE_LANE), column(high, 0, slot, AFTER_LANE)
        else:
            first, second = column(y_before, 0, slot, BEFORE_LANE), column(y_after, 1, slot, AFTER_LANE)
        return jnp.where(lane < AFTER_LANE, first, second)

    moved, _, solid_columns = gather_columns(neighbours)
    column_flow = [neighbours(FLOW + axis, 0) for axis in range(3)]
    column_results = collide(moved, column_flow, 1.0 - solid_columns[0])

    flow = flow_blocks(velocity, 0, rows)
    for group in range(rows // 8):
        first = own + 8 * group
        moved, _ = gather_cells(held, shifted, first, solid_rows)
        results = collide(moved, flow[group], 1.0 - solid_parts[8 * group // (LEVELS * TILE)])
        for number in range(19):
            later[number, pl.ds(first, 8), :] = results[number]
    for number in x_down:
        later[number, pl.ds(near, LEVELS), :] = row_results[number][:LEVELS]
    for number in x_up:
        later[number, pl.ds(far, LEVELS), :] = row_results[number][LEVELS:]

    def later_edge(number, cy, group):
        shift = LANES - 1 - AFTER_LANE - group if cy == 1 else -BEFORE_LANE - group
        return pltpu.roll(column_results[number], shift % LANES, 1)

    fill_shifted(later, shifted, groups, later_edge)

    flow = flow_blocks(velocity, 1, rows)
    for group in range(rows // 8):
        first = 8 * group
        moved, _ = gather_cells(later, shifted, own + first, solid_rows)
        results = collide(moved, flow[group], 1.0 - solid_parts[first // (LEVELS * TILE)])
        for number in range(19):
            out[number, pl.ds(first, 8), :] = results[number]


def swap_pairs(first, second, axis):
    count = lax.axis_size(axis)
    inside = [(i, i ^ 1) for i in range(count)]
    across = [(i, (i + 1) % count if i % 2 == 1 else (i - 1) % count) for i in range(count)]
    second = lax.ppermute(second, axis, across)
    return lax.ppermute(first, axis, inside), second


def per_device(adjoint_in, velocity, solid_tiles, link_blocked):
    rows_x, levels, rows_y = adjoint_in.shape[1:]
    rows = rows_x * levels
    padded = rows + 16 + 2 * GUARD
    groups = rows // 8 + 2
    parts = -(-COLUMN_QUANTITIES // (LANES // groups))
    state = adjoint_in.reshape(19, rows, rows_y)
    flow = velocity.reshape(STEPS, 3, rows, rows_y)
    solid = solid_tiles.reshape(-1, solid_tiles.shape[2])

    def shape_of(*sizes):
        return jax.ShapeDtypeStruct(sizes, jnp.float32)

    params = pltpu.CompilerParams(vmem_limit_bytes=16 * 1024 * 1024)
    anywhere = pl.BlockSpec(memory_space=pl.ANY)
    *row_sent, held, flow, tiles = pl.pallas_call(
        row_message_kernel,
        out_shape=(
            pltpu.VMEM((QUANTITIES, levels, rows_y), jnp.float32),
            pltpu.VMEM((QUANTITIES, levels, rows_y), jnp.float32),
            pltpu.VMEM((19, padded, rows_y), jnp.float32),
            pltpu.VMEM(flow.shape, flow.dtype),
            pltpu.VMEM(solid.shape, solid.dtype),
        ),
        in_specs=[anywhere] * 3,
        out_specs=(vmem,) * 5,
        scratch_shapes=[pltpu.SemaphoreType.DMA((3,))],
        compiler_params=params,
    )(*(pltpu.with_memory_space_constraint(value, pltpu.HBM) for value in (state, flow, solid)))
    row_got = swap_pairs(*row_sent, "gx")
    own_columns = pl.pallas_call(
        own_columns_kernel,
        out_shape=(shape_of(parts, 8, rows_y),) * 2,
        in_specs=[vmem] * 3,
        out_specs=(vmem,) * 2,
        compiler_params=params,
        cost_estimate=pl.CostEstimate(flops=2_000_000, bytes_accessed=1_000_000, transcendentals=0),
    )(held, flow, tiles)
    low, high = pl.pallas_call(
        functools.partial(halo_columns_kernel, groups),
        out_shape=(shape_of(parts, 8, rows_y),) * 2,
        in_specs=[vmem] * 4,
        out_specs=(vmem,) * 2,
        scratch_shapes=[pltpu.VMEM((2, SECOND, 8, rows_y), jnp.float32)],
        compiler_params=params,
    )(*own_columns, *row_got)
    size = lax.axis_size("gy")
    y_before = lax.ppermute(high, "gy", [(i, (i + 1) % size) for i in range(size)])
    y_after = lax.ppermute(low, "gy", [((i + 1) % size, i) for i in range(size)])
    count = lax.axis_size("gx") * size
    field = pltpu.VMEM((19, padded, rows_y), jnp.float32)
    solid_field = pltpu.VMEM((3, padded, rows_y), jnp.float32)
    partial, own_blocks = pl.pallas_call(
        inner_drag_kernel,
        out_shape=(
            pltpu.VMEM((8, rows_y), jnp.float32),
            pltpu.VMEM((SECOND + len(ahead_slots), 8, rows_y), jnp.float32),
        ),
        in_specs=[vmem] * 6,
        out_specs=(vmem,) * 2,
        scratch_shapes=[field, field, solid_field, pltpu.VMEM((9, padded, rows_y), jnp.float32)],
        compiler_params=params,
        cost_estimate=pl.CostEstimate(flops=1_000_000, bytes_accessed=1_000_000, transcendentals=0),
    )(held, flow, tiles, *row_got, low)
    own = pl.pallas_call(
        functools.partial(edge_drag_kernel, groups),
        out_shape=pltpu.VMEM((count, 1, rows_y), jnp.float32),
        in_specs=[vmem] * 3,
        out_specs=vmem,
        compiler_params=params,
        cost_estimate=pl.CostEstimate(flops=20_000_000_000, bytes_accessed=10_000_000, transcendentals=0),
    )(y_before, own_blocks, partial)
    shared = lax.all_to_all(own, ("gx", "gy"), split_axis=0, concat_axis=0, tiled=True)
    result = pl.pallas_call(
        main_kernel,
        out_shape=shape_of(19, rows, rows_y),
        in_specs=[vmem] * 9,
        out_specs=vmem,
        scratch_shapes=[field, field, field, solid_field, pltpu.VMEM((4, 8, rows_y), jnp.float32)],
        compiler_params=params,
        cost_estimate=pl.CostEstimate(flops=20_000_000_000, bytes_accessed=4_000_000, transcendentals=0),
    )(held, flow, tiles, *row_got, y_after, y_before, low, high)
    cell_count = rows * rows_y * count
    scale = drag_factor / math.sqrt(cell_count) * 3.0 / 36.0
    total = jnp.sum(shared[:, 0, 0])
    return (result.reshape(adjoint_in.shape), (-scale * total).reshape(1))


def solution(mesh):
    placed = (
        P(None, "gx", None, "gy"),
        P(None, None, "gx", None, "gy"),
        P("gx", None, "gy"),
        P(None, "gx", None, "gy"),
    )
    return jax.shard_map(
        per_device,
        mesh=mesh,
        in_specs=placed,
        out_specs=(P(None, "gx", None, "gy"), P()),
        check_vma=False,
    )
```

```python
import functools
import math

import jax
import jax.numpy as jnp
from jax import lax
from jax.experimental import pallas as pl
from jax.experimental.pallas import tpu as pltpu
from jax.sharding import PartitionSpec as P

TILE = 4
STEPS = 2

lattice_speeds = (
    (0, 0, 0),
    (1, 0, 0),
    (-1, 0, 0),
    (0, 1, 0),
    (0, -1, 0),
    (0, 0, 1),
    (0, 0, -1),
    (1, 1, 0),
    (-1, -1, 0),
    (1, -1, 0),
    (-1, 1, 0),
    (1, 0, 1),
    (-1, 0, -1),
    (1, 0, -1),
    (-1, 0, 1),
    (0, 1, 1),
    (0, -1, -1),
    (0, 1, -1),
    (0, -1, 1),
)
relax_rate = 1.6
drag_factor = 20.0
LEVELS = 4
LANES = 128
GUARD = 8

x_up = [n for n in range(19) if lattice_speeds[n][0] == 1]
x_down = [n for n in range(19) if lattice_speeds[n][0] == -1]
y_up = [n for n in range(19) if lattice_speeds[n][1] == 1]
y_down = [n for n in range(19) if lattice_speeds[n][1] == -1]
vmem = pl.BlockSpec(memory_space=pltpu.VMEM)

FLOW = 19
SOLID = 22
NEXT = 23
SECOND = 26
QUANTITIES = 31
NEXT_SECOND = 31
COLUMN_QUANTITIES = 34
BEFORE_LANE = 16
AFTER_LANE = 32


def opposite_of(number):
    return number + 1 if number % 2 == 1 else number - 1


def lane_index(rows=8):
    return lax.broadcasted_iota(jnp.int32, (rows, LANES), 1)


def spread_solid(solid):
    tiles = solid.shape[1]
    row = lax.broadcasted_iota(jnp.int32, (tiles, LANES), 0)
    column = lax.broadcasted_iota(jnp.int32, (tiles, LANES), 1)
    spread = (column // TILE == row).astype(jnp.float32)
    cells = jnp.dot(solid[...].astype(jnp.float32), spread, preferred_element_type=jnp.float32)
    blocks = []
    for tile_row in range(solid.shape[0] // LEVELS):
        part = cells[tile_row * LEVELS : (tile_row + 1) * LEVELS]
        blocks.append(jnp.concatenate([part, part], axis=0))
    return blocks


def flow_blocks(velocity, step, rows):
    blocks = []
    for pair in range(rows // 16):
        both = [velocity[step, axis, pl.ds(16 * pair, 16), :].astype(jnp.float32) for axis in range(3)]
        blocks.append([part[:8] for part in both])
        blocks.append([part[8:] for part in both])
    return blocks


def on_even(axis):
    return lax.rem(lax.axis_index(axis), 2) == 0


class Chosen:
    def __init__(self, choice, yes, no):
        self.choice, self.yes, self.no = choice, yes, no
        self.shape = yes.shape

    def __getitem__(self, index):
        return jnp.where(self.choice, self.yes[index], self.no[index])


def slot_place(slot, group, groups):
    per_block = LANES // groups
    return slot // per_block, (slot % per_block) * groups + group


def insert_column(parts, slot, group, groups, value, edge, ahead):
    part, place = slot_place(slot, group, groups)
    lane = lane_index()
    turned = pltpu.roll(value, (place + ahead - edge) % LANES, 1)
    parts[part] = jnp.where(lane == place + ahead, turned, parts[part])


def row_message_kernel(
    state, velocity, solid, row_first, row_second, held, flow, tiles, arrived
):
    rows = state.shape[1]
    own = pl.ds(GUARD + 8, rows)
    copies = [
        pltpu.make_async_copy(state, held.at[:, own, :], arrived.at[0]),
        pltpu.make_async_copy(velocity, flow, arrived.at[1]),
        pltpu.make_async_copy(solid, tiles, arrived.at[2]),
    ]
    for copy in copies:
        copy.start()
    for copy in copies:
        copy.wait()
    even = on_even("gx")
    low_row, high_row = GUARD + 8, GUARD + 8 + rows - LEVELS

    def put(slot, low, high):
        row_first[slot] = jnp.where(even, high, low)
        row_second[slot] = jnp.where(even, low, high)

    for number in range(19):
        put(number, held[number, pl.ds(low_row, LEVELS), :], held[number, pl.ds(high_row, LEVELS), :])
    for step, slot in ((0, FLOW), (1, NEXT)):
        for axis in range(3):
            low = flow[step, axis, pl.ds(0, 16), :].astype(jnp.float32)
            high = flow[step, axis, pl.ds(rows - 16, 16), :].astype(jnp.float32)
            put(slot + axis, low[:LEVELS], high[16 - LEVELS :])
    solid_parts = spread_solid(tiles)
    put(SOLID, solid_parts[0][:LEVELS], solid_parts[-1][:LEVELS])
    for slot in range(5):
        put(
            SECOND + slot,
            held[x_up[slot], pl.ds(low_row + LEVELS, LEVELS), :],
            held[x_down[slot], pl.ds(high_row - LEVELS, LEVELS), :],
        )


def pack_columns(parts, slot, group, groups, value):
    low_parts, high_parts = parts
    part, place = slot_place(slot, group, groups)
    lane = lane_index()
    turned = pltpu.roll(value, (place + 1) % LANES, 1)
    low_parts[part] = jnp.where(lane == place + 1, turned, low_parts[part])
    high_parts[part] = jnp.where(lane == place, turned, high_parts[part])
    if slot in y_up:
        insert_column(low_parts, SECOND + y_up.index(slot), group, groups, value, 1, 1)
    if slot in y_down:
        insert_column(high_parts, SECOND + y_down.index(slot), group, groups, value, LANES - 2, 0)
    if NEXT <= slot < NEXT + 3:
        insert_column(low_parts, NEXT_SECOND + slot - NEXT, group, groups, value, 1, 1)
        insert_column(high_parts, NEXT_SECOND + slot - NEXT, group, groups, value, LANES - 2, 0)


def own_columns_kernel(held, velocity, solid, low, high):
    rows = velocity.shape[2]
    groups = rows // 8 + 2
    solid_parts = spread_solid(solid)
    flow = [flow_blocks(velocity, step, rows) for step in range(2)]
    parts = [[jnp.zeros((8, LANES), jnp.float32) for _ in range(low.shape[0])] for _ in range(2)]
    for group in range(1, groups - 1):
        for slot in range(19):
            pack_columns(parts, slot, group, groups, held[slot, pl.ds(GUARD + 8 * group, 8), :])
        for axis in range(3):
            pack_columns(parts, FLOW + axis, group, groups, flow[0][group - 1][axis])
            pack_columns(parts, NEXT + axis, group, groups, flow[1][group - 1][axis])
        pack_columns(parts, SOLID, group, groups, solid_parts[(group - 1) * 8 // (LEVELS * TILE)])
    for part in range(low.shape[0]):
        low[part] = parts[0][part]
        high[part] = parts[1][part]


def halo_columns_kernel(groups, own_low, own_high, row_first, row_second, low_out, high_out, ends):
    count = own_low.shape[0]
    even = on_even("gx")
    after, before = Chosen(even, row_first, row_second), Chosen(even, row_second, row_first)
    parts = [[own_low[part] for part in range(count)], [own_high[part] for part in range(count)]]
    for slot in range(SECOND):
        ends[0, slot, pl.ds(LEVELS, LEVELS), :] = before[slot]
        ends[1, slot, pl.ds(0, LEVELS), :] = after[slot]
        if slot == SOLID:
            low_second, high_second = SOLID, SOLID
        else:
            low_second = SECOND + x_down.index(slot) if slot in x_down else None
            high_second = SECOND + x_up.index(slot) if slot in x_up else None
        blank = jnp.zeros((LEVELS, LANES), jnp.float32)
        ends[0, slot, pl.ds(0, LEVELS), :] = blank if low_second is None else before[low_second]
        ends[1, slot, pl.ds(LEVELS, LEVELS), :] = blank if high_second is None else after[high_second]
        pack_columns(parts, slot, 0, groups, ends[0, slot])
        pack_columns(parts, slot, groups - 1, groups, ends[1, slot])
    for part in range(count):
        low_out[part] = parts[0][part]
        high_out[part] = parts[1][part]


def collide(moved, flow, fluid):
    ux, uy, uz = flow
    total = {n: moved[n] + moved[n + 1] for n in range(1, 19, 2)}
    xy, xz, yz = total[7] + total[9], total[11] + total[13], total[15] + total[17]
    axis_x, axis_y, axis_z = 2.0 * total[1], 2.0 * total[3], 2.0 * total[5]
    density = 12.0 * moved[0] + (axis_x + axis_y + axis_z) + (xy + xz + yz)
    pxx = axis_x + xy + xz
    pyy = axis_y + xy + yz
    pzz = axis_z + xz + yz
    pxy = total[7] - total[9]
    pxz = total[11] - total[13]
    pyz = total[15] - total[17]
    dx, dy, dz = momentum(moved)
    vx = pxx * ux + pxy * uy + pxz * uz
    vy = pxy * ux + pyy * uy + pyz * uz
    vz = pxz * ux + pyz * uy + pzz * uz
    speed_sq = ux * ux + uy * uy + uz * uz
    scaled = (relax_rate / 36.0) * fluid
    base = scaled * (density + 1.5 * (speed_sq * density) - 4.5 * (ux * vx + uy * vy + uz * vz))
    scaled3 = 3.0 * scaled
    bx = scaled3 * (dx + 3.0 * vx - ux * density)
    by = scaled3 * (dy + 3.0 * vy - uy * density)
    bz = scaled3 * (dz + 3.0 * vz - uz * density)
    keep = (1.0 - relax_rate) * fluid
    results = [keep * moved[0] + base]
    for number in range(1, 19, 2):
        along = None
        for speed, part in zip(lattice_speeds[number], (bx, by, bz)):
            if speed == 0:
                continue
            if along is None:
                along = part if speed == 1 else -part
            else:
                along = along + part if speed == 1 else along - part
        results.append(keep * moved[number] + (base + along))
        results.append(keep * moved[number + 1] + (base - along))
    return results


def outside(cz):
    level = lax.broadcasted_iota(jnp.int32, (8, LANES), 0) % LEVELS
    return level == (LEVELS - 1 if cz == 1 else 0)


def link_closed(solid_there, cz):
    closed = solid_there > 0.5
    return closed | outside(cz) if cz != 0 else closed


def shift_lanes(value, cy, edge_value):
    lane = lane_index(value.shape[0])
    shifted = pltpu.roll(value, -cy % LANES, 1)
    if edge_value is None:
        return shifted
    return jnp.where(lane == (LANES - 1 if cy == 1 else 0), edge_value, shifted)


def gather_cells(held, shifted, first, solid_rows):
    here = [held[n, pl.ds(first, 8), :] for n in range(19)]
    moved, closed = [here[0]], [None]
    for number in range(1, 19):
        cx, cy, cz = lattice_speeds[number]
        field = held if cy == 0 else shifted
        there = pl.ds(first + LEVELS * cx + cz, 8)
        closed.append(link_closed(solid_rows[cy % 3, there, :], cz))
        bounced = here[opposite_of(number)]
        if cx != 0:
            bounced = bounced + 2.0 * cx
        moved.append(jnp.where(closed[number], bounced, field[number, there, :]))
    return moved, closed


def momentum(moved):
    gap = {n: moved[n] - moved[n + 1] for n in range(1, 19, 2)}
    dx = 2.0 * gap[1] + (gap[7] + gap[9]) + (gap[11] + gap[13])
    dy = 2.0 * gap[3] + (gap[7] - gap[9]) + (gap[15] + gap[17])
    dz = 2.0 * gap[5] + (gap[11] - gap[13]) + (gap[15] - gap[17])
    return dx, dy, dz


def drag_term(moved, flow, fluid):
    return fluid * sum(speed * part for speed, part in zip(flow, momentum(moved)))


def along_link(number, vector):
    total = None
    for axis, speed in enumerate(lattice_speeds[number]):
        if speed == 0:
            continue
        part = vector(axis)
        if total is None:
            total = part if speed == 1 else -part
        else:
            total = total + part if speed == 1 else total - part
    return total


def later_drag(results, closed, weight_here, weight_back):
    term = None
    for number in range(1, 19):
        cx = lattice_speeds[number][0]
        here = along_link(number, lambda axis: weight_here[axis])
        part = jnp.where(closed[opposite_of(number)], -here, weight_back(number)) * results[number]
        if cx != 0:
            part = part + jnp.where(closed[number], (2.0 * cx) * here, 0.0)
        if number < 7:
            part = 2.0 * part
        term = part if term is None else term + part
    return term


def column_reader(groups):
    def column(message, ahead, slot, lane_first, group=0):
        part, place = slot_place(slot, group, groups)
        return pltpu.roll(message[part], (lane_first - place - ahead) % LANES, 1)

    return column


def fill_held(own_held, before, after, held, rows):
    own = GUARD + 8
    near, far = own - LEVELS, own + rows
    for number in range(19):
        for group in range(rows // 8):
            there = pl.ds(own + 8 * group, 8)
            held[number, there, :] = own_held[number, there, :]
        held[number, pl.ds(near, LEVELS), :] = before[number]
        held[number, pl.ds(far, LEVELS), :] = after[number]
        if number in x_down:
            held[number, pl.ds(near - LEVELS, LEVELS), :] = before[SECOND + x_down.index(number)]
        if number in x_up:
            held[number, pl.ds(far + LEVELS, LEVELS), :] = after[SECOND + x_up.index(number)]


def fill_shifted(field, shifted, groups, edge_of):
    for number in y_up + y_down:
        cy = lattice_speeds[number][1]
        for group in range(groups):
            there = pl.ds(GUARD + 8 * group, 8)
            shifted[number, there, :] = shift_lanes(field[number, there, :], cy, edge_of(number, cy, group))


def fill_solid(solid_parts, before, after, solid_rows, groups, edge_of):
    for group in range(groups):
        first = GUARD + 8 * group
        if group in (0, groups - 1):
            halo = before[SOLID] if group == 0 else after[SOLID]
            solid_rows[0, pl.ds(first, LEVELS), :] = halo
            solid_rows[0, pl.ds(first + LEVELS, LEVELS), :] = halo
        else:
            solid_rows[0, pl.ds(first, 8), :] = solid_parts[(group - 1) * 8 // (LEVELS * TILE)]
        value = solid_rows[0, pl.ds(first, 8), :]
        for cy in (1, -1):
            solid_rows[cy % 3, pl.ds(first, 8), :] = shift_lanes(value, cy, edge_of(SOLID, cy, group))


def shift_rows(value, cx, cz):
    if cx != 0:
        upper = lax.broadcasted_iota(jnp.int32, (8, LANES), 0) < LEVELS
        swapped = pltpu.roll(value, LEVELS, 0)
        if cx == 1:
            value = jnp.where(upper, swapped, pltpu.roll(swapped, LANES - 1, 1))
        else:
            value = jnp.where(upper, pltpu.roll(swapped, 1, 1), swapped)
    if cz != 0:
        value = pltpu.roll(value, (-cz) % 8, 0)
    return value


def gather_columns(neighbours):
    here = [neighbours(n, 0) for n in range(19)]
    solid = {cy: neighbours(SOLID, cy) for cy in (0, 1, -1)}
    moved, closed = [here[0]], [None]
    for number in range(1, 19):
        cx, cy, cz = lattice_speeds[number]
        source = shift_rows(here[number] if cy == 0 else neighbours(number, cy), cx, cz)
        closed.append(link_closed(shift_rows(solid[cy], cx, cz), cz))
        moved.append(jnp.where(closed[number], here[opposite_of(number)] + 2.0 * cx, source))
    return moved, closed, solid


def inner_drag_kernel(
    own_held, velocity, solid, row_first, row_second, low, partial, own_blocks,
    held, shifted, solid_rows, weights,
):
    rows = velocity.shape[2]
    groups = rows // 8 + 2
    own = GUARD + 8
    near, far = own - LEVELS, own + rows
    even = on_even("gx")
    after, before = Chosen(even, row_first, row_second), Chosen(even, row_second, row_first)
    lane = lane_index()
    solid_parts = spread_solid(solid)

    def no_edge(slot, cy, group):
        return None

    fill_held(own_held, before, after, held, rows)
    fill_shifted(held, shifted, groups, no_edge)
    fill_solid(solid_parts, before, after, solid_rows, groups, no_edge)

    flow = flow_blocks(velocity, 1, rows)
    for axis in range(3):
        for group in range(rows // 8):
            there = pl.ds(own + 8 * group, 8)
            weights[axis, there, :] = (1.0 - solid_rows[0, there, :]) * flow[group][axis]
        for row, message in ((near, before), (far, after)):
            weights[axis, pl.ds(row, LEVELS), :] = (1.0 - message[SOLID]) * message[NEXT + axis]
        for group in range(groups):
            there = pl.ds(GUARD + 8 * group, 8)
            value = weights[axis, there, :]
            weights[3 + axis, there, :] = shift_lanes(value, 1, None)
            weights[6 + axis, there, :] = shift_lanes(value, -1, None)

    total = jnp.zeros((8, LANES), jnp.float32)
    flow = flow_blocks(velocity, 0, rows)
    for group in range(rows // 8):
        first = own + 8 * group
        moved, closed = gather_cells(held, shifted, first, solid_rows)
        fluid = 1.0 - solid_parts[8 * group // (LEVELS * TILE)]
        results = collide(moved, flow[group], fluid)

        def back(number):
            cx, cy, cz = lattice_speeds[number]
            there = pl.ds(first - LEVELS * cx - cz, 8)
            return along_link(number, lambda axis: weights[3 * (-cy % 3) + axis, there, :])

        here = [weights[axis, pl.ds(first, 8), :] for axis in range(3)]
        total = total + drag_term(moved, flow[group], fluid) + later_drag(results, closed, here, back)
    inside = jnp.logical_and(lane > 0, lane < LANES - 1)
    partial[...] = jnp.where(inside, total, 0.0)

    column = column_reader(groups)
    for slot in range(SECOND):
        own_blocks[slot] = column(low, 1, slot, AFTER_LANE)
    for place, slot in enumerate(ahead_slots):
        here = column(low, 1, slot, BEFORE_LANE)
        ahead = column(low, 1, second_slot(slot, y_up), AFTER_LANE)
        own_blocks[SECOND + place] = jnp.where(lane < AFTER_LANE, here, ahead)


ahead_slots = y_up + [SOLID, NEXT, NEXT + 1, NEXT + 2]


def second_slot(slot, moving):
    if slot in moving:
        return SECOND + moving.index(slot)
    return NEXT_SECOND + slot - NEXT if NEXT <= slot < NEXT + 3 else slot


def with_halo_rows(columns, diagonal_before, diagonal_after, groups):
    lane = lane_index()
    group = lax.rem(lane, groups)
    used = lane < LANES // groups * groups
    whole = []
    for part in range(columns.shape[0]):
        above = pltpu.roll(diagonal_before[part], LANES - (groups - 2), 1)
        below = pltpu.roll(diagonal_after[part], groups - 2, 1)
        value = jnp.where(jnp.logical_and(used, group == 0), above, columns[part])
        whole.append(jnp.where(jnp.logical_and(used, group == groups - 1), below, value))
    return whole


def edge_drag_kernel(groups, columns, diagonal_before, diagonal_after, own_blocks, partial, shared):
    lane = lane_index()
    column = column_reader(groups)
    y_before = with_halo_rows(columns, diagonal_before, diagonal_after, groups)

    def neighbours(slot, cy):
        if cy == 1:
            return own_blocks[SECOND + ahead_slots.index(slot)]
        if cy == 0:
            first, second = column(y_before, 0, slot, BEFORE_LANE), own_blocks[slot]
        else:
            first = column(y_before, 0, second_slot(slot, y_down), BEFORE_LANE)
            second = column(y_before, 0, slot, AFTER_LANE)
        return jnp.where(lane < AFTER_LANE, first, second)

    moved, closed, solid_columns = gather_columns(neighbours)
    fluid = {cy: 1.0 - solid_columns[cy] for cy in (0, 1, -1)}
    flow = [neighbours(FLOW + axis, 0) for axis in range(3)]
    results = collide(moved, flow, fluid[0])
    weight = {cy: [fluid[cy] * neighbours(NEXT + axis, cy) for axis in range(3)] for cy in (0, 1, -1)}

    def back(number):
        cx, cy, cz = lattice_speeds[number]
        return shift_rows(along_link(number, lambda axis: weight[-cy][axis]), -cx, -cz)

    term = drag_term(moved, flow, fluid[0]) + later_drag(results, closed, weight[0], back)
    place = jnp.where(lane < AFTER_LANE, lane - BEFORE_LANE, lane - AFTER_LANE)
    inside = jnp.logical_and(place > 0, place < groups - 1)
    total = partial[...] + jnp.where(inside, term, 0.0)
    shared[...] = jnp.broadcast_to(jnp.sum(total), shared.shape)


def main_kernel(
    own_held, velocity, solid, row_first, row_second, y_after, columns, diagonal_before, diagonal_after,
    low, high, out, held, shifted, later, solid_rows, row_flow,
):
    rows = velocity.shape[2]
    groups = rows // 8 + 2
    own = GUARD + 8
    near, far = own - LEVELS, own + rows
    even = on_even("gx")
    after, before = Chosen(even, row_first, row_second), Chosen(even, row_second, row_first)
    lane = lane_index()
    solid_parts = spread_solid(solid)
    column = column_reader(groups)
    y_before = with_halo_rows(columns, diagonal_before, diagonal_after, groups)

    def edge_of(slot, cy, group):
        if cy == 1:
            return column(y_after, 1, slot, LANES - 1, group)
        return column(y_before, 0, slot, 0, group)

    fill_held(own_held, before, after, held, rows)
    fill_shifted(held, shifted, groups, edge_of)
    fill_solid(solid_parts, before, after, solid_rows, groups, edge_of)
    for slot, place in ((FLOW, 0), (FLOW + 1, 1), (FLOW + 2, 2), (SOLID, 3)):
        row_flow[place, pl.ds(0, LEVELS), :] = before[slot]
        row_flow[place, pl.ds(LEVELS, LEVELS), :] = after[slot]

    def both_rows(field, index, shift):
        ends = [field[index, pl.ds(place + shift, LEVELS), :] for place in (near, far)]
        return jnp.concatenate(ends, axis=0)

    here = [both_rows(held, n, 0) for n in range(19)]
    moved = [here[0]]
    for number in range(1, 19):
        cx, cy, cz = lattice_speeds[number]
        shift = LEVELS * cx + cz
        source = both_rows(held if cy == 0 else shifted, number, shift)
        closed = link_closed(both_rows(solid_rows, cy % 3, shift), cz)
        moved.append(jnp.where(closed, here[opposite_of(number)] + 2.0 * cx, source))
    row_results = collide(moved, [row_flow[axis] for axis in range(3)], 1.0 - row_flow[3])

    def neighbours(slot, cy):
        beyond = slot if cy == 0 or slot == SOLID else SECOND + (y_up if cy == 1 else y_down).index(slot)
        if cy == 1:
            first, second = column(low, 1, slot, BEFORE_LANE), column(y_after, 1, beyond, AFTER_LANE)
        elif cy == -1:
            first, second = column(y_before, 0, beyond, BEFORE_LANE), column(high, 0, slot, AFTER_LANE)
        else:
            first, second = column(y_before, 0, slot, BEFORE_LANE), column(y_after, 1, slot, AFTER_LANE)
        return jnp.where(lane < AFTER_LANE, first, second)

    moved, _, solid_columns = gather_columns(neighbours)
    column_flow = [neighbours(FLOW + axis, 0) for axis in range(3)]
    column_results = collide(moved, column_flow, 1.0 - solid_columns[0])

    flow = flow_blocks(velocity, 0, rows)
    for group in range(rows // 8):
        first = own + 8 * group
        moved, _ = gather_cells(held, shifted, first, solid_rows)
        results = collide(moved, flow[group], 1.0 - solid_parts[8 * group // (LEVELS * TILE)])
        for number in range(19):
            later[number, pl.ds(first, 8), :] = results[number]
    for number in x_down:
        later[number, pl.ds(near, LEVELS), :] = row_results[number][:LEVELS]
    for number in x_up:
        later[number, pl.ds(far, LEVELS), :] = row_results[number][LEVELS:]

    def later_edge(number, cy, group):
        shift = LANES - 1 - AFTER_LANE - group if cy == 1 else -BEFORE_LANE - group
        return pltpu.roll(column_results[number], shift % LANES, 1)

    fill_shifted(later, shifted, groups, later_edge)

    flow = flow_blocks(velocity, 1, rows)
    for group in range(rows // 8):
        first = 8 * group
        moved, _ = gather_cells(later, shifted, own + first, solid_rows)
        results = collide(moved, flow[group], 1.0 - solid_parts[first // (LEVELS * TILE)])
        for number in range(19):
            out[number, pl.ds(first, 8), :] = results[number]


def swap_pairs(first, second, axis):
    count = lax.axis_size(axis)
    inside = [(i, i ^ 1) for i in range(count)]
    across = [(i, (i + 1) % count if i % 2 == 1 else (i - 1) % count) for i in range(count)]
    second = lax.ppermute(second, axis, across)
    return lax.ppermute(first, axis, inside), second


def from_diagonal(value, side):
    nx, ny = lax.axis_size("gx"), lax.axis_size("gy")
    pairs = [
        (i * ny + j, (i + side) % nx * ny + (j + 1) % ny) for i in range(nx) for j in range(ny)
    ]
    return lax.ppermute(value, ("gx", "gy"), pairs)


def per_device(adjoint_in, velocity, solid_tiles, link_blocked):
    rows_x, levels, rows_y = adjoint_in.shape[1:]
    rows = rows_x * levels
    padded = rows + 16 + 2 * GUARD
    groups = rows // 8 + 2
    parts = -(-COLUMN_QUANTITIES // (LANES // groups))
    state = adjoint_in.reshape(19, rows, rows_y)
    flow = velocity.reshape(STEPS, 3, rows, rows_y)
    solid = solid_tiles.reshape(-1, solid_tiles.shape[2])

    def shape_of(*sizes):
        return jax.ShapeDtypeStruct(sizes, jnp.float32)

    params = pltpu.CompilerParams(vmem_limit_bytes=16 * 1024 * 1024)
    anywhere = pl.BlockSpec(memory_space=pl.ANY)
    *row_sent, held, flow, tiles = pl.pallas_call(
        row_message_kernel,
        out_shape=(
            pltpu.VMEM((QUANTITIES, levels, rows_y), jnp.float32),
            pltpu.VMEM((QUANTITIES, levels, rows_y), jnp.float32),
            pltpu.VMEM((19, padded, rows_y), jnp.float32),
            pltpu.VMEM(flow.shape, flow.dtype),
            pltpu.VMEM(solid.shape, solid.dtype),
        ),
        in_specs=[anywhere] * 3,
        out_specs=(vmem,) * 5,
        scratch_shapes=[pltpu.SemaphoreType.DMA((3,))],
        compiler_params=params,
    )(*(pltpu.with_memory_space_constraint(value, pltpu.HBM) for value in (state, flow, solid)))
    row_got = swap_pairs(*row_sent, "gx")
    own_columns = pl.pallas_call(
        own_columns_kernel,
        out_shape=(shape_of(parts, 8, rows_y),) * 2,
        in_specs=[vmem] * 3,
        out_specs=(vmem,) * 2,
        compiler_params=params,
        cost_estimate=pl.CostEstimate(flops=2_000_000, bytes_accessed=1_000_000, transcendentals=0),
    )(held, flow, tiles)
    low, high = pl.pallas_call(
        functools.partial(halo_columns_kernel, groups),
        out_shape=(shape_of(parts, 8, rows_y),) * 2,
        in_specs=[vmem] * 4,
        out_specs=(vmem,) * 2,
        scratch_shapes=[pltpu.VMEM((2, SECOND, 8, rows_y), jnp.float32)],
        compiler_params=params,
    )(*own_columns, *row_got)
    size = lax.axis_size("gy")
    y_before = lax.ppermute(own_columns[1], "gy", [(i, (i + 1) % size) for i in range(size)])
    diagonals = [from_diagonal(own_columns[1], side) for side in (1, -1)]
    y_after = lax.ppermute(low, "gy", [((i + 1) % size, i) for i in range(size)])
    count = lax.axis_size("gx") * size
    field = pltpu.VMEM((19, padded, rows_y), jnp.float32)
    solid_field = pltpu.VMEM((3, padded, rows_y), jnp.float32)
    partial, own_blocks = pl.pallas_call(
        inner_drag_kernel,
        out_shape=(
            pltpu.VMEM((8, rows_y), jnp.float32),
            pltpu.VMEM((SECOND + len(ahead_slots), 8, rows_y), jnp.float32),
        ),
        in_specs=[vmem] * 6,
        out_specs=(vmem,) * 2,
        scratch_shapes=[field, field, solid_field, pltpu.VMEM((9, padded, rows_y), jnp.float32)],
        compiler_params=params,
        cost_estimate=pl.CostEstimate(flops=1_000_000, bytes_accessed=1_000_000, transcendentals=0),
    )(held, flow, tiles, *row_got, low)
    own = pl.pallas_call(
        functools.partial(edge_drag_kernel, groups),
        out_shape=pltpu.VMEM((count, 1, rows_y), jnp.float32),
        in_specs=[vmem] * 5,
        out_specs=vmem,
        compiler_params=params,
        cost_estimate=pl.CostEstimate(flops=20_000_000_000, bytes_accessed=10_000_000, transcendentals=0),
    )(y_before, *diagonals, own_blocks, partial)
    shared = lax.all_to_all(own, ("gx", "gy"), split_axis=0, concat_axis=0, tiled=True)
    result = pl.pallas_call(
        main_kernel,
        out_shape=shape_of(19, rows, rows_y),
        in_specs=[vmem] * 11,
        out_specs=vmem,
        scratch_shapes=[field, field, field, solid_field, pltpu.VMEM((4, 8, rows_y), jnp.float32)],
        compiler_params=params,
        cost_estimate=pl.CostEstimate(flops=20_000_000_000, bytes_accessed=4_000_000, transcendentals=0),
    )(held, flow, tiles, *row_got, y_after, y_before, *diagonals, low, high)
    cell_count = rows * rows_y * count
    scale = drag_factor / math.sqrt(cell_count) * 3.0 / 36.0
    total = jnp.sum(shared[:, 0, 0])
    return (result.reshape(adjoint_in.shape), (-scale * total).reshape(1))


def solution(mesh):
    placed = (
        P(None, "gx", None, "gy"),
        P(None, None, "gx", None, "gy"),
        P("gx", None, "gy"),
        P(None, "gx", None, "gy"),
    )
    return jax.shard_map(
        per_device,
        mesh=mesh,
        in_specs=placed,
        out_specs=(P(None, "gx", None, "gy"), P()),
        check_vma=False,
    )
```

```python
import functools
import math

import jax
import jax.numpy as jnp
from jax import lax
from jax.experimental import pallas as pl
from jax.experimental.pallas import tpu as pltpu
from jax.sharding import PartitionSpec as P

TILE = 4
STEPS = 2

lattice_speeds = (
    (0, 0, 0),
    (1, 0, 0),
    (-1, 0, 0),
    (0, 1, 0),
    (0, -1, 0),
    (0, 0, 1),
    (0, 0, -1),
    (1, 1, 0),
    (-1, -1, 0),
    (1, -1, 0),
    (-1, 1, 0),
    (1, 0, 1),
    (-1, 0, -1),
    (1, 0, -1),
    (-1, 0, 1),
    (0, 1, 1),
    (0, -1, -1),
    (0, 1, -1),
    (0, -1, 1),
)
relax_rate = 1.6
drag_factor = 20.0
LEVELS = 4
LANES = 128
GUARD = 8

x_up = [n for n in range(19) if lattice_speeds[n][0] == 1]
x_down = [n for n in range(19) if lattice_speeds[n][0] == -1]
y_up = [n for n in range(19) if lattice_speeds[n][1] == 1]
y_down = [n for n in range(19) if lattice_speeds[n][1] == -1]
vmem = pl.BlockSpec(memory_space=pltpu.VMEM)

FLOW = 19
SOLID = 22
NEXT = 23
SECOND = 26
QUANTITIES = 31
NEXT_SECOND = 31
COLUMN_QUANTITIES = 34
BEFORE_LANE = 16
AFTER_LANE = 32


def opposite_of(number):
    return number + 1 if number % 2 == 1 else number - 1


def lane_index(rows=8):
    return lax.broadcasted_iota(jnp.int32, (rows, LANES), 1)


def spread_solid(solid):
    tiles = solid.shape[1]
    row = lax.broadcasted_iota(jnp.int32, (tiles, LANES), 0)
    column = lax.broadcasted_iota(jnp.int32, (tiles, LANES), 1)
    spread = (column // TILE == row).astype(jnp.float32)
    cells = jnp.dot(solid[...].astype(jnp.float32), spread, preferred_element_type=jnp.float32)
    blocks = []
    for tile_row in range(solid.shape[0] // LEVELS):
        part = cells[tile_row * LEVELS : (tile_row + 1) * LEVELS]
        blocks.append(jnp.concatenate([part, part], axis=0))
    return blocks


def flow_blocks(velocity, step, rows):
    blocks = []
    for pair in range(rows // 16):
        both = [velocity[step, axis, pl.ds(16 * pair, 16), :].astype(jnp.float32) for axis in range(3)]
        blocks.append([part[:8] for part in both])
        blocks.append([part[8:] for part in both])
    return blocks


def on_even(axis):
    return lax.rem(lax.axis_index(axis), 2) == 0


class Chosen:
    def __init__(self, choice, yes, no):
        self.choice, self.yes, self.no = choice, yes, no
        self.shape = yes.shape

    def __getitem__(self, index):
        return jnp.where(self.choice, self.yes[index], self.no[index])


def slot_place(slot, group, groups):
    per_block = LANES // groups
    return slot // per_block, (slot % per_block) * groups + group


def insert_column(parts, slot, group, groups, value, edge, ahead):
    part, place = slot_place(slot, group, groups)
    lane = lane_index()
    turned = pltpu.roll(value, (place + ahead - edge) % LANES, 1)
    parts[part] = jnp.where(lane == place + ahead, turned, parts[part])


def row_message_kernel(
    state, velocity, solid, row_first, row_second, held, flow, tiles, arrived
):
    rows = state.shape[1]
    own = pl.ds(GUARD + 8, rows)
    copies = [
        pltpu.make_async_copy(state, held.at[:, own, :], arrived.at[0]),
        pltpu.make_async_copy(velocity, flow, arrived.at[1]),
        pltpu.make_async_copy(solid, tiles, arrived.at[2]),
    ]
    for copy in copies:
        copy.start()
    for copy in copies:
        copy.wait()
    even = on_even("gx")
    low_row, high_row = GUARD + 8, GUARD + 8 + rows - LEVELS

    def put(slot, low, high):
        row_first[slot] = jnp.where(even, high, low)
        row_second[slot] = jnp.where(even, low, high)

    for number in range(19):
        put(number, held[number, pl.ds(low_row, LEVELS), :], held[number, pl.ds(high_row, LEVELS), :])
    for step, slot in ((0, FLOW), (1, NEXT)):
        for axis in range(3):
            low = flow[step, axis, pl.ds(0, 16), :].astype(jnp.float32)
            high = flow[step, axis, pl.ds(rows - 16, 16), :].astype(jnp.float32)
            put(slot + axis, low[:LEVELS], high[16 - LEVELS :])
    solid_parts = spread_solid(tiles)
    put(SOLID, solid_parts[0][:LEVELS], solid_parts[-1][:LEVELS])
    for slot in range(5):
        put(
            SECOND + slot,
            held[x_up[slot], pl.ds(low_row + LEVELS, LEVELS), :],
            held[x_down[slot], pl.ds(high_row - LEVELS, LEVELS), :],
        )


def pack_columns(parts, slot, group, groups, value):
    low_parts, high_parts = parts
    part, place = slot_place(slot, group, groups)
    lane = lane_index()
    turned = pltpu.roll(value, (place + 1) % LANES, 1)
    low_parts[part] = jnp.where(lane == place + 1, turned, low_parts[part])
    high_parts[part] = jnp.where(lane == place, turned, high_parts[part])
    if slot in y_up:
        insert_column(low_parts, SECOND + y_up.index(slot), group, groups, value, 1, 1)
    if slot in y_down:
        insert_column(high_parts, SECOND + y_down.index(slot), group, groups, value, LANES - 2, 0)
    if NEXT <= slot < NEXT + 3:
        insert_column(low_parts, NEXT_SECOND + slot - NEXT, group, groups, value, 1, 1)
        insert_column(high_parts, NEXT_SECOND + slot - NEXT, group, groups, value, LANES - 2, 0)


def own_columns_kernel(held, velocity, solid, low, high):
    rows = velocity.shape[2]
    groups = rows // 8 + 2
    solid_parts = spread_solid(solid)
    flow = [flow_blocks(velocity, step, rows) for step in range(2)]
    parts = [[jnp.zeros((8, LANES), jnp.float32) for _ in range(low.shape[0])] for _ in range(2)]
    for group in range(1, groups - 1):
        for slot in range(19):
            pack_columns(parts, slot, group, groups, held[slot, pl.ds(GUARD + 8 * group, 8), :])
        for axis in range(3):
            pack_columns(parts, FLOW + axis, group, groups, flow[0][group - 1][axis])
            pack_columns(parts, NEXT + axis, group, groups, flow[1][group - 1][axis])
        pack_columns(parts, SOLID, group, groups, solid_parts[(group - 1) * 8 // (LEVELS * TILE)])
    for part in range(low.shape[0]):
        low[part] = parts[0][part]
        high[part] = parts[1][part]


def halo_columns_kernel(groups, own_low, own_high, row_first, row_second, low_out, high_out, ends):
    count = own_low.shape[0]
    even = on_even("gx")
    after, before = Chosen(even, row_first, row_second), Chosen(even, row_second, row_first)
    parts = [[own_low[part] for part in range(count)], [own_high[part] for part in range(count)]]
    for slot in range(SECOND):
        ends[0, slot, pl.ds(LEVELS, LEVELS), :] = before[slot]
        ends[1, slot, pl.ds(0, LEVELS), :] = after[slot]
        if slot == SOLID:
            low_second, high_second = SOLID, SOLID
        else:
            low_second = SECOND + x_down.index(slot) if slot in x_down else None
            high_second = SECOND + x_up.index(slot) if slot in x_up else None
        blank = jnp.zeros((LEVELS, LANES), jnp.float32)
        ends[0, slot, pl.ds(0, LEVELS), :] = blank if low_second is None else before[low_second]
        ends[1, slot, pl.ds(LEVELS, LEVELS), :] = blank if high_second is None else after[high_second]
        pack_columns(parts, slot, 0, groups, ends[0, slot])
        pack_columns(parts, slot, groups - 1, groups, ends[1, slot])
    for part in range(count):
        low_out[part] = parts[0][part]
        high_out[part] = parts[1][part]


def collide(moved, flow, fluid):
    ux, uy, uz = flow
    total = {n: moved[n] + moved[n + 1] for n in range(1, 19, 2)}
    xy, xz, yz = total[7] + total[9], total[11] + total[13], total[15] + total[17]
    axis_x, axis_y, axis_z = 2.0 * total[1], 2.0 * total[3], 2.0 * total[5]
    density = 12.0 * moved[0] + (axis_x + axis_y + axis_z) + (xy + xz + yz)
    pxx = axis_x + xy + xz
    pyy = axis_y + xy + yz
    pzz = axis_z + xz + yz
    pxy = total[7] - total[9]
    pxz = total[11] - total[13]
    pyz = total[15] - total[17]
    dx, dy, dz = momentum(moved)
    vx = pxx * ux + pxy * uy + pxz * uz
    vy = pxy * ux + pyy * uy + pyz * uz
    vz = pxz * ux + pyz * uy + pzz * uz
    speed_sq = ux * ux + uy * uy + uz * uz
    scaled = (relax_rate / 36.0) * fluid
    base = scaled * (density + 1.5 * (speed_sq * density) - 4.5 * (ux * vx + uy * vy + uz * vz))
    scaled3 = 3.0 * scaled
    bx = scaled3 * (dx + 3.0 * vx - ux * density)
    by = scaled3 * (dy + 3.0 * vy - uy * density)
    bz = scaled3 * (dz + 3.0 * vz - uz * density)
    keep = (1.0 - relax_rate) * fluid
    results = [keep * moved[0] + base]
    for number in range(1, 19, 2):
        along = None
        for speed, part in zip(lattice_speeds[number], (bx, by, bz)):
            if speed == 0:
                continue
            if along is None:
                along = part if speed == 1 else -part
            else:
                along = along + part if speed == 1 else along - part
        results.append(keep * moved[number] + (base + along))
        results.append(keep * moved[number + 1] + (base - along))
    return results


def outside(cz):
    level = lax.broadcasted_iota(jnp.int32, (8, LANES), 0) % LEVELS
    return level == (LEVELS - 1 if cz == 1 else 0)


def link_closed(solid_there, cz):
    closed = solid_there > 0.5
    return closed | outside(cz) if cz != 0 else closed


def shift_lanes(value, cy, edge_value):
    lane = lane_index(value.shape[0])
    shifted = pltpu.roll(value, -cy % LANES, 1)
    if edge_value is None:
        return shifted
    return jnp.where(lane == (LANES - 1 if cy == 1 else 0), edge_value, shifted)


def gather_cells(held, shifted, first, solid_rows):
    here = [held[n, pl.ds(first, 8), :] for n in range(19)]
    moved, closed = [here[0]], [None]
    for number in range(1, 19):
        cx, cy, cz = lattice_speeds[number]
        field = held if cy == 0 else shifted
        there = pl.ds(first + LEVELS * cx + cz, 8)
        closed.append(link_closed(solid_rows[cy % 3, there, :], cz))
        bounced = here[opposite_of(number)]
        if cx != 0:
            bounced = bounced + 2.0 * cx
        moved.append(jnp.where(closed[number], bounced, field[number, there, :]))
    return moved, closed


def momentum(moved):
    gap = {n: moved[n] - moved[n + 1] for n in range(1, 19, 2)}
    dx = 2.0 * gap[1] + (gap[7] + gap[9]) + (gap[11] + gap[13])
    dy = 2.0 * gap[3] + (gap[7] - gap[9]) + (gap[15] + gap[17])
    dz = 2.0 * gap[5] + (gap[11] - gap[13]) + (gap[15] - gap[17])
    return dx, dy, dz


def drag_term(moved, flow, fluid):
    return fluid * sum(speed * part for speed, part in zip(flow, momentum(moved)))


def along_link(number, vector):
    total = None
    for axis, speed in enumerate(lattice_speeds[number]):
        if speed == 0:
            continue
        part = vector(axis)
        if total is None:
            total = part if speed == 1 else -part
        else:
            total = total + part if speed == 1 else total - part
    return total


def later_drag(results, closed, weight_here, weight_back):
    term = None
    for number in range(1, 19):
        cx = lattice_speeds[number][0]
        here = along_link(number, lambda axis: weight_here[axis])
        part = jnp.where(closed[opposite_of(number)], -here, weight_back(number)) * results[number]
        if cx != 0:
            part = part + jnp.where(closed[number], (2.0 * cx) * here, 0.0)
        if number < 7:
            part = 2.0 * part
        term = part if term is None else term + part
    return term


def column_reader(groups):
    def column(message, ahead, slot, lane_first, group=0):
        part, place = slot_place(slot, group, groups)
        return pltpu.roll(message[part], (lane_first - place - ahead) % LANES, 1)

    return column


def fill_held(own_held, before, after, held, rows):
    own = GUARD + 8
    near, far = own - LEVELS, own + rows
    for number in range(19):
        for group in range(rows // 8):
            there = pl.ds(own + 8 * group, 8)
            held[number, there, :] = own_held[number, there, :]
        held[number, pl.ds(near, LEVELS), :] = before[number]
        held[number, pl.ds(far, LEVELS), :] = after[number]
        if number in x_down:
            held[number, pl.ds(near - LEVELS, LEVELS), :] = before[SECOND + x_down.index(number)]
        if number in x_up:
            held[number, pl.ds(far + LEVELS, LEVELS), :] = after[SECOND + x_up.index(number)]


def fill_shifted(field, shifted, groups, edge_of):
    for number in y_up + y_down:
        cy = lattice_speeds[number][1]
        for group in range(groups):
            there = pl.ds(GUARD + 8 * group, 8)
            shifted[number, there, :] = shift_lanes(field[number, there, :], cy, edge_of(number, cy, group))


def fill_solid(solid_parts, before, after, solid_rows, groups, edge_of):
    for group in range(groups):
        first = GUARD + 8 * group
        if group in (0, groups - 1):
            halo = before[SOLID] if group == 0 else after[SOLID]
            solid_rows[0, pl.ds(first, LEVELS), :] = halo
            solid_rows[0, pl.ds(first + LEVELS, LEVELS), :] = halo
        else:
            solid_rows[0, pl.ds(first, 8), :] = solid_parts[(group - 1) * 8 // (LEVELS * TILE)]
        value = solid_rows[0, pl.ds(first, 8), :]
        for cy in (1, -1):
            solid_rows[cy % 3, pl.ds(first, 8), :] = shift_lanes(value, cy, edge_of(SOLID, cy, group))


def shift_rows(value, cx, cz):
    if cx != 0:
        upper = lax.broadcasted_iota(jnp.int32, (8, LANES), 0) < LEVELS
        swapped = pltpu.roll(value, LEVELS, 0)
        if cx == 1:
            value = jnp.where(upper, swapped, pltpu.roll(swapped, LANES - 1, 1))
        else:
            value = jnp.where(upper, pltpu.roll(swapped, 1, 1), swapped)
    if cz != 0:
        value = pltpu.roll(value, (-cz) % 8, 0)
    return value


def gather_columns(neighbours):
    here = [neighbours(n, 0) for n in range(19)]
    solid = {cy: neighbours(SOLID, cy) for cy in (0, 1, -1)}
    moved, closed = [here[0]], [None]
    for number in range(1, 19):
        cx, cy, cz = lattice_speeds[number]
        source = shift_rows(here[number] if cy == 0 else neighbours(number, cy), cx, cz)
        closed.append(link_closed(shift_rows(solid[cy], cx, cz), cz))
        moved.append(jnp.where(closed[number], here[opposite_of(number)] + 2.0 * cx, source))
    return moved, closed, solid


def inner_drag_kernel(
    own_held, velocity, solid, row_first, row_second, low, partial, own_blocks,
    held, shifted, solid_rows, weights,
):
    rows = velocity.shape[2]
    groups = rows // 8 + 2
    own = GUARD + 8
    near, far = own - LEVELS, own + rows
    even = on_even("gx")
    after, before = Chosen(even, row_first, row_second), Chosen(even, row_second, row_first)
    lane = lane_index()
    solid_parts = spread_solid(solid)

    def no_edge(slot, cy, group):
        return None

    fill_held(own_held, before, after, held, rows)
    fill_shifted(held, shifted, groups, no_edge)
    fill_solid(solid_parts, before, after, solid_rows, groups, no_edge)

    flow = flow_blocks(velocity, 1, rows)
    for axis in range(3):
        for group in range(rows // 8):
            there = pl.ds(own + 8 * group, 8)
            weights[axis, there, :] = (1.0 - solid_rows[0, there, :]) * flow[group][axis]
        for row, message in ((near, before), (far, after)):
            weights[axis, pl.ds(row, LEVELS), :] = (1.0 - message[SOLID]) * message[NEXT + axis]
        for group in range(groups):
            there = pl.ds(GUARD + 8 * group, 8)
            value = weights[axis, there, :]
            weights[3 + axis, there, :] = shift_lanes(value, 1, None)
            weights[6 + axis, there, :] = shift_lanes(value, -1, None)

    total = jnp.zeros((8, LANES), jnp.float32)
    flow = flow_blocks(velocity, 0, rows)
    for group in range(rows // 8):
        first = own + 8 * group
        moved, closed = gather_cells(held, shifted, first, solid_rows)
        fluid = 1.0 - solid_parts[8 * group // (LEVELS * TILE)]
        results = collide(moved, flow[group], fluid)

        def back(number):
            cx, cy, cz = lattice_speeds[number]
            there = pl.ds(first - LEVELS * cx - cz, 8)
            return along_link(number, lambda axis: weights[3 * (-cy % 3) + axis, there, :])

        here = [weights[axis, pl.ds(first, 8), :] for axis in range(3)]
        total = total + drag_term(moved, flow[group], fluid) + later_drag(results, closed, here, back)
    inside = jnp.logical_and(lane > 0, lane < LANES - 1)
    partial[...] = jnp.where(inside, total, 0.0)

    column = column_reader(groups)
    for slot in range(SECOND):
        own_blocks[slot] = column(low, 1, slot, AFTER_LANE)
    for place, slot in enumerate(ahead_slots):
        here = column(low, 1, slot, BEFORE_LANE)
        ahead = column(low, 1, second_slot(slot, y_up), AFTER_LANE)
        own_blocks[SECOND + place] = jnp.where(lane < AFTER_LANE, here, ahead)


ahead_slots = y_up + [SOLID, NEXT, NEXT + 1, NEXT + 2]


def second_slot(slot, moving):
    if slot in moving:
        return SECOND + moving.index(slot)
    return NEXT_SECOND + slot - NEXT if NEXT <= slot < NEXT + 3 else slot


def halo_lanes(groups):
    lane = lane_index()
    group = lax.rem(lane, groups)
    used = lane < LANES // groups * groups
    return jnp.logical_and(used, group == 0), jnp.logical_and(used, group == groups - 1)


def hand_on_kernel(groups, columns, out):
    above, _ = halo_lanes(groups)
    for part in range(columns.shape[0]):
        value = columns[part]
        last = pltpu.roll(value, LANES - (groups - 2), 1)
        out[part] = jnp.where(above, last, pltpu.roll(value, groups - 2, 1))


def with_halo_rows(columns, handed_first, handed_second, groups):
    even = on_even("gx")
    from_before = Chosen(even, handed_second, handed_first)
    from_after = Chosen(even, handed_first, handed_second)
    above, below = halo_lanes(groups)
    whole = []
    for part in range(columns.shape[0]):
        value = jnp.where(above, from_before[part], columns[part])
        whole.append(jnp.where(below, from_after[part], value))
    return whole


def edge_drag_kernel(groups, columns, handed_first, handed_second, own_blocks, partial, shared):
    lane = lane_index()
    column = column_reader(groups)
    y_before = with_halo_rows(columns, handed_first, handed_second, groups)

    def neighbours(slot, cy):
        if cy == 1:
            return own_blocks[SECOND + ahead_slots.index(slot)]
        if cy == 0:
            first, second = column(y_before, 0, slot, BEFORE_LANE), own_blocks[slot]
        else:
            first = column(y_before, 0, second_slot(slot, y_down), BEFORE_LANE)
            second = column(y_before, 0, slot, AFTER_LANE)
        return jnp.where(lane < AFTER_LANE, first, second)

    moved, closed, solid_columns = gather_columns(neighbours)
    fluid = {cy: 1.0 - solid_columns[cy] for cy in (0, 1, -1)}
    flow = [neighbours(FLOW + axis, 0) for axis in range(3)]
    results = collide(moved, flow, fluid[0])
    weight = {cy: [fluid[cy] * neighbours(NEXT + axis, cy) for axis in range(3)] for cy in (0, 1, -1)}

    def back(number):
        cx, cy, cz = lattice_speeds[number]
        return shift_rows(along_link(number, lambda axis: weight[-cy][axis]), -cx, -cz)

    term = drag_term(moved, flow, fluid[0]) + later_drag(results, closed, weight[0], back)
    place = jnp.where(lane < AFTER_LANE, lane - BEFORE_LANE, lane - AFTER_LANE)
    inside = jnp.logical_and(place > 0, place < groups - 1)
    total = partial[...] + jnp.where(inside, term, 0.0)
    shared[...] = jnp.broadcast_to(jnp.sum(total), shared.shape)


def main_kernel(
    own_held, velocity, solid, row_first, row_second, y_after, columns, handed_first, handed_second,
    low, high, out, held, shifted, later, solid_rows, row_flow,
):
    rows = velocity.shape[2]
    groups = rows // 8 + 2
    own = GUARD + 8
    near, far = own - LEVELS, own + rows
    even = on_even("gx")
    after, before = Chosen(even, row_first, row_second), Chosen(even, row_second, row_first)
    lane = lane_index()
    solid_parts = spread_solid(solid)
    column = column_reader(groups)
    y_before = with_halo_rows(columns, handed_first, handed_second, groups)

    def edge_of(slot, cy, group):
        if cy == 1:
            return column(y_after, 1, slot, LANES - 1, group)
        return column(y_before, 0, slot, 0, group)

    fill_held(own_held, before, after, held, rows)
    fill_shifted(held, shifted, groups, edge_of)
    fill_solid(solid_parts, before, after, solid_rows, groups, edge_of)
    for slot, place in ((FLOW, 0), (FLOW + 1, 1), (FLOW + 2, 2), (SOLID, 3)):
        row_flow[place, pl.ds(0, LEVELS), :] = before[slot]
        row_flow[place, pl.ds(LEVELS, LEVELS), :] = after[slot]

    def both_rows(field, index, shift):
        ends = [field[index, pl.ds(place + shift, LEVELS), :] for place in (near, far)]
        return jnp.concatenate(ends, axis=0)

    here = [both_rows(held, n, 0) for n in range(19)]
    moved = [here[0]]
    for number in range(1, 19):
        cx, cy, cz = lattice_speeds[number]
        shift = LEVELS * cx + cz
        source = both_rows(held if cy == 0 else shifted, number, shift)
        closed = link_closed(both_rows(solid_rows, cy % 3, shift), cz)
        moved.append(jnp.where(closed, here[opposite_of(number)] + 2.0 * cx, source))
    row_results = collide(moved, [row_flow[axis] for axis in range(3)], 1.0 - row_flow[3])

    def neighbours(slot, cy):
        beyond = slot if cy == 0 or slot == SOLID else SECOND + (y_up if cy == 1 else y_down).index(slot)
        if cy == 1:
            first, second = column(low, 1, slot, BEFORE_LANE), column(y_after, 1, beyond, AFTER_LANE)
        elif cy == -1:
            first, second = column(y_before, 0, beyond, BEFORE_LANE), column(high, 0, slot, AFTER_LANE)
        else:
            first, second = column(y_before, 0, slot, BEFORE_LANE), column(y_after, 1, slot, AFTER_LANE)
        return jnp.where(lane < AFTER_LANE, first, second)

    moved, _, solid_columns = gather_columns(neighbours)
    column_flow = [neighbours(FLOW + axis, 0) for axis in range(3)]
    column_results = collide(moved, column_flow, 1.0 - solid_columns[0])

    flow = flow_blocks(velocity, 0, rows)
    for group in range(rows // 8):
        first = own + 8 * group
        moved, _ = gather_cells(held, shifted, first, solid_rows)
        results = collide(moved, flow[group], 1.0 - solid_parts[8 * group // (LEVELS * TILE)])
        for number in range(19):
            later[number, pl.ds(first, 8), :] = results[number]
    for number in x_down:
        later[number, pl.ds(near, LEVELS), :] = row_results[number][:LEVELS]
    for number in x_up:
        later[number, pl.ds(far, LEVELS), :] = row_results[number][LEVELS:]

    def later_edge(number, cy, group):
        shift = LANES - 1 - AFTER_LANE - group if cy == 1 else -BEFORE_LANE - group
        return pltpu.roll(column_results[number], shift % LANES, 1)

    fill_shifted(later, shifted, groups, later_edge)

    flow = flow_blocks(velocity, 1, rows)
    for group in range(rows // 8):
        first = 8 * group
        moved, _ = gather_cells(later, shifted, own + first, solid_rows)
        results = collide(moved, flow[group], 1.0 - solid_parts[first // (LEVELS * TILE)])
        for number in range(19):
            out[number, pl.ds(first, 8), :] = results[number]


def swap_pairs(first, second, axis):
    count = lax.axis_size(axis)
    inside = [(i, i ^ 1) for i in range(count)]
    across = [(i, (i + 1) % count if i % 2 == 1 else (i - 1) % count) for i in range(count)]
    second = lax.ppermute(second, axis, across)
    return lax.ppermute(first, axis, inside), second


def per_device(adjoint_in, velocity, solid_tiles, link_blocked):
    rows_x, levels, rows_y = adjoint_in.shape[1:]
    rows = rows_x * levels
    padded = rows + 16 + 2 * GUARD
    groups = rows // 8 + 2
    parts = -(-COLUMN_QUANTITIES // (LANES // groups))
    state = adjoint_in.reshape(19, rows, rows_y)
    flow = velocity.reshape(STEPS, 3, rows, rows_y)
    solid = solid_tiles.reshape(-1, solid_tiles.shape[2])

    def shape_of(*sizes):
        return jax.ShapeDtypeStruct(sizes, jnp.float32)

    params = pltpu.CompilerParams(vmem_limit_bytes=16 * 1024 * 1024)
    anywhere = pl.BlockSpec(memory_space=pl.ANY)
    *row_sent, held, flow, tiles = pl.pallas_call(
        row_message_kernel,
        out_shape=(
            pltpu.VMEM((QUANTITIES, levels, rows_y), jnp.float32),
            pltpu.VMEM((QUANTITIES, levels, rows_y), jnp.float32),
            pltpu.VMEM((19, padded, rows_y), jnp.float32),
            pltpu.VMEM(flow.shape, flow.dtype),
            pltpu.VMEM(solid.shape, solid.dtype),
        ),
        in_specs=[anywhere] * 3,
        out_specs=(vmem,) * 5,
        scratch_shapes=[pltpu.SemaphoreType.DMA((3,))],
        compiler_params=params,
    )(*(pltpu.with_memory_space_constraint(value, pltpu.HBM) for value in (state, flow, solid)))
    row_got = swap_pairs(*row_sent, "gx")
    own_columns = pl.pallas_call(
        own_columns_kernel,
        out_shape=(shape_of(parts, 8, rows_y),) * 2,
        in_specs=[vmem] * 3,
        out_specs=(vmem,) * 2,
        compiler_params=params,
        cost_estimate=pl.CostEstimate(flops=2_000_000, bytes_accessed=1_000_000, transcendentals=0),
    )(held, flow, tiles)
    low, high = pl.pallas_call(
        functools.partial(halo_columns_kernel, groups),
        out_shape=(shape_of(parts, 8, rows_y),) * 2,
        in_specs=[vmem] * 4,
        out_specs=(vmem,) * 2,
        scratch_shapes=[pltpu.VMEM((2, SECOND, 8, rows_y), jnp.float32)],
        compiler_params=params,
    )(*own_columns, *row_got)
    size = lax.axis_size("gy")
    y_before = lax.ppermute(own_columns[1], "gy", [(i, (i + 1) % size) for i in range(size)])
    handed = pl.pallas_call(
        functools.partial(hand_on_kernel, groups),
        out_shape=shape_of(parts, 8, rows_y),
        in_specs=[vmem],
        out_specs=vmem,
        compiler_params=params,
        cost_estimate=pl.CostEstimate(flops=10_000_000_000, bytes_accessed=100_000, transcendentals=0),
    )(y_before)
    handed = swap_pairs(handed, handed, "gx")
    y_after = lax.ppermute(low, "gy", [((i + 1) % size, i) for i in range(size)])
    count = lax.axis_size("gx") * size
    field = pltpu.VMEM((19, padded, rows_y), jnp.float32)
    solid_field = pltpu.VMEM((3, padded, rows_y), jnp.float32)
    partial, own_blocks = pl.pallas_call(
        inner_drag_kernel,
        out_shape=(
            pltpu.VMEM((8, rows_y), jnp.float32),
            pltpu.VMEM((SECOND + len(ahead_slots), 8, rows_y), jnp.float32),
        ),
        in_specs=[vmem] * 6,
        out_specs=(vmem,) * 2,
        scratch_shapes=[field, field, solid_field, pltpu.VMEM((9, padded, rows_y), jnp.float32)],
        compiler_params=params,
        cost_estimate=pl.CostEstimate(flops=1_000_000, bytes_accessed=1_000_000, transcendentals=0),
    )(held, flow, tiles, *row_got, low)
    own = pl.pallas_call(
        functools.partial(edge_drag_kernel, groups),
        out_shape=pltpu.VMEM((count, 1, rows_y), jnp.float32),
        in_specs=[vmem] * 5,
        out_specs=vmem,
        compiler_params=params,
        cost_estimate=pl.CostEstimate(flops=20_000_000_000, bytes_accessed=10_000_000, transcendentals=0),
    )(y_before, *handed, own_blocks, partial)
    shared = lax.all_to_all(own, ("gx", "gy"), split_axis=0, concat_axis=0, tiled=True)
    result = pl.pallas_call(
        main_kernel,
        out_shape=shape_of(19, rows, rows_y),
        in_specs=[vmem] * 11,
        out_specs=vmem,
        scratch_shapes=[field, field, field, solid_field, pltpu.VMEM((4, 8, rows_y), jnp.float32)],
        compiler_params=params,
        cost_estimate=pl.CostEstimate(flops=20_000_000_000, bytes_accessed=4_000_000, transcendentals=0),
    )(held, flow, tiles, *row_got, y_after, y_before, *handed, low, high)
    cell_count = rows * rows_y * count
    scale = drag_factor / math.sqrt(cell_count) * 3.0 / 36.0
    total = jnp.sum(shared[:, 0, 0])
    return (result.reshape(adjoint_in.shape), (-scale * total).reshape(1))


def solution(mesh):
    placed = (
        P(None, "gx", None, "gy"),
        P(None, None, "gx", None, "gy"),
        P("gx", None, "gy"),
        P(None, "gx", None, "gy"),
    )
    return jax.shard_map(
        per_device,
        mesh=mesh,
        in_specs=placed,
        out_specs=(P(None, "gx", None, "gy"), P()),
        check_vma=False,
    )
```

```python
import functools
import math

import jax
import jax.numpy as jnp
from jax import lax
from jax.experimental import pallas as pl
from jax.experimental.pallas import tpu as pltpu
from jax.sharding import PartitionSpec as P

TILE = 4
STEPS = 2

lattice_speeds = (
    (0, 0, 0),
    (1, 0, 0),
    (-1, 0, 0),
    (0, 1, 0),
    (0, -1, 0),
    (0, 0, 1),
    (0, 0, -1),
    (1, 1, 0),
    (-1, -1, 0),
    (1, -1, 0),
    (-1, 1, 0),
    (1, 0, 1),
    (-1, 0, -1),
    (1, 0, -1),
    (-1, 0, 1),
    (0, 1, 1),
    (0, -1, -1),
    (0, 1, -1),
    (0, -1, 1),
)
relax_rate = 1.6
drag_factor = 20.0
LEVELS = 4
LANES = 128
GUARD = 8

x_up = [n for n in range(19) if lattice_speeds[n][0] == 1]
x_down = [n for n in range(19) if lattice_speeds[n][0] == -1]
y_up = [n for n in range(19) if lattice_speeds[n][1] == 1]
y_down = [n for n in range(19) if lattice_speeds[n][1] == -1]
vmem = pl.BlockSpec(memory_space=pltpu.VMEM)

FLOW = 19
SOLID = 22
NEXT = 23
SECOND = 26
QUANTITIES = 31
NEXT_SECOND = 31
COLUMN_QUANTITIES = 34
BEFORE_LANE = 16
AFTER_LANE = 32


def opposite_of(number):
    return number + 1 if number % 2 == 1 else number - 1


def lane_index(rows=8):
    return lax.broadcasted_iota(jnp.int32, (rows, LANES), 1)


def spread_solid(solid):
    tiles = solid.shape[1]
    row = lax.broadcasted_iota(jnp.int32, (tiles, LANES), 0)
    column = lax.broadcasted_iota(jnp.int32, (tiles, LANES), 1)
    spread = (column // TILE == row).astype(jnp.float32)
    cells = jnp.dot(solid[...].astype(jnp.float32), spread, preferred_element_type=jnp.float32)
    blocks = []
    for tile_row in range(solid.shape[0] // LEVELS):
        part = cells[tile_row * LEVELS : (tile_row + 1) * LEVELS]
        blocks.append(jnp.concatenate([part, part], axis=0))
    return blocks


def flow_blocks(velocity, step, rows):
    blocks = []
    for pair in range(rows // 16):
        both = [velocity[step, axis, pl.ds(16 * pair, 16), :].astype(jnp.float32) for axis in range(3)]
        blocks.append([part[:8] for part in both])
        blocks.append([part[8:] for part in both])
    return blocks


def on_even(axis):
    return lax.rem(lax.axis_index(axis), 2) == 0


class Chosen:
    def __init__(self, choice, yes, no):
        self.choice, self.yes, self.no = choice, yes, no
        self.shape = yes.shape

    def __getitem__(self, index):
        return jnp.where(self.choice, self.yes[index], self.no[index])


def slot_place(slot, group, groups):
    per_block = LANES // groups
    return slot // per_block, (slot % per_block) * groups + group


def insert_column(parts, slot, group, groups, value, edge, ahead):
    part, place = slot_place(slot, group, groups)
    lane = lane_index()
    turned = pltpu.roll(value, (place + ahead - edge) % LANES, 1)
    parts[part] = jnp.where(lane == place + ahead, turned, parts[part])


def row_message_kernel(
    state, velocity, solid, row_first, row_second, held, flow, tiles, arrived
):
    rows = state.shape[1]
    own = pl.ds(GUARD + 8, rows)
    copies = [
        pltpu.make_async_copy(state, held.at[:, own, :], arrived.at[0]),
        pltpu.make_async_copy(velocity, flow, arrived.at[1]),
        pltpu.make_async_copy(solid, tiles, arrived.at[2]),
    ]
    for copy in copies:
        copy.start()
    for copy in copies:
        copy.wait()
    even = on_even("gx")
    low_row, high_row = GUARD + 8, GUARD + 8 + rows - LEVELS

    def put(slot, low, high):
        row_first[slot] = jnp.where(even, high, low)
        row_second[slot] = jnp.where(even, low, high)

    for number in range(19):
        put(number, held[number, pl.ds(low_row, LEVELS), :], held[number, pl.ds(high_row, LEVELS), :])
    for step, slot in ((0, FLOW), (1, NEXT)):
        for axis in range(3):
            low = flow[step, axis, pl.ds(0, 16), :].astype(jnp.float32)
            high = flow[step, axis, pl.ds(rows - 16, 16), :].astype(jnp.float32)
            put(slot + axis, low[:LEVELS], high[16 - LEVELS :])
    solid_parts = spread_solid(tiles)
    put(SOLID, solid_parts[0][:LEVELS], solid_parts[-1][:LEVELS])
    for slot in range(5):
        put(
            SECOND + slot,
            held[x_up[slot], pl.ds(low_row + LEVELS, LEVELS), :],
            held[x_down[slot], pl.ds(high_row - LEVELS, LEVELS), :],
        )


def pack_columns(parts, slot, group, groups, value):
    low_parts, high_parts = parts
    part, place = slot_place(slot, group, groups)
    lane = lane_index()
    turned = pltpu.roll(value, (place + 1) % LANES, 1)
    low_parts[part] = jnp.where(lane == place + 1, turned, low_parts[part])
    high_parts[part] = jnp.where(lane == place, turned, high_parts[part])
    if slot in y_up:
        insert_column(low_parts, SECOND + y_up.index(slot), group, groups, value, 1, 1)
    if slot in y_down:
        insert_column(high_parts, SECOND + y_down.index(slot), group, groups, value, LANES - 2, 0)
    if NEXT <= slot < NEXT + 3:
        insert_column(low_parts, NEXT_SECOND + slot - NEXT, group, groups, value, 1, 1)
        insert_column(high_parts, NEXT_SECOND + slot - NEXT, group, groups, value, LANES - 2, 0)


def own_columns_kernel(held, velocity, solid, low, high):
    rows = velocity.shape[2]
    groups = rows // 8 + 2
    solid_parts = spread_solid(solid)
    flow = [flow_blocks(velocity, step, rows) for step in range(2)]
    parts = [[jnp.zeros((8, LANES), jnp.float32) for _ in range(low.shape[0])] for _ in range(2)]
    for group in range(1, groups - 1):
        for slot in range(19):
            pack_columns(parts, slot, group, groups, held[slot, pl.ds(GUARD + 8 * group, 8), :])
        for axis in range(3):
            pack_columns(parts, FLOW + axis, group, groups, flow[0][group - 1][axis])
            pack_columns(parts, NEXT + axis, group, groups, flow[1][group - 1][axis])
        pack_columns(parts, SOLID, group, groups, solid_parts[(group - 1) * 8 // (LEVELS * TILE)])
    for part in range(low.shape[0]):
        low[part] = parts[0][part]
        high[part] = parts[1][part]


def halo_columns_kernel(groups, own_low, own_high, row_first, row_second, low_out, high_out, ends):
    count = own_low.shape[0]
    even = on_even("gx")
    after, before = Chosen(even, row_first, row_second), Chosen(even, row_second, row_first)
    parts = [[own_low[part] for part in range(count)], [own_high[part] for part in range(count)]]
    for slot in range(SECOND):
        ends[0, slot, pl.ds(LEVELS, LEVELS), :] = before[slot]
        ends[1, slot, pl.ds(0, LEVELS), :] = after[slot]
        if slot == SOLID:
            low_second, high_second = SOLID, SOLID
        else:
            low_second = SECOND + x_down.index(slot) if slot in x_down else None
            high_second = SECOND + x_up.index(slot) if slot in x_up else None
        blank = jnp.zeros((LEVELS, LANES), jnp.float32)
        ends[0, slot, pl.ds(0, LEVELS), :] = blank if low_second is None else before[low_second]
        ends[1, slot, pl.ds(LEVELS, LEVELS), :] = blank if high_second is None else after[high_second]
        pack_columns(parts, slot, 0, groups, ends[0, slot])
        pack_columns(parts, slot, groups - 1, groups, ends[1, slot])
    for part in range(count):
        low_out[part] = parts[0][part]
        high_out[part] = parts[1][part]


def collide(moved, flow, fluid):
    ux, uy, uz = flow
    total = {n: moved[n] + moved[n + 1] for n in range(1, 19, 2)}
    xy, xz, yz = total[7] + total[9], total[11] + total[13], total[15] + total[17]
    axis_x, axis_y, axis_z = 2.0 * total[1], 2.0 * total[3], 2.0 * total[5]
    density = 12.0 * moved[0] + (axis_x + axis_y + axis_z) + (xy + xz + yz)
    pxx = axis_x + xy + xz
    pyy = axis_y + xy + yz
    pzz = axis_z + xz + yz
    pxy = total[7] - total[9]
    pxz = total[11] - total[13]
    pyz = total[15] - total[17]
    dx, dy, dz = momentum(moved)
    vx = pxx * ux + pxy * uy + pxz * uz
    vy = pxy * ux + pyy * uy + pyz * uz
    vz = pxz * ux + pyz * uy + pzz * uz
    speed_sq = ux * ux + uy * uy + uz * uz
    scaled = (relax_rate / 36.0) * fluid
    base = scaled * (density + 1.5 * (speed_sq * density) - 4.5 * (ux * vx + uy * vy + uz * vz))
    scaled3 = 3.0 * scaled
    bx = scaled3 * (dx + 3.0 * vx - ux * density)
    by = scaled3 * (dy + 3.0 * vy - uy * density)
    bz = scaled3 * (dz + 3.0 * vz - uz * density)
    keep = (1.0 - relax_rate) * fluid
    results = [keep * moved[0] + base]
    for number in range(1, 19, 2):
        along = None
        for speed, part in zip(lattice_speeds[number], (bx, by, bz)):
            if speed == 0:
                continue
            if along is None:
                along = part if speed == 1 else -part
            else:
                along = along + part if speed == 1 else along - part
        results.append(keep * moved[number] + (base + along))
        results.append(keep * moved[number + 1] + (base - along))
    return results


def outside(cz):
    level = lax.broadcasted_iota(jnp.int32, (8, LANES), 0) % LEVELS
    return level == (LEVELS - 1 if cz == 1 else 0)


def link_closed(solid_there, cz):
    closed = solid_there > 0.5
    return closed | outside(cz) if cz != 0 else closed


def shift_lanes(value, cy, edge_value):
    lane = lane_index(value.shape[0])
    shifted = pltpu.roll(value, -cy % LANES, 1)
    if edge_value is None:
        return shifted
    return jnp.where(lane == (LANES - 1 if cy == 1 else 0), edge_value, shifted)


def gather_cells(held, shifted, first, solid_rows):
    here = [held[n, pl.ds(first, 8), :] for n in range(19)]
    moved, closed = [here[0]], [None]
    for number in range(1, 19):
        cx, cy, cz = lattice_speeds[number]
        field = held if cy == 0 else shifted
        there = pl.ds(first + LEVELS * cx + cz, 8)
        closed.append(link_closed(solid_rows[cy % 3, there, :], cz))
        bounced = here[opposite_of(number)]
        if cx != 0:
            bounced = bounced + 2.0 * cx
        moved.append(jnp.where(closed[number], bounced, field[number, there, :]))
    return moved, closed


def momentum(moved):
    gap = {n: moved[n] - moved[n + 1] for n in range(1, 19, 2)}
    dx = 2.0 * gap[1] + (gap[7] + gap[9]) + (gap[11] + gap[13])
    dy = 2.0 * gap[3] + (gap[7] - gap[9]) + (gap[15] + gap[17])
    dz = 2.0 * gap[5] + (gap[11] - gap[13]) + (gap[15] - gap[17])
    return dx, dy, dz


def drag_term(moved, flow, fluid):
    return fluid * sum(speed * part for speed, part in zip(flow, momentum(moved)))


def along_link(number, vector):
    total = None
    for axis, speed in enumerate(lattice_speeds[number]):
        if speed == 0:
            continue
        part = vector(axis)
        if total is None:
            total = part if speed == 1 else -part
        else:
            total = total + part if speed == 1 else total - part
    return total


def later_drag(results, closed, weight_here, weight_back):
    term = None
    for number in range(1, 19):
        cx = lattice_speeds[number][0]
        here = along_link(number, lambda axis: weight_here[axis])
        part = jnp.where(closed[opposite_of(number)], -here, weight_back(number)) * results[number]
        if cx != 0:
            part = part + jnp.where(closed[number], (2.0 * cx) * here, 0.0)
        if number < 7:
            part = 2.0 * part
        term = part if term is None else term + part
    return term


def column_reader(groups):
    def column(message, ahead, slot, lane_first, group=0):
        part, place = slot_place(slot, group, groups)
        return pltpu.roll(message[part], (lane_first - place - ahead) % LANES, 1)

    return column


def fill_held(own_held, before, after, held, rows):
    own = GUARD + 8
    near, far = own - LEVELS, own + rows
    for number in range(19):
        for group in range(rows // 8):
            there = pl.ds(own + 8 * group, 8)
            held[number, there, :] = own_held[number, there, :]
        held[number, pl.ds(near, LEVELS), :] = before[number]
        held[number, pl.ds(far, LEVELS), :] = after[number]
        if number in x_down:
            held[number, pl.ds(near - LEVELS, LEVELS), :] = before[SECOND + x_down.index(number)]
        if number in x_up:
            held[number, pl.ds(far + LEVELS, LEVELS), :] = after[SECOND + x_up.index(number)]


def fill_shifted(field, shifted, groups, edge_of):
    for number in y_up + y_down:
        cy = lattice_speeds[number][1]
        for group in range(groups):
            there = pl.ds(GUARD + 8 * group, 8)
            shifted[number, there, :] = shift_lanes(field[number, there, :], cy, edge_of(number, cy, group))


def fill_solid(solid_parts, before, after, solid_rows, groups, edge_of):
    for group in range(groups):
        first = GUARD + 8 * group
        if group in (0, groups - 1):
            halo = before[SOLID] if group == 0 else after[SOLID]
            solid_rows[0, pl.ds(first, LEVELS), :] = halo
            solid_rows[0, pl.ds(first + LEVELS, LEVELS), :] = halo
        else:
            solid_rows[0, pl.ds(first, 8), :] = solid_parts[(group - 1) * 8 // (LEVELS * TILE)]
        value = solid_rows[0, pl.ds(first, 8), :]
        for cy in (1, -1):
            solid_rows[cy % 3, pl.ds(first, 8), :] = shift_lanes(value, cy, edge_of(SOLID, cy, group))


def shift_rows(value, cx, cz):
    if cx != 0:
        upper = lax.broadcasted_iota(jnp.int32, (8, LANES), 0) < LEVELS
        swapped = pltpu.roll(value, LEVELS, 0)
        if cx == 1:
            value = jnp.where(upper, swapped, pltpu.roll(swapped, LANES - 1, 1))
        else:
            value = jnp.where(upper, pltpu.roll(swapped, 1, 1), swapped)
    if cz != 0:
        value = pltpu.roll(value, (-cz) % 8, 0)
    return value


def gather_columns(neighbours):
    here = [neighbours(n, 0) for n in range(19)]
    solid = {cy: neighbours(SOLID, cy) for cy in (0, 1, -1)}
    moved, closed = [here[0]], [None]
    for number in range(1, 19):
        cx, cy, cz = lattice_speeds[number]
        source = shift_rows(here[number] if cy == 0 else neighbours(number, cy), cx, cz)
        closed.append(link_closed(shift_rows(solid[cy], cx, cz), cz))
        moved.append(jnp.where(closed[number], here[opposite_of(number)] + 2.0 * cx, source))
    return moved, closed, solid


def inner_drag_kernel(
    own_held, velocity, solid, row_first, row_second, low, partial, own_blocks,
    held, shifted, solid_rows, weights,
):
    rows = velocity.shape[2]
    groups = rows // 8 + 2
    own = GUARD + 8
    near, far = own - LEVELS, own + rows
    even = on_even("gx")
    after, before = Chosen(even, row_first, row_second), Chosen(even, row_second, row_first)
    lane = lane_index()
    solid_parts = spread_solid(solid)

    def no_edge(slot, cy, group):
        return None

    fill_held(own_held, before, after, held, rows)
    fill_shifted(held, shifted, groups, no_edge)
    fill_solid(solid_parts, before, after, solid_rows, groups, no_edge)

    flow = flow_blocks(velocity, 1, rows)
    for axis in range(3):
        for group in range(rows // 8):
            there = pl.ds(own + 8 * group, 8)
            weights[axis, there, :] = (1.0 - solid_rows[0, there, :]) * flow[group][axis]
        for row, message in ((near, before), (far, after)):
            weights[axis, pl.ds(row, LEVELS), :] = (1.0 - message[SOLID]) * message[NEXT + axis]
        for group in range(groups):
            there = pl.ds(GUARD + 8 * group, 8)
            value = weights[axis, there, :]
            weights[3 + axis, there, :] = shift_lanes(value, 1, None)
            weights[6 + axis, there, :] = shift_lanes(value, -1, None)

    total = jnp.zeros((8, LANES), jnp.float32)
    flow = flow_blocks(velocity, 0, rows)
    for group in range(rows // 8):
        first = own + 8 * group
        moved, closed = gather_cells(held, shifted, first, solid_rows)
        fluid = 1.0 - solid_parts[8 * group // (LEVELS * TILE)]
        results = collide(moved, flow[group], fluid)

        def back(number):
            cx, cy, cz = lattice_speeds[number]
            there = pl.ds(first - LEVELS * cx - cz, 8)
            return along_link(number, lambda axis: weights[3 * (-cy % 3) + axis, there, :])

        here = [weights[axis, pl.ds(first, 8), :] for axis in range(3)]
        total = total + drag_term(moved, flow[group], fluid) + later_drag(results, closed, here, back)
    inside = jnp.logical_and(lane > 0, lane < LANES - 1)
    partial[...] = jnp.where(inside, total, 0.0)

    column = column_reader(groups)
    for slot in range(SECOND):
        own_blocks[slot] = column(low, 1, slot, AFTER_LANE)
    for place, slot in enumerate(ahead_slots):
        here = column(low, 1, slot, BEFORE_LANE)
        ahead = column(low, 1, second_slot(slot, y_up), AFTER_LANE)
        own_blocks[SECOND + place] = jnp.where(lane < AFTER_LANE, here, ahead)


ahead_slots = y_up + [SOLID, NEXT, NEXT + 1, NEXT + 2]


def second_slot(slot, moving):
    if slot in moving:
        return SECOND + moving.index(slot)
    return NEXT_SECOND + slot - NEXT if NEXT <= slot < NEXT + 3 else slot


def halo_lanes(groups, ahead):
    lane = lane_index()
    group = lax.rem(lane + groups - ahead, groups)
    used = jnp.logical_and(lane >= ahead, lane < LANES // groups * groups + ahead)
    return jnp.logical_and(used, group == 0), jnp.logical_and(used, group == groups - 1)


def hand_on_kernel(groups, ahead, columns, *rest):
    out = rest[-1]
    above, _ = halo_lanes(groups, ahead)
    for part in range(columns.shape[0]):
        value = columns[part]
        last = pltpu.roll(value, LANES - (groups - 2), 1)
        out[part] = jnp.where(above, last, pltpu.roll(value, groups - 2, 1))


def with_halo_rows(columns, handed_first, handed_second, groups, ahead):
    even = on_even("gx")
    from_before = Chosen(even, handed_second, handed_first)
    from_after = Chosen(even, handed_first, handed_second)
    above, below = halo_lanes(groups, ahead)
    whole = []
    for part in range(columns.shape[0]):
        value = jnp.where(above, from_before[part], columns[part])
        whole.append(jnp.where(below, from_after[part], value))
    return whole


def edge_drag_kernel(groups, columns, handed_first, handed_second, own_blocks, partial, shared):
    lane = lane_index()
    column = column_reader(groups)
    y_before = with_halo_rows(columns, handed_first, handed_second, groups, 0)

    def neighbours(slot, cy):
        if cy == 1:
            return own_blocks[SECOND + ahead_slots.index(slot)]
        if cy == 0:
            first, second = column(y_before, 0, slot, BEFORE_LANE), own_blocks[slot]
        else:
            first = column(y_before, 0, second_slot(slot, y_down), BEFORE_LANE)
            second = column(y_before, 0, slot, AFTER_LANE)
        return jnp.where(lane < AFTER_LANE, first, second)

    moved, closed, solid_columns = gather_columns(neighbours)
    fluid = {cy: 1.0 - solid_columns[cy] for cy in (0, 1, -1)}
    flow = [neighbours(FLOW + axis, 0) for axis in range(3)]
    results = collide(moved, flow, fluid[0])
    weight = {cy: [fluid[cy] * neighbours(NEXT + axis, cy) for axis in range(3)] for cy in (0, 1, -1)}

    def back(number):
        cx, cy, cz = lattice_speeds[number]
        return shift_rows(along_link(number, lambda axis: weight[-cy][axis]), -cx, -cz)

    term = drag_term(moved, flow, fluid[0]) + later_drag(results, closed, weight[0], back)
    place = jnp.where(lane < AFTER_LANE, lane - BEFORE_LANE, lane - AFTER_LANE)
    inside = jnp.logical_and(place > 0, place < groups - 1)
    total = partial[...] + jnp.where(inside, term, 0.0)
    shared[...] = jnp.broadcast_to(jnp.sum(total), shared.shape)


def main_kernel(
    own_held, velocity, solid, row_first, row_second, columns, handed_first, handed_second,
    columns_after, after_first, after_second, low, high, out, held, shifted, later, solid_rows, row_flow,
):
    rows = velocity.shape[2]
    groups = rows // 8 + 2
    own = GUARD + 8
    near, far = own - LEVELS, own + rows
    even = on_even("gx")
    after, before = Chosen(even, row_first, row_second), Chosen(even, row_second, row_first)
    lane = lane_index()
    solid_parts = spread_solid(solid)
    column = column_reader(groups)
    y_before = with_halo_rows(columns, handed_first, handed_second, groups, 0)
    y_after = with_halo_rows(columns_after, after_first, after_second, groups, 1)

    def edge_of(slot, cy, group):
        if cy == 1:
            return column(y_after, 1, slot, LANES - 1, group)
        return column(y_before, 0, slot, 0, group)

    fill_held(own_held, before, after, held, rows)
    fill_shifted(held, shifted, groups, edge_of)
    fill_solid(solid_parts, before, after, solid_rows, groups, edge_of)
    for slot, place in ((FLOW, 0), (FLOW + 1, 1), (FLOW + 2, 2), (SOLID, 3)):
        row_flow[place, pl.ds(0, LEVELS), :] = before[slot]
        row_flow[place, pl.ds(LEVELS, LEVELS), :] = after[slot]

    def both_rows(field, index, shift):
        ends = [field[index, pl.ds(place + shift, LEVELS), :] for place in (near, far)]
        return jnp.concatenate(ends, axis=0)

    here = [both_rows(held, n, 0) for n in range(19)]
    moved = [here[0]]
    for number in range(1, 19):
        cx, cy, cz = lattice_speeds[number]
        shift = LEVELS * cx + cz
        source = both_rows(held if cy == 0 else shifted, number, shift)
        closed = link_closed(both_rows(solid_rows, cy % 3, shift), cz)
        moved.append(jnp.where(closed, here[opposite_of(number)] + 2.0 * cx, source))
    row_results = collide(moved, [row_flow[axis] for axis in range(3)], 1.0 - row_flow[3])

    def neighbours(slot, cy):
        beyond = slot if cy == 0 or slot == SOLID else SECOND + (y_up if cy == 1 else y_down).index(slot)
        if cy == 1:
            first, second = column(low, 1, slot, BEFORE_LANE), column(y_after, 1, beyond, AFTER_LANE)
        elif cy == -1:
            first, second = column(y_before, 0, beyond, BEFORE_LANE), column(high, 0, slot, AFTER_LANE)
        else:
            first, second = column(y_before, 0, slot, BEFORE_LANE), column(y_after, 1, slot, AFTER_LANE)
        return jnp.where(lane < AFTER_LANE, first, second)

    moved, _, solid_columns = gather_columns(neighbours)
    column_flow = [neighbours(FLOW + axis, 0) for axis in range(3)]
    column_results = collide(moved, column_flow, 1.0 - solid_columns[0])

    flow = flow_blocks(velocity, 0, rows)
    for group in range(rows // 8):
        first = own + 8 * group
        moved, _ = gather_cells(held, shifted, first, solid_rows)
        results = collide(moved, flow[group], 1.0 - solid_parts[8 * group // (LEVELS * TILE)])
        for number in range(19):
            later[number, pl.ds(first, 8), :] = results[number]
    for number in x_down:
        later[number, pl.ds(near, LEVELS), :] = row_results[number][:LEVELS]
    for number in x_up:
        later[number, pl.ds(far, LEVELS), :] = row_results[number][LEVELS:]

    def later_edge(number, cy, group):
        shift = LANES - 1 - AFTER_LANE - group if cy == 1 else -BEFORE_LANE - group
        return pltpu.roll(column_results[number], shift % LANES, 1)

    fill_shifted(later, shifted, groups, later_edge)

    flow = flow_blocks(velocity, 1, rows)
    for group in range(rows // 8):
        first = 8 * group
        moved, _ = gather_cells(later, shifted, own + first, solid_rows)
        results = collide(moved, flow[group], 1.0 - solid_parts[first // (LEVELS * TILE)])
        for number in range(19):
            out[number, pl.ds(first, 8), :] = results[number]


def swap_pairs(first, second, axis):
    count = lax.axis_size(axis)
    inside = [(i, i ^ 1) for i in range(count)]
    across = [(i, (i + 1) % count if i % 2 == 1 else (i - 1) % count) for i in range(count)]
    second = lax.ppermute(second, axis, across)
    return lax.ppermute(first, axis, inside), second


def per_device(adjoint_in, velocity, solid_tiles, link_blocked):
    rows_x, levels, rows_y = adjoint_in.shape[1:]
    rows = rows_x * levels
    padded = rows + 16 + 2 * GUARD
    groups = rows // 8 + 2
    parts = -(-COLUMN_QUANTITIES // (LANES // groups))
    state = adjoint_in.reshape(19, rows, rows_y)
    flow = velocity.reshape(STEPS, 3, rows, rows_y)
    solid = solid_tiles.reshape(-1, solid_tiles.shape[2])

    def shape_of(*sizes):
        return jax.ShapeDtypeStruct(sizes, jnp.float32)

    params = pltpu.CompilerParams(vmem_limit_bytes=16 * 1024 * 1024)
    anywhere = pl.BlockSpec(memory_space=pl.ANY)
    *row_sent, held, flow, tiles = pl.pallas_call(
        row_message_kernel,
        out_shape=(
            pltpu.VMEM((QUANTITIES, levels, rows_y), jnp.float32),
            pltpu.VMEM((QUANTITIES, levels, rows_y), jnp.float32),
            pltpu.VMEM((19, padded, rows_y), jnp.float32),
            pltpu.VMEM(flow.shape, flow.dtype),
            pltpu.VMEM(solid.shape, solid.dtype),
        ),
        in_specs=[anywhere] * 3,
        out_specs=(vmem,) * 5,
        scratch_shapes=[pltpu.SemaphoreType.DMA((3,))],
        compiler_params=params,
    )(*(pltpu.with_memory_space_constraint(value, pltpu.HBM) for value in (state, flow, solid)))
    row_got = swap_pairs(*row_sent, "gx")
    own_columns = pl.pallas_call(
        own_columns_kernel,
        out_shape=(shape_of(parts, 8, rows_y),) * 2,
        in_specs=[vmem] * 3,
        out_specs=(vmem,) * 2,
        compiler_params=params,
        cost_estimate=pl.CostEstimate(flops=2_000_000, bytes_accessed=1_000_000, transcendentals=0),
    )(held, flow, tiles)
    low, high = pl.pallas_call(
        functools.partial(halo_columns_kernel, groups),
        out_shape=(shape_of(parts, 8, rows_y),) * 2,
        in_specs=[vmem] * 4,
        out_specs=(vmem,) * 2,
        scratch_shapes=[pltpu.VMEM((2, SECOND, 8, rows_y), jnp.float32)],
        compiler_params=params,
    )(*own_columns, *row_got)
    size = lax.axis_size("gy")
    y_before = lax.ppermute(own_columns[1], "gy", [(i, (i + 1) % size) for i in range(size)])
    def hand_on(columns, ahead, *later_than):
        handed = pl.pallas_call(
            functools.partial(hand_on_kernel, groups, ahead),
            out_shape=shape_of(parts, 8, rows_y),
            in_specs=[vmem] * (1 + len(later_than)),
            out_specs=vmem,
            compiler_params=params,
            cost_estimate=pl.CostEstimate(flops=10_000_000_000, bytes_accessed=100_000, transcendentals=0),
        )(columns, *later_than)
        return swap_pairs(handed, handed, "gx")

    handed = hand_on(y_before, 0)
    y_after = lax.ppermute(own_columns[0], "gy", [((i + 1) % size, i) for i in range(size)])
    count = lax.axis_size("gx") * size
    field = pltpu.VMEM((19, padded, rows_y), jnp.float32)
    solid_field = pltpu.VMEM((3, padded, rows_y), jnp.float32)
    partial, own_blocks = pl.pallas_call(
        inner_drag_kernel,
        out_shape=(
            pltpu.VMEM((8, rows_y), jnp.float32),
            pltpu.VMEM((SECOND + len(ahead_slots), 8, rows_y), jnp.float32),
        ),
        in_specs=[vmem] * 6,
        out_specs=(vmem,) * 2,
        scratch_shapes=[field, field, solid_field, pltpu.VMEM((9, padded, rows_y), jnp.float32)],
        compiler_params=params,
        cost_estimate=pl.CostEstimate(flops=20_000_000_000, bytes_accessed=1_000_000, transcendentals=0),
    )(held, flow, tiles, *row_got, low)
    own = pl.pallas_call(
        functools.partial(edge_drag_kernel, groups),
        out_shape=pltpu.VMEM((count, 1, rows_y), jnp.float32),
        in_specs=[vmem] * 5,
        out_specs=vmem,
        compiler_params=params,
        cost_estimate=pl.CostEstimate(flops=1_000_000, bytes_accessed=1_000_000, transcendentals=0),
    )(y_before, *handed, own_blocks, partial)
    handed_after = hand_on(y_after, 1, own)
    shared = lax.all_to_all(own, ("gx", "gy"), split_axis=0, concat_axis=0, tiled=True)
    result = pl.pallas_call(
        main_kernel,
        out_shape=shape_of(19, rows, rows_y),
        in_specs=[vmem] * 13,
        out_specs=vmem,
        scratch_shapes=[field, field, field, solid_field, pltpu.VMEM((4, 8, rows_y), jnp.float32)],
        compiler_params=params,
        cost_estimate=pl.CostEstimate(flops=1_000_000, bytes_accessed=1_000_000, transcendentals=0),
    )(held, flow, tiles, *row_got, y_before, *handed, y_after, *handed_after, low, high)
    cell_count = rows * rows_y * count
    scale = drag_factor / math.sqrt(cell_count) * 3.0 / 36.0
    total = jnp.sum(shared[:, 0, 0])
    return (result.reshape(adjoint_in.shape), (-scale * total).reshape(1))


def solution(mesh):
    placed = (
        P(None, "gx", None, "gy"),
        P(None, None, "gx", None, "gy"),
        P("gx", None, "gy"),
        P(None, "gx", None, "gy"),
    )
    return jax.shard_map(
        per_device,
        mesh=mesh,
        in_specs=placed,
        out_specs=(P(None, "gx", None, "gy"), P()),
        check_vma=False,
    )
```

```python
import functools
import math

import jax
import jax.numpy as jnp
from jax import lax
from jax.experimental import pallas as pl
from jax.experimental.pallas import tpu as pltpu
from jax.sharding import PartitionSpec as P

TILE = 4
STEPS = 2

lattice_speeds = (
    (0, 0, 0),
    (1, 0, 0),
    (-1, 0, 0),
    (0, 1, 0),
    (0, -1, 0),
    (0, 0, 1),
    (0, 0, -1),
    (1, 1, 0),
    (-1, -1, 0),
    (1, -1, 0),
    (-1, 1, 0),
    (1, 0, 1),
    (-1, 0, -1),
    (1, 0, -1),
    (-1, 0, 1),
    (0, 1, 1),
    (0, -1, -1),
    (0, 1, -1),
    (0, -1, 1),
)
relax_rate = 1.6
drag_factor = 20.0
LEVELS = 4
LANES = 128
GUARD = 8

x_up = [n for n in range(19) if lattice_speeds[n][0] == 1]
x_down = [n for n in range(19) if lattice_speeds[n][0] == -1]
y_up = [n for n in range(19) if lattice_speeds[n][1] == 1]
y_down = [n for n in range(19) if lattice_speeds[n][1] == -1]
vmem = pl.BlockSpec(memory_space=pltpu.VMEM)

FLOW = 19
SOLID = 22
NEXT = 23
SECOND = 26
QUANTITIES = 31
NEXT_SECOND = 31
COLUMN_QUANTITIES = 34
BEFORE_LANE = 16
AFTER_LANE = 32


def opposite_of(number):
    return number + 1 if number % 2 == 1 else number - 1


def lane_index(rows=8):
    return lax.broadcasted_iota(jnp.int32, (rows, LANES), 1)


def spread_solid(solid):
    tiles = solid.shape[1]
    row = lax.broadcasted_iota(jnp.int32, (tiles, LANES), 0)
    column = lax.broadcasted_iota(jnp.int32, (tiles, LANES), 1)
    spread = (column // TILE == row).astype(jnp.float32)
    cells = jnp.dot(solid[...].astype(jnp.float32), spread, preferred_element_type=jnp.float32)
    blocks = []
    for tile_row in range(solid.shape[0] // LEVELS):
        part = cells[tile_row * LEVELS : (tile_row + 1) * LEVELS]
        blocks.append(jnp.concatenate([part, part], axis=0))
    return blocks


def flow_blocks(velocity, step, rows):
    blocks = []
    for pair in range(rows // 16):
        both = [velocity[step, axis, pl.ds(16 * pair, 16), :].astype(jnp.float32) for axis in range(3)]
        blocks.append([part[:8] for part in both])
        blocks.append([part[8:] for part in both])
    return blocks


def on_even(axis):
    return lax.rem(lax.axis_index(axis), 2) == 0


class Chosen:
    def __init__(self, choice, yes, no):
        self.choice, self.yes, self.no = choice, yes, no
        self.shape = yes.shape

    def __getitem__(self, index):
        return jnp.where(self.choice, self.yes[index], self.no[index])


def slot_place(slot, group, groups):
    per_block = LANES // groups
    return slot // per_block, (slot % per_block) * groups + group


def insert_column(parts, slot, group, groups, value, edge, ahead):
    part, place = slot_place(slot, group, groups)
    lane = lane_index()
    turned = pltpu.roll(value, (place + ahead - edge) % LANES, 1)
    parts[part] = jnp.where(lane == place + ahead, turned, parts[part])


def row_message_kernel(
    state, velocity, solid, row_first, row_second, held, flow, tiles, arrived
):
    rows = state.shape[1]
    own = pl.ds(GUARD + 8, rows)
    copies = [
        pltpu.make_async_copy(state, held.at[:, own, :], arrived.at[0]),
        pltpu.make_async_copy(velocity, flow, arrived.at[1]),
        pltpu.make_async_copy(solid, tiles, arrived.at[2]),
    ]
    for copy in copies:
        copy.start()
    for copy in copies:
        copy.wait()
    even = on_even("gx")
    low_row, high_row = GUARD + 8, GUARD + 8 + rows - LEVELS

    def put(slot, low, high):
        row_first[slot] = jnp.where(even, high, low)
        row_second[slot] = jnp.where(even, low, high)

    for number in range(19):
        put(number, held[number, pl.ds(low_row, LEVELS), :], held[number, pl.ds(high_row, LEVELS), :])
    for step, slot in ((0, FLOW), (1, NEXT)):
        for axis in range(3):
            low = flow[step, axis, pl.ds(0, 16), :].astype(jnp.float32)
            high = flow[step, axis, pl.ds(rows - 16, 16), :].astype(jnp.float32)
            put(slot + axis, low[:LEVELS], high[16 - LEVELS :])
    solid_parts = spread_solid(tiles)
    put(SOLID, solid_parts[0][:LEVELS], solid_parts[-1][:LEVELS])
    for slot in range(5):
        put(
            SECOND + slot,
            held[x_up[slot], pl.ds(low_row + LEVELS, LEVELS), :],
            held[x_down[slot], pl.ds(high_row - LEVELS, LEVELS), :],
        )


def pack_columns(parts, slot, group, groups, value):
    for message, edge, step, ahead, moving in ((parts[0], 0, 1, 1, y_up), (parts[1], LANES - 1, -1, 0, y_down)):
        if message is None:
            continue
        insert_column(message, slot, group, groups, value, edge, ahead)
        second = second_slot(slot, moving)
        if second != slot:
            insert_column(message, second, group, groups, value, edge + step, ahead)


def own_columns_kernel(side, held, velocity, solid, *rest):
    out = rest[-1]
    rows = velocity.shape[2]
    groups = rows // 8 + 2
    solid_parts = spread_solid(solid)
    flow = [flow_blocks(velocity, step, rows) for step in range(2)]
    parts = [None, None]
    parts[side] = [jnp.zeros((8, LANES), jnp.float32) for _ in range(out.shape[0])]
    for group in range(1, groups - 1):
        for slot in range(19):
            pack_columns(parts, slot, group, groups, held[slot, pl.ds(GUARD + 8 * group, 8), :])
        for axis in range(3):
            pack_columns(parts, FLOW + axis, group, groups, flow[0][group - 1][axis])
            pack_columns(parts, NEXT + axis, group, groups, flow[1][group - 1][axis])
        pack_columns(parts, SOLID, group, groups, solid_parts[(group - 1) * 8 // (LEVELS * TILE)])
    for part in range(out.shape[0]):
        out[part] = parts[side][part]


def halo_columns_kernel(groups, own_low, own_high, row_first, row_second, low_out, high_out, ends):
    count = own_high.shape[0]
    even = on_even("gx")
    after, before = Chosen(even, row_first, row_second), Chosen(even, row_second, row_first)
    parts = [[own_low[part] for part in range(count)], [own_high[part] for part in range(count)]]
    for slot in range(SECOND):
        ends[0, slot, pl.ds(LEVELS, LEVELS), :] = before[slot]
        ends[1, slot, pl.ds(0, LEVELS), :] = after[slot]
        if slot == SOLID:
            low_second, high_second = SOLID, SOLID
        else:
            low_second = SECOND + x_down.index(slot) if slot in x_down else None
            high_second = SECOND + x_up.index(slot) if slot in x_up else None
        blank = jnp.zeros((LEVELS, LANES), jnp.float32)
        ends[0, slot, pl.ds(0, LEVELS), :] = blank if low_second is None else before[low_second]
        ends[1, slot, pl.ds(LEVELS, LEVELS), :] = blank if high_second is None else after[high_second]
        pack_columns(parts, slot, 0, groups, ends[0, slot])
        pack_columns(parts, slot, groups - 1, groups, ends[1, slot])
    for part in range(count):
        low_out[part] = parts[0][part]
        high_out[part] = parts[1][part]


def collide(moved, flow, fluid):
    ux, uy, uz = flow
    total = {n: moved[n] + moved[n + 1] for n in range(1, 19, 2)}
    xy, xz, yz = total[7] + total[9], total[11] + total[13], total[15] + total[17]
    axis_x, axis_y, axis_z = 2.0 * total[1], 2.0 * total[3], 2.0 * total[5]
    density = 12.0 * moved[0] + (axis_x + axis_y + axis_z) + (xy + xz + yz)
    pxx = axis_x + xy + xz
    pyy = axis_y + xy + yz
    pzz = axis_z + xz + yz
    pxy = total[7] - total[9]
    pxz = total[11] - total[13]
    pyz = total[15] - total[17]
    dx, dy, dz = momentum(moved)
    vx = pxx * ux + pxy * uy + pxz * uz
    vy = pxy * ux + pyy * uy + pyz * uz
    vz = pxz * ux + pyz * uy + pzz * uz
    speed_sq = ux * ux + uy * uy + uz * uz
    scaled = (relax_rate / 36.0) * fluid
    base = scaled * (density + 1.5 * (speed_sq * density) - 4.5 * (ux * vx + uy * vy + uz * vz))
    scaled3 = 3.0 * scaled
    bx = scaled3 * (dx + 3.0 * vx - ux * density)
    by = scaled3 * (dy + 3.0 * vy - uy * density)
    bz = scaled3 * (dz + 3.0 * vz - uz * density)
    keep = (1.0 - relax_rate) * fluid
    results = [keep * moved[0] + base]
    for number in range(1, 19, 2):
        along = None
        for speed, part in zip(lattice_speeds[number], (bx, by, bz)):
            if speed == 0:
                continue
            if along is None:
                along = part if speed == 1 else -part
            else:
                along = along + part if speed == 1 else along - part
        results.append(keep * moved[number] + (base + along))
        results.append(keep * moved[number + 1] + (base - along))
    return results


def outside(cz):
    level = lax.broadcasted_iota(jnp.int32, (8, LANES), 0) % LEVELS
    return level == (LEVELS - 1 if cz == 1 else 0)


def link_closed(solid_there, cz):
    closed = solid_there > 0.5
    return closed | outside(cz) if cz != 0 else closed


def shift_lanes(value, cy, edge_value):
    lane = lane_index(value.shape[0])
    shifted = pltpu.roll(value, -cy % LANES, 1)
    if edge_value is None:
        return shifted
    return jnp.where(lane == (LANES - 1 if cy == 1 else 0), edge_value, shifted)


def gather_cells(held, shifted, first, solid_rows):
    here = [held[n, pl.ds(first, 8), :] for n in range(19)]
    moved, closed = [here[0]], [None]
    for number in range(1, 19):
        cx, cy, cz = lattice_speeds[number]
        field = held if cy == 0 else shifted
        there = pl.ds(first + LEVELS * cx + cz, 8)
        closed.append(link_closed(solid_rows[cy % 3, there, :], cz))
        bounced = here[opposite_of(number)]
        if cx != 0:
            bounced = bounced + 2.0 * cx
        moved.append(jnp.where(closed[number], bounced, field[number, there, :]))
    return moved, closed


def momentum(moved):
    gap = {n: moved[n] - moved[n + 1] for n in range(1, 19, 2)}
    dx = 2.0 * gap[1] + (gap[7] + gap[9]) + (gap[11] + gap[13])
    dy = 2.0 * gap[3] + (gap[7] - gap[9]) + (gap[15] + gap[17])
    dz = 2.0 * gap[5] + (gap[11] - gap[13]) + (gap[15] - gap[17])
    return dx, dy, dz


def drag_term(moved, flow, fluid):
    return fluid * sum(speed * part for speed, part in zip(flow, momentum(moved)))


def along_link(number, vector):
    total = None
    for axis, speed in enumerate(lattice_speeds[number]):
        if speed == 0:
            continue
        part = vector(axis)
        if total is None:
            total = part if speed == 1 else -part
        else:
            total = total + part if speed == 1 else total - part
    return total


def later_drag(results, closed, weight_here, weight_back):
    term = None
    for number in range(1, 19):
        cx = lattice_speeds[number][0]
        here = along_link(number, lambda axis: weight_here[axis])
        part = jnp.where(closed[opposite_of(number)], -here, weight_back(number)) * results[number]
        if cx != 0:
            part = part + jnp.where(closed[number], (2.0 * cx) * here, 0.0)
        if number < 7:
            part = 2.0 * part
        term = part if term is None else term + part
    return term


def column_reader(groups):
    def column(message, ahead, slot, lane_first, group=0):
        part, place = slot_place(slot, group, groups)
        return pltpu.roll(message[part], (lane_first - place - ahead) % LANES, 1)

    return column


def fill_held(own_held, before, after, held, rows):
    own = GUARD + 8
    near, far = own - LEVELS, own + rows
    for number in range(19):
        for group in range(rows // 8):
            there = pl.ds(own + 8 * group, 8)
            held[number, there, :] = own_held[number, there, :]
        held[number, pl.ds(near, LEVELS), :] = before[number]
        held[number, pl.ds(far, LEVELS), :] = after[number]
        if number in x_down:
            held[number, pl.ds(near - LEVELS, LEVELS), :] = before[SECOND + x_down.index(number)]
        if number in x_up:
            held[number, pl.ds(far + LEVELS, LEVELS), :] = after[SECOND + x_up.index(number)]


def fill_shifted(field, shifted, groups, edge_of):
    for number in y_up + y_down:
        cy = lattice_speeds[number][1]
        for group in range(groups):
            there = pl.ds(GUARD + 8 * group, 8)
            shifted[number, there, :] = shift_lanes(field[number, there, :], cy, edge_of(number, cy, group))


def fill_solid(solid_parts, before, after, solid_rows, groups, edge_of):
    for group in range(groups):
        first = GUARD + 8 * group
        if group in (0, groups - 1):
            halo = before[SOLID] if group == 0 else after[SOLID]
            solid_rows[0, pl.ds(first, LEVELS), :] = halo
            solid_rows[0, pl.ds(first + LEVELS, LEVELS), :] = halo
        else:
            solid_rows[0, pl.ds(first, 8), :] = solid_parts[(group - 1) * 8 // (LEVELS * TILE)]
        value = solid_rows[0, pl.ds(first, 8), :]
        for cy in (1, -1):
            solid_rows[cy % 3, pl.ds(first, 8), :] = shift_lanes(value, cy, edge_of(SOLID, cy, group))


def shift_rows(value, cx, cz):
    if cx != 0:
        upper = lax.broadcasted_iota(jnp.int32, (8, LANES), 0) < LEVELS
        swapped = pltpu.roll(value, LEVELS, 0)
        if cx == 1:
            value = jnp.where(upper, swapped, pltpu.roll(swapped, LANES - 1, 1))
        else:
            value = jnp.where(upper, pltpu.roll(swapped, 1, 1), swapped)
    if cz != 0:
        value = pltpu.roll(value, (-cz) % 8, 0)
    return value


def gather_columns(neighbours):
    here = [neighbours(n, 0) for n in range(19)]
    solid = {cy: neighbours(SOLID, cy) for cy in (0, 1, -1)}
    moved, closed = [here[0]], [None]
    for number in range(1, 19):
        cx, cy, cz = lattice_speeds[number]
        source = shift_rows(here[number] if cy == 0 else neighbours(number, cy), cx, cz)
        closed.append(link_closed(shift_rows(solid[cy], cx, cz), cz))
        moved.append(jnp.where(closed[number], here[opposite_of(number)] + 2.0 * cx, source))
    return moved, closed, solid


def inner_drag_kernel(
    own_held, velocity, solid, row_first, row_second, low, partial, own_blocks,
    held, shifted, solid_rows, weights,
):
    rows = velocity.shape[2]
    groups = rows // 8 + 2
    own = GUARD + 8
    near, far = own - LEVELS, own + rows
    even = on_even("gx")
    after, before = Chosen(even, row_first, row_second), Chosen(even, row_second, row_first)
    lane = lane_index()
    solid_parts = spread_solid(solid)

    def no_edge(slot, cy, group):
        return None

    fill_held(own_held, before, after, held, rows)
    fill_shifted(held, shifted, groups, no_edge)
    fill_solid(solid_parts, before, after, solid_rows, groups, no_edge)

    flow = flow_blocks(velocity, 1, rows)
    for axis in range(3):
        for group in range(rows // 8):
            there = pl.ds(own + 8 * group, 8)
            weights[axis, there, :] = (1.0 - solid_rows[0, there, :]) * flow[group][axis]
        for row, message in ((near, before), (far, after)):
            weights[axis, pl.ds(row, LEVELS), :] = (1.0 - message[SOLID]) * message[NEXT + axis]
        for group in range(groups):
            there = pl.ds(GUARD + 8 * group, 8)
            value = weights[axis, there, :]
            weights[3 + axis, there, :] = shift_lanes(value, 1, None)
            weights[6 + axis, there, :] = shift_lanes(value, -1, None)

    total = jnp.zeros((8, LANES), jnp.float32)
    flow = flow_blocks(velocity, 0, rows)
    for group in range(rows // 8):
        first = own + 8 * group
        moved, closed = gather_cells(held, shifted, first, solid_rows)
        fluid = 1.0 - solid_parts[8 * group // (LEVELS * TILE)]
        results = collide(moved, flow[group], fluid)

        def back(number):
            cx, cy, cz = lattice_speeds[number]
            there = pl.ds(first - LEVELS * cx - cz, 8)
            return along_link(number, lambda axis: weights[3 * (-cy % 3) + axis, there, :])

        here = [weights[axis, pl.ds(first, 8), :] for axis in range(3)]
        total = total + drag_term(moved, flow[group], fluid) + later_drag(results, closed, here, back)
    inside = jnp.logical_and(lane > 0, lane < LANES - 1)
    partial[...] = jnp.where(inside, total, 0.0)

    column = column_reader(groups)
    for slot in range(SECOND):
        own_blocks[slot] = column(low, 1, slot, AFTER_LANE)
    for place, slot in enumerate(ahead_slots):
        here = column(low, 1, slot, BEFORE_LANE)
        ahead = column(low, 1, second_slot(slot, y_up), AFTER_LANE)
        own_blocks[SECOND + place] = jnp.where(lane < AFTER_LANE, here, ahead)


ahead_slots = y_up + [SOLID, NEXT, NEXT + 1, NEXT + 2]


def second_slot(slot, moving):
    if slot in moving:
        return SECOND + moving.index(slot)
    return NEXT_SECOND + slot - NEXT if NEXT <= slot < NEXT + 3 else slot


def halo_lanes(groups, ahead):
    lane = lane_index()
    group = lax.rem(lane + groups - ahead, groups)
    used = jnp.logical_and(lane >= ahead, lane < LANES // groups * groups + ahead)
    return jnp.logical_and(used, group == 0), jnp.logical_and(used, group == groups - 1)


def hand_on_kernel(groups, ahead, columns, *rest):
    out = rest[-1]
    above, _ = halo_lanes(groups, ahead)
    for part in range(out.shape[0]):
        value = columns[part]
        last = pltpu.roll(value, LANES - (groups - 2), 1)
        out[part] = jnp.where(above, last, pltpu.roll(value, groups - 2, 1))


def with_halo_rows(columns, handed_first, handed_second, groups, ahead):
    even = on_even("gx")
    from_before = Chosen(even, handed_second, handed_first)
    from_after = Chosen(even, handed_first, handed_second)
    above, below = halo_lanes(groups, ahead)
    whole = []
    for part in range(handed_first.shape[0]):
        value = jnp.where(above, from_before[part], columns[part])
        whole.append(jnp.where(below, from_after[part], value))
    return whole


def edge_drag_kernel(groups, columns, handed_first, handed_second, own_blocks, partial, shared):
    lane = lane_index()
    column = column_reader(groups)
    y_before = with_halo_rows(columns, handed_first, handed_second, groups, 0)

    def neighbours(slot, cy):
        if cy == 1:
            return own_blocks[SECOND + ahead_slots.index(slot)]
        if cy == 0:
            first, second = column(y_before, 0, slot, BEFORE_LANE), own_blocks[slot]
        else:
            first = column(y_before, 0, second_slot(slot, y_down), BEFORE_LANE)
            second = column(y_before, 0, slot, AFTER_LANE)
        return jnp.where(lane < AFTER_LANE, first, second)

    moved, closed, solid_columns = gather_columns(neighbours)
    fluid = {cy: 1.0 - solid_columns[cy] for cy in (0, 1, -1)}
    flow = [neighbours(FLOW + axis, 0) for axis in range(3)]
    results = collide(moved, flow, fluid[0])
    weight = {cy: [fluid[cy] * neighbours(NEXT + axis, cy) for axis in range(3)] for cy in (0, 1, -1)}

    def back(number):
        cx, cy, cz = lattice_speeds[number]
        return shift_rows(along_link(number, lambda axis: weight[-cy][axis]), -cx, -cz)

    term = drag_term(moved, flow, fluid[0]) + later_drag(results, closed, weight[0], back)
    place = jnp.where(lane < AFTER_LANE, lane - BEFORE_LANE, lane - AFTER_LANE)
    inside = jnp.logical_and(place > 0, place < groups - 1)
    total = partial[...] + jnp.where(inside, term, 0.0)
    shared[...] = jnp.broadcast_to(jnp.sum(total), shared.shape)


def main_kernel(
    own_held, velocity, solid, row_first, row_second, columns, handed_first, handed_second,
    columns_after, after_first, after_second, low, high, out, held, shifted, later, solid_rows, row_flow,
):
    rows = velocity.shape[2]
    groups = rows // 8 + 2
    own = GUARD + 8
    near, far = own - LEVELS, own + rows
    even = on_even("gx")
    after, before = Chosen(even, row_first, row_second), Chosen(even, row_second, row_first)
    lane = lane_index()
    solid_parts = spread_solid(solid)
    column = column_reader(groups)
    y_before = with_halo_rows(columns, handed_first, handed_second, groups, 0)
    y_after = with_halo_rows(columns_after, after_first, after_second, groups, 1)

    def edge_of(slot, cy, group):
        if cy == 1:
            return column(y_after, 1, slot, LANES - 1, group)
        return column(y_before, 0, slot, 0, group)

    fill_held(own_held, before, after, held, rows)
    fill_shifted(held, shifted, groups, edge_of)
    fill_solid(solid_parts, before, after, solid_rows, groups, edge_of)
    for slot, place in ((FLOW, 0), (FLOW + 1, 1), (FLOW + 2, 2), (SOLID, 3)):
        row_flow[place, pl.ds(0, LEVELS), :] = before[slot]
        row_flow[place, pl.ds(LEVELS, LEVELS), :] = after[slot]

    def both_rows(field, index, shift):
        ends = [field[index, pl.ds(place + shift, LEVELS), :] for place in (near, far)]
        return jnp.concatenate(ends, axis=0)

    here = [both_rows(held, n, 0) for n in range(19)]
    moved = [here[0]]
    for number in range(1, 19):
        cx, cy, cz = lattice_speeds[number]
        shift = LEVELS * cx + cz
        source = both_rows(held if cy == 0 else shifted, number, shift)
        closed = link_closed(both_rows(solid_rows, cy % 3, shift), cz)
        moved.append(jnp.where(closed, here[opposite_of(number)] + 2.0 * cx, source))
    row_results = collide(moved, [row_flow[axis] for axis in range(3)], 1.0 - row_flow[3])

    def neighbours(slot, cy):
        beyond = slot if cy == 0 or slot == SOLID else SECOND + (y_up if cy == 1 else y_down).index(slot)
        if cy == 1:
            first, second = column(low, 1, slot, BEFORE_LANE), column(y_after, 1, beyond, AFTER_LANE)
        elif cy == -1:
            first, second = column(y_before, 0, beyond, BEFORE_LANE), column(high, 0, slot, AFTER_LANE)
        else:
            first, second = column(y_before, 0, slot, BEFORE_LANE), column(y_after, 1, slot, AFTER_LANE)
        return jnp.where(lane < AFTER_LANE, first, second)

    moved, _, solid_columns = gather_columns(neighbours)
    column_flow = [neighbours(FLOW + axis, 0) for axis in range(3)]
    column_results = collide(moved, column_flow, 1.0 - solid_columns[0])

    flow = flow_blocks(velocity, 0, rows)
    for group in range(rows // 8):
        first = own + 8 * group
        moved, _ = gather_cells(held, shifted, first, solid_rows)
        results = collide(moved, flow[group], 1.0 - solid_parts[8 * group // (LEVELS * TILE)])
        for number in range(19):
            later[number, pl.ds(first, 8), :] = results[number]
    for number in x_down:
        later[number, pl.ds(near, LEVELS), :] = row_results[number][:LEVELS]
    for number in x_up:
        later[number, pl.ds(far, LEVELS), :] = row_results[number][LEVELS:]

    def later_edge(number, cy, group):
        shift = LANES - 1 - AFTER_LANE - group if cy == 1 else -BEFORE_LANE - group
        return pltpu.roll(column_results[number], shift % LANES, 1)

    fill_shifted(later, shifted, groups, later_edge)

    flow = flow_blocks(velocity, 1, rows)
    for group in range(rows // 8):
        first = 8 * group
        moved, _ = gather_cells(later, shifted, own + first, solid_rows)
        results = collide(moved, flow[group], 1.0 - solid_parts[first // (LEVELS * TILE)])
        for number in range(19):
            out[number, pl.ds(first, 8), :] = results[number]


def swap_pairs(first, second, axis):
    count = lax.axis_size(axis)
    inside = [(i, i ^ 1) for i in range(count)]
    across = [(i, (i + 1) % count if i % 2 == 1 else (i - 1) % count) for i in range(count)]
    second = lax.ppermute(second, axis, across)
    return lax.ppermute(first, axis, inside), second


def per_device(adjoint_in, velocity, solid_tiles, link_blocked):
    rows_x, levels, rows_y = adjoint_in.shape[1:]
    rows = rows_x * levels
    padded = rows + 16 + 2 * GUARD
    groups = rows // 8 + 2
    parts = -(-COLUMN_QUANTITIES // (LANES // groups))
    state = adjoint_in.reshape(19, rows, rows_y)
    flow = velocity.reshape(STEPS, 3, rows, rows_y)
    solid = solid_tiles.reshape(-1, solid_tiles.shape[2])

    def shape_of(*sizes):
        return jax.ShapeDtypeStruct(sizes, jnp.float32)

    params = pltpu.CompilerParams(vmem_limit_bytes=16 * 1024 * 1024)
    anywhere = pl.BlockSpec(memory_space=pl.ANY)
    *row_sent, held, flow, tiles = pl.pallas_call(
        row_message_kernel,
        out_shape=(
            pltpu.VMEM((QUANTITIES, levels, rows_y), jnp.float32),
            pltpu.VMEM((QUANTITIES, levels, rows_y), jnp.float32),
            pltpu.VMEM((19, padded, rows_y), jnp.float32),
            pltpu.VMEM(flow.shape, flow.dtype),
            pltpu.VMEM(solid.shape, solid.dtype),
        ),
        in_specs=[anywhere] * 3,
        out_specs=(vmem,) * 5,
        scratch_shapes=[pltpu.SemaphoreType.DMA((3,))],
        compiler_params=params,
    )(*(pltpu.with_memory_space_constraint(value, pltpu.HBM) for value in (state, flow, solid)))
    row_got = swap_pairs(*row_sent, "gx")
    def pack(side, size, *later_than):
        return pl.pallas_call(
            functools.partial(own_columns_kernel, side),
            out_shape=shape_of(size, 8, rows_y),
            in_specs=[vmem] * (3 + len(later_than)),
            out_specs=vmem,
            compiler_params=params,
            cost_estimate=pl.CostEstimate(flops=2_000_000, bytes_accessed=1_000_000, transcendentals=0),
        )(held, flow, tiles, *later_than)

    own_high = pack(1, parts)
    own_low = pack(0, 16)
    own_columns = own_low, own_high
    low, high = pl.pallas_call(
        functools.partial(halo_columns_kernel, groups),
        out_shape=(shape_of(parts, 8, rows_y),) * 2,
        in_specs=[vmem] * 4,
        out_specs=(vmem,) * 2,
        scratch_shapes=[pltpu.VMEM((2, SECOND, 8, rows_y), jnp.float32)],
        compiler_params=params,
    )(*own_columns, *row_got)
    size = lax.axis_size("gy")
    y_before = lax.ppermute(own_columns[1], "gy", [(i, (i + 1) % size) for i in range(size)])
    def hand_on(columns, ahead, *later_than):
        handed = pl.pallas_call(
            functools.partial(hand_on_kernel, groups, ahead),
            out_shape=shape_of(parts, 8, rows_y),
            in_specs=[vmem] * (1 + len(later_than)),
            out_specs=vmem,
            compiler_params=params,
            cost_estimate=pl.CostEstimate(flops=10_000_000_000, bytes_accessed=100_000, transcendentals=0),
        )(columns, *later_than)
        return swap_pairs(handed, handed, "gx")

    handed = hand_on(y_before, 0)
    y_after = lax.ppermute(own_columns[0], "gy", [((i + 1) % size, i) for i in range(size)])
    count = lax.axis_size("gx") * size
    field = pltpu.VMEM((19, padded, rows_y), jnp.float32)
    solid_field = pltpu.VMEM((3, padded, rows_y), jnp.float32)
    partial, own_blocks = pl.pallas_call(
        inner_drag_kernel,
        out_shape=(
            pltpu.VMEM((8, rows_y), jnp.float32),
            pltpu.VMEM((SECOND + len(ahead_slots), 8, rows_y), jnp.float32),
        ),
        in_specs=[vmem] * 6,
        out_specs=(vmem,) * 2,
        scratch_shapes=[field, field, solid_field, pltpu.VMEM((9, padded, rows_y), jnp.float32)],
        compiler_params=params,
        cost_estimate=pl.CostEstimate(flops=20_000_000_000, bytes_accessed=1_000_000, transcendentals=0),
    )(held, flow, tiles, *row_got, low)
    own = pl.pallas_call(
        functools.partial(edge_drag_kernel, groups),
        out_shape=pltpu.VMEM((count, 1, rows_y), jnp.float32),
        in_specs=[vmem] * 5,
        out_specs=vmem,
        compiler_params=params,
        cost_estimate=pl.CostEstimate(flops=1_000_000, bytes_accessed=1_000_000, transcendentals=0),
    )(y_before, *handed, own_blocks, partial)
    handed_after = hand_on(y_after, 1, own)
    shared = lax.all_to_all(own, ("gx", "gy"), split_axis=0, concat_axis=0, tiled=True)
    result = pl.pallas_call(
        main_kernel,
        out_shape=shape_of(19, rows, rows_y),
        in_specs=[vmem] * 13,
        out_specs=vmem,
        scratch_shapes=[field, field, field, solid_field, pltpu.VMEM((4, 8, rows_y), jnp.float32)],
        compiler_params=params,
        cost_estimate=pl.CostEstimate(flops=1_000_000, bytes_accessed=1_000_000, transcendentals=0),
    )(held, flow, tiles, *row_got, y_before, *handed, y_after, *handed_after, low, high)
    cell_count = rows * rows_y * count
    scale = drag_factor / math.sqrt(cell_count) * 3.0 / 36.0
    total = jnp.sum(shared[:, 0, 0])
    return (result.reshape(adjoint_in.shape), (-scale * total).reshape(1))


def solution(mesh):
    placed = (
        P(None, "gx", None, "gy"),
        P(None, None, "gx", None, "gy"),
        P("gx", None, "gy"),
        P(None, "gx", None, "gy"),
    )
    return jax.shard_map(
        per_device,
        mesh=mesh,
        in_specs=placed,
        out_specs=(P(None, "gx", None, "gy"), P()),
        check_vma=False,
    )
```

```python
import functools
import math

import jax
import jax.numpy as jnp
from jax import lax
from jax.experimental import pallas as pl
from jax.experimental.pallas import tpu as pltpu
from jax.sharding import PartitionSpec as P

TILE = 4
STEPS = 2

lattice_speeds = (
    (0, 0, 0),
    (1, 0, 0),
    (-1, 0, 0),
    (0, 1, 0),
    (0, -1, 0),
    (0, 0, 1),
    (0, 0, -1),
    (1, 1, 0),
    (-1, -1, 0),
    (1, -1, 0),
    (-1, 1, 0),
    (1, 0, 1),
    (-1, 0, -1),
    (1, 0, -1),
    (-1, 0, 1),
    (0, 1, 1),
    (0, -1, -1),
    (0, 1, -1),
    (0, -1, 1),
)
relax_rate = 1.6
drag_factor = 20.0
LEVELS = 4
LANES = 128
GUARD = 8

x_up = [n for n in range(19) if lattice_speeds[n][0] == 1]
x_down = [n for n in range(19) if lattice_speeds[n][0] == -1]
y_up = [n for n in range(19) if lattice_speeds[n][1] == 1]
y_down = [n for n in range(19) if lattice_speeds[n][1] == -1]
vmem = pl.BlockSpec(memory_space=pltpu.VMEM)

FLOW = 19
SOLID = 22
NEXT = 23
SECOND = 26
QUANTITIES = 31
NEXT_SECOND = 31
COLUMN_QUANTITIES = 34
BEFORE_LANE = 16
AFTER_LANE = 32


def opposite_of(number):
    return number + 1 if number % 2 == 1 else number - 1


def lane_index(rows=8):
    return lax.broadcasted_iota(jnp.int32, (rows, LANES), 1)


def spread_solid(solid):
    tiles = solid.shape[1]
    row = lax.broadcasted_iota(jnp.int32, (tiles, LANES), 0)
    column = lax.broadcasted_iota(jnp.int32, (tiles, LANES), 1)
    spread = (column // TILE == row).astype(jnp.float32)
    cells = jnp.dot(solid[...].astype(jnp.float32), spread, preferred_element_type=jnp.float32)
    blocks = []
    for tile_row in range(solid.shape[0] // LEVELS):
        part = cells[tile_row * LEVELS : (tile_row + 1) * LEVELS]
        blocks.append(jnp.concatenate([part, part], axis=0))
    return blocks


def flow_blocks(velocity, step, rows):
    blocks = []
    for pair in range(rows // 16):
        both = [velocity[step, axis, pl.ds(16 * pair, 16), :].astype(jnp.float32) for axis in range(3)]
        blocks.append([part[:8] for part in both])
        blocks.append([part[8:] for part in both])
    return blocks


def on_even(axis):
    return lax.rem(lax.axis_index(axis), 2) == 0


class Chosen:
    def __init__(self, choice, yes, no):
        self.choice, self.yes, self.no = choice, yes, no
        self.shape = yes.shape

    def __getitem__(self, index):
        return jnp.where(self.choice, self.yes[index], self.no[index])


def slot_place(slot, group, groups):
    per_block = LANES // groups
    return slot // per_block, (slot % per_block) * groups + group


def insert_column(parts, slot, group, groups, value, edge, ahead):
    part, place = slot_place(slot, group, groups)
    lane = lane_index()
    turned = pltpu.roll(value, (place + ahead - edge) % LANES, 1)
    parts[part] = jnp.where(lane == place + ahead, turned, parts[part])


def first_columns_kernel(
    state, velocity, solid, high, held, flow, tiles, arrived
):
    rows = state.shape[1]
    groups = rows // 8 + 2
    own = pl.ds(GUARD + 8, rows)
    chunks = ((0, 5), (5, 5), (10, 5), (15, 4))
    copies = [
        pltpu.make_async_copy(velocity, flow, arrived.at[0]),
        pltpu.make_async_copy(solid, tiles, arrived.at[1]),
    ]
    for place, (first, count) in enumerate(chunks):
        part = pl.ds(first, count)
        copies.append(pltpu.make_async_copy(state.at[part], held.at[part, own, :], arrived.at[2 + place]))
    for copy in copies:
        copy.start()
    parts = [None, [jnp.zeros((8, LANES), jnp.float32) for _ in range(high.shape[0])]]
    copies[0].wait()
    blocks = [flow_blocks(flow, step, rows) for step in range(2)]
    for group in range(1, groups - 1):
        for axis in range(3):
            pack_columns(parts, FLOW + axis, group, groups, blocks[0][group - 1][axis])
            pack_columns(parts, NEXT + axis, group, groups, blocks[1][group - 1][axis])
    copies[1].wait()
    solid_parts = spread_solid(tiles)
    for group in range(1, groups - 1):
        pack_columns(parts, SOLID, group, groups, solid_parts[(group - 1) * 8 // (LEVELS * TILE)])
    for copy, (first, count) in zip(copies[2:], chunks):
        copy.wait()
        for slot in range(first, first + count):
            for group in range(1, groups - 1):
                pack_columns(parts, slot, group, groups, held[slot, pl.ds(GUARD + 8 * group, 8), :])
    for part in range(high.shape[0]):
        high[part] = parts[1][part]


def row_message_kernel(held, flow, tiles, row_first, row_second):
    rows = flow.shape[2]
    even = on_even("gx")
    low_row, high_row = GUARD + 8, GUARD + 8 + rows - LEVELS

    def put(slot, low, high):
        row_first[slot] = jnp.where(even, high, low)
        row_second[slot] = jnp.where(even, low, high)

    for number in range(19):
        put(number, held[number, pl.ds(low_row, LEVELS), :], held[number, pl.ds(high_row, LEVELS), :])
    for step, slot in ((0, FLOW), (1, NEXT)):
        for axis in range(3):
            low = flow[step, axis, pl.ds(0, 16), :].astype(jnp.float32)
            high = flow[step, axis, pl.ds(rows - 16, 16), :].astype(jnp.float32)
            put(slot + axis, low[:LEVELS], high[16 - LEVELS :])
    solid_parts = spread_solid(tiles)
    put(SOLID, solid_parts[0][:LEVELS], solid_parts[-1][:LEVELS])
    for slot in range(5):
        put(
            SECOND + slot,
            held[x_up[slot], pl.ds(low_row + LEVELS, LEVELS), :],
            held[x_down[slot], pl.ds(high_row - LEVELS, LEVELS), :],
        )


def pack_columns(parts, slot, group, groups, value):
    for message, edge, step, ahead, moving in ((parts[0], 0, 1, 1, y_up), (parts[1], LANES - 1, -1, 0, y_down)):
        if message is None:
            continue
        insert_column(message, slot, group, groups, value, edge, ahead)
        second = second_slot(slot, moving)
        if second != slot:
            insert_column(message, second, group, groups, value, edge + step, ahead)


def own_columns_kernel(held, velocity, solid, row_sent, out):
    rows = velocity.shape[2]
    groups = rows // 8 + 2
    solid_parts = spread_solid(solid)
    flow = [flow_blocks(velocity, step, rows) for step in range(2)]
    parts = [[jnp.zeros((8, LANES), jnp.float32) for _ in range(out.shape[0])], None]
    for group in range(1, groups - 1):
        for slot in range(19):
            pack_columns(parts, slot, group, groups, held[slot, pl.ds(GUARD + 8 * group, 8), :])
        for axis in range(3):
            pack_columns(parts, FLOW + axis, group, groups, flow[0][group - 1][axis])
            pack_columns(parts, NEXT + axis, group, groups, flow[1][group - 1][axis])
        pack_columns(parts, SOLID, group, groups, solid_parts[(group - 1) * 8 // (LEVELS * TILE)])
    for part in range(out.shape[0]):
        out[part] = parts[0][part]


def halo_columns_kernel(groups, own_low, own_high, row_first, row_second, low_out, high_out, ends):
    count = own_high.shape[0]
    even = on_even("gx")
    after, before = Chosen(even, row_first, row_second), Chosen(even, row_second, row_first)
    parts = [[own_low[part] for part in range(count)], [own_high[part] for part in range(count)]]
    for slot in range(SECOND):
        ends[0, slot, pl.ds(LEVELS, LEVELS), :] = before[slot]
        ends[1, slot, pl.ds(0, LEVELS), :] = after[slot]
        if slot == SOLID:
            low_second, high_second = SOLID, SOLID
        else:
            low_second = SECOND + x_down.index(slot) if slot in x_down else None
            high_second = SECOND + x_up.index(slot) if slot in x_up else None
        blank = jnp.zeros((LEVELS, LANES), jnp.float32)
        ends[0, slot, pl.ds(0, LEVELS), :] = blank if low_second is None else before[low_second]
        ends[1, slot, pl.ds(LEVELS, LEVELS), :] = blank if high_second is None else after[high_second]
        pack_columns(parts, slot, 0, groups, ends[0, slot])
        pack_columns(parts, slot, groups - 1, groups, ends[1, slot])
    for part in range(count):
        low_out[part] = parts[0][part]
        high_out[part] = parts[1][part]


def collide(moved, flow, fluid):
    ux, uy, uz = flow
    total = {n: moved[n] + moved[n + 1] for n in range(1, 19, 2)}
    xy, xz, yz = total[7] + total[9], total[11] + total[13], total[15] + total[17]
    axis_x, axis_y, axis_z = 2.0 * total[1], 2.0 * total[3], 2.0 * total[5]
    density = 12.0 * moved[0] + (axis_x + axis_y + axis_z) + (xy + xz + yz)
    pxx = axis_x + xy + xz
    pyy = axis_y + xy + yz
    pzz = axis_z + xz + yz
    pxy = total[7] - total[9]
    pxz = total[11] - total[13]
    pyz = total[15] - total[17]
    dx, dy, dz = momentum(moved)
    vx = pxx * ux + pxy * uy + pxz * uz
    vy = pxy * ux + pyy * uy + pyz * uz
    vz = pxz * ux + pyz * uy + pzz * uz
    speed_sq = ux * ux + uy * uy + uz * uz
    scaled = (relax_rate / 36.0) * fluid
    base = scaled * (density + 1.5 * (speed_sq * density) - 4.5 * (ux * vx + uy * vy + uz * vz))
    scaled3 = 3.0 * scaled
    bx = scaled3 * (dx + 3.0 * vx - ux * density)
    by = scaled3 * (dy + 3.0 * vy - uy * density)
    bz = scaled3 * (dz + 3.0 * vz - uz * density)
    keep = (1.0 - relax_rate) * fluid
    results = [keep * moved[0] + base]
    for number in range(1, 19, 2):
        along = None
        for speed, part in zip(lattice_speeds[number], (bx, by, bz)):
            if speed == 0:
                continue
            if along is None:
                along = part if speed == 1 else -part
            else:
                along = along + part if speed == 1 else along - part
        results.append(keep * moved[number] + (base + along))
        results.append(keep * moved[number + 1] + (base - along))
    return results


def outside(cz):
    level = lax.broadcasted_iota(jnp.int32, (8, LANES), 0) % LEVELS
    return level == (LEVELS - 1 if cz == 1 else 0)


def link_closed(solid_there, cz):
    closed = solid_there > 0.5
    return closed | outside(cz) if cz != 0 else closed


def shift_lanes(value, cy, edge_value):
    lane = lane_index(value.shape[0])
    shifted = pltpu.roll(value, -cy % LANES, 1)
    if edge_value is None:
        return shifted
    return jnp.where(lane == (LANES - 1 if cy == 1 else 0), edge_value, shifted)


def gather_cells(held, shifted, first, solid_rows):
    here = [held[n, pl.ds(first, 8), :] for n in range(19)]
    moved, closed = [here[0]], [None]
    for number in range(1, 19):
        cx, cy, cz = lattice_speeds[number]
        field = held if cy == 0 else shifted
        there = pl.ds(first + LEVELS * cx + cz, 8)
        closed.append(link_closed(solid_rows[cy % 3, there, :], cz))
        bounced = here[opposite_of(number)]
        if cx != 0:
            bounced = bounced + 2.0 * cx
        moved.append(jnp.where(closed[number], bounced, field[number, there, :]))
    return moved, closed


def momentum(moved):
    gap = {n: moved[n] - moved[n + 1] for n in range(1, 19, 2)}
    dx = 2.0 * gap[1] + (gap[7] + gap[9]) + (gap[11] + gap[13])
    dy = 2.0 * gap[3] + (gap[7] - gap[9]) + (gap[15] + gap[17])
    dz = 2.0 * gap[5] + (gap[11] - gap[13]) + (gap[15] - gap[17])
    return dx, dy, dz


def drag_term(moved, flow, fluid):
    return fluid * sum(speed * part for speed, part in zip(flow, momentum(moved)))


def along_link(number, vector):
    total = None
    for axis, speed in enumerate(lattice_speeds[number]):
        if speed == 0:
            continue
        part = vector(axis)
        if total is None:
            total = part if speed == 1 else -part
        else:
            total = total + part if speed == 1 else total - part
    return total


def later_drag(results, closed, weight_here, weight_back):
    term = None
    for number in range(1, 19):
        cx = lattice_speeds[number][0]
        here = along_link(number, lambda axis: weight_here[axis])
        part = jnp.where(closed[opposite_of(number)], -here, weight_back(number)) * results[number]
        if cx != 0:
            part = part + jnp.where(closed[number], (2.0 * cx) * here, 0.0)
        if number < 7:
            part = 2.0 * part
        term = part if term is None else term + part
    return term


def column_reader(groups):
    def column(message, ahead, slot, lane_first, group=0):
        part, place = slot_place(slot, group, groups)
        return pltpu.roll(message[part], (lane_first - place - ahead) % LANES, 1)

    return column


def fill_held(own_held, before, after, held, rows):
    own = GUARD + 8
    near, far = own - LEVELS, own + rows
    for number in range(19):
        for group in range(rows // 8):
            there = pl.ds(own + 8 * group, 8)
            held[number, there, :] = own_held[number, there, :]
        held[number, pl.ds(near, LEVELS), :] = before[number]
        held[number, pl.ds(far, LEVELS), :] = after[number]
        if number in x_down:
            held[number, pl.ds(near - LEVELS, LEVELS), :] = before[SECOND + x_down.index(number)]
        if number in x_up:
            held[number, pl.ds(far + LEVELS, LEVELS), :] = after[SECOND + x_up.index(number)]


def fill_shifted(field, shifted, groups, edge_of):
    for number in y_up + y_down:
        cy = lattice_speeds[number][1]
        for group in range(groups):
            there = pl.ds(GUARD + 8 * group, 8)
            shifted[number, there, :] = shift_lanes(field[number, there, :], cy, edge_of(number, cy, group))


def fill_solid(solid_parts, before, after, solid_rows, groups, edge_of):
    for group in range(groups):
        first = GUARD + 8 * group
        if group in (0, groups - 1):
            halo = before[SOLID] if group == 0 else after[SOLID]
            solid_rows[0, pl.ds(first, LEVELS), :] = halo
            solid_rows[0, pl.ds(first + LEVELS, LEVELS), :] = halo
        else:
            solid_rows[0, pl.ds(first, 8), :] = solid_parts[(group - 1) * 8 // (LEVELS * TILE)]
        value = solid_rows[0, pl.ds(first, 8), :]
        for cy in (1, -1):
            solid_rows[cy % 3, pl.ds(first, 8), :] = shift_lanes(value, cy, edge_of(SOLID, cy, group))


def shift_rows(value, cx, cz):
    if cx != 0:
        upper = lax.broadcasted_iota(jnp.int32, (8, LANES), 0) < LEVELS
        swapped = pltpu.roll(value, LEVELS, 0)
        if cx == 1:
            value = jnp.where(upper, swapped, pltpu.roll(swapped, LANES - 1, 1))
        else:
            value = jnp.where(upper, pltpu.roll(swapped, 1, 1), swapped)
    if cz != 0:
        value = pltpu.roll(value, (-cz) % 8, 0)
    return value


def gather_columns(neighbours):
    here = [neighbours(n, 0) for n in range(19)]
    solid = {cy: neighbours(SOLID, cy) for cy in (0, 1, -1)}
    moved, closed = [here[0]], [None]
    for number in range(1, 19):
        cx, cy, cz = lattice_speeds[number]
        source = shift_rows(here[number] if cy == 0 else neighbours(number, cy), cx, cz)
        closed.append(link_closed(shift_rows(solid[cy], cx, cz), cz))
        moved.append(jnp.where(closed[number], here[opposite_of(number)] + 2.0 * cx, source))
    return moved, closed, solid


def inner_drag_kernel(
    own_held, velocity, solid, row_first, row_second, low, partial, own_blocks,
    held, shifted, solid_rows, weights,
):
    rows = velocity.shape[2]
    groups = rows // 8 + 2
    own = GUARD + 8
    near, far = own - LEVELS, own + rows
    even = on_even("gx")
    after, before = Chosen(even, row_first, row_second), Chosen(even, row_second, row_first)
    lane = lane_index()
    solid_parts = spread_solid(solid)

    def no_edge(slot, cy, group):
        return None

    fill_held(own_held, before, after, held, rows)
    fill_shifted(held, shifted, groups, no_edge)
    fill_solid(solid_parts, before, after, solid_rows, groups, no_edge)

    flow = flow_blocks(velocity, 1, rows)
    for axis in range(3):
        for group in range(rows // 8):
            there = pl.ds(own + 8 * group, 8)
            weights[axis, there, :] = (1.0 - solid_rows[0, there, :]) * flow[group][axis]
        for row, message in ((near, before), (far, after)):
            weights[axis, pl.ds(row, LEVELS), :] = (1.0 - message[SOLID]) * message[NEXT + axis]
        for group in range(groups):
            there = pl.ds(GUARD + 8 * group, 8)
            value = weights[axis, there, :]
            weights[3 + axis, there, :] = shift_lanes(value, 1, None)
            weights[6 + axis, there, :] = shift_lanes(value, -1, None)

    total = jnp.zeros((8, LANES), jnp.float32)
    flow = flow_blocks(velocity, 0, rows)
    for group in range(rows // 8):
        first = own + 8 * group
        moved, closed = gather_cells(held, shifted, first, solid_rows)
        fluid = 1.0 - solid_parts[8 * group // (LEVELS * TILE)]
        results = collide(moved, flow[group], fluid)

        def back(number):
            cx, cy, cz = lattice_speeds[number]
            there = pl.ds(first - LEVELS * cx - cz, 8)
            return along_link(number, lambda axis: weights[3 * (-cy % 3) + axis, there, :])

        here = [weights[axis, pl.ds(first, 8), :] for axis in range(3)]
        total = total + drag_term(moved, flow[group], fluid) + later_drag(results, closed, here, back)
    inside = jnp.logical_and(lane > 0, lane < LANES - 1)
    partial[...] = jnp.where(inside, total, 0.0)

    column = column_reader(groups)
    for slot in range(SECOND):
        own_blocks[slot] = column(low, 1, slot, AFTER_LANE)
    for place, slot in enumerate(ahead_slots):
        here = column(low, 1, slot, BEFORE_LANE)
        ahead = column(low, 1, second_slot(slot, y_up), AFTER_LANE)
        own_blocks[SECOND + place] = jnp.where(lane < AFTER_LANE, here, ahead)


ahead_slots = y_up + [SOLID, NEXT, NEXT + 1, NEXT + 2]


def second_slot(slot, moving):
    if slot in moving:
        return SECOND + moving.index(slot)
    return NEXT_SECOND + slot - NEXT if NEXT <= slot < NEXT + 3 else slot


def halo_lanes(groups, ahead):
    lane = lane_index()
    group = lax.rem(lane + groups - ahead, groups)
    used = jnp.logical_and(lane >= ahead, lane < LANES // groups * groups + ahead)
    return jnp.logical_and(used, group == 0), jnp.logical_and(used, group == groups - 1)


def hand_on_kernel(groups, ahead, columns, *rest):
    out = rest[-1]
    above, _ = halo_lanes(groups, ahead)
    for part in range(out.shape[0]):
        value = columns[part]
        last = pltpu.roll(value, LANES - (groups - 2), 1)
        out[part] = jnp.where(above, last, pltpu.roll(value, groups - 2, 1))


def with_halo_rows(columns, handed_first, handed_second, groups, ahead):
    even = on_even("gx")
    from_before = Chosen(even, handed_second, handed_first)
    from_after = Chosen(even, handed_first, handed_second)
    above, below = halo_lanes(groups, ahead)
    whole = []
    for part in range(handed_first.shape[0]):
        value = jnp.where(above, from_before[part], columns[part])
        whole.append(jnp.where(below, from_after[part], value))
    return whole


def edge_drag_kernel(groups, columns, handed_first, handed_second, own_blocks, partial, shared):
    lane = lane_index()
    column = column_reader(groups)
    y_before = with_halo_rows(columns, handed_first, handed_second, groups, 0)

    def neighbours(slot, cy):
        if cy == 1:
            return own_blocks[SECOND + ahead_slots.index(slot)]
        if cy == 0:
            first, second = column(y_before, 0, slot, BEFORE_LANE), own_blocks[slot]
        else:
            first = column(y_before, 0, second_slot(slot, y_down), BEFORE_LANE)
            second = column(y_before, 0, slot, AFTER_LANE)
        return jnp.where(lane < AFTER_LANE, first, second)

    moved, closed, solid_columns = gather_columns(neighbours)
    fluid = {cy: 1.0 - solid_columns[cy] for cy in (0, 1, -1)}
    flow = [neighbours(FLOW + axis, 0) for axis in range(3)]
    results = collide(moved, flow, fluid[0])
    weight = {cy: [fluid[cy] * neighbours(NEXT + axis, cy) for axis in range(3)] for cy in (0, 1, -1)}

    def back(number):
        cx, cy, cz = lattice_speeds[number]
        return shift_rows(along_link(number, lambda axis: weight[-cy][axis]), -cx, -cz)

    term = drag_term(moved, flow, fluid[0]) + later_drag(results, closed, weight[0], back)
    place = jnp.where(lane < AFTER_LANE, lane - BEFORE_LANE, lane - AFTER_LANE)
    inside = jnp.logical_and(place > 0, place < groups - 1)
    total = partial[...] + jnp.where(inside, term, 0.0)
    shared[...] = jnp.broadcast_to(jnp.sum(total), shared.shape)


def main_kernel(
    own_held, velocity, solid, row_first, row_second, columns, handed_first, handed_second,
    columns_after, after_first, after_second, low, high, out, held, shifted, later, solid_rows, row_flow,
):
    rows = velocity.shape[2]
    groups = rows // 8 + 2
    own = GUARD + 8
    near, far = own - LEVELS, own + rows
    even = on_even("gx")
    after, before = Chosen(even, row_first, row_second), Chosen(even, row_second, row_first)
    lane = lane_index()
    solid_parts = spread_solid(solid)
    column = column_reader(groups)
    y_before = with_halo_rows(columns, handed_first, handed_second, groups, 0)
    y_after = with_halo_rows(columns_after, after_first, after_second, groups, 1)

    def edge_of(slot, cy, group):
        if cy == 1:
            return column(y_after, 1, slot, LANES - 1, group)
        return column(y_before, 0, slot, 0, group)

    fill_held(own_held, before, after, held, rows)
    fill_shifted(held, shifted, groups, edge_of)
    fill_solid(solid_parts, before, after, solid_rows, groups, edge_of)
    for slot, place in ((FLOW, 0), (FLOW + 1, 1), (FLOW + 2, 2), (SOLID, 3)):
        row_flow[place, pl.ds(0, LEVELS), :] = before[slot]
        row_flow[place, pl.ds(LEVELS, LEVELS), :] = after[slot]

    def both_rows(field, index, shift):
        ends = [field[index, pl.ds(place + shift, LEVELS), :] for place in (near, far)]
        return jnp.concatenate(ends, axis=0)

    here = [both_rows(held, n, 0) for n in range(19)]
    moved = [here[0]]
    for number in range(1, 19):
        cx, cy, cz = lattice_speeds[number]
        shift = LEVELS * cx + cz
        source = both_rows(held if cy == 0 else shifted, number, shift)
        closed = link_closed(both_rows(solid_rows, cy % 3, shift), cz)
        moved.append(jnp.where(closed, here[opposite_of(number)] + 2.0 * cx, source))
    row_results = collide(moved, [row_flow[axis] for axis in range(3)], 1.0 - row_flow[3])

    def neighbours(slot, cy):
        beyond = slot if cy == 0 or slot == SOLID else SECOND + (y_up if cy == 1 else y_down).index(slot)
        if cy == 1:
            first, second = column(low, 1, slot, BEFORE_LANE), column(y_after, 1, beyond, AFTER_LANE)
        elif cy == -1:
            first, second = column(y_before, 0, beyond, BEFORE_LANE), column(high, 0, slot, AFTER_LANE)
        else:
            first, second = column(y_before, 0, slot, BEFORE_LANE), column(y_after, 1, slot, AFTER_LANE)
        return jnp.where(lane < AFTER_LANE, first, second)

    moved, _, solid_columns = gather_columns(neighbours)
    column_flow = [neighbours(FLOW + axis, 0) for axis in range(3)]
    column_results = collide(moved, column_flow, 1.0 - solid_columns[0])

    flow = flow_blocks(velocity, 0, rows)
    for group in range(rows // 8):
        first = own + 8 * group
        moved, _ = gather_cells(held, shifted, first, solid_rows)
        results = collide(moved, flow[group], 1.0 - solid_parts[8 * group // (LEVELS * TILE)])
        for number in range(19):
            later[number, pl.ds(first, 8), :] = results[number]
    for number in x_down:
        later[number, pl.ds(near, LEVELS), :] = row_results[number][:LEVELS]
    for number in x_up:
        later[number, pl.ds(far, LEVELS), :] = row_results[number][LEVELS:]

    def later_edge(number, cy, group):
        shift = LANES - 1 - AFTER_LANE - group if cy == 1 else -BEFORE_LANE - group
        return pltpu.roll(column_results[number], shift % LANES, 1)

    fill_shifted(later, shifted, groups, later_edge)

    flow = flow_blocks(velocity, 1, rows)
    for group in range(rows // 8):
        first = 8 * group
        moved, _ = gather_cells(later, shifted, own + first, solid_rows)
        results = collide(moved, flow[group], 1.0 - solid_parts[first // (LEVELS * TILE)])
        for number in range(19):
            out[number, pl.ds(first, 8), :] = results[number]


def swap_pairs(first, second, axis):
    count = lax.axis_size(axis)
    inside = [(i, i ^ 1) for i in range(count)]
    across = [(i, (i + 1) % count if i % 2 == 1 else (i - 1) % count) for i in range(count)]
    second = lax.ppermute(second, axis, across)
    return lax.ppermute(first, axis, inside), second


def per_device(adjoint_in, velocity, solid_tiles, link_blocked):
    rows_x, levels, rows_y = adjoint_in.shape[1:]
    rows = rows_x * levels
    padded = rows + 16 + 2 * GUARD
    groups = rows // 8 + 2
    parts = -(-COLUMN_QUANTITIES // (LANES // groups))
    state = adjoint_in.reshape(19, rows, rows_y)
    flow = velocity.reshape(STEPS, 3, rows, rows_y)
    solid = solid_tiles.reshape(-1, solid_tiles.shape[2])

    def shape_of(*sizes):
        return jax.ShapeDtypeStruct(sizes, jnp.float32)

    params = pltpu.CompilerParams(vmem_limit_bytes=16 * 1024 * 1024)
    anywhere = pl.BlockSpec(memory_space=pl.ANY)
    own_high, held, flow, tiles = pl.pallas_call(
        first_columns_kernel,
        out_shape=(
            pltpu.VMEM((parts, 8, rows_y), jnp.float32),
            pltpu.VMEM((19, padded, rows_y), jnp.float32),
            pltpu.VMEM(flow.shape, flow.dtype),
            pltpu.VMEM(solid.shape, solid.dtype),
        ),
        in_specs=[anywhere] * 3,
        out_specs=(vmem,) * 4,
        scratch_shapes=[pltpu.SemaphoreType.DMA((6,))],
        compiler_params=params,
    )(*(pltpu.with_memory_space_constraint(value, pltpu.HBM) for value in (state, flow, solid)))
    row_sent = pl.pallas_call(
        row_message_kernel,
        out_shape=(pltpu.VMEM((QUANTITIES, levels, rows_y), jnp.float32),) * 2,
        in_specs=[vmem] * 3,
        out_specs=(vmem,) * 2,
        compiler_params=params,
    )(held, flow, tiles)
    row_got = swap_pairs(*row_sent, "gx")
    own_low = pl.pallas_call(
        own_columns_kernel,
        out_shape=shape_of(16, 8, rows_y),
        in_specs=[vmem] * 4,
        out_specs=vmem,
        compiler_params=params,
        cost_estimate=pl.CostEstimate(flops=2_000_000, bytes_accessed=1_000_000, transcendentals=0),
    )(held, flow, tiles, row_sent[0])
    own_columns = own_low, own_high
    low, high = pl.pallas_call(
        functools.partial(halo_columns_kernel, groups),
        out_shape=(shape_of(parts, 8, rows_y),) * 2,
        in_specs=[vmem] * 4,
        out_specs=(vmem,) * 2,
        scratch_shapes=[pltpu.VMEM((2, SECOND, 8, rows_y), jnp.float32)],
        compiler_params=params,
    )(*own_columns, *row_got)
    size = lax.axis_size("gy")
    y_before = lax.ppermute(own_columns[1], "gy", [(i, (i + 1) % size) for i in range(size)])
    def hand_on(columns, ahead, *later_than):
        handed = pl.pallas_call(
            functools.partial(hand_on_kernel, groups, ahead),
            out_shape=shape_of(parts, 8, rows_y),
            in_specs=[vmem] * (1 + len(later_than)),
            out_specs=vmem,
            compiler_params=params,
            cost_estimate=pl.CostEstimate(flops=10_000_000_000, bytes_accessed=100_000, transcendentals=0),
        )(columns, *later_than)
        return swap_pairs(handed, handed, "gx")

    handed = hand_on(y_before, 0)
    y_after = lax.ppermute(own_columns[0], "gy", [((i + 1) % size, i) for i in range(size)])
    count = lax.axis_size("gx") * size
    field = pltpu.VMEM((19, padded, rows_y), jnp.float32)
    solid_field = pltpu.VMEM((3, padded, rows_y), jnp.float32)
    partial, own_blocks = pl.pallas_call(
        inner_drag_kernel,
        out_shape=(
            pltpu.VMEM((8, rows_y), jnp.float32),
            pltpu.VMEM((SECOND + len(ahead_slots), 8, rows_y), jnp.float32),
        ),
        in_specs=[vmem] * 6,
        out_specs=(vmem,) * 2,
        scratch_shapes=[field, field, solid_field, pltpu.VMEM((9, padded, rows_y), jnp.float32)],
        compiler_params=params,
        cost_estimate=pl.CostEstimate(flops=20_000_000_000, bytes_accessed=1_000_000, transcendentals=0),
    )(held, flow, tiles, *row_got, low)
    own = pl.pallas_call(
        functools.partial(edge_drag_kernel, groups),
        out_shape=pltpu.VMEM((count, 1, rows_y), jnp.float32),
        in_specs=[vmem] * 5,
        out_specs=vmem,
        compiler_params=params,
        cost_estimate=pl.CostEstimate(flops=1_000_000, bytes_accessed=1_000_000, transcendentals=0),
    )(y_before, *handed, own_blocks, partial)
    handed_after = hand_on(y_after, 1, own)
    shared = lax.all_to_all(own, ("gx", "gy"), split_axis=0, concat_axis=0, tiled=True)
    result = pl.pallas_call(
        main_kernel,
        out_shape=shape_of(19, rows, rows_y),
        in_specs=[vmem] * 13,
        out_specs=vmem,
        scratch_shapes=[field, field, field, solid_field, pltpu.VMEM((4, 8, rows_y), jnp.float32)],
        compiler_params=params,
        cost_estimate=pl.CostEstimate(flops=1_000_000, bytes_accessed=1_000_000, transcendentals=0),
    )(held, flow, tiles, *row_got, y_before, *handed, y_after, *handed_after, low, high)
    cell_count = rows * rows_y * count
    scale = drag_factor / math.sqrt(cell_count) * 3.0 / 36.0
    total = jnp.sum(shared[:, 0, 0])
    return (result.reshape(adjoint_in.shape), (-scale * total).reshape(1))


def solution(mesh):
    placed = (
        P(None, "gx", None, "gy"),
        P(None, None, "gx", None, "gy"),
        P("gx", None, "gy"),
        P(None, "gx", None, "gy"),
    )
    return jax.shard_map(
        per_device,
        mesh=mesh,
        in_specs=placed,
        out_specs=(P(None, "gx", None, "gy"), P()),
        check_vma=False,
    )
```

```python
import functools
import math

import jax
import jax.numpy as jnp
from jax import lax
from jax.experimental import pallas as pl
from jax.experimental.pallas import tpu as pltpu
from jax.sharding import PartitionSpec as P

TILE = 4
STEPS = 2

lattice_speeds = (
    (0, 0, 0),
    (1, 0, 0),
    (-1, 0, 0),
    (0, 1, 0),
    (0, -1, 0),
    (0, 0, 1),
    (0, 0, -1),
    (1, 1, 0),
    (-1, -1, 0),
    (1, -1, 0),
    (-1, 1, 0),
    (1, 0, 1),
    (-1, 0, -1),
    (1, 0, -1),
    (-1, 0, 1),
    (0, 1, 1),
    (0, -1, -1),
    (0, 1, -1),
    (0, -1, 1),
)
relax_rate = 1.6
drag_factor = 20.0
LEVELS = 4
LANES = 128
GUARD = 8

x_up = [n for n in range(19) if lattice_speeds[n][0] == 1]
x_down = [n for n in range(19) if lattice_speeds[n][0] == -1]
y_up = [n for n in range(19) if lattice_speeds[n][1] == 1]
y_down = [n for n in range(19) if lattice_speeds[n][1] == -1]
vmem = pl.BlockSpec(memory_space=pltpu.VMEM)

FLOW = 19
SOLID = 22
NEXT = 23
SECOND = 26
QUANTITIES = 31
NEXT_SECOND = 31
COLUMN_QUANTITIES = 34
BEFORE_LANE = 16
AFTER_LANE = 32


def opposite_of(number):
    return number + 1 if number % 2 == 1 else number - 1


def lane_index(rows=8):
    return lax.broadcasted_iota(jnp.int32, (rows, LANES), 1)


def spread_solid(solid):
    tiles = solid.shape[1]
    row = lax.broadcasted_iota(jnp.int32, (tiles, LANES), 0)
    column = lax.broadcasted_iota(jnp.int32, (tiles, LANES), 1)
    spread = (column // TILE == row).astype(jnp.float32)
    cells = jnp.dot(solid[...].astype(jnp.float32), spread, preferred_element_type=jnp.float32)
    blocks = []
    for tile_row in range(solid.shape[0] // LEVELS):
        part = cells[tile_row * LEVELS : (tile_row + 1) * LEVELS]
        blocks.append(jnp.concatenate([part, part], axis=0))
    return blocks


def flow_blocks(velocity, step, rows):
    blocks = []
    for pair in range(rows // 16):
        both = [velocity[step, axis, pl.ds(16 * pair, 16), :].astype(jnp.float32) for axis in range(3)]
        blocks.append([part[:8] for part in both])
        blocks.append([part[8:] for part in both])
    return blocks


def on_even(axis):
    return lax.rem(lax.axis_index(axis), 2) == 0


class Chosen:
    def __init__(self, choice, yes, no):
        self.choice, self.yes, self.no = choice, yes, no
        self.shape = yes.shape

    def __getitem__(self, index):
        return jnp.where(self.choice, self.yes[index], self.no[index])


def slot_place(slot, group, groups):
    per_block = LANES // groups
    return slot // per_block, (slot % per_block) * groups + group


def insert_column(parts, slot, group, groups, value, edge, ahead):
    part, place = slot_place(slot, group, groups)
    lane = lane_index()
    turned = pltpu.roll(value, (place + ahead - edge) % LANES, 1)
    parts[part] = jnp.where(lane == place + ahead, turned, parts[part])


def row_message_kernel(
    state, velocity, solid, row_first, row_second, held, flow, tiles, arrived
):
    rows = state.shape[1]
    own = pl.ds(GUARD + 8, rows)
    copies = [
        pltpu.make_async_copy(state, held.at[:, own, :], arrived.at[0]),
        pltpu.make_async_copy(velocity, flow, arrived.at[1]),
        pltpu.make_async_copy(solid, tiles, arrived.at[2]),
    ]
    for copy in copies:
        copy.start()
    for copy in copies:
        copy.wait()
    even = on_even("gx")
    low_row, high_row = GUARD + 8, GUARD + 8 + rows - LEVELS

    def put(slot, low, high):
        row_first[slot] = jnp.where(even, high, low)
        row_second[slot] = jnp.where(even, low, high)

    for number in range(19):
        put(number, held[number, pl.ds(low_row, LEVELS), :], held[number, pl.ds(high_row, LEVELS), :])
    for step, slot in ((0, FLOW), (1, NEXT)):
        for axis in range(3):
            low = flow[step, axis, pl.ds(0, 16), :].astype(jnp.float32)
            high = flow[step, axis, pl.ds(rows - 16, 16), :].astype(jnp.float32)
            put(slot + axis, low[:LEVELS], high[16 - LEVELS :])
    solid_parts = spread_solid(tiles)
    put(SOLID, solid_parts[0][:LEVELS], solid_parts[-1][:LEVELS])
    for slot in range(5):
        put(
            SECOND + slot,
            held[x_up[slot], pl.ds(low_row + LEVELS, LEVELS), :],
            held[x_down[slot], pl.ds(high_row - LEVELS, LEVELS), :],
        )


def pack_columns(parts, slot, group, groups, value):
    for message, edge, step, ahead, moving in ((parts[0], 0, 1, 1, y_up), (parts[1], LANES - 1, -1, 0, y_down)):
        if message is None:
            continue
        insert_column(message, slot, group, groups, value, edge, ahead)
        second = second_slot(slot, moving)
        if second != slot:
            insert_column(message, second, group, groups, value, edge + step, ahead)


def own_columns_kernel(side, held, velocity, solid, *rest):
    out = rest[-1]
    rows = velocity.shape[2]
    groups = rows // 8 + 2
    solid_parts = spread_solid(solid)
    flow = [flow_blocks(velocity, step, rows) for step in range(2)]
    parts = [None, None]
    parts[side] = [jnp.zeros((8, LANES), jnp.float32) for _ in range(out.shape[0])]
    for group in range(1, groups - 1):
        for slot in range(19):
            pack_columns(parts, slot, group, groups, held[slot, pl.ds(GUARD + 8 * group, 8), :])
        for axis in range(3):
            pack_columns(parts, FLOW + axis, group, groups, flow[0][group - 1][axis])
            pack_columns(parts, NEXT + axis, group, groups, flow[1][group - 1][axis])
        pack_columns(parts, SOLID, group, groups, solid_parts[(group - 1) * 8 // (LEVELS * TILE)])
    for part in range(out.shape[0]):
        out[part] = parts[side][part]


def halo_columns_kernel(groups, own_low, own_high, row_first, row_second, low_out, high_out, ends):
    count = own_high.shape[0]
    even = on_even("gx")
    after, before = Chosen(even, row_first, row_second), Chosen(even, row_second, row_first)
    parts = [[own_low[part] for part in range(count)], [own_high[part] for part in range(count)]]
    for slot in range(SECOND):
        ends[0, slot, pl.ds(LEVELS, LEVELS), :] = before[slot]
        ends[1, slot, pl.ds(0, LEVELS), :] = after[slot]
        if slot == SOLID:
            low_second, high_second = SOLID, SOLID
        else:
            low_second = SECOND + x_down.index(slot) if slot in x_down else None
            high_second = SECOND + x_up.index(slot) if slot in x_up else None
        blank = jnp.zeros((LEVELS, LANES), jnp.float32)
        ends[0, slot, pl.ds(0, LEVELS), :] = blank if low_second is None else before[low_second]
        ends[1, slot, pl.ds(LEVELS, LEVELS), :] = blank if high_second is None else after[high_second]
        pack_columns(parts, slot, 0, groups, ends[0, slot])
        pack_columns(parts, slot, groups - 1, groups, ends[1, slot])
    for part in range(count):
        low_out[part] = parts[0][part]
        high_out[part] = parts[1][part]


def collide(moved, flow, fluid):
    ux, uy, uz = flow
    total = {n: moved[n] + moved[n + 1] for n in range(1, 19, 2)}
    xy, xz, yz = total[7] + total[9], total[11] + total[13], total[15] + total[17]
    axis_x, axis_y, axis_z = 2.0 * total[1], 2.0 * total[3], 2.0 * total[5]
    density = 12.0 * moved[0] + (axis_x + axis_y + axis_z) + (xy + xz + yz)
    pxx = axis_x + xy + xz
    pyy = axis_y + xy + yz
    pzz = axis_z + xz + yz
    pxy = total[7] - total[9]
    pxz = total[11] - total[13]
    pyz = total[15] - total[17]
    dx, dy, dz = momentum(moved)
    vx = pxx * ux + pxy * uy + pxz * uz
    vy = pxy * ux + pyy * uy + pyz * uz
    vz = pxz * ux + pyz * uy + pzz * uz
    speed_sq = ux * ux + uy * uy + uz * uz
    scaled = (relax_rate / 36.0) * fluid
    base = scaled * (density + 1.5 * (speed_sq * density) - 4.5 * (ux * vx + uy * vy + uz * vz))
    scaled3 = 3.0 * scaled
    bx = scaled3 * (dx + 3.0 * vx - ux * density)
    by = scaled3 * (dy + 3.0 * vy - uy * density)
    bz = scaled3 * (dz + 3.0 * vz - uz * density)
    keep = (1.0 - relax_rate) * fluid
    results = [keep * moved[0] + base]
    for number in range(1, 19, 2):
        along = None
        for speed, part in zip(lattice_speeds[number], (bx, by, bz)):
            if speed == 0:
                continue
            if along is None:
                along = part if speed == 1 else -part
            else:
                along = along + part if speed == 1 else along - part
        results.append(keep * moved[number] + (base + along))
        results.append(keep * moved[number + 1] + (base - along))
    return results


def outside(cz):
    level = lax.broadcasted_iota(jnp.int32, (8, LANES), 0) % LEVELS
    return level == (LEVELS - 1 if cz == 1 else 0)


def link_closed(solid_there, cz):
    closed = solid_there > 0.5
    return closed | outside(cz) if cz != 0 else closed


def shift_lanes(value, cy, edge_value):
    lane = lane_index(value.shape[0])
    shifted = pltpu.roll(value, -cy % LANES, 1)
    if edge_value is None:
        return shifted
    return jnp.where(lane == (LANES - 1 if cy == 1 else 0), edge_value, shifted)


def gather_cells(held, shifted, first, solid_rows):
    here = [held[n, pl.ds(first, 8), :] for n in range(19)]
    moved, closed = [here[0]], [None]
    for number in range(1, 19):
        cx, cy, cz = lattice_speeds[number]
        field = held if cy == 0 else shifted
        there = pl.ds(first + LEVELS * cx + cz, 8)
        closed.append(link_closed(solid_rows[cy % 3, there, :], cz))
        bounced = here[opposite_of(number)]
        if cx != 0:
            bounced = bounced + 2.0 * cx
        moved.append(jnp.where(closed[number], bounced, field[number, there, :]))
    return moved, closed


def momentum(moved):
    gap = {n: moved[n] - moved[n + 1] for n in range(1, 19, 2)}
    dx = 2.0 * gap[1] + (gap[7] + gap[9]) + (gap[11] + gap[13])
    dy = 2.0 * gap[3] + (gap[7] - gap[9]) + (gap[15] + gap[17])
    dz = 2.0 * gap[5] + (gap[11] - gap[13]) + (gap[15] - gap[17])
    return dx, dy, dz


def drag_term(moved, flow, fluid):
    return fluid * sum(speed * part for speed, part in zip(flow, momentum(moved)))


def along_link(number, vector):
    total = None
    for axis, speed in enumerate(lattice_speeds[number]):
        if speed == 0:
            continue
        part = vector(axis)
        if total is None:
            total = part if speed == 1 else -part
        else:
            total = total + part if speed == 1 else total - part
    return total


def later_drag(results, closed, weight_here, weight_back):
    term = None
    for number in range(1, 19):
        cx = lattice_speeds[number][0]
        here = along_link(number, lambda axis: weight_here[axis])
        part = jnp.where(closed[opposite_of(number)], -here, weight_back(number)) * results[number]
        if cx != 0:
            part = part + jnp.where(closed[number], (2.0 * cx) * here, 0.0)
        if number < 7:
            part = 2.0 * part
        term = part if term is None else term + part
    return term


def column_reader(groups):
    def column(message, ahead, slot, lane_first, group=0):
        part, place = slot_place(slot, group, groups)
        return pltpu.roll(message[part], (lane_first - place - ahead) % LANES, 1)

    return column


def fill_held(own_held, before, after, held, rows):
    own = GUARD + 8
    near, far = own - LEVELS, own + rows
    for number in range(19):
        for group in range(rows // 8):
            there = pl.ds(own + 8 * group, 8)
            held[number, there, :] = own_held[number, there, :]
        held[number, pl.ds(near, LEVELS), :] = before[number]
        held[number, pl.ds(far, LEVELS), :] = after[number]
        if number in x_down:
            held[number, pl.ds(near - LEVELS, LEVELS), :] = before[SECOND + x_down.index(number)]
        if number in x_up:
            held[number, pl.ds(far + LEVELS, LEVELS), :] = after[SECOND + x_up.index(number)]


def fill_shifted(field, shifted, groups, edge_of):
    for number in y_up + y_down:
        cy = lattice_speeds[number][1]
        for group in range(groups):
            there = pl.ds(GUARD + 8 * group, 8)
            shifted[number, there, :] = shift_lanes(field[number, there, :], cy, edge_of(number, cy, group))


def fill_solid(solid_parts, before, after, solid_rows, groups, edge_of):
    for group in range(groups):
        first = GUARD + 8 * group
        if group in (0, groups - 1):
            halo = before[SOLID] if group == 0 else after[SOLID]
            solid_rows[0, pl.ds(first, LEVELS), :] = halo
            solid_rows[0, pl.ds(first + LEVELS, LEVELS), :] = halo
        else:
            solid_rows[0, pl.ds(first, 8), :] = solid_parts[(group - 1) * 8 // (LEVELS * TILE)]
        value = solid_rows[0, pl.ds(first, 8), :]
        for cy in (1, -1):
            solid_rows[cy % 3, pl.ds(first, 8), :] = shift_lanes(value, cy, edge_of(SOLID, cy, group))


def shift_rows(value, cx, cz):
    if cx != 0:
        upper = lax.broadcasted_iota(jnp.int32, (8, LANES), 0) < LEVELS
        swapped = pltpu.roll(value, LEVELS, 0)
        if cx == 1:
            value = jnp.where(upper, swapped, pltpu.roll(swapped, LANES - 1, 1))
        else:
            value = jnp.where(upper, pltpu.roll(swapped, 1, 1), swapped)
    if cz != 0:
        value = pltpu.roll(value, (-cz) % 8, 0)
    return value


def gather_columns(neighbours):
    here = [neighbours(n, 0) for n in range(19)]
    solid = {cy: neighbours(SOLID, cy) for cy in (0, 1, -1)}
    moved, closed = [here[0]], [None]
    for number in range(1, 19):
        cx, cy, cz = lattice_speeds[number]
        source = shift_rows(here[number] if cy == 0 else neighbours(number, cy), cx, cz)
        closed.append(link_closed(shift_rows(solid[cy], cx, cz), cz))
        moved.append(jnp.where(closed[number], here[opposite_of(number)] + 2.0 * cx, source))
    return moved, closed, solid


def inner_drag_kernel(
    own_held, velocity, solid, row_first, row_second, low, partial, own_blocks,
    held, shifted, solid_rows, weights,
):
    rows = velocity.shape[2]
    groups = rows // 8 + 2
    own = GUARD + 8
    near, far = own - LEVELS, own + rows
    even = on_even("gx")
    after, before = Chosen(even, row_first, row_second), Chosen(even, row_second, row_first)
    lane = lane_index()
    solid_parts = spread_solid(solid)

    def no_edge(slot, cy, group):
        return None

    fill_held(own_held, before, after, held, rows)
    fill_shifted(held, shifted, groups, no_edge)
    fill_solid(solid_parts, before, after, solid_rows, groups, no_edge)

    flow = flow_blocks(velocity, 1, rows)
    for axis in range(3):
        for group in range(rows // 8):
            there = pl.ds(own + 8 * group, 8)
            weights[axis, there, :] = (1.0 - solid_rows[0, there, :]) * flow[group][axis]
        for row, message in ((near, before), (far, after)):
            weights[axis, pl.ds(row, LEVELS), :] = (1.0 - message[SOLID]) * message[NEXT + axis]
        for group in range(groups):
            there = pl.ds(GUARD + 8 * group, 8)
            value = weights[axis, there, :]
            weights[3 + axis, there, :] = shift_lanes(value, 1, None)
            weights[6 + axis, there, :] = shift_lanes(value, -1, None)

    total = jnp.zeros((8, LANES), jnp.float32)
    flow = flow_blocks(velocity, 0, rows)
    for group in range(rows // 8):
        first = own + 8 * group
        moved, closed = gather_cells(held, shifted, first, solid_rows)
        fluid = 1.0 - solid_parts[8 * group // (LEVELS * TILE)]
        results = collide(moved, flow[group], fluid)

        def back(number):
            cx, cy, cz = lattice_speeds[number]
            there = pl.ds(first - LEVELS * cx - cz, 8)
            return along_link(number, lambda axis: weights[3 * (-cy % 3) + axis, there, :])

        here = [weights[axis, pl.ds(first, 8), :] for axis in range(3)]
        total = total + drag_term(moved, flow[group], fluid) + later_drag(results, closed, here, back)
    inside = jnp.logical_and(lane > 0, lane < LANES - 1)
    partial[...] = jnp.where(inside, total, 0.0)

    column = column_reader(groups)
    for slot in range(SECOND):
        own_blocks[slot] = column(low, 1, slot, AFTER_LANE)
    for place, slot in enumerate(ahead_slots):
        here = column(low, 1, slot, BEFORE_LANE)
        ahead = column(low, 1, second_slot(slot, y_up), AFTER_LANE)
        own_blocks[SECOND + place] = jnp.where(lane < AFTER_LANE, here, ahead)


ahead_slots = y_up + [SOLID, NEXT, NEXT + 1, NEXT + 2]


def second_slot(slot, moving):
    if slot in moving:
        return SECOND + moving.index(slot)
    return NEXT_SECOND + slot - NEXT if NEXT <= slot < NEXT + 3 else slot


def halo_lanes(groups, ahead):
    lane = lane_index()
    group = lax.rem(lane + groups - ahead, groups)
    used = jnp.logical_and(lane >= ahead, lane < LANES // groups * groups + ahead)
    return jnp.logical_and(used, group == 0), jnp.logical_and(used, group == groups - 1)


def hand_on_kernel(groups, ahead, columns, *rest):
    out = rest[-1]
    above, _ = halo_lanes(groups, ahead)
    for part in range(out.shape[0]):
        value = columns[part]
        last = pltpu.roll(value, LANES - (groups - 2), 1)
        out[part] = jnp.where(above, last, pltpu.roll(value, groups - 2, 1))


def with_halo_rows(columns, handed_first, handed_second, groups, ahead):
    even = on_even("gx")
    from_before = Chosen(even, handed_second, handed_first)
    from_after = Chosen(even, handed_first, handed_second)
    above, below = halo_lanes(groups, ahead)
    whole = []
    for part in range(handed_first.shape[0]):
        value = jnp.where(above, from_before[part], columns[part])
        whole.append(jnp.where(below, from_after[part], value))
    return whole


def with_diagonals(columns, from_before, from_after, groups):
    above, below = halo_lanes(groups, 0)
    whole = []
    for part in range(columns.shape[0]):
        last = pltpu.roll(from_before[part], LANES - (groups - 2), 1)
        first = pltpu.roll(from_after[part], groups - 2, 1)
        whole.append(jnp.where(above, last, jnp.where(below, first, columns[part])))
    return whole


def edge_drag_kernel(groups, columns, diagonal_before, diagonal_after, own_blocks, partial, shared):
    lane = lane_index()
    column = column_reader(groups)
    y_before = with_diagonals(columns, diagonal_before, diagonal_after, groups)

    def neighbours(slot, cy):
        if cy == 1:
            return own_blocks[SECOND + ahead_slots.index(slot)]
        if cy == 0:
            first, second = column(y_before, 0, slot, BEFORE_LANE), own_blocks[slot]
        else:
            first = column(y_before, 0, second_slot(slot, y_down), BEFORE_LANE)
            second = column(y_before, 0, slot, AFTER_LANE)
        return jnp.where(lane < AFTER_LANE, first, second)

    moved, closed, solid_columns = gather_columns(neighbours)
    fluid = {cy: 1.0 - solid_columns[cy] for cy in (0, 1, -1)}
    flow = [neighbours(FLOW + axis, 0) for axis in range(3)]
    results = collide(moved, flow, fluid[0])
    weight = {cy: [fluid[cy] * neighbours(NEXT + axis, cy) for axis in range(3)] for cy in (0, 1, -1)}

    def back(number):
        cx, cy, cz = lattice_speeds[number]
        return shift_rows(along_link(number, lambda axis: weight[-cy][axis]), -cx, -cz)

    term = drag_term(moved, flow, fluid[0]) + later_drag(results, closed, weight[0], back)
    place = jnp.where(lane < AFTER_LANE, lane - BEFORE_LANE, lane - AFTER_LANE)
    inside = jnp.logical_and(place > 0, place < groups - 1)
    total = partial[...] + jnp.where(inside, term, 0.0)
    shared[...] = jnp.broadcast_to(jnp.sum(total), shared.shape)


def main_kernel(
    own_held, velocity, solid, row_first, row_second, columns, diagonal_before, diagonal_after,
    columns_after, after_first, after_second, low, high, out, held, shifted, later, solid_rows, row_flow,
):
    rows = velocity.shape[2]
    groups = rows // 8 + 2
    own = GUARD + 8
    near, far = own - LEVELS, own + rows
    even = on_even("gx")
    after, before = Chosen(even, row_first, row_second), Chosen(even, row_second, row_first)
    lane = lane_index()
    solid_parts = spread_solid(solid)
    column = column_reader(groups)
    y_before = with_diagonals(columns, diagonal_before, diagonal_after, groups)
    y_after = with_halo_rows(columns_after, after_first, after_second, groups, 1)

    def edge_of(slot, cy, group):
        if cy == 1:
            return column(y_after, 1, slot, LANES - 1, group)
        return column(y_before, 0, slot, 0, group)

    fill_held(own_held, before, after, held, rows)
    fill_shifted(held, shifted, groups, edge_of)
    fill_solid(solid_parts, before, after, solid_rows, groups, edge_of)
    for slot, place in ((FLOW, 0), (FLOW + 1, 1), (FLOW + 2, 2), (SOLID, 3)):
        row_flow[place, pl.ds(0, LEVELS), :] = before[slot]
        row_flow[place, pl.ds(LEVELS, LEVELS), :] = after[slot]

    def both_rows(field, index, shift):
        ends = [field[index, pl.ds(place + shift, LEVELS), :] for place in (near, far)]
        return jnp.concatenate(ends, axis=0)

    here = [both_rows(held, n, 0) for n in range(19)]
    moved = [here[0]]
    for number in range(1, 19):
        cx, cy, cz = lattice_speeds[number]
        shift = LEVELS * cx + cz
        source = both_rows(held if cy == 0 else shifted, number, shift)
        closed = link_closed(both_rows(solid_rows, cy % 3, shift), cz)
        moved.append(jnp.where(closed, here[opposite_of(number)] + 2.0 * cx, source))
    row_results = collide(moved, [row_flow[axis] for axis in range(3)], 1.0 - row_flow[3])

    def neighbours(slot, cy):
        beyond = slot if cy == 0 or slot == SOLID else SECOND + (y_up if cy == 1 else y_down).index(slot)
        if cy == 1:
            first, second = column(low, 1, slot, BEFORE_LANE), column(y_after, 1, beyond, AFTER_LANE)
        elif cy == -1:
            first, second = column(y_before, 0, beyond, BEFORE_LANE), column(high, 0, slot, AFTER_LANE)
        else:
            first, second = column(y_before, 0, slot, BEFORE_LANE), column(y_after, 1, slot, AFTER_LANE)
        return jnp.where(lane < AFTER_LANE, first, second)

    moved, _, solid_columns = gather_columns(neighbours)
    column_flow = [neighbours(FLOW + axis, 0) for axis in range(3)]
    column_results = collide(moved, column_flow, 1.0 - solid_columns[0])

    flow = flow_blocks(velocity, 0, rows)
    for group in range(rows // 8):
        first = own + 8 * group
        moved, _ = gather_cells(held, shifted, first, solid_rows)
        results = collide(moved, flow[group], 1.0 - solid_parts[8 * group // (LEVELS * TILE)])
        for number in range(19):
            later[number, pl.ds(first, 8), :] = results[number]
    for number in x_down:
        later[number, pl.ds(near, LEVELS), :] = row_results[number][:LEVELS]
    for number in x_up:
        later[number, pl.ds(far, LEVELS), :] = row_results[number][LEVELS:]

    def later_edge(number, cy, group):
        shift = LANES - 1 - AFTER_LANE - group if cy == 1 else -BEFORE_LANE - group
        return pltpu.roll(column_results[number], shift % LANES, 1)

    fill_shifted(later, shifted, groups, later_edge)

    flow = flow_blocks(velocity, 1, rows)
    for group in range(rows // 8):
        first = 8 * group
        moved, _ = gather_cells(later, shifted, own + first, solid_rows)
        results = collide(moved, flow[group], 1.0 - solid_parts[first // (LEVELS * TILE)])
        for number in range(19):
            out[number, pl.ds(first, 8), :] = results[number]


def swap_pairs(first, second, axis):
    count = lax.axis_size(axis)
    inside = [(i, i ^ 1) for i in range(count)]
    across = [(i, (i + 1) % count if i % 2 == 1 else (i - 1) % count) for i in range(count)]
    second = lax.ppermute(second, axis, across)
    return lax.ppermute(first, axis, inside), second


def from_diagonal(value, side):
    nx, ny = lax.axis_size("gx"), lax.axis_size("gy")
    pairs = [
        (i * ny + j, (i + side) % nx * ny + (j + 1) % ny) for i in range(nx) for j in range(ny)
    ]
    return lax.ppermute(value, ("gx", "gy"), pairs)


def per_device(adjoint_in, velocity, solid_tiles, link_blocked):
    rows_x, levels, rows_y = adjoint_in.shape[1:]
    rows = rows_x * levels
    padded = rows + 16 + 2 * GUARD
    groups = rows // 8 + 2
    parts = -(-COLUMN_QUANTITIES // (LANES // groups))
    state = adjoint_in.reshape(19, rows, rows_y)
    flow = velocity.reshape(STEPS, 3, rows, rows_y)
    solid = solid_tiles.reshape(-1, solid_tiles.shape[2])

    def shape_of(*sizes):
        return jax.ShapeDtypeStruct(sizes, jnp.float32)

    params = pltpu.CompilerParams(vmem_limit_bytes=16 * 1024 * 1024)
    anywhere = pl.BlockSpec(memory_space=pl.ANY)
    *row_sent, held, flow, tiles = pl.pallas_call(
        row_message_kernel,
        out_shape=(
            pltpu.VMEM((QUANTITIES, levels, rows_y), jnp.float32),
            pltpu.VMEM((QUANTITIES, levels, rows_y), jnp.float32),
            pltpu.VMEM((19, padded, rows_y), jnp.float32),
            pltpu.VMEM(flow.shape, flow.dtype),
            pltpu.VMEM(solid.shape, solid.dtype),
        ),
        in_specs=[anywhere] * 3,
        out_specs=(vmem,) * 5,
        scratch_shapes=[pltpu.SemaphoreType.DMA((3,))],
        compiler_params=params,
    )(*(pltpu.with_memory_space_constraint(value, pltpu.HBM) for value in (state, flow, solid)))
    row_got = swap_pairs(*row_sent, "gx")
    def pack(side, size, *later_than):
        return pl.pallas_call(
            functools.partial(own_columns_kernel, side),
            out_shape=shape_of(size, 8, rows_y),
            in_specs=[vmem] * (3 + len(later_than)),
            out_specs=vmem,
            compiler_params=params,
            cost_estimate=pl.CostEstimate(flops=2_000_000, bytes_accessed=1_000_000, transcendentals=0),
        )(held, flow, tiles, *later_than)

    own_high = pack(1, parts)
    own_low = pack(0, 16)
    own_columns = own_low, own_high
    low, high = pl.pallas_call(
        functools.partial(halo_columns_kernel, groups),
        out_shape=(shape_of(parts, 8, rows_y),) * 2,
        in_specs=[vmem] * 4,
        out_specs=(vmem,) * 2,
        scratch_shapes=[pltpu.VMEM((2, SECOND, 8, rows_y), jnp.float32)],
        compiler_params=params,
    )(*own_columns, *row_got)
    size = lax.axis_size("gy")
    y_before = lax.ppermute(own_columns[1], "gy", [(i, (i + 1) % size) for i in range(size)])
    def hand_on(columns, ahead, *later_than):
        handed = pl.pallas_call(
            functools.partial(hand_on_kernel, groups, ahead),
            out_shape=shape_of(parts, 8, rows_y),
            in_specs=[vmem] * (1 + len(later_than)),
            out_specs=vmem,
            compiler_params=params,
            cost_estimate=pl.CostEstimate(flops=10_000_000_000, bytes_accessed=100_000, transcendentals=0),
        )(columns, *later_than)
        return swap_pairs(handed, handed, "gx")

    diagonals = [from_diagonal(own_columns[1], side) for side in (1, -1)]
    y_after = lax.ppermute(own_columns[0], "gy", [((i + 1) % size, i) for i in range(size)])
    count = lax.axis_size("gx") * size
    field = pltpu.VMEM((19, padded, rows_y), jnp.float32)
    solid_field = pltpu.VMEM((3, padded, rows_y), jnp.float32)
    partial, own_blocks = pl.pallas_call(
        inner_drag_kernel,
        out_shape=(
            pltpu.VMEM((8, rows_y), jnp.float32),
            pltpu.VMEM((SECOND + len(ahead_slots), 8, rows_y), jnp.float32),
        ),
        in_specs=[vmem] * 6,
        out_specs=(vmem,) * 2,
        scratch_shapes=[field, field, solid_field, pltpu.VMEM((9, padded, rows_y), jnp.float32)],
        compiler_params=params,
        cost_estimate=pl.CostEstimate(flops=20_000_000_000, bytes_accessed=1_000_000, transcendentals=0),
    )(held, flow, tiles, *row_got, low)
    own = pl.pallas_call(
        functools.partial(edge_drag_kernel, groups),
        out_shape=pltpu.VMEM((count, 1, rows_y), jnp.float32),
        in_specs=[vmem] * 5,
        out_specs=vmem,
        compiler_params=params,
        cost_estimate=pl.CostEstimate(flops=1_000_000, bytes_accessed=1_000_000, transcendentals=0),
    )(y_before, *diagonals, own_blocks, partial)
    handed_after = hand_on(y_after, 1, own)
    shared = lax.all_to_all(own, ("gx", "gy"), split_axis=0, concat_axis=0, tiled=True)
    result = pl.pallas_call(
        main_kernel,
        out_shape=shape_of(19, rows, rows_y),
        in_specs=[vmem] * 13,
        out_specs=vmem,
        scratch_shapes=[field, field, field, solid_field, pltpu.VMEM((4, 8, rows_y), jnp.float32)],
        compiler_params=params,
        cost_estimate=pl.CostEstimate(flops=1_000_000, bytes_accessed=1_000_000, transcendentals=0),
    )(held, flow, tiles, *row_got, y_before, *diagonals, y_after, *handed_after, low, high)
    cell_count = rows * rows_y * count
    scale = drag_factor / math.sqrt(cell_count) * 3.0 / 36.0
    total = jnp.sum(shared[:, 0, 0])
    return (result.reshape(adjoint_in.shape), (-scale * total).reshape(1))


def solution(mesh):
    placed = (
        P(None, "gx", None, "gy"),
        P(None, None, "gx", None, "gy"),
        P("gx", None, "gy"),
        P(None, "gx", None, "gy"),
    )
    return jax.shard_map(
        per_device,
        mesh=mesh,
        in_specs=placed,
        out_specs=(P(None, "gx", None, "gy"), P()),
        check_vma=False,
    )
```

```python
import functools
import math

import jax
import jax.numpy as jnp
from jax import lax
from jax.experimental import pallas as pl
from jax.experimental.pallas import tpu as pltpu
from jax.sharding import PartitionSpec as P

TILE = 4
STEPS = 2

lattice_speeds = (
    (0, 0, 0),
    (1, 0, 0),
    (-1, 0, 0),
    (0, 1, 0),
    (0, -1, 0),
    (0, 0, 1),
    (0, 0, -1),
    (1, 1, 0),
    (-1, -1, 0),
    (1, -1, 0),
    (-1, 1, 0),
    (1, 0, 1),
    (-1, 0, -1),
    (1, 0, -1),
    (-1, 0, 1),
    (0, 1, 1),
    (0, -1, -1),
    (0, 1, -1),
    (0, -1, 1),
)
relax_rate = 1.6
drag_factor = 20.0
LEVELS = 4
LANES = 128
GUARD = 8

x_up = [n for n in range(19) if lattice_speeds[n][0] == 1]
x_down = [n for n in range(19) if lattice_speeds[n][0] == -1]
y_up = [n for n in range(19) if lattice_speeds[n][1] == 1]
y_down = [n for n in range(19) if lattice_speeds[n][1] == -1]
vmem = pl.BlockSpec(memory_space=pltpu.VMEM)

FLOW = 19
SOLID = 22
NEXT = 23
SECOND = 26
QUANTITIES = 31
NEXT_SECOND = 31
COLUMN_QUANTITIES = 34
BEFORE_LANE = 16
AFTER_LANE = 32


def opposite_of(number):
    return number + 1 if number % 2 == 1 else number - 1


def lane_index(rows=8):
    return lax.broadcasted_iota(jnp.int32, (rows, LANES), 1)


def spread_solid(solid):
    tiles = solid.shape[1]
    row = lax.broadcasted_iota(jnp.int32, (tiles, LANES), 0)
    column = lax.broadcasted_iota(jnp.int32, (tiles, LANES), 1)
    spread = (column // TILE == row).astype(jnp.float32)
    cells = jnp.dot(solid[...].astype(jnp.float32), spread, preferred_element_type=jnp.float32)
    blocks = []
    for tile_row in range(solid.shape[0] // LEVELS):
        part = cells[tile_row * LEVELS : (tile_row + 1) * LEVELS]
        blocks.append(jnp.concatenate([part, part], axis=0))
    return blocks


def flow_blocks(velocity, step, rows):
    blocks = []
    for pair in range(rows // 16):
        both = [velocity[step, axis, pl.ds(16 * pair, 16), :].astype(jnp.float32) for axis in range(3)]
        blocks.append([part[:8] for part in both])
        blocks.append([part[8:] for part in both])
    return blocks


def on_even(axis):
    return lax.rem(lax.axis_index(axis), 2) == 0


class Chosen:
    def __init__(self, choice, yes, no):
        self.choice, self.yes, self.no = choice, yes, no
        self.shape = yes.shape

    def __getitem__(self, index):
        return jnp.where(self.choice, self.yes[index], self.no[index])


def slot_place(slot, group, groups):
    per_block = LANES // groups
    return slot // per_block, (slot % per_block) * groups + group


def insert_column(parts, slot, group, groups, value, edge, ahead):
    part, place = slot_place(slot, group, groups)
    lane = lane_index()
    turned = pltpu.roll(value, (place + ahead - edge) % LANES, 1)
    parts[part] = jnp.where(lane == place + ahead, turned, parts[part])


def copy_kernel(state, velocity, solid, held, flow, tiles, arrived):
    own = pl.ds(GUARD + 8, state.shape[1])
    copies = [
        pltpu.make_async_copy(state, held.at[:, own, :], arrived.at[0]),
        pltpu.make_async_copy(velocity, flow, arrived.at[1]),
        pltpu.make_async_copy(solid, tiles, arrived.at[2]),
    ]
    for copy in copies:
        copy.start()
    for copy in copies:
        copy.wait()


def row_message_kernel(held, flow, tiles, row_first, row_second):
    rows = flow.shape[2]
    even = on_even("gx")
    low_row, high_row = GUARD + 8, GUARD + 8 + rows - LEVELS

    def put(slot, low, high):
        row_first[slot] = jnp.where(even, high, low)
        row_second[slot] = jnp.where(even, low, high)

    for number in range(19):
        put(number, held[number, pl.ds(low_row, LEVELS), :], held[number, pl.ds(high_row, LEVELS), :])
    for step, slot in ((0, FLOW), (1, NEXT)):
        for axis in range(3):
            low = flow[step, axis, pl.ds(0, 16), :].astype(jnp.float32)
            high = flow[step, axis, pl.ds(rows - 16, 16), :].astype(jnp.float32)
            put(slot + axis, low[:LEVELS], high[16 - LEVELS :])
    solid_parts = spread_solid(tiles)
    put(SOLID, solid_parts[0][:LEVELS], solid_parts[-1][:LEVELS])
    for slot in range(5):
        put(
            SECOND + slot,
            held[x_up[slot], pl.ds(low_row + LEVELS, LEVELS), :],
            held[x_down[slot], pl.ds(high_row - LEVELS, LEVELS), :],
        )


def pack_columns(parts, slot, group, groups, value):
    for message, edge, step, ahead, moving in ((parts[0], 0, 1, 1, y_up), (parts[1], LANES - 1, -1, 0, y_down)):
        if message is None:
            continue
        insert_column(message, slot, group, groups, value, edge, ahead)
        second = second_slot(slot, moving)
        if second != slot:
            insert_column(message, second, group, groups, value, edge + step, ahead)


def own_columns_kernel(side, held, velocity, solid, *rest):
    out = rest[-1]
    rows = velocity.shape[2]
    groups = rows // 8 + 2
    solid_parts = spread_solid(solid)
    flow = [flow_blocks(velocity, step, rows) for step in range(2)]
    parts = [None, None]
    parts[side] = [jnp.zeros((8, LANES), jnp.float32) for _ in range(out.shape[0])]
    for group in range(1, groups - 1):
        for slot in range(19):
            pack_columns(parts, slot, group, groups, held[slot, pl.ds(GUARD + 8 * group, 8), :])
        for axis in range(3):
            pack_columns(parts, FLOW + axis, group, groups, flow[0][group - 1][axis])
            pack_columns(parts, NEXT + axis, group, groups, flow[1][group - 1][axis])
        pack_columns(parts, SOLID, group, groups, solid_parts[(group - 1) * 8 // (LEVELS * TILE)])
    for part in range(out.shape[0]):
        out[part] = parts[side][part]


def halo_columns_kernel(groups, own_low, own_high, row_first, row_second, low_out, high_out, ends):
    count = own_high.shape[0]
    even = on_even("gx")
    after, before = Chosen(even, row_first, row_second), Chosen(even, row_second, row_first)
    parts = [[own_low[part] for part in range(count)], [own_high[part] for part in range(count)]]
    for slot in range(SECOND):
        ends[0, slot, pl.ds(LEVELS, LEVELS), :] = before[slot]
        ends[1, slot, pl.ds(0, LEVELS), :] = after[slot]
        if slot == SOLID:
            low_second, high_second = SOLID, SOLID
        else:
            low_second = SECOND + x_down.index(slot) if slot in x_down else None
            high_second = SECOND + x_up.index(slot) if slot in x_up else None
        blank = jnp.zeros((LEVELS, LANES), jnp.float32)
        ends[0, slot, pl.ds(0, LEVELS), :] = blank if low_second is None else before[low_second]
        ends[1, slot, pl.ds(LEVELS, LEVELS), :] = blank if high_second is None else after[high_second]
        pack_columns(parts, slot, 0, groups, ends[0, slot])
        pack_columns(parts, slot, groups - 1, groups, ends[1, slot])
    for part in range(count):
        low_out[part] = parts[0][part]
        high_out[part] = parts[1][part]


def collide(moved, flow, fluid):
    ux, uy, uz = flow
    total = {n: moved[n] + moved[n + 1] for n in range(1, 19, 2)}
    xy, xz, yz = total[7] + total[9], total[11] + total[13], total[15] + total[17]
    axis_x, axis_y, axis_z = 2.0 * total[1], 2.0 * total[3], 2.0 * total[5]
    density = 12.0 * moved[0] + (axis_x + axis_y + axis_z) + (xy + xz + yz)
    pxx = axis_x + xy + xz
    pyy = axis_y + xy + yz
    pzz = axis_z + xz + yz
    pxy = total[7] - total[9]
    pxz = total[11] - total[13]
    pyz = total[15] - total[17]
    dx, dy, dz = momentum(moved)
    vx = pxx * ux + pxy * uy + pxz * uz
    vy = pxy * ux + pyy * uy + pyz * uz
    vz = pxz * ux + pyz * uy + pzz * uz
    speed_sq = ux * ux + uy * uy + uz * uz
    scaled = (relax_rate / 36.0) * fluid
    base = scaled * (density + 1.5 * (speed_sq * density) - 4.5 * (ux * vx + uy * vy + uz * vz))
    scaled3 = 3.0 * scaled
    bx = scaled3 * (dx + 3.0 * vx - ux * density)
    by = scaled3 * (dy + 3.0 * vy - uy * density)
    bz = scaled3 * (dz + 3.0 * vz - uz * density)
    keep = (1.0 - relax_rate) * fluid
    results = [keep * moved[0] + base]
    for number in range(1, 19, 2):
        along = None
        for speed, part in zip(lattice_speeds[number], (bx, by, bz)):
            if speed == 0:
                continue
            if along is None:
                along = part if speed == 1 else -part
            else:
                along = along + part if speed == 1 else along - part
        results.append(keep * moved[number] + (base + along))
        results.append(keep * moved[number + 1] + (base - along))
    return results


def outside(cz):
    level = lax.broadcasted_iota(jnp.int32, (8, LANES), 0) % LEVELS
    return level == (LEVELS - 1 if cz == 1 else 0)


def link_closed(solid_there, cz):
    closed = solid_there > 0.5
    return closed | outside(cz) if cz != 0 else closed


def shift_lanes(value, cy, edge_value):
    lane = lane_index(value.shape[0])
    shifted = pltpu.roll(value, -cy % LANES, 1)
    if edge_value is None:
        return shifted
    return jnp.where(lane == (LANES - 1 if cy == 1 else 0), edge_value, shifted)


def gather_cells(held, shifted, first, solid_rows):
    here = [held[n, pl.ds(first, 8), :] for n in range(19)]
    moved, closed = [here[0]], [None]
    for number in range(1, 19):
        cx, cy, cz = lattice_speeds[number]
        field = held if cy == 0 else shifted
        there = pl.ds(first + LEVELS * cx + cz, 8)
        closed.append(link_closed(solid_rows[cy % 3, there, :], cz))
        bounced = here[opposite_of(number)]
        if cx != 0:
            bounced = bounced + 2.0 * cx
        moved.append(jnp.where(closed[number], bounced, field[number, there, :]))
    return moved, closed


def momentum(moved):
    gap = {n: moved[n] - moved[n + 1] for n in range(1, 19, 2)}
    dx = 2.0 * gap[1] + (gap[7] + gap[9]) + (gap[11] + gap[13])
    dy = 2.0 * gap[3] + (gap[7] - gap[9]) + (gap[15] + gap[17])
    dz = 2.0 * gap[5] + (gap[11] - gap[13]) + (gap[15] - gap[17])
    return dx, dy, dz


def drag_term(moved, flow, fluid):
    return fluid * sum(speed * part for speed, part in zip(flow, momentum(moved)))


def along_link(number, vector):
    total = None
    for axis, speed in enumerate(lattice_speeds[number]):
        if speed == 0:
            continue
        part = vector(axis)
        if total is None:
            total = part if speed == 1 else -part
        else:
            total = total + part if speed == 1 else total - part
    return total


def later_drag(results, closed, weight_here, weight_back):
    term = None
    for number in range(1, 19):
        cx = lattice_speeds[number][0]
        here = along_link(number, lambda axis: weight_here[axis])
        part = jnp.where(closed[opposite_of(number)], -here, weight_back(number)) * results[number]
        if cx != 0:
            part = part + jnp.where(closed[number], (2.0 * cx) * here, 0.0)
        if number < 7:
            part = 2.0 * part
        term = part if term is None else term + part
    return term


def column_reader(groups):
    def column(message, ahead, slot, lane_first, group=0):
        part, place = slot_place(slot, group, groups)
        return pltpu.roll(message[part], (lane_first - place - ahead) % LANES, 1)

    return column


def fill_held(own_held, before, after, held, rows):
    own = GUARD + 8
    near, far = own - LEVELS, own + rows
    for number in range(19):
        for group in range(rows // 8):
            there = pl.ds(own + 8 * group, 8)
            held[number, there, :] = own_held[number, there, :]
        held[number, pl.ds(near, LEVELS), :] = before[number]
        held[number, pl.ds(far, LEVELS), :] = after[number]
        if number in x_down:
            held[number, pl.ds(near - LEVELS, LEVELS), :] = before[SECOND + x_down.index(number)]
        if number in x_up:
            held[number, pl.ds(far + LEVELS, LEVELS), :] = after[SECOND + x_up.index(number)]


def fill_shifted(field, shifted, groups, edge_of):
    for number in y_up + y_down:
        cy = lattice_speeds[number][1]
        for group in range(groups):
            there = pl.ds(GUARD + 8 * group, 8)
            shifted[number, there, :] = shift_lanes(field[number, there, :], cy, edge_of(number, cy, group))


def fill_solid(solid_parts, before, after, solid_rows, groups, edge_of):
    for group in range(groups):
        first = GUARD + 8 * group
        if group in (0, groups - 1):
            halo = before[SOLID] if group == 0 else after[SOLID]
            solid_rows[0, pl.ds(first, LEVELS), :] = halo
            solid_rows[0, pl.ds(first + LEVELS, LEVELS), :] = halo
        else:
            solid_rows[0, pl.ds(first, 8), :] = solid_parts[(group - 1) * 8 // (LEVELS * TILE)]
        value = solid_rows[0, pl.ds(first, 8), :]
        for cy in (1, -1):
            solid_rows[cy % 3, pl.ds(first, 8), :] = shift_lanes(value, cy, edge_of(SOLID, cy, group))


def shift_rows(value, cx, cz):
    if cx != 0:
        upper = lax.broadcasted_iota(jnp.int32, (8, LANES), 0) < LEVELS
        swapped = pltpu.roll(value, LEVELS, 0)
        if cx == 1:
            value = jnp.where(upper, swapped, pltpu.roll(swapped, LANES - 1, 1))
        else:
            value = jnp.where(upper, pltpu.roll(swapped, 1, 1), swapped)
    if cz != 0:
        value = pltpu.roll(value, (-cz) % 8, 0)
    return value


def gather_columns(neighbours):
    here = [neighbours(n, 0) for n in range(19)]
    solid = {cy: neighbours(SOLID, cy) for cy in (0, 1, -1)}
    moved, closed = [here[0]], [None]
    for number in range(1, 19):
        cx, cy, cz = lattice_speeds[number]
        source = shift_rows(here[number] if cy == 0 else neighbours(number, cy), cx, cz)
        closed.append(link_closed(shift_rows(solid[cy], cx, cz), cz))
        moved.append(jnp.where(closed[number], here[opposite_of(number)] + 2.0 * cx, source))
    return moved, closed, solid


def inner_drag_kernel(
    own_held, velocity, solid, row_first, row_second, low, partial, own_blocks,
    held, shifted, solid_rows, weights,
):
    rows = velocity.shape[2]
    groups = rows // 8 + 2
    own = GUARD + 8
    near, far = own - LEVELS, own + rows
    even = on_even("gx")
    after, before = Chosen(even, row_first, row_second), Chosen(even, row_second, row_first)
    lane = lane_index()
    solid_parts = spread_solid(solid)

    def no_edge(slot, cy, group):
        return None

    fill_held(own_held, before, after, held, rows)
    fill_shifted(held, shifted, groups, no_edge)
    fill_solid(solid_parts, before, after, solid_rows, groups, no_edge)

    flow = flow_blocks(velocity, 1, rows)
    for axis in range(3):
        for group in range(rows // 8):
            there = pl.ds(own + 8 * group, 8)
            weights[axis, there, :] = (1.0 - solid_rows[0, there, :]) * flow[group][axis]
        for row, message in ((near, before), (far, after)):
            weights[axis, pl.ds(row, LEVELS), :] = (1.0 - message[SOLID]) * message[NEXT + axis]
        for group in range(groups):
            there = pl.ds(GUARD + 8 * group, 8)
            value = weights[axis, there, :]
            weights[3 + axis, there, :] = shift_lanes(value, 1, None)
            weights[6 + axis, there, :] = shift_lanes(value, -1, None)

    total = jnp.zeros((8, LANES), jnp.float32)
    flow = flow_blocks(velocity, 0, rows)
    for group in range(rows // 8):
        first = own + 8 * group
        moved, closed = gather_cells(held, shifted, first, solid_rows)
        fluid = 1.0 - solid_parts[8 * group // (LEVELS * TILE)]
        results = collide(moved, flow[group], fluid)

        def back(number):
            cx, cy, cz = lattice_speeds[number]
            there = pl.ds(first - LEVELS * cx - cz, 8)
            return along_link(number, lambda axis: weights[3 * (-cy % 3) + axis, there, :])

        here = [weights[axis, pl.ds(first, 8), :] for axis in range(3)]
        total = total + drag_term(moved, flow[group], fluid) + later_drag(results, closed, here, back)
    inside = jnp.logical_and(lane > 0, lane < LANES - 1)
    partial[...] = jnp.where(inside, total, 0.0)

    column = column_reader(groups)
    for slot in range(SECOND):
        own_blocks[slot] = column(low, 1, slot, AFTER_LANE)
    for place, slot in enumerate(ahead_slots):
        here = column(low, 1, slot, BEFORE_LANE)
        ahead = column(low, 1, second_slot(slot, y_up), AFTER_LANE)
        own_blocks[SECOND + place] = jnp.where(lane < AFTER_LANE, here, ahead)


ahead_slots = y_up + [SOLID, NEXT, NEXT + 1, NEXT + 2]


def second_slot(slot, moving):
    if slot in moving:
        return SECOND + moving.index(slot)
    return NEXT_SECOND + slot - NEXT if NEXT <= slot < NEXT + 3 else slot


def halo_lanes(groups, ahead):
    lane = lane_index()
    group = lax.rem(lane + groups - ahead, groups)
    used = jnp.logical_and(lane >= ahead, lane < LANES // groups * groups + ahead)
    return jnp.logical_and(used, group == 0), jnp.logical_and(used, group == groups - 1)


def hand_on_kernel(groups, ahead, columns, *rest):
    out = rest[-1]
    above, _ = halo_lanes(groups, ahead)
    for part in range(out.shape[0]):
        value = columns[part]
        last = pltpu.roll(value, LANES - (groups - 2), 1)
        out[part] = jnp.where(above, last, pltpu.roll(value, groups - 2, 1))


def with_halo_rows(columns, handed_first, handed_second, groups, ahead):
    even = on_even("gx")
    from_before = Chosen(even, handed_second, handed_first)
    from_after = Chosen(even, handed_first, handed_second)
    above, below = halo_lanes(groups, ahead)
    whole = []
    for part in range(handed_first.shape[0]):
        value = jnp.where(above, from_before[part], columns[part])
        whole.append(jnp.where(below, from_after[part], value))
    return whole


def edge_drag_kernel(groups, columns, handed_first, handed_second, own_blocks, partial, shared, summed):
    lane = lane_index()
    column = column_reader(groups)
    y_before = with_halo_rows(columns, handed_first, handed_second, groups, 0)

    def neighbours(slot, cy):
        if cy == 1:
            return own_blocks[SECOND + ahead_slots.index(slot)]
        if cy == 0:
            first, second = column(y_before, 0, slot, BEFORE_LANE), own_blocks[slot]
        else:
            first = column(y_before, 0, second_slot(slot, y_down), BEFORE_LANE)
            second = column(y_before, 0, slot, AFTER_LANE)
        return jnp.where(lane < AFTER_LANE, first, second)

    moved, closed, solid_columns = gather_columns(neighbours)
    fluid = {cy: 1.0 - solid_columns[cy] for cy in (0, 1, -1)}
    flow = [neighbours(FLOW + axis, 0) for axis in range(3)]
    results = collide(moved, flow, fluid[0])
    weight = {cy: [fluid[cy] * neighbours(NEXT + axis, cy) for axis in range(3)] for cy in (0, 1, -1)}

    def back(number):
        cx, cy, cz = lattice_speeds[number]
        return shift_rows(along_link(number, lambda axis: weight[-cy][axis]), -cx, -cz)

    term = drag_term(moved, flow, fluid[0]) + later_drag(results, closed, weight[0], back)
    place = jnp.where(lane < AFTER_LANE, lane - BEFORE_LANE, lane - AFTER_LANE)
    inside = jnp.logical_and(place > 0, place < groups - 1)
    total = partial[...] + jnp.where(inside, term, 0.0)
    summed[...] = total
    shared[...] = jnp.broadcast_to(jnp.sum(total), shared.shape)


def main_kernel(
    own_held, velocity, solid, row_first, row_second, columns, handed_first, handed_second,
    columns_after, after_first, after_second, low, high, out, held, shifted, later, solid_rows, row_flow,
):
    rows = velocity.shape[2]
    groups = rows // 8 + 2
    own = GUARD + 8
    near, far = own - LEVELS, own + rows
    even = on_even("gx")
    after, before = Chosen(even, row_first, row_second), Chosen(even, row_second, row_first)
    lane = lane_index()
    solid_parts = spread_solid(solid)
    column = column_reader(groups)
    y_before = with_halo_rows(columns, handed_first, handed_second, groups, 0)
    y_after = with_halo_rows(columns_after, after_first, after_second, groups, 1)

    def edge_of(slot, cy, group):
        if cy == 1:
            return column(y_after, 1, slot, LANES - 1, group)
        return column(y_before, 0, slot, 0, group)

    fill_held(own_held, before, after, held, rows)
    fill_shifted(held, shifted, groups, edge_of)
    fill_solid(solid_parts, before, after, solid_rows, groups, edge_of)
    for slot, place in ((FLOW, 0), (FLOW + 1, 1), (FLOW + 2, 2), (SOLID, 3)):
        row_flow[place, pl.ds(0, LEVELS), :] = before[slot]
        row_flow[place, pl.ds(LEVELS, LEVELS), :] = after[slot]

    def both_rows(field, index, shift):
        ends = [field[index, pl.ds(place + shift, LEVELS), :] for place in (near, far)]
        return jnp.concatenate(ends, axis=0)

    here = [both_rows(held, n, 0) for n in range(19)]
    moved = [here[0]]
    for number in range(1, 19):
        cx, cy, cz = lattice_speeds[number]
        shift = LEVELS * cx + cz
        source = both_rows(held if cy == 0 else shifted, number, shift)
        closed = link_closed(both_rows(solid_rows, cy % 3, shift), cz)
        moved.append(jnp.where(closed, here[opposite_of(number)] + 2.0 * cx, source))
    row_results = collide(moved, [row_flow[axis] for axis in range(3)], 1.0 - row_flow[3])

    def neighbours(slot, cy):
        beyond = slot if cy == 0 or slot == SOLID else SECOND + (y_up if cy == 1 else y_down).index(slot)
        if cy == 1:
            first, second = column(low, 1, slot, BEFORE_LANE), column(y_after, 1, beyond, AFTER_LANE)
        elif cy == -1:
            first, second = column(y_before, 0, beyond, BEFORE_LANE), column(high, 0, slot, AFTER_LANE)
        else:
            first, second = column(y_before, 0, slot, BEFORE_LANE), column(y_after, 1, slot, AFTER_LANE)
        return jnp.where(lane < AFTER_LANE, first, second)

    moved, _, solid_columns = gather_columns(neighbours)
    column_flow = [neighbours(FLOW + axis, 0) for axis in range(3)]
    column_results = collide(moved, column_flow, 1.0 - solid_columns[0])

    flow = flow_blocks(velocity, 0, rows)
    for group in range(rows // 8):
        first = own + 8 * group
        moved, _ = gather_cells(held, shifted, first, solid_rows)
        results = collide(moved, flow[group], 1.0 - solid_parts[8 * group // (LEVELS * TILE)])
        for number in range(19):
            later[number, pl.ds(first, 8), :] = results[number]
    for number in x_down:
        later[number, pl.ds(near, LEVELS), :] = row_results[number][:LEVELS]
    for number in x_up:
        later[number, pl.ds(far, LEVELS), :] = row_results[number][LEVELS:]

    def later_edge(number, cy, group):
        shift = LANES - 1 - AFTER_LANE - group if cy == 1 else -BEFORE_LANE - group
        return pltpu.roll(column_results[number], shift % LANES, 1)

    fill_shifted(later, shifted, groups, later_edge)

    flow = flow_blocks(velocity, 1, rows)
    for group in range(rows // 8):
        first = 8 * group
        moved, _ = gather_cells(later, shifted, own + first, solid_rows)
        results = collide(moved, flow[group], 1.0 - solid_parts[first // (LEVELS * TILE)])
        for number in range(19):
            out[number, pl.ds(first, 8), :] = results[number]


def swap_pairs(first, second, axis):
    count = lax.axis_size(axis)
    inside = [(i, i ^ 1) for i in range(count)]
    across = [(i, (i + 1) % count if i % 2 == 1 else (i - 1) % count) for i in range(count)]
    second = lax.ppermute(second, axis, across)
    return lax.ppermute(first, axis, inside), second


def per_device(adjoint_in, velocity, solid_tiles, link_blocked):
    rows_x, levels, rows_y = adjoint_in.shape[1:]
    rows = rows_x * levels
    padded = rows + 16 + 2 * GUARD
    groups = rows // 8 + 2
    parts = -(-COLUMN_QUANTITIES // (LANES // groups))
    state = adjoint_in.reshape(19, rows, rows_y)
    flow = velocity.reshape(STEPS, 3, rows, rows_y)
    solid = solid_tiles.reshape(-1, solid_tiles.shape[2])

    def shape_of(*sizes):
        return jax.ShapeDtypeStruct(sizes, jnp.float32)

    params = pltpu.CompilerParams(vmem_limit_bytes=16 * 1024 * 1024)
    anywhere = pl.BlockSpec(memory_space=pl.ANY)
    held, flow, tiles = pl.pallas_call(
        copy_kernel,
        out_shape=(
            pltpu.VMEM((19, padded, rows_y), jnp.float32),
            pltpu.VMEM(flow.shape, flow.dtype),
            pltpu.VMEM(solid.shape, solid.dtype),
        ),
        in_specs=[anywhere] * 3,
        out_specs=(vmem,) * 3,
        scratch_shapes=[pltpu.SemaphoreType.DMA((3,))],
        compiler_params=params,
    )(*(pltpu.with_memory_space_constraint(value, pltpu.HBM) for value in (state, flow, solid)))
    row_sent = pl.pallas_call(
        row_message_kernel,
        out_shape=(pltpu.VMEM((QUANTITIES, levels, rows_y), jnp.float32),) * 2,
        in_specs=[vmem] * 3,
        out_specs=(vmem,) * 2,
        compiler_params=params,
    )(held, flow, tiles)
    row_got = swap_pairs(*row_sent, "gx")
    def pack(side, size, *later_than):
        return pl.pallas_call(
            functools.partial(own_columns_kernel, side),
            out_shape=shape_of(size, 8, rows_y),
            in_specs=[vmem] * (3 + len(later_than)),
            out_specs=vmem,
            compiler_params=params,
            cost_estimate=pl.CostEstimate(flops=2_000_000, bytes_accessed=1_000_000, transcendentals=0),
        )(held, flow, tiles, *later_than)

    own_high = pack(1, parts)
    own_low = pack(0, 16, row_sent[0])
    own_columns = own_low, own_high
    low, high = pl.pallas_call(
        functools.partial(halo_columns_kernel, groups),
        out_shape=(shape_of(parts, 8, rows_y),) * 2,
        in_specs=[vmem] * 4,
        out_specs=(vmem,) * 2,
        scratch_shapes=[pltpu.VMEM((2, SECOND, 8, rows_y), jnp.float32)],
        compiler_params=params,
    )(*own_columns, *row_got)
    size = lax.axis_size("gy")
    y_before = lax.ppermute(own_columns[1], "gy", [(i, (i + 1) % size) for i in range(size)])
    def hand_on(columns, ahead, *later_than):
        handed = pl.pallas_call(
            functools.partial(hand_on_kernel, groups, ahead),
            out_shape=shape_of(parts, 8, rows_y),
            in_specs=[vmem] * (1 + len(later_than)),
            out_specs=vmem,
            compiler_params=params,
            cost_estimate=pl.CostEstimate(flops=10_000_000_000, bytes_accessed=100_000, transcendentals=0),
        )(columns, *later_than)
        return swap_pairs(handed, handed, "gx")

    handed = hand_on(y_before, 0)
    y_after = lax.ppermute(own_columns[0], "gy", [((i + 1) % size, i) for i in range(size)])
    count = lax.axis_size("gx") * size
    field = pltpu.VMEM((19, padded, rows_y), jnp.float32)
    solid_field = pltpu.VMEM((3, padded, rows_y), jnp.float32)
    partial, own_blocks = pl.pallas_call(
        inner_drag_kernel,
        out_shape=(
            pltpu.VMEM((8, rows_y), jnp.float32),
            pltpu.VMEM((SECOND + len(ahead_slots), 8, rows_y), jnp.float32),
        ),
        in_specs=[vmem] * 6,
        out_specs=(vmem,) * 2,
        scratch_shapes=[field, field, solid_field, pltpu.VMEM((9, padded, rows_y), jnp.float32)],
        compiler_params=params,
        cost_estimate=pl.CostEstimate(flops=20_000_000_000, bytes_accessed=1_000_000, transcendentals=0),
    )(held, flow, tiles, *row_got, low)
    own, summed = pl.pallas_call(
        functools.partial(edge_drag_kernel, groups),
        out_shape=(shape_of(count, 1, rows_y), pltpu.VMEM((8, rows_y), jnp.float32)),
        in_specs=[vmem] * 5,
        out_specs=(vmem,) * 2,
        compiler_params=params,
        cost_estimate=pl.CostEstimate(flops=1_000_000, bytes_accessed=1_000_000, transcendentals=0),
    )(y_before, *handed, own_blocks, partial)
    handed_after = hand_on(y_after, 1, summed)
    shared = lax.all_to_all(own, ("gx", "gy"), split_axis=0, concat_axis=0, tiled=True)
    result = pl.pallas_call(
        main_kernel,
        out_shape=shape_of(19, rows, rows_y),
        in_specs=[vmem] * 13,
        out_specs=vmem,
        scratch_shapes=[field, field, field, solid_field, pltpu.VMEM((4, 8, rows_y), jnp.float32)],
        compiler_params=params,
        cost_estimate=pl.CostEstimate(flops=1_000_000, bytes_accessed=1_000_000, transcendentals=0),
    )(held, flow, tiles, *row_got, y_before, *handed, y_after, *handed_after, low, high)
    cell_count = rows * rows_y * count
    scale = drag_factor / math.sqrt(cell_count) * 3.0 / 36.0
    total = jnp.sum(shared[:, 0, 0])
    return (result.reshape(adjoint_in.shape), (-scale * total).reshape(1))


def solution(mesh):
    placed = (
        P(None, "gx", None, "gy"),
        P(None, None, "gx", None, "gy"),
        P("gx", None, "gy"),
        P(None, "gx", None, "gy"),
    )
    return jax.shard_map(
        per_device,
        mesh=mesh,
        in_specs=placed,
        out_specs=(P(None, "gx", None, "gy"), P()),
        check_vma=False,
    )
```

```python
import functools
import math

import jax
import jax.numpy as jnp
from jax import lax
from jax.experimental import pallas as pl
from jax.experimental.pallas import tpu as pltpu
from jax.sharding import PartitionSpec as P

TILE = 4
STEPS = 2

lattice_speeds = (
    (0, 0, 0),
    (1, 0, 0),
    (-1, 0, 0),
    (0, 1, 0),
    (0, -1, 0),
    (0, 0, 1),
    (0, 0, -1),
    (1, 1, 0),
    (-1, -1, 0),
    (1, -1, 0),
    (-1, 1, 0),
    (1, 0, 1),
    (-1, 0, -1),
    (1, 0, -1),
    (-1, 0, 1),
    (0, 1, 1),
    (0, -1, -1),
    (0, 1, -1),
    (0, -1, 1),
)
relax_rate = 1.6
drag_factor = 20.0
LEVELS = 4
LANES = 128
GUARD = 8

x_up = [n for n in range(19) if lattice_speeds[n][0] == 1]
x_down = [n for n in range(19) if lattice_speeds[n][0] == -1]
y_up = [n for n in range(19) if lattice_speeds[n][1] == 1]
y_down = [n for n in range(19) if lattice_speeds[n][1] == -1]
vmem = pl.BlockSpec(memory_space=pltpu.VMEM)

FLOW = 19
SOLID = 22
NEXT = 23
SECOND = 26
QUANTITIES = 31
NEXT_SECOND = 31
COLUMN_QUANTITIES = 34
BEFORE_LANE = 16
AFTER_LANE = 32


def opposite_of(number):
    return number + 1 if number % 2 == 1 else number - 1


def lane_index(rows=8):
    return lax.broadcasted_iota(jnp.int32, (rows, LANES), 1)


def spread_solid(solid):
    tiles = solid.shape[1]
    row = lax.broadcasted_iota(jnp.int32, (tiles, LANES), 0)
    column = lax.broadcasted_iota(jnp.int32, (tiles, LANES), 1)
    spread = (column // TILE == row).astype(jnp.float32)
    cells = jnp.dot(solid[...].astype(jnp.float32), spread, preferred_element_type=jnp.float32)
    blocks = []
    for tile_row in range(solid.shape[0] // LEVELS):
        part = cells[tile_row * LEVELS : (tile_row + 1) * LEVELS]
        blocks.append(jnp.concatenate([part, part], axis=0))
    return blocks


def flow_blocks(velocity, step, rows):
    blocks = []
    for pair in range(rows // 16):
        both = [velocity[step, axis, pl.ds(16 * pair, 16), :].astype(jnp.float32) for axis in range(3)]
        blocks.append([part[:8] for part in both])
        blocks.append([part[8:] for part in both])
    return blocks


def on_even(axis):
    return lax.rem(lax.axis_index(axis), 2) == 0


class Chosen:
    def __init__(self, choice, yes, no):
        self.choice, self.yes, self.no = choice, yes, no
        self.shape = yes.shape

    def __getitem__(self, index):
        return jnp.where(self.choice, self.yes[index], self.no[index])


def slot_place(slot, group, groups):
    per_block = LANES // groups
    return slot // per_block, (slot % per_block) * groups + group


def insert_column(parts, slot, group, groups, value, edge, ahead):
    part, place = slot_place(slot, group, groups)
    lane = lane_index()
    turned = pltpu.roll(value, (place + ahead - edge) % LANES, 1)
    parts[part] = jnp.where(lane == place + ahead, turned, parts[part])


def copy_kernel(state, velocity, solid, held, flow, tiles, arrived):
    own = pl.ds(GUARD + 8, state.shape[1])
    copies = [
        pltpu.make_async_copy(state, held.at[:, own, :], arrived.at[0]),
        pltpu.make_async_copy(velocity, flow, arrived.at[1]),
        pltpu.make_async_copy(solid, tiles, arrived.at[2]),
    ]
    for copy in copies:
        copy.start()
    for copy in copies:
        copy.wait()


def row_message_kernel(held, flow, tiles, columns_sent, row_first, row_second):
    rows = flow.shape[2]
    even = on_even("gx")
    low_row, high_row = GUARD + 8, GUARD + 8 + rows - LEVELS

    def put(slot, low, high):
        row_first[slot] = jnp.where(even, high, low)
        row_second[slot] = jnp.where(even, low, high)

    for number in range(19):
        put(number, held[number, pl.ds(low_row, LEVELS), :], held[number, pl.ds(high_row, LEVELS), :])
    for step, slot in ((0, FLOW), (1, NEXT)):
        for axis in range(3):
            low = flow[step, axis, pl.ds(0, 16), :].astype(jnp.float32)
            high = flow[step, axis, pl.ds(rows - 16, 16), :].astype(jnp.float32)
            put(slot + axis, low[:LEVELS], high[16 - LEVELS :])
    solid_parts = spread_solid(tiles)
    put(SOLID, solid_parts[0][:LEVELS], solid_parts[-1][:LEVELS])
    for slot in range(5):
        put(
            SECOND + slot,
            held[x_up[slot], pl.ds(low_row + LEVELS, LEVELS), :],
            held[x_down[slot], pl.ds(high_row - LEVELS, LEVELS), :],
        )


def pack_columns(parts, slot, group, groups, value):
    for message, edge, step, ahead, moving in ((parts[0], 0, 1, 1, y_up), (parts[1], LANES - 1, -1, 0, y_down)):
        if message is None:
            continue
        insert_column(message, slot, group, groups, value, edge, ahead)
        second = second_slot(slot, moving)
        if second != slot:
            insert_column(message, second, group, groups, value, edge + step, ahead)


def own_columns_kernel(side, held, velocity, solid, *rest):
    out = rest[-1]
    rows = velocity.shape[2]
    groups = rows // 8 + 2
    solid_parts = spread_solid(solid)
    flow = [flow_blocks(velocity, step, rows) for step in range(2)]
    parts = [None, None]
    parts[side] = [jnp.zeros((8, LANES), jnp.float32) for _ in range(out.shape[0])]
    for group in range(1, groups - 1):
        for slot in range(19):
            pack_columns(parts, slot, group, groups, held[slot, pl.ds(GUARD + 8 * group, 8), :])
        for axis in range(3):
            pack_columns(parts, FLOW + axis, group, groups, flow[0][group - 1][axis])
            pack_columns(parts, NEXT + axis, group, groups, flow[1][group - 1][axis])
        pack_columns(parts, SOLID, group, groups, solid_parts[(group - 1) * 8 // (LEVELS * TILE)])
    for part in range(out.shape[0]):
        out[part] = parts[side][part]


def halo_columns_kernel(groups, own_low, own_high, row_first, row_second, low_out, high_out, ends):
    count = own_high.shape[0]
    even = on_even("gx")
    after, before = Chosen(even, row_first, row_second), Chosen(even, row_second, row_first)
    parts = [[own_low[part] for part in range(count)], [own_high[part] for part in range(count)]]
    for slot in range(SECOND):
        ends[0, slot, pl.ds(LEVELS, LEVELS), :] = before[slot]
        ends[1, slot, pl.ds(0, LEVELS), :] = after[slot]
        if slot == SOLID:
            low_second, high_second = SOLID, SOLID
        else:
            low_second = SECOND + x_down.index(slot) if slot in x_down else None
            high_second = SECOND + x_up.index(slot) if slot in x_up else None
        blank = jnp.zeros((LEVELS, LANES), jnp.float32)
        ends[0, slot, pl.ds(0, LEVELS), :] = blank if low_second is None else before[low_second]
        ends[1, slot, pl.ds(LEVELS, LEVELS), :] = blank if high_second is None else after[high_second]
        pack_columns(parts, slot, 0, groups, ends[0, slot])
        pack_columns(parts, slot, groups - 1, groups, ends[1, slot])
    for part in range(count):
        low_out[part] = parts[0][part]
        high_out[part] = parts[1][part]


def collide(moved, flow, fluid):
    ux, uy, uz = flow
    total = {n: moved[n] + moved[n + 1] for n in range(1, 19, 2)}
    xy, xz, yz = total[7] + total[9], total[11] + total[13], total[15] + total[17]
    axis_x, axis_y, axis_z = 2.0 * total[1], 2.0 * total[3], 2.0 * total[5]
    density = 12.0 * moved[0] + (axis_x + axis_y + axis_z) + (xy + xz + yz)
    pxx = axis_x + xy + xz
    pyy = axis_y + xy + yz
    pzz = axis_z + xz + yz
    pxy = total[7] - total[9]
    pxz = total[11] - total[13]
    pyz = total[15] - total[17]
    dx, dy, dz = momentum(moved)
    vx = pxx * ux + pxy * uy + pxz * uz
    vy = pxy * ux + pyy * uy + pyz * uz
    vz = pxz * ux + pyz * uy + pzz * uz
    speed_sq = ux * ux + uy * uy + uz * uz
    scaled = (relax_rate / 36.0) * fluid
    base = scaled * (density + 1.5 * (speed_sq * density) - 4.5 * (ux * vx + uy * vy + uz * vz))
    scaled3 = 3.0 * scaled
    bx = scaled3 * (dx + 3.0 * vx - ux * density)
    by = scaled3 * (dy + 3.0 * vy - uy * density)
    bz = scaled3 * (dz + 3.0 * vz - uz * density)
    keep = (1.0 - relax_rate) * fluid
    results = [keep * moved[0] + base]
    for number in range(1, 19, 2):
        along = None
        for speed, part in zip(lattice_speeds[number], (bx, by, bz)):
            if speed == 0:
                continue
            if along is None:
                along = part if speed == 1 else -part
            else:
                along = along + part if speed == 1 else along - part
        results.append(keep * moved[number] + (base + along))
        results.append(keep * moved[number + 1] + (base - along))
    return results


def outside(cz):
    level = lax.broadcasted_iota(jnp.int32, (8, LANES), 0) % LEVELS
    return level == (LEVELS - 1 if cz == 1 else 0)


def link_closed(solid_there, cz):
    closed = solid_there > 0.5
    return closed | outside(cz) if cz != 0 else closed


def shift_lanes(value, cy, edge_value):
    lane = lane_index(value.shape[0])
    shifted = pltpu.roll(value, -cy % LANES, 1)
    if edge_value is None:
        return shifted
    return jnp.where(lane == (LANES - 1 if cy == 1 else 0), edge_value, shifted)


def gather_cells(held, shifted, first, solid_rows):
    here = [held[n, pl.ds(first, 8), :] for n in range(19)]
    moved, closed = [here[0]], [None]
    for number in range(1, 19):
        cx, cy, cz = lattice_speeds[number]
        field = held if cy == 0 else shifted
        there = pl.ds(first + LEVELS * cx + cz, 8)
        closed.append(link_closed(solid_rows[cy % 3, there, :], cz))
        bounced = here[opposite_of(number)]
        if cx != 0:
            bounced = bounced + 2.0 * cx
        moved.append(jnp.where(closed[number], bounced, field[number, there, :]))
    return moved, closed


def momentum(moved):
    gap = {n: moved[n] - moved[n + 1] for n in range(1, 19, 2)}
    dx = 2.0 * gap[1] + (gap[7] + gap[9]) + (gap[11] + gap[13])
    dy = 2.0 * gap[3] + (gap[7] - gap[9]) + (gap[15] + gap[17])
    dz = 2.0 * gap[5] + (gap[11] - gap[13]) + (gap[15] - gap[17])
    return dx, dy, dz


def drag_term(moved, flow, fluid):
    return fluid * sum(speed * part for speed, part in zip(flow, momentum(moved)))


def along_link(number, vector):
    total = None
    for axis, speed in enumerate(lattice_speeds[number]):
        if speed == 0:
            continue
        part = vector(axis)
        if total is None:
            total = part if speed == 1 else -part
        else:
            total = total + part if speed == 1 else total - part
    return total


def later_drag(results, closed, weight_here, weight_back):
    term = None
    for number in range(1, 19):
        cx = lattice_speeds[number][0]
        here = along_link(number, lambda axis: weight_here[axis])
        part = jnp.where(closed[opposite_of(number)], -here, weight_back(number)) * results[number]
        if cx != 0:
            part = part + jnp.where(closed[number], (2.0 * cx) * here, 0.0)
        if number < 7:
            part = 2.0 * part
        term = part if term is None else term + part
    return term


def column_reader(groups):
    def column(message, ahead, slot, lane_first, group=0):
        part, place = slot_place(slot, group, groups)
        return pltpu.roll(message[part], (lane_first - place - ahead) % LANES, 1)

    return column


def fill_held(own_held, before, after, held, rows):
    own = GUARD + 8
    near, far = own - LEVELS, own + rows
    for number in range(19):
        for group in range(rows // 8):
            there = pl.ds(own + 8 * group, 8)
            held[number, there, :] = own_held[number, there, :]
        held[number, pl.ds(near, LEVELS), :] = before[number]
        held[number, pl.ds(far, LEVELS), :] = after[number]
        if number in x_down:
            held[number, pl.ds(near - LEVELS, LEVELS), :] = before[SECOND + x_down.index(number)]
        if number in x_up:
            held[number, pl.ds(far + LEVELS, LEVELS), :] = after[SECOND + x_up.index(number)]


def fill_shifted(field, shifted, groups, edge_of):
    for number in y_up + y_down:
        cy = lattice_speeds[number][1]
        for group in range(groups):
            there = pl.ds(GUARD + 8 * group, 8)
            shifted[number, there, :] = shift_lanes(field[number, there, :], cy, edge_of(number, cy, group))


def fill_solid(solid_parts, before, after, solid_rows, groups, edge_of):
    for group in range(groups):
        first = GUARD + 8 * group
        if group in (0, groups - 1):
            halo = before[SOLID] if group == 0 else after[SOLID]
            solid_rows[0, pl.ds(first, LEVELS), :] = halo
            solid_rows[0, pl.ds(first + LEVELS, LEVELS), :] = halo
        else:
            solid_rows[0, pl.ds(first, 8), :] = solid_parts[(group - 1) * 8 // (LEVELS * TILE)]
        value = solid_rows[0, pl.ds(first, 8), :]
        for cy in (1, -1):
            solid_rows[cy % 3, pl.ds(first, 8), :] = shift_lanes(value, cy, edge_of(SOLID, cy, group))


def shift_rows(value, cx, cz):
    if cx != 0:
        upper = lax.broadcasted_iota(jnp.int32, (8, LANES), 0) < LEVELS
        swapped = pltpu.roll(value, LEVELS, 0)
        if cx == 1:
            value = jnp.where(upper, swapped, pltpu.roll(swapped, LANES - 1, 1))
        else:
            value = jnp.where(upper, pltpu.roll(swapped, 1, 1), swapped)
    if cz != 0:
        value = pltpu.roll(value, (-cz) % 8, 0)
    return value


def gather_columns(neighbours):
    here = [neighbours(n, 0) for n in range(19)]
    solid = {cy: neighbours(SOLID, cy) for cy in (0, 1, -1)}
    moved, closed = [here[0]], [None]
    for number in range(1, 19):
        cx, cy, cz = lattice_speeds[number]
        source = shift_rows(here[number] if cy == 0 else neighbours(number, cy), cx, cz)
        closed.append(link_closed(shift_rows(solid[cy], cx, cz), cz))
        moved.append(jnp.where(closed[number], here[opposite_of(number)] + 2.0 * cx, source))
    return moved, closed, solid


def inner_drag_kernel(
    own_held, velocity, solid, row_first, row_second, low, partial, own_blocks,
    held, shifted, solid_rows, weights,
):
    rows = velocity.shape[2]
    groups = rows // 8 + 2
    own = GUARD + 8
    near, far = own - LEVELS, own + rows
    even = on_even("gx")
    after, before = Chosen(even, row_first, row_second), Chosen(even, row_second, row_first)
    lane = lane_index()
    solid_parts = spread_solid(solid)

    def no_edge(slot, cy, group):
        return None

    fill_held(own_held, before, after, held, rows)
    fill_shifted(held, shifted, groups, no_edge)
    fill_solid(solid_parts, before, after, solid_rows, groups, no_edge)

    flow = flow_blocks(velocity, 1, rows)
    for axis in range(3):
        for group in range(rows // 8):
            there = pl.ds(own + 8 * group, 8)
            weights[axis, there, :] = (1.0 - solid_rows[0, there, :]) * flow[group][axis]
        for row, message in ((near, before), (far, after)):
            weights[axis, pl.ds(row, LEVELS), :] = (1.0 - message[SOLID]) * message[NEXT + axis]
        for group in range(groups):
            there = pl.ds(GUARD + 8 * group, 8)
            value = weights[axis, there, :]
            weights[3 + axis, there, :] = shift_lanes(value, 1, None)
            weights[6 + axis, there, :] = shift_lanes(value, -1, None)

    total = jnp.zeros((8, LANES), jnp.float32)
    flow = flow_blocks(velocity, 0, rows)
    for group in range(rows // 8):
        first = own + 8 * group
        moved, closed = gather_cells(held, shifted, first, solid_rows)
        fluid = 1.0 - solid_parts[8 * group // (LEVELS * TILE)]
        results = collide(moved, flow[group], fluid)

        def back(number):
            cx, cy, cz = lattice_speeds[number]
            there = pl.ds(first - LEVELS * cx - cz, 8)
            return along_link(number, lambda axis: weights[3 * (-cy % 3) + axis, there, :])

        here = [weights[axis, pl.ds(first, 8), :] for axis in range(3)]
        total = total + drag_term(moved, flow[group], fluid) + later_drag(results, closed, here, back)
    inside = jnp.logical_and(lane > 0, lane < LANES - 1)
    partial[...] = jnp.where(inside, total, 0.0)

    column = column_reader(groups)
    for slot in range(SECOND):
        own_blocks[slot] = column(low, 1, slot, AFTER_LANE)
    for place, slot in enumerate(ahead_slots):
        here = column(low, 1, slot, BEFORE_LANE)
        ahead = column(low, 1, second_slot(slot, y_up), AFTER_LANE)
        own_blocks[SECOND + place] = jnp.where(lane < AFTER_LANE, here, ahead)


ahead_slots = y_up + [SOLID, NEXT, NEXT + 1, NEXT + 2]


def second_slot(slot, moving):
    if slot in moving:
        return SECOND + moving.index(slot)
    return NEXT_SECOND + slot - NEXT if NEXT <= slot < NEXT + 3 else slot


def halo_lanes(groups, ahead):
    lane = lane_index()
    group = lax.rem(lane + groups - ahead, groups)
    used = jnp.logical_and(lane >= ahead, lane < LANES // groups * groups + ahead)
    return jnp.logical_and(used, group == 0), jnp.logical_and(used, group == groups - 1)


def hand_on_kernel(groups, ahead, columns, *rest):
    out = rest[-1]
    above, _ = halo_lanes(groups, ahead)
    for part in range(out.shape[0]):
        value = columns[part]
        last = pltpu.roll(value, LANES - (groups - 2), 1)
        out[part] = jnp.where(above, last, pltpu.roll(value, groups - 2, 1))


def with_halo_rows(columns, handed_first, handed_second, groups, ahead):
    even = on_even("gx")
    from_before = Chosen(even, handed_second, handed_first)
    from_after = Chosen(even, handed_first, handed_second)
    above, below = halo_lanes(groups, ahead)
    whole = []
    for part in range(handed_first.shape[0]):
        last, first = from_before[part], from_after[part]
        if ahead == 0:
            last = pltpu.roll(last, LANES - (groups - 2), 1)
            first = pltpu.roll(first, groups - 2, 1)
        value = jnp.where(above, last, columns[part])
        whole.append(jnp.where(below, first, value))
    return whole


def edge_drag_kernel(groups, columns, handed_first, handed_second, own_blocks, partial, shared, summed):
    lane = lane_index()
    column = column_reader(groups)
    y_before = with_halo_rows(columns, handed_first, handed_second, groups, 0)

    def neighbours(slot, cy):
        if cy == 1:
            return own_blocks[SECOND + ahead_slots.index(slot)]
        if cy == 0:
            first, second = column(y_before, 0, slot, BEFORE_LANE), own_blocks[slot]
        else:
            first = column(y_before, 0, second_slot(slot, y_down), BEFORE_LANE)
            second = column(y_before, 0, slot, AFTER_LANE)
        return jnp.where(lane < AFTER_LANE, first, second)

    moved, closed, solid_columns = gather_columns(neighbours)
    fluid = {cy: 1.0 - solid_columns[cy] for cy in (0, 1, -1)}
    flow = [neighbours(FLOW + axis, 0) for axis in range(3)]
    results = collide(moved, flow, fluid[0])
    weight = {cy: [fluid[cy] * neighbours(NEXT + axis, cy) for axis in range(3)] for cy in (0, 1, -1)}

    def back(number):
        cx, cy, cz = lattice_speeds[number]
        return shift_rows(along_link(number, lambda axis: weight[-cy][axis]), -cx, -cz)

    term = drag_term(moved, flow, fluid[0]) + later_drag(results, closed, weight[0], back)
    place = jnp.where(lane < AFTER_LANE, lane - BEFORE_LANE, lane - AFTER_LANE)
    inside = jnp.logical_and(place > 0, place < groups - 1)
    total = partial[...] + jnp.where(inside, term, 0.0)
    summed[...] = total
    shared[...] = jnp.broadcast_to(jnp.sum(total), shared.shape)


def main_kernel(
    own_held, velocity, solid, row_first, row_second, columns, handed_first, handed_second,
    columns_after, after_first, after_second, low, high, out, held, shifted, later, solid_rows, row_flow,
):
    rows = velocity.shape[2]
    groups = rows // 8 + 2
    own = GUARD + 8
    near, far = own - LEVELS, own + rows
    even = on_even("gx")
    after, before = Chosen(even, row_first, row_second), Chosen(even, row_second, row_first)
    lane = lane_index()
    solid_parts = spread_solid(solid)
    column = column_reader(groups)
    y_before = with_halo_rows(columns, handed_first, handed_second, groups, 0)
    y_after = with_halo_rows(columns_after, after_first, after_second, groups, 1)

    def edge_of(slot, cy, group):
        if cy == 1:
            return column(y_after, 1, slot, LANES - 1, group)
        return column(y_before, 0, slot, 0, group)

    fill_held(own_held, before, after, held, rows)
    fill_shifted(held, shifted, groups, edge_of)
    fill_solid(solid_parts, before, after, solid_rows, groups, edge_of)
    for slot, place in ((FLOW, 0), (FLOW + 1, 1), (FLOW + 2, 2), (SOLID, 3)):
        row_flow[place, pl.ds(0, LEVELS), :] = before[slot]
        row_flow[place, pl.ds(LEVELS, LEVELS), :] = after[slot]

    def both_rows(field, index, shift):
        ends = [field[index, pl.ds(place + shift, LEVELS), :] for place in (near, far)]
        return jnp.concatenate(ends, axis=0)

    here = [both_rows(held, n, 0) for n in range(19)]
    moved = [here[0]]
    for number in range(1, 19):
        cx, cy, cz = lattice_speeds[number]
        shift = LEVELS * cx + cz
        source = both_rows(held if cy == 0 else shifted, number, shift)
        closed = link_closed(both_rows(solid_rows, cy % 3, shift), cz)
        moved.append(jnp.where(closed, here[opposite_of(number)] + 2.0 * cx, source))
    row_results = collide(moved, [row_flow[axis] for axis in range(3)], 1.0 - row_flow[3])

    def neighbours(slot, cy):
        beyond = slot if cy == 0 or slot == SOLID else SECOND + (y_up if cy == 1 else y_down).index(slot)
        if cy == 1:
            first, second = column(low, 1, slot, BEFORE_LANE), column(y_after, 1, beyond, AFTER_LANE)
        elif cy == -1:
            first, second = column(y_before, 0, beyond, BEFORE_LANE), column(high, 0, slot, AFTER_LANE)
        else:
            first, second = column(y_before, 0, slot, BEFORE_LANE), column(y_after, 1, slot, AFTER_LANE)
        return jnp.where(lane < AFTER_LANE, first, second)

    moved, _, solid_columns = gather_columns(neighbours)
    column_flow = [neighbours(FLOW + axis, 0) for axis in range(3)]
    column_results = collide(moved, column_flow, 1.0 - solid_columns[0])

    flow = flow_blocks(velocity, 0, rows)
    for group in range(rows // 8):
        first = own + 8 * group
        moved, _ = gather_cells(held, shifted, first, solid_rows)
        results = collide(moved, flow[group], 1.0 - solid_parts[8 * group // (LEVELS * TILE)])
        for number in range(19):
            later[number, pl.ds(first, 8), :] = results[number]
    for number in x_down:
        later[number, pl.ds(near, LEVELS), :] = row_results[number][:LEVELS]
    for number in x_up:
        later[number, pl.ds(far, LEVELS), :] = row_results[number][LEVELS:]

    def later_edge(number, cy, group):
        shift = LANES - 1 - AFTER_LANE - group if cy == 1 else -BEFORE_LANE - group
        return pltpu.roll(column_results[number], shift % LANES, 1)

    fill_shifted(later, shifted, groups, later_edge)

    flow = flow_blocks(velocity, 1, rows)
    for group in range(rows // 8):
        first = 8 * group
        moved, _ = gather_cells(later, shifted, own + first, solid_rows)
        results = collide(moved, flow[group], 1.0 - solid_parts[first // (LEVELS * TILE)])
        for number in range(19):
            out[number, pl.ds(first, 8), :] = results[number]


def swap_pairs(first, second, axis):
    count = lax.axis_size(axis)
    inside = [(i, i ^ 1) for i in range(count)]
    across = [(i, (i + 1) % count if i % 2 == 1 else (i - 1) % count) for i in range(count)]
    second = lax.ppermute(second, axis, across)
    return lax.ppermute(first, axis, inside), second


def per_device(adjoint_in, velocity, solid_tiles, link_blocked):
    rows_x, levels, rows_y = adjoint_in.shape[1:]
    rows = rows_x * levels
    padded = rows + 16 + 2 * GUARD
    groups = rows // 8 + 2
    parts = -(-COLUMN_QUANTITIES // (LANES // groups))
    state = adjoint_in.reshape(19, rows, rows_y)
    flow = velocity.reshape(STEPS, 3, rows, rows_y)
    solid = solid_tiles.reshape(-1, solid_tiles.shape[2])

    def shape_of(*sizes):
        return jax.ShapeDtypeStruct(sizes, jnp.float32)

    params = pltpu.CompilerParams(vmem_limit_bytes=16 * 1024 * 1024)
    anywhere = pl.BlockSpec(memory_space=pl.ANY)
    held, flow, tiles = pl.pallas_call(
        copy_kernel,
        out_shape=(
            pltpu.VMEM((19, padded, rows_y), jnp.float32),
            pltpu.VMEM(flow.shape, flow.dtype),
            pltpu.VMEM(solid.shape, solid.dtype),
        ),
        in_specs=[anywhere] * 3,
        out_specs=(vmem,) * 3,
        scratch_shapes=[pltpu.SemaphoreType.DMA((3,))],
        compiler_params=params,
    )(*(pltpu.with_memory_space_constraint(value, pltpu.HBM) for value in (state, flow, solid)))
    def pack(side, size, *later_than):
        return pl.pallas_call(
            functools.partial(own_columns_kernel, side),
            out_shape=shape_of(size, 8, rows_y),
            in_specs=[vmem] * (3 + len(later_than)),
            out_specs=vmem,
            compiler_params=params,
            cost_estimate=pl.CostEstimate(flops=2_000_000, bytes_accessed=1_000_000, transcendentals=0),
        )(held, flow, tiles, *later_than)

    own_high = pack(1, parts)
    row_sent = pl.pallas_call(
        row_message_kernel,
        out_shape=(pltpu.VMEM((QUANTITIES, levels, rows_y), jnp.float32),) * 2,
        in_specs=[vmem] * 4,
        out_specs=(vmem,) * 2,
        compiler_params=params,
    )(held, flow, tiles, own_high)
    row_got = swap_pairs(*row_sent, "gx")
    own_low = pack(0, 16, row_sent[0])
    own_columns = own_low, own_high
    low, high = pl.pallas_call(
        functools.partial(halo_columns_kernel, groups),
        out_shape=(shape_of(parts, 8, rows_y),) * 2,
        in_specs=[vmem] * 4,
        out_specs=(vmem,) * 2,
        scratch_shapes=[pltpu.VMEM((2, SECOND, 8, rows_y), jnp.float32)],
        compiler_params=params,
    )(*own_columns, *row_got)
    size = lax.axis_size("gy")
    y_before = lax.ppermute(own_columns[1], "gy", [(i, (i + 1) % size) for i in range(size)])
    def hand_on(columns, ahead, *later_than):
        handed = pl.pallas_call(
            functools.partial(hand_on_kernel, groups, ahead),
            out_shape=shape_of(parts, 8, rows_y),
            in_specs=[vmem] * (1 + len(later_than)),
            out_specs=vmem,
            compiler_params=params,
            cost_estimate=pl.CostEstimate(flops=10_000_000_000, bytes_accessed=100_000, transcendentals=0),
        )(columns, *later_than)
        return swap_pairs(handed, handed, "gx")

    handed = swap_pairs(y_before, y_before, "gx")
    y_after = lax.ppermute(own_columns[0], "gy", [((i + 1) % size, i) for i in range(size)])
    count = lax.axis_size("gx") * size
    field = pltpu.VMEM((19, padded, rows_y), jnp.float32)
    solid_field = pltpu.VMEM((3, padded, rows_y), jnp.float32)
    partial, own_blocks = pl.pallas_call(
        inner_drag_kernel,
        out_shape=(
            pltpu.VMEM((8, rows_y), jnp.float32),
            pltpu.VMEM((SECOND + len(ahead_slots), 8, rows_y), jnp.float32),
        ),
        in_specs=[vmem] * 6,
        out_specs=(vmem,) * 2,
        scratch_shapes=[field, field, solid_field, pltpu.VMEM((9, padded, rows_y), jnp.float32)],
        compiler_params=params,
        cost_estimate=pl.CostEstimate(flops=20_000_000_000, bytes_accessed=1_000_000, transcendentals=0),
    )(held, flow, tiles, *row_got, low)
    own, summed = pl.pallas_call(
        functools.partial(edge_drag_kernel, groups),
        out_shape=(shape_of(count, 1, rows_y), pltpu.VMEM((8, rows_y), jnp.float32)),
        in_specs=[vmem] * 5,
        out_specs=(vmem,) * 2,
        compiler_params=params,
        cost_estimate=pl.CostEstimate(flops=1_000_000, bytes_accessed=1_000_000, transcendentals=0),
    )(y_before, *handed, own_blocks, partial)
    handed_after = hand_on(y_after, 1, summed)
    shared = lax.all_to_all(own, ("gx", "gy"), split_axis=0, concat_axis=0, tiled=True)
    result = pl.pallas_call(
        main_kernel,
        out_shape=shape_of(19, rows, rows_y),
        in_specs=[vmem] * 13,
        out_specs=vmem,
        scratch_shapes=[field, field, field, solid_field, pltpu.VMEM((4, 8, rows_y), jnp.float32)],
        compiler_params=params,
        cost_estimate=pl.CostEstimate(flops=1_000_000, bytes_accessed=1_000_000, transcendentals=0),
    )(held, flow, tiles, *row_got, y_before, *handed, y_after, *handed_after, low, high)
    cell_count = rows * rows_y * count
    scale = drag_factor / math.sqrt(cell_count) * 3.0 / 36.0
    total = jnp.sum(shared[:, 0, 0])
    return (result.reshape(adjoint_in.shape), (-scale * total).reshape(1))


def solution(mesh):
    placed = (
        P(None, "gx", None, "gy"),
        P(None, None, "gx", None, "gy"),
        P("gx", None, "gy"),
        P(None, "gx", None, "gy"),
    )
    return jax.shard_map(
        per_device,
        mesh=mesh,
        in_specs=placed,
        out_specs=(P(None, "gx", None, "gy"), P()),
        check_vma=False,
    )
```
